32 devices in a mesh: seq: 8 (over z, y), mp: 4 (over x, core).
Axes of the slice: x: 2, y: 2, z: 4, core: 2. Of those that a mesh axis runs over, the one named last changes fastest.
Arguments:
- block_input: bfloat16 [2, 16384, 512], P(None, ('seq', 'mp')), may hold values from -6 to 6
- cotangent: bfloat16 [2, 16384, 512], P(None, 'seq'), may hold values from -6 to 6
- span_offset: int32 [2], replicated, may hold values from 1 to 127
- doc_lengths: int32 [2, 8], replicated, may hold values from 1 to 15360, 16384 in all within a row
- ln1_gain: float32 [512], replicated, may hold values from 0.5 to 1.5
- ln1_bias: float32 [512], replicated, may hold values from -3 to 3
- w_query: bfloat16 [512, 512], P('seq', 'mp'), may hold values from -0.25 to 0.25
- w_key: bfloat16 [512, 512], P('seq', 'mp'), may hold values from -0.25 to 0.25
- w_value: bfloat16 [512, 512], P('seq', 'mp'), may hold values from -0.25 to 0.25
- query_bias: float32 [512], replicated, may hold values from -3 to 3
- value_bias: float32 [512], replicated, may hold values from -3 to 3
- w_out: bfloat16 [512, 512], P('mp', 'seq'), may hold values from -2 to 2
- out_bias: float32 [512], replicated, may hold values from -3 to 3
- ln2_gain: float32 [512], replicated, may hold values from 0.5 to 1.5
- ln2_bias: float32 [512], replicated, may hold values from -3 to 3
- w_up: bfloat16 [512, 2048], P('seq', 'mp'), may hold values from -0.25 to 0.25
- up_bias: float32 [2048], replicated, may hold values from -3 to 3
- w_down: bfloat16 [2048, 512], P('mp', 'seq'), may hold values from -0.75 to 0.75
- down_bias: float32 [512], replicated, may hold values from -3 to 3
Outputs:
- result: bfloat16 [2, 16384, 512], P(None, ('seq', 'mp'))
- input_grad: float32 [2, 16384, 512], P(None, ('seq', 'mp'))
- grad_ln1_gain: float32 [512], replicated
- grad_ln1_bias: float32 [512], replicated
- grad_w_query: float32 [512, 512], P('seq', 'mp')
- grad_w_key: float32 [512, 512], P('seq', 'mp')
- grad_w_value: float32 [512, 512], P('seq', 'mp')
- grad_query_bias: float32 [512], replicated
- grad_value_bias: float32 [512], replicated
- grad_w_out: float32 [512, 512], P('mp', 'seq')
- grad_out_bias: float32 [512], replicated
- grad_ln2_gain: float32 [512], replicated
- grad_ln2_bias: float32 [512], replicated
- grad_w_up: float32 [512, 2048], P('seq', 'mp')
- grad_up_bias: float32 [2048], replicated
- grad_w_down: float32 [2048, 512], P('mp', 'seq')
- grad_down_bias: float32 [512], replicated
The draws below stay inside these ranges and needn't reach their ends.
Inputs may be any that keep to these rules, and one draw needn't show every extreme that they name: `doc_lengths`: each row's 8 lengths add up to 16384, and one document of each row has exactly 15360 positions.
All inputs are finite; a program needn't handle non-finite values.
Results may differ from the reference program's by a relative error of at most 0.012.
The reference program's roundings to bfloat16 on the way count: a program that leaves them out, or rounds other values in their place, can miss the bound.
Values may be sent and summed in bfloat16 or wider, within the bound.
No kernel may reach another device: no remote copies, remote signals or barrier semaphores. Data moves between devices by JAX's collectives and lax.ppermute only.
A program may use at most 128 MiB of HBM per device.

```python
import math
import jax
import jax.numpy as jnp
import numpy as np
from jax import lax

D = 512
HEADS = 8
FF = 2048
HEAD_DIM = 64
SPAN = 128
QBLOCK = 512
NDOC = 8
TOK_DEV = 2048
MICRO = 2
SEQ_LEN = 16384


def draw_span_offset(key, part):
    key = jax.random.fold_in(key, 11)
    key_base, key_pick = jax.random.split(key)
    offsets = jax.random.randint(key_base, (MICRO,), 1, SPAN, dtype=jnp.int32)
    ranking = jax.random.permutation(key_pick, MICRO)
    indices = jnp.arange(MICRO, dtype=jnp.int32)
    offsets = jnp.where(indices == ranking[0], 1, offsets)
    return jnp.where(indices == ranking[1], SPAN - 1, offsets).astype(jnp.int32)


def block_levels(key, shape, shards, low, largest):
    level, own = 1.0, jax.random.fold_in(key, 6)
    for dim, shards_of in shards:
        steps = jnp.exp(jax.random.uniform(jax.random.fold_in(own, dim), (shards_of,), jnp.float32, low / len(shards), largest / len(shards)))
        level = level * jnp.repeat(steps, shape[dim] // shards_of).reshape([-1 if axis == dim else 1 for axis in range(len(shape))])
    return level


def split_up(count, total, limit, slope):
    portions = [(1 << 20) // math.isqrt(rank ** slope) + 1 for rank in range(2, count + 1)]
    rest, given = total - limit - (count - 1), [1] * (count - 1)
    while rest > 0:
        free = [i for i in range(count - 1) if given[i] < limit]
        whole, remaining = sum([portions[i] for i in free]), rest
        for i in free:
            more = min(limit - given[i], max(1, remaining * portions[i] // whole), rest)
            given[i] = given[i] + more
            rest = rest - more
    return np.array([limit] + given)


def uneven(rng, count, total, most, slope):
    if count == 2:
        one = jax.random.randint(rng, (), max(1, total - most), min(most, total - 1) + 1)
        return jnp.stack([one, total - one])
    sizes = jnp.asarray(split_up(count, total, most, slope), jnp.int32)
    twos = (count - 1) // 2
    giver, receiver = sizes[1:1 + 2 * twos:2], sizes[2:2 + 2 * twos:2]
    margin = jnp.minimum(giver - 1, most - receiver)
    shifted = jax.random.randint(jax.random.fold_in(rng, 1), (twos,), 0, 1 << 20) % (margin + 1)
    sizes = sizes.at[1:1 + 2 * twos:2].set(giver - shifted).at[2:2 + 2 * twos:2].set(receiver + shifted)
    return sizes[jax.random.permutation(jax.random.fold_in(rng, 2), count)]


def normal_values(stream_key, dims, width, limit, shards=(), kind=jnp.bfloat16):
    loudness = block_levels(stream_key, dims, shards, -0.22, 0.18) if shards else 1.0
    values = jax.random.normal(stream_key, dims, jnp.float32) * width * loudness
    return jnp.minimum(jnp.maximum(values, -limit), limit).astype(kind)


def setup_inputs(seed: int = 0) -> dict:
    seeds = jax.random.split(jax.random.key(seed), 20)
    return {
        "block_input": normal_values(seeds[0], (MICRO, SEQ_LEN, D), 1.0, 6.0, ((1, 32),)),
        "cotangent": normal_values(seeds[1], (MICRO, SEQ_LEN, D), 1.0, 6.0, ((1, 8),)),
        "span_offset": draw_span_offset(jax.random.fold_in(seeds[19], 71), 0),
        "doc_lengths": jax.vmap(lambda own: uneven(own, NDOC, SEQ_LEN, SEQ_LEN - TOK_DEV // 2, 2))(jax.random.split(seeds[3], MICRO)).reshape((MICRO, NDOC)).astype(jnp.int32),
        "ln1_gain": jnp.clip(1.0 + 0.1 * jax.random.normal(seeds[4], (D,), jnp.float32), 0.5, 1.5),
        "ln1_bias": normal_values(seeds[5], (D,), 0.5, 3.0, (), jnp.float32),
        "w_query": normal_values(seeds[6], (D, D), D ** -0.5, 0.25, ((0, 8), (1, 4))),
        "w_key": normal_values(seeds[7], (D, D), D ** -0.5, 0.25, ((0, 8), (1, 4))),
        "w_value": normal_values(seeds[8], (D, D), D ** -0.5, 0.25, ((0, 8), (1, 4))),
        "query_bias": normal_values(seeds[9], (D,), 0.5, 3.0, (), jnp.float32),
        "value_bias": normal_values(seeds[10], (D,), 0.5, 3.0, (), jnp.float32),
        "w_out": normal_values(seeds[11], (D, D), (D // 64) ** -0.5, 2.0, ((0, 4), (1, 8))),
        "out_bias": normal_values(seeds[12], (D,), 0.5, 3.0, (), jnp.float32),
        "ln2_gain": jnp.clip(1.0 + 0.1 * jax.random.normal(seeds[13], (D,), jnp.float32), 0.5, 1.5),
        "ln2_bias": normal_values(seeds[14], (D,), 0.5, 3.0, (), jnp.float32),
        "w_up": normal_values(seeds[15], (D, FF), D ** -0.5, 0.25, ((0, 8), (1, 4))),
        "up_bias": normal_values(seeds[16], (FF,), 0.5, 3.0, (), jnp.float32),
        "w_down": normal_values(seeds[17], (FF, D), (FF // 32) ** -0.5, 0.75, ((0, 4), (1, 8))),
        "down_bias": normal_values(seeds[18], (D,), 0.5, 3.0, (), jnp.float32),
    }


EPSILON = 1e-05
NEGATIVE = -1e+30

@jax.custom_vjp
def low(v):
    return lax.optimization_barrier(v.astype(jnp.bfloat16)).astype(jnp.float32)

@jax.custom_vjp
def low_back(v):
    return v

def low_keep(v):
    return (low(v), None)

def low_pass(kept, grad):
    return (grad,)

def back_keep(v):
    return (v, None)

def back_low(kept, grad):
    return (low(grad),)
low.defvjp(low_keep, low_pass)
low_back.defvjp(back_keep, back_low)

def matmul(left, right):
    return jnp.dot(left, right, precision=lax.Precision.HIGHEST, preferred_element_type=jnp.float32)

def einsum_high(form, left, right):
    return jnp.einsum(form, left, right, precision=lax.Precision.HIGHEST, preferred_element_type=jnp.float32)

def normalize(inputs, norm_gain, norm_shift):
    row_mean = lax.optimization_barrier(jnp.mean(inputs, axis=-1, keepdims=True))
    centred = inputs - row_mean
    variance = lax.optimization_barrier(jnp.mean(centred * centred, axis=-1, keepdims=True))
    return centred * lax.rsqrt(variance + EPSILON) * norm_gain + norm_shift

def doc_index(positions, doc_ends):
    return lax.optimization_barrier(jnp.sum((doc_ends[None, :] <= positions[:, None]).astype(jnp.int32), axis=1))

def span_index(positions, offset):
    return (positions - offset + SPAN) // SPAN

def block_masks(query_pos, key_pos, offset, doc_ends, summary_docs):
    query_doc = doc_index(query_pos, doc_ends)
    key_doc = doc_index(key_pos, doc_ends)
    query_span = span_index(query_pos, offset)
    key_span = span_index(key_pos, offset)
    local_ok = (key_pos[None, :] >= 0) & (key_pos[None, :] <= query_pos[:, None])
    local_ok = local_ok & (key_span[None, :] == query_span[:, None]) & (key_doc[None, :] == query_doc[:, None])
    summary_ids = jnp.arange(summary_docs.shape[0], dtype=jnp.int32)
    summary_ok = (summary_ids[None, :] < query_span[:, None]) & (summary_docs[None, :] == query_doc[:, None])
    return (local_ok, summary_ok)

def row_forward(inputs, offset, doc_ends, params):
    ln1_gain, ln1_bias, w_query, w_key, w_value, query_bias, value_bias, w_out, out_bias, ln2_gain, ln2_bias, w_up, up_bias, w_down, down_bias = params
    length = inputs.shape[0]
    summary_count = length // SPAN
    score_scale = 1.0 / math.sqrt(HEAD_DIM)
    normed_one = low(normalize(inputs, ln1_gain, ln1_bias))
    queries = low(low_back(matmul(normed_one, w_query) + query_bias))
    key_rows = low(low_back(matmul(normed_one, w_key)))
    value_rows = low(low_back(matmul(normed_one, w_value) + value_bias))
    leading = jnp.zeros((SPAN, D), jnp.float32)
    pad_keys = jnp.concatenate((leading, key_rows), axis=0)
    pad_values = jnp.concatenate((leading, value_rows), axis=0)
    span_pos = offset - SPAN + jnp.arange(length, dtype=jnp.int32)
    span_doc = doc_index(span_pos, doc_ends).reshape(summary_count, SPAN)
    summary_ends = offset - 1 + SPAN * jnp.arange(summary_count, dtype=jnp.int32)
    summary_docs = doc_index(summary_ends, doc_ends)
    group_member = ((span_pos.reshape(summary_count, SPAN) >= 0) & (span_doc == summary_docs[:, None])).astype(jnp.float32)
    inv_count = lax.rsqrt(lax.optimization_barrier(jnp.sum(group_member, axis=1)))
    span_keys = lax.dynamic_slice_in_dim(pad_keys, offset, length, 0).reshape(summary_count, SPAN, D)
    span_values = lax.dynamic_slice_in_dim(pad_values, offset, length, 0).reshape(summary_count, SPAN, D)
    summ_keys = low(einsum_high('js,jsd->jd', group_member, span_keys) * inv_count[:, None])
    summ_values = low(einsum_high('js,jsd->jd', group_member, span_values) * inv_count[:, None])
    summ_keys = summ_keys.reshape(summary_count, HEADS, HEAD_DIM)
    summ_values = summ_values.reshape(summary_count, HEADS, HEAD_DIM)

    def attend(block_id):
        first_row = block_id * QBLOCK
        block_queries = lax.dynamic_slice_in_dim(queries, first_row, QBLOCK, 0).reshape(QBLOCK, HEADS, HEAD_DIM)
        block_keys = lax.dynamic_slice_in_dim(pad_keys, first_row, QBLOCK + SPAN, 0).reshape(QBLOCK + SPAN, HEADS, HEAD_DIM)
        block_values = lax.dynamic_slice_in_dim(pad_values, first_row, QBLOCK + SPAN, 0).reshape(QBLOCK + SPAN, HEADS, HEAD_DIM)
        query_pos = first_row + jnp.arange(QBLOCK, dtype=jnp.int32)
        key_pos = first_row - SPAN + jnp.arange(QBLOCK + SPAN, dtype=jnp.int32)
        local_ok, summary_ok = block_masks(query_pos, key_pos, offset, doc_ends, summary_docs)
        local_scores = jnp.where(local_ok[None], low_back(einsum_high('qhd,khd->hqk', block_queries, block_keys) * score_scale), NEGATIVE)
        summary_scores = jnp.where(summary_ok[None], low_back(einsum_high('qhd,jhd->hqj', block_queries, summ_keys) * score_scale), NEGATIVE)
        joint = jnp.concatenate((local_scores, summary_scores), axis=-1)
        row_top = lax.optimization_barrier(jnp.max(joint, axis=-1, keepdims=True))
        exp_scores = jnp.exp(joint - row_top)
        probs = low(exp_scores / lax.optimization_barrier(jnp.sum(exp_scores, axis=-1, keepdims=True)))
        mixed = einsum_high('hqk,khd->qhd', probs[:, :, :QBLOCK + SPAN], block_values)
        mixed = mixed + einsum_high('hqj,jhd->qhd', probs[:, :, QBLOCK + SPAN:], summ_values)
        return mixed.reshape(QBLOCK, D)
    blocks_out = lax.map(jax.checkpoint(attend), jnp.arange(length // QBLOCK, dtype=jnp.int32))
    attended = low(low_back(blocks_out.reshape(length, D)))
    resid_mid = inputs + low_back(matmul(attended, w_out) + out_bias)
    second_normed_rows = low(normalize(resid_mid, ln2_gain, ln2_bias))
    up_proj = low_back(matmul(second_normed_rows, w_up) + up_bias)
    activated = low(jax.nn.gelu(up_proj, approximate=True))
    return resid_mid + low_back(matmul(activated, w_down) + down_bias)

def reference(block_input, cotangent, span_offset, doc_lengths, ln1_gain, ln1_bias, w_query, w_key, w_value, query_bias, value_bias, w_out, out_bias, ln2_gain, ln2_bias, w_up, up_bias, w_down, down_bias):
    params = tuple((weight.astype(jnp.float32) for weight in (ln1_gain, ln1_bias, w_query, w_key, w_value, query_bias, value_bias, w_out, out_bias, ln2_gain, ln2_bias, w_up, up_bias, w_down, down_bias)))

    def one_row(total_values, batch_slot):
        inputs, grad_out, offset, lengths = batch_slot
        doc_ends = jnp.cumsum(lengths).astype(jnp.int32)

        def forward(inputs_f, params_f):
            return row_forward(inputs_f, offset, doc_ends, params_f)
        output, pullback = jax.vjp(forward, inputs.astype(jnp.float32), params)
        grad_in, grad_params = pullback(grad_out.astype(jnp.float32))
        total_values = jax.tree.map(jnp.add, total_values, grad_params)
        return (total_values, (output.astype(jnp.bfloat16), grad_in))
    zeros_init = tuple((jnp.zeros_like(weight) for weight in params))
    total_values, (outputs, grad_inputs) = lax.scan(one_row, zeros_init, (block_input, cotangent, span_offset, doc_lengths))
    return (outputs, grad_inputs, total_values[0], total_values[1], total_values[2], total_values[3], total_values[4], total_values[5], total_values[6], total_values[7], total_values[8], total_values[9], total_values[10], total_values[11], total_values[12], total_values[13], total_values[14])
```

```python
from functools import partial
import math

import jax
import jax.numpy as jnp
from jax import lax
from jax.experimental import pallas as pl
from jax.experimental.pallas import tpu as pltpu
from jax.sharding import PartitionSpec as P

D = 512
FF = 2048
HEAD_DIM = 64
SPAN = 128
LANES = 128
EPSILON = 1e-05
NEGATIVE = -1e30
SCALE = 1.0 / math.sqrt(HEAD_DIM)
F32 = jnp.float32
BF16 = jnp.bfloat16
AXES = ("seq", "mp")
MIB = 1 << 20
VMEM = pl.BlockSpec(memory_space=pltpu.VMEM)
SMEM = pl.BlockSpec(memory_space=pltpu.SMEM)
ANY = pl.BlockSpec(memory_space=pl.ANY)


def dot(left, right):
    return lax.dot_general(left, right, (((1,), (0,)), ((), ())), preferred_element_type=F32)


def dot_cols(left, right):
    return lax.dot_general(left, right, (((1,), (1,)), ((), ())), preferred_element_type=F32)


def unit(rows):
    centred = rows - jnp.mean(rows, axis=-1, keepdims=True)
    inverse = lax.rsqrt(jnp.mean(centred * centred, axis=-1, keepdims=True) + EPSILON)
    return centred * inverse, inverse


def unit_back(grad, hat, inverse):
    shift = jnp.mean(grad, axis=-1, keepdims=True)
    slope = jnp.mean(grad * hat, axis=-1, keepdims=True)
    return (grad - shift - hat * slope) * inverse


def row_info(info, mi):
    return info[0], info[1 + mi], [info[3 + 8 * mi + c] for c in range(8)]


def doc_start(positions, ends):
    start = jnp.zeros_like(positions)
    for end in ends:
        start = jnp.where(positions >= end, end, start)
    return start


def summary_range(summary_ids, offset, ends):
    last = offset - 1 + SPAN * summary_ids
    first = jnp.maximum(doc_start(last, ends), last - (SPAN - 1))
    return first, last


def iota(shape, dim):
    return lax.broadcasted_iota(jnp.int32, shape, dim)


def summary_kernel(info, x_ref, out_ref):
    rows = x_ref.shape[1]
    sums = []
    for mi in range(2):
        dev, offset, ends = row_info(info, mi)
        first, last = summary_range(dev * (rows // SPAN) + iota((8, 1), 0), offset, ends)
        pos = dev * rows + iota((1, rows), 1)
        member = jnp.where((pos >= first) & (pos <= last), 1.0, 0.0).astype(BF16)
        hat, _ = unit(x_ref[mi].astype(F32))
        high = hat.astype(BF16)
        rest = (hat - high.astype(F32)).astype(BF16)
        total = dot(member, high) + dot(member, rest)
        sums.append(total * lax.rsqrt((last - first + 1).astype(F32)))
    both = jnp.concatenate(sums, axis=0).astype(BF16)
    for lane in range(D // LANES):
        out_ref[16 * lane : 16 * lane + 16, :] = both[:, lane * LANES : (lane + 1) * LANES]


def picker(by):
    return jnp.where(iota((SPAN, 2 * SPAN), 1) == iota((SPAN, 2 * SPAN), 0) + by, 1.0, 0.0).astype(BF16)


def pick_rows(pick, rows):
    high = rows.astype(BF16)
    return dot(pick, high) + dot(pick, (rows - high.astype(F32)).astype(BF16))


def fill_masks(info, bias_ref, tiles, summaries, length):
    for mi in range(2):
        dev, offset, ends = row_info(info, mi)
        ends_col = offset - 1 + SPAN * iota((summaries, 1), 0)
        for t in range(tiles):
            base = SPAN * (dev * tiles + t) + offset - SPAN
            qpos = base + iota((1, SPAN), 1)
            qpos = jnp.where(qpos < 0, qpos + length, qpos)
            kpos = base + iota((SPAN, 1), 0)
            kpos = jnp.where(kpos < 0, kpos + length, kpos)
            span_first = jnp.where(qpos < base, base, jnp.where(qpos >= base + SPAN, base + length, base))
            doc_first = doc_start(qpos, ends)
            local_ok = (kpos >= jnp.maximum(doc_first, span_first)) & (kpos <= qpos)
            summary_ok = (ends_col >= doc_first) & (ends_col < span_first)
            bias_ref[mi, t, 0:SPAN, :] = jnp.where(local_ok, 0.0, NEGATIVE)
            bias_ref[mi, t, SPAN : SPAN + summaries, :] = jnp.where(summary_ok, 0.0, NEGATIVE)


def split_heads(pair):
    low = iota(pair.shape, 1) < HEAD_DIM
    zero = jnp.zeros_like(pair)
    return jnp.concatenate((jnp.where(low, pair, zero), jnp.where(low, zero, pair)), axis=0)


def join_heads(turned):
    half = turned.shape[1] // 2
    return jnp.concatenate((turned[:HEAD_DIM, :half], turned[HEAD_DIM:, half:]), axis=0).T


def attend_kernel(
    apart, info, block_of, row_of, slots_ref, x_ref, left_ref, gain, shift, qbias, vbias, near_ref, far_ref, *refs
):
    if apart:
        all_ref, *refs = refs
    (xs_ref, nb_ref, q_ref, k_ref, v_ref, att_ref, ks_ref, vs_ref, lse_ref, sums_ref, w_ref) = refs[:11]
    stack_ref, wide_ref, bias_ref, sem = refs[11:]
    rows = x_ref.shape[1]
    tiles = rows // SPAN
    summaries = ks_ref.shape[1]
    half, shard, _ = near_ref.shape
    length = summaries * SPAN

    def place(d, carry):
        for source, slot in ((near_ref, d), (far_ref, half + d)):
            first = pl.multiple_of(row_of[slot] * shard, 16)
            pltpu.make_async_copy(
                source.at[d, :, 0:384], w_ref.at[block_of[slot], pl.ds(first, shard), :], sem.at[0]
            ).start()
            if not apart:
                pltpu.make_async_copy(
                    source.at[d, 0:64, 384:512], stack_ref.at[slot], sem.at[1]
                ).start()
        return carry

    lax.fori_loop(0, half, place, 0)
    if apart:
        pltpu.make_async_copy(all_ref, stack_ref, sem.at[1]).start()
    fill_masks(info, bias_ref, tiles, summaries, length)
    for mi in range(2):
        wide_ref[0:SPAN, :] = left_ref[mi]
        wide_ref[SPAN : SPAN + rows, :] = x_ref[mi]
        pick = picker(info[1 + mi])
        for t in range(tiles):
            rolled = dot(pick, wide_ref[t * SPAN : (t + 2) * SPAN, :])
            xs_ref[mi, t * SPAN : (t + 1) * SPAN, :] = rolled.astype(BF16)
            hat, _ = unit(rolled)
            nb_ref[mi, t * SPAN : (t + 1) * SPAN, :] = (hat * gain[...] + shift[...]).astype(BF16)
    pltpu.make_async_copy(stack_ref, stack_ref, sem.at[1]).wait()
    pltpu.make_async_copy(w_ref, w_ref, sem.at[0]).wait()
    for mi in range(2):
        _, offset, ends = row_info(info, mi)
        first, last = summary_range(iota((summaries, 1), 0), offset, ends)
        root = jnp.sqrt((last - first + 1).astype(F32))
        for base in range(0, stack_ref.shape[0], 32):
            named = slots_ref[mi : mi + 1, 16 * base : 16 * base + 512]
            pick = jnp.where(iota((summaries, 1), 0) == named, 1.0, 0.0).astype(BF16)
            for lane in range(D // LANES):
                lanes = slice(lane * LANES, (lane + 1) * LANES)
                piece = stack_ref[base : base + 32, 16 * lane : 16 * lane + 16, :].reshape(512, LANES)
                found = dot(pick, piece)
                sums_ref[mi, :, lanes] = found if base == 0 else sums_ref[mi, :, lanes] + found
        summed = sums_ref[mi] * gain[...] + root * shift[...]
        high = summed.astype(BF16)
        rest = (summed - high.astype(F32)).astype(BF16)
        normed = nb_ref[mi]
        for m in range(4):
            lanes = slice(m * LANES, (m + 1) * LANES)
            w = w_ref[m]
            projected = dot(normed, w)
            q_ref[mi, :, lanes] = (projected[:, :128] + qbias[:, lanes]).astype(BF16)
            k_ref[mi, :, lanes] = projected[:, 128:256].astype(BF16)
            v_ref[mi, :, lanes] = (projected[:, 256:] + vbias[:, lanes]).astype(BF16)
            w_kv = w[:, 128:]
            pooled = dot(high, w_kv) + dot(rest, w_kv)
            ks_ref[mi, :, lanes] = pooled[:, :128].astype(BF16)
            vs_ref[mi, :, lanes] = (pooled[:, 128:] + root * vbias[:, lanes]).astype(BF16)

    def heads(i, carry):
        mi, pair = i // 4, i % 4
        lanes = pl.ds(pl.multiple_of(pair * LANES, LANES), LANES)
        skeys = ks_ref[mi, :, lanes]
        svalues = vs_ref[mi, :, lanes].T
        for t in range(tiles):
            here = slice(t * SPAN, (t + 1) * SPAN)
            queries = split_heads(q_ref[mi, here, lanes] * SCALE)
            keys = jnp.concatenate((k_ref[mi, here, lanes], skeys), axis=0)
            bias = bias_ref[mi, t]
            scores = dot_cols(keys, queries) + jnp.concatenate((bias, bias), axis=1)
            top = jnp.max(scores, axis=0, keepdims=True)
            grown = jnp.exp(scores - top)
            total = jnp.sum(grown, axis=0, keepdims=True)
            probs = (grown * (1.0 / total)).astype(BF16)
            values = jnp.concatenate((v_ref[mi, here, lanes].T, svalues), axis=1)
            att_ref[mi, here, lanes] = join_heads(dot(values, probs)).astype(BF16)
            lse_ref[i, t] = top + jnp.log(total)
        return carry

    lax.fori_loop(0, 8, heads, 0)


def gelu_pair(u):
    c0 = math.sqrt(2.0 / math.pi)
    square = u * u
    t = jnp.tanh(c0 * u * (1.0 + 0.044715 * square))
    half = 0.5 * (1.0 + t)
    slope = half + (0.5 * c0) * u * (1.0 - t * t) * (1.0 + (3 * 0.044715) * square)
    return u * half, slope


def mlp_kernel(
    block_of, row_of, xs_ref, att_ref, x_cot_ref, obias, gain, shift, ubias, dbias, near_ref, far_ref,
    result_ref, gmid_ref, gatt_ref, small_ref, gub_ref, keep_ref, send_ref,
    wo_ref, wu_ref, wd_ref, resid_ref, acc_ref, gn_ref, n_ref, nt_ref, ct_ref, gu_ref, gd_ref, go_ref,
    guw_ref, gdw_ref, gow_ref, sem, out_sem,
):
    total_rows = xs_ref.shape[0]
    half, shard, _ = near_ref.shape
    step = 256
    steps = total_rows // step

    def place(d, carry):
        for source, slot in ((near_ref, d), (far_ref, half + d)):
            rows = pl.ds(pl.multiple_of(row_of[slot] * shard, 16), shard)
            block = block_of[slot]
            narrow = pl.ds(pl.multiple_of(block * 128, 128), 128)
            broad = pl.ds(pl.multiple_of(block * 512, 512), 512)
            pltpu.make_async_copy(source.at[d, :, 0:128], wo_ref.at[rows, narrow], sem.at[0]).start()
            pltpu.make_async_copy(source.at[d, :, 128:640], wu_ref.at[rows, broad], sem.at[1]).start()
            pltpu.make_async_copy(source.at[d, :, 640:1152], wd_ref.at[rows, broad], sem.at[2]).start()
        return carry

    lax.fori_loop(0, half, place, 0)
    small_ref[...] = jnp.zeros_like(small_ref)
    gub_ref[...] = jnp.zeros_like(gub_ref)
    gow_ref[...] = jnp.zeros_like(gow_ref)
    pltpu.make_async_copy(wo_ref, wo_ref, sem.at[0]).wait()

    def first(r, carry):
        rows = pl.ds(pl.multiple_of(r * step, step), step)
        resid = xs_ref[rows, :].astype(F32) + dot_cols(att_ref[rows, :], wo_ref[...]) + obias[...]
        resid_ref[rows, :] = resid
        hat, _ = unit(resid)
        normed = (hat * gain[...] + shift[...]).astype(BF16)
        cot = x_cot_ref[rows, :]
        n_ref[rows, :] = normed
        nt_ref[:, rows] = normed.T
        ct_ref[:, rows] = cot.T
        acc_ref[rows, :] = resid + dbias[...]
        gn_ref[rows, :] = jnp.zeros((step, D), F32)
        small_ref[3:4, :] += jnp.sum(cot.astype(F32), axis=0, keepdims=True)
        return carry

    lax.fori_loop(0, steps, first, 0)
    pltpu.make_async_copy(wu_ref, wu_ref, sem.at[1]).wait()
    pltpu.make_async_copy(wd_ref, wd_ref, sem.at[2]).wait()

    def chunk(ch, carry):
        cols = pl.ds(pl.multiple_of(ch * 512, 512), 512)
        guw_ref[...] = jnp.zeros_like(guw_ref)
        gdw_ref[...] = jnp.zeros_like(gdw_ref)

        def block(r, inner):
            rows = pl.ds(pl.multiple_of(r * step, step), step)
            w_up, w_down = wu_ref[:, cols], wd_ref[:, cols]
            act, slope = gelu_pair(dot(n_ref[rows, :], w_up) + ubias[:, cols])
            act = act.astype(BF16)
            grad = (dot(x_cot_ref[rows, :], w_down) * slope).astype(BF16)
            acc_ref[rows, :] += dot_cols(act, w_down)
            gn_ref[rows, :] += dot_cols(grad, w_up)
            guw_ref[...] += dot(nt_ref[:, rows], grad)
            gdw_ref[...] += dot(ct_ref[:, rows], act)
            gub_ref[:, cols] += jnp.sum(grad.astype(F32), axis=0, keepdims=True)
            return inner

        lax.fori_loop(0, steps, block, 0)
        gu_ref[:, cols] = guw_ref[...].astype(BF16)
        gd_ref[:, cols] = gdw_ref[...].astype(BF16)
        return carry

    lax.fori_loop(0, 4, chunk, 0)

    def last(r, carry):
        rows = pl.ds(pl.multiple_of(r * step, step), step)
        result_ref[rows, :] = acc_ref[rows, :].astype(BF16)
        hat, inverse = unit(resid_ref[rows, :])
        grad = gn_ref[rows, :]
        small_ref[0:1, :] += jnp.sum(grad * hat, axis=0, keepdims=True)
        small_ref[1:2, :] += jnp.sum(grad, axis=0, keepdims=True)
        gmid = x_cot_ref[rows, :].astype(F32) + unit_back(grad * gain[...], hat, inverse)
        gmid_ref[rows, :] = gmid
        branch = gmid.astype(BF16)
        small_ref[2:3, :] += jnp.sum(branch.astype(F32), axis=0, keepdims=True)
        gatt_ref[rows, :] = dot(branch, wo_ref[...]).astype(BF16)
        gow_ref[...] += dot(branch.T, att_ref[rows, :])
        return carry

    lax.fori_loop(0, steps, last, 0)
    go_ref[...] = gow_ref[...].astype(BF16)

    def emit(d, carry):
        for target, slot in ((keep_ref, d), (send_ref, half + d)):
            rows = pl.ds(pl.multiple_of(row_of[slot] * shard, 16), shard)
            block = block_of[slot]
            narrow = pl.ds(pl.multiple_of(block * 128, 128), 128)
            broad = pl.ds(pl.multiple_of(block * 512, 512), 512)
            pltpu.make_async_copy(go_ref.at[rows, narrow], target.at[d, :, 0:128], out_sem.at[0]).start()
            pltpu.make_async_copy(gu_ref.at[rows, broad], target.at[d, :, 128:640], out_sem.at[1]).start()
            pltpu.make_async_copy(gd_ref.at[rows, broad], target.at[d, :, 640:1152], out_sem.at[2]).start()
        return carry

    lax.fori_loop(0, half, emit, 0)
    pltpu.make_async_copy(go_ref, go_ref, out_sem.at[0]).wait()
    pltpu.make_async_copy(gu_ref, gu_ref, out_sem.at[1]).wait()
    pltpu.make_async_copy(gd_ref, gd_ref, out_sem.at[2]).wait()


def attend_back_kernel(
    info, q_ref, k_ref, v_ref, ks_ref, vs_ref, lse_ref, gatt_ref,
    gq_ref, gk_ref, gv_ref, gks_ref, gvs_ref, bias_ref,
):
    rows = q_ref.shape[1]
    tiles = rows // SPAN
    summaries = ks_ref.shape[1]
    fill_masks(info, bias_ref, tiles, summaries, summaries * SPAN)

    def heads(i, carry):
        mi, pair = i // 4, i % 4
        lanes = pl.ds(pl.multiple_of(pair * LANES, LANES), LANES)
        skeys = ks_ref[mi, :, lanes]
        svalues = vs_ref[mi, :, lanes]
        skeys_t = skeys.T
        sum_k = jnp.zeros((summaries, LANES), F32)
        sum_v = jnp.zeros((summaries, LANES), F32)
        for t in range(tiles):
            here = slice(t * SPAN, (t + 1) * SPAN)
            queries = split_heads(q_ref[mi, here, lanes] * SCALE)
            grads = split_heads(gatt_ref[mi, here, lanes])
            own_keys = k_ref[mi, here, lanes]
            keys = jnp.concatenate((own_keys, skeys), axis=0)
            values = jnp.concatenate((v_ref[mi, here, lanes], svalues), axis=0)
            bias = bias_ref[mi, t]
            scores = dot_cols(keys, queries) + jnp.concatenate((bias, bias), axis=1)
            probs = jnp.exp(scores - lse_ref[i, t])
            gprobs = dot_cols(values, grads)
            delta = jnp.sum(probs * gprobs, axis=0, keepdims=True)
            gscores = (probs * (gprobs - delta)).astype(BF16)
            keys_t = jnp.concatenate((own_keys.T, skeys_t), axis=1)
            gq_ref[mi, here, lanes] = (join_heads(dot(keys_t, gscores)) * SCALE).astype(BF16)
            grad_k = dot(gscores, queries)
            grad_v = dot(probs.astype(BF16), grads)
            gk_ref[mi, here, lanes] = grad_k[:SPAN].astype(BF16)
            gv_ref[mi, here, lanes] = grad_v[:SPAN].astype(BF16)
            sum_k += grad_k[SPAN:]
            sum_v += grad_v[SPAN:]
        gks_ref[mi, :, lanes] = sum_k
        gvs_ref[mi, :, lanes] = sum_v
        return carry

    lax.fori_loop(0, 8, heads, 0)


def project_back_kernel(
    apart, info, block_of, row_of, slots_ref, xs_ref, nb_ref, gq_ref, gk_ref, gv_ref, gks_ref, gvs_ref, sums_ref,
    w_ref, gain, shift, gn_ref, small_ref, keep_ref, send_ref, *refs
):
    if apart:
        all_ref, *refs = refs
    gw_ref, gwb_ref, back_ref, stack_ref, sem = refs
    rows = xs_ref.shape[1]
    summaries = gks_ref.shape[1]
    half, shard, _ = keep_ref.shape
    small_ref[...] = jnp.zeros_like(small_ref)
    for mi in range(2):
        _, offset, ends = row_info(info, mi)
        first, last = summary_range(iota((summaries, 1), 0), offset, ends)
        root = jnp.sqrt((last - first + 1).astype(F32))
        sums = sums_ref[mi]
        pooled = (sums * gain[...] + root * shift[...]).astype(BF16).T
        normed = nb_ref[mi].T
        grad_n = jnp.zeros((rows, D), F32)
        grad_s = jnp.zeros((summaries, D), F32)
        for m in range(4):
            lanes = slice(m * LANES, (m + 1) * LANES)
            gq, gk, gv = gq_ref[mi, :, lanes], gk_ref[mi, :, lanes], gv_ref[mi, :, lanes]
            gks, gvs = gks_ref[mi, :, lanes], gvs_ref[mi, :, lanes]
            small_ref[2:3, lanes] += jnp.sum(gq.astype(F32), axis=0, keepdims=True)
            small_ref[3:4, lanes] += jnp.sum(gv.astype(F32), axis=0, keepdims=True) + jnp.sum(
                root * gvs, axis=0, keepdims=True
            )
            grads = jnp.concatenate((gq, gk, gv), axis=1)
            pooled_grads = jnp.concatenate((gks, gvs), axis=1).astype(BF16)
            w = w_ref[m]
            grad_n += dot_cols(grads, w)
            grad_s += dot_cols(pooled_grads, w[:, 128:])
            grad_w = dot(normed, grads)
            grad_kv = dot(pooled, pooled_grads)
            if mi == 0:
                gw_ref[m] = grad_w
            else:
                gw_ref[m] += grad_w
            gw_ref[m, :, 128:384] += grad_kv
        hat, _ = unit(xs_ref[mi].astype(F32))
        gn_ref[mi] = grad_n
        back_ref[mi] = grad_s.astype(BF16)
        small_ref[0:1, :] += jnp.sum(grad_n * hat, axis=0, keepdims=True) + jnp.sum(
            grad_s * sums, axis=0, keepdims=True
        )
        small_ref[1:2, :] += jnp.sum(grad_n, axis=0, keepdims=True) + jnp.sum(
            root * grad_s, axis=0, keepdims=True
        )
    for m in range(4):
        gwb_ref[m] = gw_ref[m].astype(BF16)
    for base in range(0, stack_ref.shape[0], 32):
        names = [slots_ref[mi : mi + 1, 16 * base : 16 * base + 512] for mi in range(2)]
        spread = [
            jnp.where(iota((summaries, 1), 0) == named, 1.0, 0.0).astype(BF16).T for named in names
        ]
        for lane in range(D // LANES):
            lanes = slice(lane * LANES, (lane + 1) * LANES)
            piece = dot(spread[0], back_ref[0, :, lanes]) + dot(spread[1], back_ref[1, :, lanes])
            stack_ref[base : base + 32, 16 * lane : 16 * lane + 16, :] = piece.astype(BF16).reshape(
                32, 16, LANES
            )

    def emit(d, carry):
        for target, slot in ((keep_ref, d), (send_ref, half + d)):
            first_row = pl.multiple_of(row_of[slot] * shard, 16)
            pltpu.make_async_copy(
                gwb_ref.at[block_of[slot], pl.ds(first_row, shard), :], target.at[d, :, 0:384], sem.at[0]
            ).start()
            if not apart:
                pltpu.make_async_copy(
                    stack_ref.at[slot], target.at[d, 0:64, 384:512], sem.at[1]
                ).start()
        return carry

    lax.fori_loop(0, half, emit, 0)
    if apart:
        pltpu.make_async_copy(stack_ref, all_ref, sem.at[1]).start()
    pltpu.make_async_copy(gwb_ref, gwb_ref, sem.at[0]).wait()
    pltpu.make_async_copy(stack_ref, stack_ref, sem.at[1]).wait()


def input_back_kernel(
    info, x_ref, gn_ref, gn_right, gmid_ref, gmid_right, pooled_ref, gain, out_ref
):
    rows = x_ref.shape[1]
    for mi in range(2):
        dev, offset, ends = row_info(info, mi)
        first, last = summary_range(dev * (rows // SPAN) + iota((8, 1), 0), offset, ends)
        lows = jnp.concatenate(
            [pooled_ref[16 * i + 8 * mi : 16 * i + 8 * mi + 8, :] for i in range(D // LANES)], axis=1
        )
        lows = (lows * lax.rsqrt((last - first + 1).astype(F32))).astype(BF16)
        ids = dev * (rows // SPAN) + iota((1, 8), 1)
        first, last = summary_range(ids, offset, ends)
        pos = dev * rows + iota((rows, 1), 0)
        member = jnp.where((pos >= first) & (pos <= last), 1.0, 0.0).astype(BF16)
        pick = picker(SPAN - offset)
        for t in range(rows // SPAN):
            here = slice(t * SPAN, (t + 1) * SPAN)
            if (t + 2) * SPAN <= rows:
                grad = gn_ref[mi, t * SPAN : (t + 2) * SPAN, :]
                gmid = gmid_ref[mi, t * SPAN : (t + 2) * SPAN, :]
            else:
                grad = jnp.concatenate((gn_ref[mi, here, :], gn_right[mi].astype(F32)), axis=0)
                gmid = jnp.concatenate((gmid_ref[mi, here, :], gmid_right[mi].astype(F32)), axis=0)
            grad = pick_rows(pick, grad) + dot(member[here], lows)
            hat, inverse = unit(x_ref[mi, here, :].astype(F32))
            out_ref[mi, here, :] = pick_rows(pick, gmid) + unit_back(grad * gain[...], hat, inverse)


def call(kernel, outs, in_specs, out_specs=None, scratch=(), limit=56, flops=0, moved=0):
    return pl.pallas_call(
        kernel,
        out_shape=outs,
        in_specs=in_specs,
        out_specs=out_specs if out_specs is not None else [VMEM] * len(outs),
        scratch_shapes=list(scratch),
        compiler_params=pltpu.CompilerParams(vmem_limit_bytes=limit * MIB),
        cost_estimate=pl.CostEstimate(flops=flops, bytes_accessed=moved, transcendentals=0),
    )


def per_device(
    block_input, cotangent, span_offset, doc_lengths, ln1_gain, ln1_bias, w_query, w_key, w_value,
    query_bias, value_bias, w_out, out_bias, ln2_gain, ln2_bias, w_up, up_bias, w_down, down_bias,
):
    groups, ranks = lax.axis_size("seq"), lax.axis_size("mp")
    count = groups * ranks
    mp_index = lax.axis_index("mp")
    dev = lax.axis_index("seq") * ranks + mp_index
    rows = block_input.shape[1]
    tiles = rows // SPAN
    summaries = tiles * count
    shard = w_query.shape[0]
    bits = count.bit_length() - 1
    stages = [(b, b) for b in range(bits - 1, 2, -1)] + [(1, 2), (2, 1)]
    direct = shard == 64

    def swap(value, stage):
        pairs = [(i, i ^ (1 << stage[i & 1])) for i in range(count)]
        return lax.ppermute(value, AXES, pairs)

    def turn(value, by):
        return lax.ppermute(value, AXES, [(i, (i + by) % count) for i in range(count)])

    core = dev & 1
    slot = jnp.arange(count, dtype=jnp.int32)
    far = slot // (count // 2)
    mask = far
    for i, (even, odd) in enumerate(stages):
        where = jnp.where((core ^ far) == 0, even, odd)
        mask = mask | (((slot >> i) & 1) << where)
    owner = dev ^ mask
    if not direct:
        owner = slot
    member_slot = jnp.arange(16, dtype=jnp.int32)
    slots = owner[:, None] * tiles + (member_slot % 8)[None, :]
    valid = (member_slot % 8 <= tiles)[None, :]
    slots = jnp.stack(
        [
            jnp.where(valid & (member_slot // 8 == mi)[None, :], slots, -1).reshape(-1)
            for mi in range(2)
        ]
    )
    block_of, row_of = owner % ranks, owner // ranks
    doc_ends = jnp.cumsum(doc_lengths, axis=1).astype(jnp.int32)
    info = jnp.concatenate((dev[None], span_offset, doc_ends.reshape(-1))).astype(jnp.int32)

    def gather(value):
        part = value[None]
        for stage in stages:
            part = jnp.concatenate((part, swap(part, stage)), axis=0)
        return part, swap(part, (0, 0))

    def scatter(keep, send, small=None):
        keep = keep.astype(F32)
        for stage in [(0, 0)] + stages[::-1]:
            if small is not None:
                high = small.astype(BF16)
                rest = (small - high.astype(F32)).astype(BF16)
                small = high.astype(F32) + rest.astype(F32)
                pad = jnp.concatenate((high, rest, jnp.zeros((8, D), BF16)), axis=0)
                flat = send.reshape(-1, D)
                got = swap(jnp.concatenate((flat, pad), axis=0), stage)
                size = flat.shape[0]
                small = small + (got[size : size + 4].astype(F32) + got[size + 4 : size + 8].astype(F32))
                got = got[:size].reshape(send.shape)
            else:
                got = swap(send, stage)
            total = keep + got.astype(F32)
            half = total.shape[0] // 2
            if half:
                keep, send = total[:half], total[half:].astype(BF16)
        return total[0], small

    def gather_whole(value):
        both = lax.all_gather(value, "seq", axis=0, tiled=True)
        both = lax.all_gather(both, "mp", axis=0)
        return both[: ranks // 2], both[ranks // 2 :]

    def scatter_whole(keep, send):
        both = jnp.concatenate((keep, send), axis=0).astype(F32)
        total = lax.psum_scatter(both, "mp", scatter_dimension=0, tiled=True)[0]
        return lax.psum_scatter(total, "seq", scatter_dimension=0, tiled=True)

    def row(vector):
        return vector[None, :]

    def shape(dims, kind):
        return jax.ShapeDtypeStruct(dims, kind)

    half, tall = (count // 2, shard) if direct else (ranks // 2, shard * groups)
    width = 4 * LANES if direct else 3 * LANES
    apart = not direct
    cot_own = lax.dynamic_slice_in_dim(cotangent, mp_index * rows, rows, 1)
    edges = turn(jnp.stack((block_input[:, rows - SPAN :], cot_own[:, rows - SPAN :])), 1)
    own_sums = call(summary_kernel, [shape((64, LANES), BF16)], [SMEM, VMEM])(info, block_input)[0]

    w_qkv = jnp.concatenate((w_query, w_key, w_value), axis=1)
    w_rest = jnp.concatenate((w_out.T, w_up, w_down.T), axis=1)
    if direct:
        near_a, far_a = gather(jnp.concatenate((w_qkv, own_sums), axis=1))
        near_b, far_b = gather(w_rest)
        more = ()
    else:
        near_a, far_a = gather_whole(w_qkv)
        near_b, far_b = gather_whole(w_rest)
        more = (lax.all_gather(own_sums, AXES, axis=0),)
        block_of, row_of = jnp.arange(ranks, dtype=jnp.int32), jnp.zeros((ranks,), jnp.int32)

    wide = (2, rows, D)
    xs, nb, q, k, v, att, ks, vs, lse, sums, w_full = call(
        partial(attend_kernel, apart),
        [shape(wide, BF16)] * 6
        + [shape((2, summaries, D), BF16)] * 2
        + [shape((8, tiles, 1, 2 * SPAN), F32), shape((2, summaries, D), F32)]
        + [shape((4, D, 3 * LANES), BF16)],
        [SMEM, SMEM, SMEM] + [VMEM] * 7 + [ANY] * (2 + len(more)),
        scratch=[
            pltpu.VMEM((count, 64, LANES), BF16),
            pltpu.VMEM((rows + SPAN, D), BF16),
            pltpu.VMEM((2, tiles, SPAN + summaries, SPAN), F32),
            pltpu.SemaphoreType.DMA((2,)),
        ],
        flops=6 << 30,
        moved=8 << 20,
    )(
        info, block_of, row_of, slots, block_input, edges[0], row(ln1_gain), row(ln1_bias),
        row(query_bias), row(value_bias), near_a, far_a, *more,
    )
    flat = (2 * rows, D)
    cot_wide = jnp.concatenate((edges[1], cot_own), axis=1)
    cot_s = jnp.stack(
        [lax.dynamic_slice_in_dim(cot_wide[i], span_offset[i], rows, 0) for i in range(2)]
    )
    result, gmid, gatt, small_b, grad_ub, keep_b, send_b = call(
        mlp_kernel,
        [shape(flat, BF16), shape(flat, F32), shape(flat, BF16), shape((8, D), F32), shape((1, FF), F32)]
        + [shape((half, tall, 1152), BF16)] * 2,
        [SMEM, SMEM] + [VMEM] * 8 + [ANY] * 2,
        [VMEM] * 5 + [ANY] * 2,
        scratch=[
            pltpu.VMEM((D, D), BF16), pltpu.VMEM((D, FF), BF16), pltpu.VMEM((D, FF), BF16),
            pltpu.VMEM(flat, F32), pltpu.VMEM(flat, F32), pltpu.VMEM(flat, F32),
            pltpu.VMEM(flat, BF16), pltpu.VMEM((D, 2 * rows), BF16), pltpu.VMEM((D, 2 * rows), BF16),
            pltpu.VMEM((D, FF), BF16), pltpu.VMEM((D, FF), BF16), pltpu.VMEM((D, D), BF16),
            pltpu.VMEM((D, D), F32), pltpu.VMEM((D, D), F32), pltpu.VMEM((D, D), F32),
            pltpu.SemaphoreType.DMA((3,)), pltpu.SemaphoreType.DMA((3,)),
        ],
        flops=14 << 30,
        moved=24 << 20,
    )(
        block_of, row_of, xs.reshape(flat), att.reshape(flat), cot_s.reshape(flat), row(out_bias),
        row(ln2_gain), row(ln2_bias), row(up_bias), row(down_bias), near_b, far_b,
    )
    early = lax.psum((small_b[:4], grad_ub), AXES)
    back = turn(
        jnp.stack((result.reshape(wide)[:, :SPAN], gmid.reshape(wide)[:, :SPAN].astype(BF16))), -1
    )
    sum_b = scatter(keep_b, send_b)[0] if direct else scatter_whole(keep_b, send_b)
    gq, gk, gv, gks, gvs = call(
        attend_back_kernel,
        [shape(wide, BF16)] * 3 + [shape((2, summaries, D), F32)] * 2,
        [SMEM] + [VMEM] * 7,
        scratch=[pltpu.VMEM((2, tiles, SPAN + summaries, SPAN), F32)],
        flops=8 << 30,
        moved=8 << 20,
    )(info, q, k, v, ks, vs, lse, gatt.reshape(wide))
    gn, small_a, keep_a, send_a, *more = call(
        partial(project_back_kernel, apart),
        [shape(wide, F32), shape((8, D), F32)]
        + [shape((half, tall, width), BF16)] * 2
        + [shape((count, 64, LANES), BF16)] * apart,
        [SMEM] * 3 + [VMEM] * 12,
        [VMEM] * 2 + [ANY] * (2 + apart),
        scratch=[
            pltpu.VMEM((4, D, 3 * LANES), F32), pltpu.VMEM((4, D, 3 * LANES), BF16),
            pltpu.VMEM((2, summaries, D), BF16), pltpu.VMEM((count, 64, LANES), BF16),
            pltpu.SemaphoreType.DMA((2,)),
        ],
        flops=4 << 30,
        moved=8 << 20,
    )(
        info, block_of, row_of, slots, xs, nb, gq, gk, gv, gks, gvs, sums, w_full, row(ln1_gain),
        row(ln1_bias),
    )
    gn_back = turn(gn[:, :SPAN].astype(BF16), -1)
    if direct:
        sum_a, late = scatter(keep_a, send_a, small_a[:4])
        pooled = sum_a[:, 384:]
    else:
        sum_a, late = scatter_whole(keep_a, send_a), lax.psum(small_a[:4], AXES)
        pooled = lax.psum_scatter(more[0].astype(F32), AXES, scatter_dimension=0, tiled=True)[0]
    input_grad = call(
        input_back_kernel,
        [shape(wide, F32)],
        [SMEM] + [VMEM] * 7,
    )(info, block_input, gn, gn_back, gmid.reshape(wide), back[1], pooled, row(ln1_gain))[0]
    result_wide = jnp.concatenate((result.reshape(wide), back[0]), axis=1)
    result_own = jnp.stack(
        [lax.dynamic_slice_in_dim(result_wide[i], SPAN - span_offset[i], rows, 0) for i in range(2)]
    )
    small_sum, ub_sum = early
    return (
        result_own,
        input_grad,
        late[0],
        late[1],
        sum_a[:, :128],
        sum_a[:, 128:256],
        sum_a[:, 256:384],
        late[2],
        late[3],
        sum_b[:, :128].T,
        small_sum[2],
        small_sum[0],
        small_sum[1],
        sum_b[:, 128:640],
        ub_sum[0],
        sum_b[:, 640:].T,
        small_sum[3],
    )


def solution(mesh):
    vector, matrix, turned = P(), P("seq", "mp"), P("mp", "seq")
    own, group = P(None, ("seq", "mp"), None), P(None, "seq", None)
    return jax.shard_map(
        per_device,
        mesh=mesh,
        in_specs=(own, group, vector, vector, vector, vector, matrix, matrix, matrix, vector, vector)
        + (turned, vector, vector, vector, matrix, vector, turned, vector),
        out_specs=(own, own, vector, vector, matrix, matrix, matrix, vector, vector, turned, vector)
        + (vector, vector, matrix, vector, turned, vector),
        check_vma=False,
    )
```

```python
from functools import partial
import math

import jax
import jax.numpy as jnp
from jax import lax
from jax.experimental import pallas as pl
from jax.experimental.pallas import tpu as pltpu
from jax.sharding import PartitionSpec as P

D = 512
FF = 2048
HEAD_DIM = 64
SPAN = 128
LANES = 128
EPSILON = 1e-05
NEGATIVE = -1e30
SCALE = 1.0 / math.sqrt(HEAD_DIM)
F32 = jnp.float32
BF16 = jnp.bfloat16
AXES = ("seq", "mp")
MIB = 1 << 20
VMEM = pl.BlockSpec(memory_space=pltpu.VMEM)
SMEM = pl.BlockSpec(memory_space=pltpu.SMEM)
ANY = pl.BlockSpec(memory_space=pl.ANY)


def dot(left, right):
    return lax.dot_general(left, right, (((1,), (0,)), ((), ())), preferred_element_type=F32)


def dot_cols(left, right):
    return lax.dot_general(left, right, (((1,), (1,)), ((), ())), preferred_element_type=F32)


def unit(rows):
    centred = rows - jnp.mean(rows, axis=-1, keepdims=True)
    inverse = lax.rsqrt(jnp.mean(centred * centred, axis=-1, keepdims=True) + EPSILON)
    return centred * inverse, inverse


def unit_back(grad, hat, inverse):
    shift = jnp.mean(grad, axis=-1, keepdims=True)
    slope = jnp.mean(grad * hat, axis=-1, keepdims=True)
    return (grad - shift - hat * slope) * inverse


def row_info(place, offsets, lengths, mi):
    ends = []
    for c in range(lengths.shape[1]):
        ends.append(lengths[mi, c] + (ends[-1] if ends else 0))
    return place[0], offsets[mi], ends


def doc_start(positions, ends):
    start = jnp.zeros_like(positions)
    for end in ends:
        start = jnp.where(positions >= end, end, start)
    return start


def summary_range(summary_ids, offset, ends):
    last = offset - 1 + SPAN * summary_ids
    first = jnp.maximum(doc_start(last, ends), last - (SPAN - 1))
    return first, last


def iota(shape, dim):
    return lax.broadcasted_iota(jnp.int32, shape, dim)


def roll_rows(ref, by):
    whole = pl.multiple_of((by // 8) * 8, 8)
    return pltpu.roll(ref[pl.ds(whole, SPAN + 8), :], SPAN + 8 - (by - whole), axis=0)[:SPAN]


def prepare_kernel(
    place, offsets, lengths, x_ref, cot_ref, wq_ref, wk_ref, wv_ref, out_ref, x_edge_ref, cot_edge_ref, sem
):
    rows = x_ref.shape[1]
    last_rows = pl.multiple_of(place[1] * rows + (rows - SPAN), SPAN)
    copy = pltpu.make_async_copy(cot_ref.at[:, pl.ds(last_rows, SPAN), :], cot_edge_ref, sem.at[0])
    copy.start()
    shard = wq_ref.shape[0]
    for i, ref in enumerate((wq_ref, wk_ref, wv_ref)):
        out_ref[0, 0:shard, i * LANES : (i + 1) * LANES] = ref[...]
    sums = []
    for mi in range(2):
        dev, offset, ends = row_info(place, offsets, lengths, mi)
        first, last = summary_range(dev * (rows // SPAN) + iota((8, 1), 0), offset, ends)
        pos = dev * rows + iota((1, rows), 1)
        member = jnp.where((pos >= first) & (pos <= last), 1.0, 0.0).astype(BF16)
        x_edge_ref[mi] = x_ref[mi, rows - SPAN :, :]
        hat, _ = unit(x_ref[mi].astype(F32))
        high = hat.astype(BF16)
        rest = (hat - high.astype(F32)).astype(BF16)
        total = dot(member, high) + dot(member, rest)
        sums.append(total * lax.rsqrt((last - first + 1).astype(F32)))
    both = jnp.concatenate(sums, axis=0).astype(BF16)
    for lane in range(D // LANES):
        out_ref[0, 16 * lane : 16 * lane + 16, 384:512] = both[:, lane * LANES : (lane + 1) * LANES]
    copy.wait()


def fill_masks(place, offsets, lengths, mi, bias_ref, tiles, summaries, length):
    dev, offset, ends = row_info(place, offsets, lengths, mi)
    ends_col = offset - 1 + SPAN * iota((summaries, 1), 0)
    for t in range(tiles):
        base = SPAN * (dev * tiles + t) + offset - SPAN
        qpos = base + iota((1, SPAN), 1)
        qpos = jnp.where(qpos < 0, qpos + length, qpos)
        kpos = base + iota((SPAN, 1), 0)
        kpos = jnp.where(kpos < 0, kpos + length, kpos)
        span_first = jnp.where(qpos >= base + SPAN, base + length, base)
        doc_first = doc_start(qpos, ends)
        local_ok = (kpos >= jnp.maximum(doc_first, span_first)) & (kpos <= qpos)
        summary_ok = (ends_col >= doc_first) & (ends_col < span_first)
        bias_ref[t, 0:SPAN, :] = jnp.where(local_ok, 0.0, NEGATIVE)
        bias_ref[t, SPAN : SPAN + summaries, :] = jnp.where(summary_ok, 0.0, NEGATIVE)


def split_heads(pair):
    low = iota(pair.shape, 1) < HEAD_DIM
    zero = jnp.zeros_like(pair)
    return jnp.concatenate((jnp.where(low, pair, zero), jnp.where(low, zero, pair)), axis=0)


def join_heads(turned):
    half = turned.shape[1] // 2
    return jnp.concatenate((turned[:HEAD_DIM, :half], turned[HEAD_DIM:, half:]), axis=0).T


def project_kernel(
    apart, place_ref, offsets, lengths, block_of, row_of, slots_ref, x_ref, left_ref, gain, shift, qbias, vbias,
    near_ref, far_ref, *refs
):
    if apart:
        all_ref, *refs = refs
    xs_ref, qkv_ref, skv_ref, sums_ref, w_ref, stack_ref, wide_ref, rows_ref, sem = refs
    rows = x_ref.shape[1]
    tiles = rows // SPAN
    summaries = skv_ref.shape[1]
    half, shard, _ = near_ref.shape

    def place(d, carry):
        for source, slot in ((near_ref, d), (far_ref, half + d)):
            here = pl.ds(pl.multiple_of(row_of[slot] * shard, 16), shard)
            cols = pl.ds(pl.multiple_of(block_of[slot] * 384, 128), 384)
            pltpu.make_async_copy(source.at[d, :, 0:384], w_ref.at[here, cols], sem.at[0]).start()
            if not apart:
                pltpu.make_async_copy(
                    source.at[d, 0:64, 384:512], stack_ref.at[slot], sem.at[1]
                ).start()
        return carry

    lax.fori_loop(0, half, place, 0)
    if apart:
        pltpu.make_async_copy(all_ref, stack_ref, sem.at[1]).start()
    for mi in range(2):
        wide_ref[0:SPAN, :] = left_ref[mi].astype(F32)
        wide_ref[SPAN : SPAN + rows, :] = x_ref[mi].astype(F32)
        for t in range(tiles):
            here = slice(t * SPAN, (t + 1) * SPAN)
            rolled = roll_rows(wide_ref, t * SPAN + offsets[mi])
            xs_ref[mi, here, :] = rolled.astype(BF16)
            hat, _ = unit(rolled)
            rows_ref[mi, here, :] = (hat * gain[...] + shift[...]).astype(BF16)
    pltpu.make_async_copy(stack_ref, stack_ref, sem.at[1]).wait()
    roots = []
    for mi in range(2):
        _, offset, ends = row_info(place_ref, offsets, lengths, mi)
        first, last = summary_range(iota((summaries, 1), 0), offset, ends)
        root = jnp.sqrt((last - first + 1).astype(F32))
        roots.append(root)
        for base in range(0, stack_ref.shape[0], 32):
            named = slots_ref[mi : mi + 1, 16 * base : 16 * base + 512]
            pick = jnp.where(iota((summaries, 1), 0) == named, 1.0, 0.0).astype(BF16)
            piece = jnp.concatenate(
                [
                    stack_ref[base : base + 32, 16 * lane : 16 * lane + 16, :].reshape(512, LANES)
                    for lane in range(D // LANES)
                ],
                axis=1,
            )
            found = dot(pick, piece)
            sums_ref[mi] = found if base == 0 else sums_ref[mi] + found
        summed = sums_ref[mi] * gain[...] + root * shift[...]
        high = summed.astype(BF16)
        rows_ref[mi, rows : rows + summaries, :] = high
        rows_ref[mi, rows + summaries : rows + 2 * summaries, :] = (summed - high.astype(F32)).astype(BF16)
    pltpu.make_async_copy(w_ref, w_ref, sem.at[0]).wait()
    none = jnp.zeros((1, LANES), F32)
    for m in range(4):
        lanes = slice(m * LANES, (m + 1) * LANES)
        cols = slice(m * 384, (m + 1) * 384)
        bias = jnp.concatenate((qbias[:, lanes], none, vbias[:, lanes]), axis=1)
        for mi in range(2):
            projected = dot(rows_ref[mi], w_ref[:, cols])
            qkv_ref[mi, :, cols] = (projected[:rows] + bias).astype(BF16)
            pooled = projected[rows : rows + summaries] + projected[rows + summaries :]
            skv_ref[mi, :, cols] = (pooled + roots[mi] * bias).astype(BF16)


def pair_of(ref, here, pair):
    def part(i):
        return ref[0, here, pl.ds(pl.multiple_of(pair * 384 + i * LANES, LANES), LANES)]

    return part(0), part(1), part(2)


def attend_kernel(mi, place, offsets, lengths, qkv_ref, skv_ref, *refs):
    att_ref, lse_ref, bias_ref = refs[-3:]
    rows = qkv_ref.shape[1]
    tiles = rows // SPAN
    summaries = skv_ref.shape[1]
    fill_masks(place, offsets, lengths, mi, bias_ref, tiles, summaries, summaries * SPAN)

    def heads(pair, carry):
        lanes = pl.ds(pl.multiple_of(pair * LANES, LANES), LANES)
        _, skeys, svalues = pair_of(skv_ref, slice(None), pair)
        svalues = svalues.T
        spans = [pair_of(qkv_ref, slice(t * SPAN, (t + 1) * SPAN), pair) for t in range(tiles)]
        scores = []
        for t, (queries, keys, _) in enumerate(spans):
            bias = bias_ref[t]
            keys = jnp.concatenate((keys, skeys), axis=0)
            scores.append(dot_cols(keys, split_heads(queries * SCALE)) + jnp.concatenate((bias, bias), axis=1))
        probs = []
        for t in range(tiles):
            top = jnp.max(scores[t], axis=0, keepdims=True)
            grown = jnp.exp(scores[t] - top)
            total = jnp.sum(grown, axis=0, keepdims=True)
            probs.append((grown * (1.0 / total)).astype(BF16))
            lse_ref[0, pair, t] = top + jnp.log(total)
        for t, (_, _, values) in enumerate(spans):
            values = jnp.concatenate((values.T, svalues), axis=1)
            att_ref[0, t * SPAN : (t + 1) * SPAN, lanes] = join_heads(dot(values, probs[t])).astype(BF16)
        return carry

    lax.fori_loop(0, 4, heads, 0)


def gelu_pair(u):
    c0 = math.sqrt(2.0 / math.pi)
    square = u * u
    t = jnp.tanh(c0 * u * (1.0 + 0.044715 * square))
    half = 0.5 * (1.0 + t)
    slope = half + (0.5 * c0) * u * (1.0 - t * t) * (1.0 + (3 * 0.044715) * square)
    return u * half, slope


def mlp_kernel(
    place_ref, offsets, block_of, row_of, xs_ref, att_ref, left_ref, obias, gain, shift, ubias, dbias, cot_ref,
    near_ref, far_ref,
    result_ref, gmid_ref, edge_ref, gatt_ref, small_ref, gub_ref, keep_ref, send_ref,
    wo_ref, wu_ref, wd_ref, resid_ref, acc_ref, gn_ref, n_ref, c_ref, nt_ref, ct_ref, gu_ref, gd_ref, go_ref,
    guw_ref, gdw_ref, gow_ref, wide_ref, low_ref, sem, out_sem,
):
    rows = xs_ref.shape[1]
    tiles = rows // SPAN
    half, shard, _ = near_ref.shape
    own = pl.ds(pl.multiple_of(place_ref[1] * rows, SPAN), rows)
    own_copy = pltpu.make_async_copy(cot_ref.at[:, own, :], low_ref, sem.at[3])
    own_copy.start()

    def columns(block, width):
        return pl.ds(pl.multiple_of(block * width, 128), width)

    def place(first):
        def body(d, carry):
            for source, slot in ((near_ref, d), (far_ref, half + d)):
                here = pl.ds(pl.multiple_of(row_of[slot] * shard, 16), shard)
                block = block_of[slot]
                if first:
                    pltpu.make_async_copy(
                        source.at[d, :, 0:128], wo_ref.at[here, columns(block, 128)], sem.at[0]
                    ).start()
                else:
                    wide = columns(block, 512)
                    pltpu.make_async_copy(source.at[d, :, 128:640], wu_ref.at[here, wide], sem.at[1]).start()
                    pltpu.make_async_copy(source.at[d, :, 640:1152], wd_ref.at[here, wide], sem.at[2]).start()
            return carry

        lax.fori_loop(0, half, body, 0)

    place(True)
    place(False)
    small_ref[...] = jnp.zeros_like(small_ref)
    gub_ref[...] = jnp.zeros_like(gub_ref)
    gow_ref[...] = jnp.zeros_like(gow_ref)
    own_copy.wait()
    pltpu.make_async_copy(wo_ref, wo_ref, sem.at[0]).wait()
    for mi in range(2):
        all_rows = slice(mi * rows, (mi + 1) * rows)
        wide_ref[0:SPAN, :] = left_ref[mi].astype(F32)
        wide_ref[SPAN : SPAN + rows, :] = low_ref[mi].astype(F32)
        for t in range(tiles):
            rolled = roll_rows(wide_ref, t * SPAN + offsets[mi])
            small_ref[3:4, :] += jnp.sum(rolled, axis=0, keepdims=True)
            c_ref[mi * rows + t * SPAN : mi * rows + (t + 1) * SPAN, :] = rolled.astype(BF16)
        resid = xs_ref[mi].astype(F32) + dot_cols(att_ref[mi], wo_ref[...]) + obias[...]
        resid_ref[all_rows, :] = resid
        hat, _ = unit(resid)
        normed = (hat * gain[...] + shift[...]).astype(BF16)
        n_ref[all_rows, :] = normed
        nt_ref[:, all_rows] = normed.T
        ct_ref[:, all_rows] = c_ref[all_rows, :].T
        acc_ref[all_rows, :] = resid + dbias[...]
        gn_ref[all_rows, :] = jnp.zeros((rows, D), F32)
    pltpu.make_async_copy(wu_ref, wu_ref, sem.at[1]).wait()
    pltpu.make_async_copy(wd_ref, wd_ref, sem.at[2]).wait()

    def emit(pick, copies):
        def body(d, carry):
            for target, slot in ((keep_ref, d), (send_ref, half + d)):

                @pl.when(pick(block_of[slot]))
                def _():
                    here = pl.ds(pl.multiple_of(row_of[slot] * shard, 16), shard)
                    for source, width, cols, i in copies:
                        pltpu.make_async_copy(
                            source.at[here, columns(block_of[slot], width)], target.at[d, :, cols], out_sem.at[i]
                        ).start()

            return carry

        lax.fori_loop(0, half, body, 0)

    def chunk(ch, carry):
        cols = columns(ch, 512)
        for mi in range(2):
            here = slice(mi * rows, (mi + 1) * rows)
            w_up, w_down = wu_ref[:, cols], wd_ref[:, cols]
            act, slope = gelu_pair(dot(n_ref[here, :], w_up) + ubias[:, cols])
            act = act.astype(BF16)
            grad = (dot(c_ref[here, :], w_down) * slope).astype(BF16)
            acc_ref[here, :] += dot_cols(act, w_down)
            gn_ref[here, :] += dot_cols(grad, w_up)
            grad_up, grad_down = dot(nt_ref[:, here], grad), dot(ct_ref[:, here], act)
            if mi == 0:
                guw_ref[...] = grad_up
                gdw_ref[...] = grad_down
            else:
                gu_ref[:, cols] = (guw_ref[...] + grad_up).astype(BF16)
                gd_ref[:, cols] = (gdw_ref[...] + grad_down).astype(BF16)
            gub_ref[:, cols] += jnp.sum(grad.astype(F32), axis=0, keepdims=True)
        emit(lambda b: b == ch, ((gu_ref, 512, slice(128, 640), 1), (gd_ref, 512, slice(640, 1152), 2)))
        return carry

    lax.fori_loop(0, 4, chunk, 0)
    for mi in range(2):
        here = slice(mi * rows, (mi + 1) * rows)
        result_ref[mi] = acc_ref[here, :].astype(BF16)
        hat, inverse = unit(resid_ref[here, :])
        grad = gn_ref[here, :]
        small_ref[0:1, :] += jnp.sum(grad * hat, axis=0, keepdims=True)
        small_ref[1:2, :] += jnp.sum(grad, axis=0, keepdims=True)
        branch = (c_ref[here, :].astype(F32) + unit_back(grad * gain[...], hat, inverse)).astype(BF16)
        gmid_ref[mi] = branch
        edge_ref[0, mi] = result_ref[mi, 0:SPAN, :]
        edge_ref[1, mi] = branch[0:SPAN]
        small_ref[2:3, :] += jnp.sum(branch.astype(F32), axis=0, keepdims=True)
        gatt_ref[mi] = dot(branch, wo_ref[...]).astype(BF16)
        grad_out = dot(branch.T, att_ref[mi])
        gow_ref[...] = grad_out if mi == 0 else gow_ref[...] + grad_out
    go_ref[...] = gow_ref[...].astype(BF16)
    emit(lambda b: b >= 0, ((go_ref, 128, slice(0, 128), 0),))
    pltpu.make_async_copy(gu_ref, gu_ref, out_sem.at[1]).wait()
    pltpu.make_async_copy(gd_ref, gd_ref, out_sem.at[2]).wait()
    pltpu.make_async_copy(go_ref, go_ref, out_sem.at[0]).wait()


def attend_back_kernel(mi, place, offsets, lengths, qkv_ref, skv_ref, lse_ref, gatt_ref, *refs):
    grad_ref, pooled_ref, bias_ref = refs[-3:]
    rows = qkv_ref.shape[1]
    tiles = rows // SPAN
    summaries = skv_ref.shape[1]
    fill_masks(place, offsets, lengths, mi, bias_ref, tiles, summaries, summaries * SPAN)

    def heads(pair, carry):
        lanes = pl.ds(pl.multiple_of(pair * LANES, LANES), LANES)

        def columns(i):
            return pl.ds(pl.multiple_of(pair * 384 + i * LANES, LANES), LANES)

        _, skeys, svalues = pair_of(skv_ref, slice(None), pair)
        skeys_t = skeys.T
        sum_k = jnp.zeros((summaries, LANES), F32)
        sum_v = jnp.zeros((summaries, LANES), F32)
        held = []
        for t in range(tiles):
            here = slice(t * SPAN, (t + 1) * SPAN)
            queries, keys, values = pair_of(qkv_ref, here, pair)
            queries = split_heads(queries * SCALE)
            grads = split_heads(gatt_ref[0, here, lanes])
            bias = bias_ref[t]
            scores = dot_cols(jnp.concatenate((keys, skeys), axis=0), queries)
            gprobs = dot_cols(jnp.concatenate((values, svalues), axis=0), grads)
            held.append((queries, keys, grads, scores + jnp.concatenate((bias, bias), axis=1), gprobs))
        for t, (queries, keys, grads, scores, gprobs) in enumerate(held):
            here = slice(t * SPAN, (t + 1) * SPAN)
            probs = jnp.exp(scores - lse_ref[0, pair, t])
            delta = jnp.sum(probs * gprobs, axis=0, keepdims=True)
            gscores = (probs * (gprobs - delta)).astype(BF16)
            keys_t = jnp.concatenate((keys.T, skeys_t), axis=1)
            grad_q = join_heads(dot(keys_t, gscores)) * SCALE
            grad_k = dot(gscores, queries)
            grad_v = dot(probs.astype(BF16), grads)
            grad_ref[0, here, columns(0)] = grad_q.astype(BF16)
            grad_ref[0, here, columns(1)] = grad_k[:SPAN].astype(BF16)
            grad_ref[0, here, columns(2)] = grad_v[:SPAN].astype(BF16)
            sum_k += grad_k[SPAN:]
            sum_v += grad_v[SPAN:]
        pooled_ref[0, :, columns(0)] = jnp.zeros((summaries, LANES), BF16)
        pooled_ref[0, :, columns(1)] = sum_k.astype(BF16)
        pooled_ref[0, :, columns(2)] = sum_v.astype(BF16)
        return carry

    lax.fori_loop(0, 4, heads, 0)


def weights_back_kernel(
    apart, place, offsets, lengths, block_of, row_of, slots_ref, xs_ref, grad_ref, pooled_ref, sums_ref, w_ref,
    gain, shift, small_ref, gub_ref, line_ref, keep_ref, send_ref, *refs
):
    if apart:
        all_ref, *refs = refs
    gwb_ref, back_ref, stack_ref, pad_ref, sem = refs
    rows = xs_ref.shape[1]
    summaries = pooled_ref.shape[1]
    half = block_of.shape[0] // 2
    shard = keep_ref.shape[0] // half
    turned = []
    column = jnp.zeros((1, 3 * D), F32)
    for mi in range(2):
        _, offset, ends = row_info(place, offsets, lengths, mi)
        first, last = summary_range(iota((summaries, 1), 0), offset, ends)
        root = jnp.sqrt((last - first + 1).astype(F32))
        hat, _ = unit(xs_ref[mi].astype(F32))
        turned += [hat.astype(BF16).T, sums_ref[mi].astype(BF16).T]
        column += jnp.sum(grad_ref[mi].astype(F32), axis=0, keepdims=True)
        column += jnp.sum(root * pooled_ref[mi].astype(F32), axis=0, keepdims=True)
        back_ref[mi] = dot_cols(pooled_ref[mi], w_ref[...]).astype(BF16)
    turned = jnp.concatenate(turned, axis=1)
    gain_col, shift_col = gain[...].T, shift[...].T
    grad_gain = jnp.zeros((D, 1), F32)
    grad_shift = jnp.zeros((D, 1), F32)
    for m in range(4):
        cols = slice(m * 384, (m + 1) * 384)
        lanes = slice(m * LANES, (m + 1) * LANES)
        grads = jnp.concatenate([ref[mi, :, cols] for mi in range(2) for ref in (grad_ref, pooled_ref)], axis=0)
        hats, w, sums = dot(turned, grads), w_ref[:, cols].astype(F32), column[:, cols]
        grad_gain += jnp.sum(hats * w, axis=1, keepdims=True)
        grad_shift += jnp.sum(sums * w, axis=1, keepdims=True)
        gwb_ref[:, cols] = (hats * gain_col + shift_col * sums).astype(BF16)
        line_ref[10:11, lanes] = sums[:, :128]
        line_ref[11:12, lanes] = sums[:, 256:]
    line_ref[8:9, :] = grad_gain.T
    line_ref[9:10, :] = grad_shift.T
    line_ref[0:4, :] = small_ref[0:4, :]
    for i in range(4):
        line_ref[4 + i : 5 + i, :] = gub_ref[:, i * D : (i + 1) * D]
    line_ref[12:16, :] = jnp.zeros((4, D), F32)
    for base in range(0, stack_ref.shape[0], 32):
        names = [slots_ref[mi : mi + 1, 16 * base : 16 * base + 512] for mi in range(2)]
        spread = [
            jnp.where(iota((summaries, 1), 0) == named, 1.0, 0.0).astype(BF16).T for named in names
        ]
        piece = (dot(spread[0], back_ref[0]) + dot(spread[1], back_ref[1])).astype(BF16)
        for lane in range(D // LANES):
            part = piece[:, lane * LANES : (lane + 1) * LANES]
            stack_ref[base : base + 32, 16 * lane : 16 * lane + 16, :] = part.reshape(32, 16, LANES)

    def emit(d, carry):
        for target, slot in ((keep_ref, d), (send_ref, half + d)):
            first_row = pl.multiple_of(row_of[slot] * shard, 16)
            cols = pl.ds(pl.multiple_of(block_of[slot] * 384, 128), 384)
            here = target.at[pl.ds(pl.multiple_of(d * shard, 16), shard), :]
            pltpu.make_async_copy(
                gwb_ref.at[pl.ds(first_row, shard), cols], here.at[:, 0:384], sem.at[0]
            ).start()
            if not apart:
                pltpu.make_async_copy(stack_ref.at[slot], here.at[:, 384:512], sem.at[1]).start()
        return carry

    lax.fori_loop(0, half, emit, 0)
    if apart:
        pltpu.make_async_copy(stack_ref, all_ref, sem.at[1]).start()
    else:
        high = line_ref[...].astype(BF16)
        pad_ref[0:16, :] = high
        pad_ref[16:32, :] = (line_ref[...] - high.astype(F32)).astype(BF16)
        size = half * shard
        copy = pltpu.make_async_copy(pad_ref, send_ref.at[size : size + 32, :], sem.at[2])
        copy.start()
        copy.wait()
    pltpu.make_async_copy(gwb_ref, gwb_ref, sem.at[0]).wait()
    pltpu.make_async_copy(stack_ref, stack_ref, sem.at[1]).wait()


def rows_back_kernel(grad_ref, w_ref, gn_ref, edge_ref):
    gn_ref[0] = dot_cols(grad_ref[0], w_ref[...]).astype(BF16)
    edge_ref[0] = gn_ref[0, 0:SPAN, :]


def fold_kernel(keep_ref, mine_ref, got_ref, next_ref, *send_refs):
    size = keep_ref.shape[0]
    part = size // (1 + len(send_refs))
    mine = mine_ref[0:16, :].astype(F32) + mine_ref[16:32, :].astype(F32)
    lines = mine + (got_ref[size : size + 16, :].astype(F32) + got_ref[size + 16 : size + 32, :].astype(F32))
    high = lines.astype(BF16)
    rest = (lines - high.astype(F32)).astype(BF16)
    next_ref[...] = keep_ref[0:part, :].astype(F32) + got_ref[0:part, :].astype(F32)
    for i, send_ref in enumerate(send_refs):
        here = slice((i + 1) * part, (i + 2) * part)
        send_ref[0:part, :] = (keep_ref[here, :].astype(F32) + got_ref[here, :].astype(F32)).astype(BF16)
        send_ref[part : part + 16, :] = high
        send_ref[part + 16 : part + 32, :] = rest


def lines_of(ref):
    size = ref.shape[0] - 32
    return ref[size : size + 16, :].astype(F32) + ref[size + 16 : size + 32, :].astype(F32)


def two_tiles(ref, right, mi, t):
    if (t + 2) * SPAN <= ref.shape[1]:
        return ref[mi, t * SPAN : (t + 2) * SPAN, :]
    return jnp.concatenate((ref[mi, t * SPAN :, :], right[mi]), axis=0)


def unroll_kernel(offsets, result_ref, gmid_ref, right_ref, out_ref, part_ref, wide_ref):
    mi = pl.program_id(0)
    for t in range(result_ref.shape[1] // SPAN):
        here = slice(t * SPAN, (t + 1) * SPAN)
        for i, (ref, target) in enumerate(((result_ref, out_ref), (gmid_ref, part_ref))):
            wide_ref[i] = two_tiles(ref, right_ref.at[i], 0, t).astype(F32)
            target[0, here, :] = roll_rows(wide_ref.at[i], SPAN - offsets[mi]).astype(BF16)


def input_part_kernel(offsets, x_ref, gmid_ref, gn_ref, right_ref, gain, part_ref, wide_ref):
    mi = pl.program_id(0)
    for t in range(x_ref.shape[1] // SPAN):
        here = slice(t * SPAN, (t + 1) * SPAN)
        wide_ref[...] = two_tiles(gn_ref, right_ref, 0, t).astype(F32)
        grad = roll_rows(wide_ref, SPAN - offsets[mi])
        hat, inverse = unit(x_ref[0, here, :].astype(F32))
        part_ref[0, here, :] = gmid_ref[0, here, :].astype(F32) + unit_back(grad * gain[...], hat, inverse)


def finish_rest_kernel(keep_ref, a_ref, b_ref, c_ref, wo_ref, wu_ref, wd_ref):
    total = keep_ref[...] + (a_ref[...].astype(F32) + (b_ref[...].astype(F32) + c_ref[...].astype(F32)))
    wo_ref[...] = total[:, :128]
    wu_ref[...] = total[:, 128:640]
    wd_ref[...] = total[:, 640:]


def finish_kernel(
    direct, place, offsets, lengths, x_ref, part_ref, gain, *refs
):
    if direct:
        keep_ref, mine_ref, a_ref, b_ref, c_ref, out_ref, wq_ref, wk_ref, wv_ref, *line_refs = refs
        size = keep_ref.shape[0]
        total = (keep_ref[...] + a_ref[0:size, :].astype(F32)) + (
            b_ref[0:size, :].astype(F32) + c_ref[0:size, :].astype(F32)
        )
        wq_ref[...], wk_ref[...], wv_ref[...] = total[:, :128], total[:, 128:256], total[:, 256:384]
        pooled = total[:, 384:]
        lines = (lines_of(mine_ref) + lines_of(a_ref)) + (lines_of(b_ref) + lines_of(c_ref))
        ub_ref, *line_refs = line_refs
        for i in range(4):
            ub_ref[:, i * D : (i + 1) * D] = lines[4 + i : 5 + i, :]
        for ref, i in zip(line_refs, (0, 1, 2, 3, 8, 9, 10, 11)):
            ref[...] = lines[i : i + 1, :]
    else:
        pooled_ref, out_ref = refs
        pooled = pooled_ref[...]
    rows = x_ref.shape[1]
    for mi in range(2):
        dev, offset, ends = row_info(place, offsets, lengths, mi)
        first, last = summary_range(dev * (rows // SPAN) + iota((8, 1), 0), offset, ends)
        lows = jnp.concatenate(
            [pooled[16 * i + 8 * mi : 16 * i + 8 * mi + 8, :] for i in range(D // LANES)], axis=1
        )
        lows = (lows * gain[...] * lax.rsqrt((last - first + 1).astype(F32))).astype(BF16)
        first, last = summary_range(dev * (rows // SPAN) + iota((1, 8), 1), offset, ends)
        for t in range(rows // SPAN):
            here = slice(t * SPAN, (t + 1) * SPAN)
            pos = dev * rows + t * SPAN + iota((SPAN, 1), 0)
            member = jnp.where((pos >= first) & (pos <= last), 1.0, 0.0).astype(BF16)
            hat, inverse = unit(x_ref[mi, here, :].astype(F32))
            out_ref[mi, here, :] = part_ref[mi, here, :] + unit_back(dot(member, lows), hat, inverse)


def call(kernel, outs, in_specs, out_specs=None, scratch=(), limit=56, **more):
    return pl.pallas_call(
        kernel,
        out_shape=outs,
        in_specs=in_specs,
        out_specs=out_specs if out_specs is not None else [VMEM] * len(outs),
        scratch_shapes=list(scratch),
        compiler_params=pltpu.CompilerParams(vmem_limit_bytes=limit * MIB),
        cost_estimate=pl.CostEstimate(flops=1, bytes_accessed=1, transcendentals=0),
        **more,
    )


def call_row(kernel, mi, facts, arrays, outs, before, scratch, **more):
    def block(dims):
        return pl.BlockSpec((1,) + dims[1:], lambda i: (mi,) + (0,) * (len(dims) - 1))

    aliases = {3 + len(arrays) + i: i for i in range(len(before))}
    return call(
        partial(kernel, mi), outs, [SMEM] * 3 + [block(a.shape) for a in arrays] + [ANY] * len(before),
        [block(o.shape) for o in outs], scratch, grid=(1,), input_output_aliases=aliases, **more,
    )(*facts, *arrays, *before)


def tie(value, *others):
    return lax.optimization_barrier((value,) + others)[0]


def per_device(
    block_input, cotangent, span_offset, doc_lengths, ln1_gain, ln1_bias, w_query, w_key, w_value,
    query_bias, value_bias, w_out, out_bias, ln2_gain, ln2_bias, w_up, up_bias, w_down, down_bias,
):
    groups, ranks = lax.axis_size("seq"), lax.axis_size("mp")
    count = groups * ranks
    mp_index = lax.axis_index("mp")
    dev = lax.axis_index("seq") * ranks + mp_index
    rows = block_input.shape[1]
    tiles = rows // SPAN
    summaries = tiles * count
    shard = w_query.shape[0]
    bits = count.bit_length() - 1
    stages = [(b, b) for b in range(bits - 1, 2, -1)] + [(1, 2), (2, 1)]
    direct = shard == 64

    def swap(value, stage):
        pairs = [(i, i ^ (1 << stage[i & 1])) for i in range(count)]
        return lax.ppermute(value, AXES, pairs)

    def turn(value, by):
        return lax.ppermute(value, AXES, [(i, (i + by) % count) for i in range(count)])

    core = dev & 1
    slot = jnp.arange(count, dtype=jnp.int32)
    far = slot // (count // 2)
    mask = far
    for i, (even, odd) in enumerate(stages):
        where = jnp.where((core ^ far) == 0, even, odd)
        mask = mask | (((slot >> i) & 1) << where)
    owner = dev ^ mask
    if not direct:
        owner = slot
    member_slot = jnp.arange(16, dtype=jnp.int32)
    slots = owner[:, None] * tiles + (member_slot % 8)[None, :]
    valid = (member_slot % 8 <= tiles)[None, :]
    slots = jnp.stack(
        [
            jnp.where(valid & (member_slot // 8 == mi)[None, :], slots, -1).reshape(-1)
            for mi in range(2)
        ]
    )
    block_of, row_of = owner % ranks, owner // ranks
    facts = (jnp.stack((dev, mp_index)), span_offset, doc_lengths)

    def reach(value, flip):
        return lax.ppermute(value, AXES, [(i, i ^ flip) for i in range(count)])

    def spread(values):
        return [reach(value, flip) for value, flip in zip(values, (16, 8, 24))]

    def join(near, far):
        return jnp.concatenate((near, far), axis=0)

    def fold(keep, got):
        total = keep + got.astype(F32)
        half = total.shape[0] // 2
        return total[:half], total[half:].astype(BF16)

    def whole_blocks(arrays):
        return [pl.BlockSpec(a.shape, lambda i, n=len(a.shape): (0,) * n) for a in arrays]

    def fold_lines(keep, sent, got, sends=1):
        size = keep.shape[0]
        part = size // (1 + sends)
        outs = [shape((part, D), F32)] + [shape((part + 32, D), BF16)] * sends
        mine = pl.BlockSpec((32, D), lambda i: (size // 32, 0))
        both = whole_blocks((keep, got))
        return call(fold_kernel, outs, [both[0], mine, both[1]], whole_blocks(outs), grid=(1,))(keep, sent, got)

    def gather_whole(value):
        both = lax.all_gather(value, "seq", axis=0, tiled=True)
        both = lax.all_gather(both, "mp", axis=0)
        return both[: ranks // 2], both[ranks // 2 :]

    def scatter_whole(keep, send):
        both = jnp.concatenate((keep, send), axis=0).astype(F32)
        total = lax.psum_scatter(both, "mp", scatter_dimension=0, tiled=True)[0]
        return lax.psum_scatter(total, "seq", scatter_dimension=0, tiled=True)

    def row(vector):
        return vector[None, :]

    def shape(dims, kind):
        return jax.ShapeDtypeStruct(dims, kind)

    half, tall = (count // 2, shard) if direct else (ranks // 2, shard * groups)
    width = 4 * LANES if direct else 3 * LANES
    apart = not direct
    wide, three = (2, rows, D), (2, rows, 3 * D)
    flat, pooled_dims = (2 * rows, D), (2, summaries, D)
    masks = [pltpu.VMEM((tiles, SPAN + summaries, SPAN), F32)]
    w_rest = jnp.concatenate((w_out.T, w_up, w_down.T), axis=1)

    def prepare():
        return call(
            prepare_kernel, [shape((1, max(shard, 64), D), BF16)] + [shape((2, SPAN, D), BF16)] * 2,
            [SMEM] * 3 + [VMEM, ANY] + [VMEM] * 3, [VMEM] * 3,
            scratch=[pltpu.SemaphoreType.DMA((1,))],
        )(*facts, block_input, cotangent, w_query, w_key, w_value)

    part_a, x_edge, cot_edge = prepare()
    if direct:
        got_a = spread([part_a] * 3)
        x_left = turn(tie(x_edge, part_a), 1)
        part_b = tie(w_rest[None], got_a[0])
        got_b = spread([part_b] * 3)
        part_a = tie(jnp.concatenate([part_a] + got_a, axis=0), x_left)
        part_a = tie(join(part_a, swap(part_a, stages[2])), *got_b)
        got_a = swap(part_a, stages[3])
        part_b = tie(jnp.concatenate([part_b] + got_b, axis=0), part_a)
        got_b = swap(part_b, stages[2])
        near_a = join(part_a, got_a)
        far_a = swap(near_a, (0, 0))
        part_b = join(part_b, tie(got_b, near_a))
        got_b = swap(part_b, stages[3])
        cot_left = turn(tie(cot_edge, part_b), 1)
        more = ()
    else:
        x_left, cot_left = turn(x_edge, 1), turn(cot_edge, 1)
        near_a, far_a = gather_whole(part_a[0, :shard, :384])
        near_b, far_b = gather_whole(w_rest)
        more = (lax.all_gather(part_a[0, :64, 384:], AXES, axis=0),)
        block_of, row_of = jnp.arange(ranks, dtype=jnp.int32), jnp.zeros((ranks,), jnp.int32)

    xs, qkv, skv, sums, w_full = call(
        partial(project_kernel, apart),
        [shape(wide, BF16), shape(three, BF16), shape((2, summaries, 3 * D), BF16), shape(pooled_dims, F32)]
        + [shape((D, 3 * D), BF16)],
        [SMEM] * 5 + [VMEM] * 7 + [ANY] * (2 + len(more)),
        scratch=[
            pltpu.VMEM((count, 64, LANES), BF16),
            pltpu.VMEM((rows + SPAN, D), F32),
            pltpu.VMEM((2, rows + 2 * summaries, D), BF16),
            pltpu.SemaphoreType.DMA((2,)),
        ],
    )(
        *facts, block_of, row_of, slots, block_input, x_left, row(ln1_gain), row(ln1_bias),
        row(query_bias), row(value_bias), near_a, far_a, *more,
    )
    outs = [shape(wide, BF16), shape((2, 4, tiles, 1, 2 * SPAN), F32)]
    seen = call_row(attend_kernel, 0, facts, (qkv, skv), outs, (), masks)
    if direct:
        near_b = join(part_b, tie(got_b, seen[0], cot_left))
        far_b = swap(near_b, (0, 0))
        seen = [tie(seen[0], near_b)] + list(seen[1:])
    att, lse = call_row(attend_kernel, 1, facts, (qkv, skv), outs, tuple(seen), masks)
    result, gmid, edge, gatt, small_b, grad_ub, keep_b, send_b = call(
        mlp_kernel,
        [shape(wide, BF16)] * 2 + [shape((2, 2, SPAN, D), BF16), shape(wide, BF16)] + [shape((8, D), F32), shape((1, FF), F32)]
        + [shape((half, tall, 1152), BF16)] * 2,
        [SMEM] * 4 + [VMEM] * 8 + [ANY] * 3,
        [VMEM] * 6 + [ANY] * 2,
        scratch=[
            pltpu.VMEM((D, D), BF16), pltpu.VMEM((D, FF), BF16), pltpu.VMEM((D, FF), BF16),
            pltpu.VMEM(flat, F32), pltpu.VMEM(flat, F32), pltpu.VMEM(flat, F32),
            pltpu.VMEM(flat, BF16), pltpu.VMEM(flat, BF16),
            pltpu.VMEM((D, 2 * rows), BF16), pltpu.VMEM((D, 2 * rows), BF16),
            pltpu.VMEM((D, FF), BF16), pltpu.VMEM((D, FF), BF16), pltpu.VMEM((D, D), BF16),
            pltpu.VMEM((D, D), F32), pltpu.VMEM((D, D), F32), pltpu.VMEM((D, D), F32),
            pltpu.VMEM((rows + SPAN, D), F32), pltpu.VMEM(wide, BF16),
            pltpu.SemaphoreType.DMA((4,)), pltpu.SemaphoreType.DMA((3,)),
        ],
    )(
        facts[0], span_offset, block_of, row_of, xs, att, cot_left, row(out_bias), row(ln2_gain), row(ln2_bias),
        row(up_bias), row(down_bias), cotangent, near_b, far_b,
    )
    arrays = (qkv, skv, lse, gatt)
    outs = [shape(three, BF16), shape((2, summaries, 3 * D), BF16)]
    if direct:
        got_b = swap(send_b, (0, 0))
        back = turn(tie(edge, send_b), -1)
    grads = call_row(attend_back_kernel, 0, facts, arrays, outs, (), masks)
    if direct:
        keep_b, send_b = fold(keep_b.astype(F32), tie(got_b, grads[0], back))
        got_b = swap(send_b, stages[3])
        grads = [tie(grads[0], send_b)] + list(grads[1:])
    grads = call_row(attend_back_kernel, 1, facts, arrays, outs, tuple(grads), masks)
    lines, keep_a, send_a, *more = call(
        partial(weights_back_kernel, apart),
        [shape((16, D), F32)]
        + [shape((half * tall, width), BF16), shape((half * tall + (32 if direct else 0), width), BF16)]
        + [shape((count, 64, LANES), BF16)] * apart,
        [SMEM] * 5 + [VMEM] * 10,
        [VMEM] + [ANY] * (2 + apart),
        scratch=[
            pltpu.VMEM((D, 3 * D), BF16), pltpu.VMEM(pooled_dims, BF16), pltpu.VMEM((count, 64, LANES), BF16),
            pltpu.VMEM((32, D), BF16), pltpu.SemaphoreType.DMA((3,)),
        ],
    )(
        *facts, block_of, row_of, slots, xs, *grads, sums, w_full, row(ln1_gain), row(ln1_bias), small_b, grad_ub,
    )

    def by_row(dims):
        return pl.BlockSpec((1,) + dims[1:], lambda i: (i,) + (0,) * (len(dims) - 1))

    once = pl.BlockSpec((1, D), lambda i: (0, 0))
    edge_dims = (2, SPAN, D)

    def rows_back(*after):
        return call(
            rows_back_kernel, [shape(wide, BF16), shape(edge_dims, BF16)],
            [by_row(three), pl.BlockSpec((D, 3 * D), lambda i: (0, 0))], [by_row(wide), by_row(edge_dims)], grid=(2,),
        )(grads[0], tie(w_full, *after))

    def unroll(back):
        return call(
            unroll_kernel, [shape(wide, BF16)] * 2,
            [SMEM, by_row(wide), by_row(wide), pl.BlockSpec((2, 1, SPAN, D), lambda i: (0, i, 0, 0))],
            [by_row(wide)] * 2, [pltpu.VMEM((2, 2 * SPAN, D), F32)], grid=(2,),
        )(span_offset, result, gmid, back)

    def input_part(gmid, gn, back):
        return call(
            input_part_kernel, [shape(wide, F32)], [SMEM] + [by_row(wide)] * 3 + [by_row(edge_dims), once],
            [by_row(wide)], [pltpu.VMEM((2 * SPAN, D), F32)], grid=(2,),
        )(span_offset, block_input, gmid, gn, back, row(ln1_gain))[0]

    final = [SMEM] * 3 + [VMEM] * 3
    if direct:
        got_a = swap(send_a, (0, 0))
        keep_b, send_b = fold(keep_b, tie(got_b, send_a))
        got_b = swap(send_b, stages[2])
        gn, edge = rows_back(send_b)
        keep_a, send_a = fold_lines(keep_a, send_a, tie(got_a, gn))
        got_a = swap(send_a, stages[3])
        gn_back = turn(tie(edge, send_a), -1)
        total = keep_b + tie(got_b, send_a).astype(F32)
        got_b = spread([total[i].astype(BF16) for i in (1, 2, 3)])
        keep_b = total[0]
        result_own, gmid_own = unroll(tie(back, send_a))
        keep_a, send_a = fold_lines(keep_a, send_a, tie(got_a, gmid_own))
        got_a = swap(send_a, stages[2])
        part = input_part(gmid_own, gn, tie(gn_back, send_a))
        keep_a, *send_a = fold_lines(keep_a, send_a, tie(got_a, part), 3)
        got_a = spread(send_a)
        grad_wo, grad_wu, grad_wd = call(
            finish_rest_kernel, [shape((shard, LANES), F32), shape((shard, 512), F32), shape((shard, 512), F32)],
            [VMEM] * 4,
        )(keep_b, *(tie(got, send_a[0]) for got in got_b))
        input_grad, grad_wq, grad_wk, grad_wv, grad_ub, *small = call(
            partial(finish_kernel, True),
            [shape(wide, F32)] + [shape((shard, LANES), F32)] * 3 + [shape((1, FF), F32)] + [shape((1, D), F32)] * 8,
            final + [VMEM] * 5,
        )(*facts, block_input, part, row(ln1_gain), keep_a, send_a[0], *(tie(got, grad_wo) for got in got_a))
        grad_wo, grad_wd = grad_wo.T, grad_wd.T
        small = [a.reshape(D) for a in small]
        grad_ub = grad_ub.reshape(FF)
    else:
        keep_a, send_a = (a.reshape(half, tall, width) for a in (keep_a, send_a))
        result_own, gmid_own = unroll(turn(edge, -1))
        gn, edge = rows_back()
        part = input_part(gmid_own, gn, turn(edge, -1))
        sum_a, sum_b = scatter_whole(keep_a, send_a), scatter_whole(keep_b, send_b)
        grad_wq, grad_wk, grad_wv = (sum_a[:, i : i + LANES] for i in (0, 128, 256))
        grad_wo, grad_wu, grad_wd = sum_b[:, :128].T, sum_b[:, 128:640], sum_b[:, 640:].T
        pooled = lax.psum_scatter(more[0].astype(F32), AXES, scatter_dimension=0, tiled=True)[0]
        lines = lax.psum(lines, AXES)
        grad_ub = lines[4:8].reshape(FF)
        small = [lines[i] for i in (0, 1, 2, 3, 8, 9, 10, 11)]
        input_grad = call(partial(finish_kernel, False), [shape(wide, F32)], final + [VMEM])(
            *facts, block_input, part, row(ln1_gain), pooled
        )[0]
    grad_gain_two, grad_shift_two, grad_obias, grad_dbias, grad_gain_one, grad_shift_one, grad_qb, grad_vb = small
    return (
        result_own,
        input_grad,
        grad_gain_one,
        grad_shift_one,
        grad_wq,
        grad_wk,
        grad_wv,
        grad_qb,
        grad_vb,
        grad_wo,
        grad_obias,
        grad_gain_two,
        grad_shift_two,
        grad_wu,
        grad_ub,
        grad_wd,
        grad_dbias,
    )


def solution(mesh):
    vector, matrix, turned = P(), P("seq", "mp"), P("mp", "seq")
    own, group = P(None, ("seq", "mp"), None), P(None, "seq", None)
    return jax.shard_map(
        per_device,
        mesh=mesh,
        in_specs=(own, group, vector, vector, vector, vector, matrix, matrix, matrix, vector, vector)
        + (turned, vector, vector, vector, matrix, vector, turned, vector),
        out_specs=(own, own, vector, vector, matrix, matrix, matrix, vector, vector, turned, vector)
        + (vector, vector, matrix, vector, turned, vector),
        check_vma=False,
    )
```

```python
from functools import partial
import math

import jax
import jax.numpy as jnp
from jax import lax
from jax.experimental import pallas as pl
from jax.experimental.pallas import tpu as pltpu
from jax.sharding import PartitionSpec as P

D = 512
FF = 2048
HEAD_DIM = 64
SPAN = 128
LANES = 128
EPSILON = 1e-05
NEGATIVE = -1e30
SCALE = 1.0 / math.sqrt(HEAD_DIM)
F32 = jnp.float32
BF16 = jnp.bfloat16
AXES = ("seq", "mp")
MIB = 1 << 20
VMEM = pl.BlockSpec(memory_space=pltpu.VMEM)
SMEM = pl.BlockSpec(memory_space=pltpu.SMEM)
ANY = pl.BlockSpec(memory_space=pl.ANY)
HBM = pl.BlockSpec(memory_space=pltpu.HBM)


def dot(left, right):
    return lax.dot_general(left, right, (((1,), (0,)), ((), ())), preferred_element_type=F32)


def dot_cols(left, right):
    return lax.dot_general(left, right, (((1,), (1,)), ((), ())), preferred_element_type=F32)


def unit(rows):
    centred = rows - jnp.mean(rows, axis=-1, keepdims=True)
    inverse = lax.rsqrt(jnp.mean(centred * centred, axis=-1, keepdims=True) + EPSILON)
    return centred * inverse, inverse


def unit_back(grad, hat, inverse):
    shift = jnp.mean(grad, axis=-1, keepdims=True)
    slope = jnp.mean(grad * hat, axis=-1, keepdims=True)
    return (grad - shift - hat * slope) * inverse


def row_info(place, offsets, lengths, mi):
    ends = []
    for c in range(lengths.shape[1]):
        ends.append(lengths[mi, c] + (ends[-1] if ends else 0))
    return place[0], offsets[mi], ends


def doc_start(positions, ends):
    start = jnp.zeros_like(positions)
    for end in ends:
        start = jnp.where(positions >= end, end, start)
    return start


def summary_range(summary_ids, offset, ends):
    last = offset - 1 + SPAN * summary_ids
    first = jnp.maximum(doc_start(last, ends), last - (SPAN - 1))
    return first, last


def iota(shape, dim):
    return lax.broadcasted_iota(jnp.int32, shape, dim)


def roll_rows(ref, by):
    whole = pl.multiple_of((by // 8) * 8, 8)
    return pltpu.roll(ref[pl.ds(whole, SPAN + 8), :], SPAN + 8 - (by - whole), axis=0)[:SPAN]


def prepare_kernel(
    place, offsets, lengths, x_ref, cot_ref, wq_ref, wk_ref, wv_ref, out_ref, edge_ref, rows_ref, sem
):
    rows = x_ref.shape[1]
    last_rows = pl.multiple_of(place[1] * rows + (rows - SPAN), SPAN)
    shard = wq_ref.shape[0]
    copies = [pltpu.make_async_copy(x_ref.at[mi], rows_ref.at[mi], sem.at[mi]) for mi in range(2)]
    copies += [
        pltpu.make_async_copy(ref, out_ref.at[0, 0:shard, i * LANES : (i + 1) * LANES], sem.at[2 + i])
        for i, ref in enumerate((wq_ref, wk_ref, wv_ref))
    ]
    copies.append(pltpu.make_async_copy(cot_ref.at[:, pl.ds(last_rows, SPAN), :], edge_ref, sem.at[5]))
    for copy in copies:
        copy.start()
    sums = []
    for mi in range(2):
        dev, offset, ends = row_info(place, offsets, lengths, mi)
        first, last = summary_range(dev * (rows // SPAN) + iota((8, 1), 0), offset, ends)
        pos = dev * rows + iota((1, rows), 1)
        member = jnp.where((pos >= first) & (pos <= last), 1.0, 0.0).astype(BF16)
        copies[mi].wait()
        hat, _ = unit(rows_ref[mi].astype(F32))
        high = hat.astype(BF16)
        rest = (hat - high.astype(F32)).astype(BF16)
        total = dot(member, high) + dot(member, rest)
        sums.append(total * lax.rsqrt((last - first + 1).astype(F32)))
    both = jnp.concatenate(sums, axis=0).astype(BF16)
    for copy in copies[2:]:
        copy.wait()
    for lane in range(D // LANES):
        out_ref[0, 16 * lane : 16 * lane + 16, 384:512] = both[:, lane * LANES : (lane + 1) * LANES]


def fill_masks(place, offsets, lengths, mi, bias_ref, tiles, summaries, length):
    dev, offset, ends = row_info(place, offsets, lengths, mi)
    ends_col = offset - 1 + SPAN * iota((summaries, 1), 0)
    for t in range(tiles):
        base = SPAN * (dev * tiles + t) + offset - SPAN
        qpos = base + iota((1, SPAN), 1)
        qpos = jnp.where(qpos < 0, qpos + length, qpos)
        kpos = base + iota((SPAN, 1), 0)
        kpos = jnp.where(kpos < 0, kpos + length, kpos)
        span_first = jnp.where(qpos >= base + SPAN, base + length, base)
        doc_first = doc_start(qpos, ends)
        local_ok = (kpos >= jnp.maximum(doc_first, span_first)) & (kpos <= qpos)
        summary_ok = (ends_col >= doc_first) & (ends_col < span_first)
        bias_ref[t, 0:SPAN, :] = jnp.where(local_ok, 0.0, NEGATIVE)
        bias_ref[t, SPAN : SPAN + summaries, :] = jnp.where(summary_ok, 0.0, NEGATIVE)


def split_heads(pair):
    low = iota(pair.shape, 1) < HEAD_DIM
    zero = jnp.zeros_like(pair)
    return jnp.concatenate((jnp.where(low, pair, zero), jnp.where(low, zero, pair)), axis=0)


def join_heads(turned):
    half = turned.shape[1] // 2
    return jnp.concatenate((turned[:HEAD_DIM, :half], turned[HEAD_DIM:, half:]), axis=0).T


def project_kernel(
    apart, place_ref, offsets, lengths, block_of, row_of, slots_ref, x_ref, left_ref, gain, shift, qbias, vbias,
    near_ref, far_ref, *refs
):
    if apart:
        all_ref, *refs = refs
    xs_ref, qkv_ref, skv_ref, sums_ref, w_ref, stack_ref, wide_ref, rows_ref, sem = refs
    rows = x_ref.shape[1]
    tiles = rows // SPAN
    summaries = skv_ref.shape[1]
    half, shard, _ = near_ref.shape

    def place(d, carry):
        for source, slot in ((near_ref, d), (far_ref, half + d)):
            here = pl.ds(pl.multiple_of(row_of[slot] * shard, 16), shard)
            cols = pl.ds(pl.multiple_of(block_of[slot] * 384, 128), 384)
            pltpu.make_async_copy(source.at[d, :, 0:384], w_ref.at[here, cols], sem.at[0]).start()
            if not apart:
                pltpu.make_async_copy(
                    source.at[d, 0:64, 384:512], stack_ref.at[slot], sem.at[1]
                ).start()
        return carry

    lax.fori_loop(0, half, place, 0)
    if apart:
        pltpu.make_async_copy(all_ref, stack_ref, sem.at[1]).start()
    for mi in range(2):
        wide_ref[0:SPAN, :] = left_ref[mi].astype(F32)
        wide_ref[SPAN : SPAN + rows, :] = x_ref[mi].astype(F32)
        for t in range(tiles):
            here = slice(t * SPAN, (t + 1) * SPAN)
            rolled = roll_rows(wide_ref, t * SPAN + offsets[mi])
            xs_ref[mi, here, :] = rolled.astype(BF16)
            hat, _ = unit(rolled)
            rows_ref[mi, here, :] = (hat * gain[...] + shift[...]).astype(BF16)
    pltpu.make_async_copy(stack_ref, stack_ref, sem.at[1]).wait()
    roots = []
    for mi in range(2):
        _, offset, ends = row_info(place_ref, offsets, lengths, mi)
        first, last = summary_range(iota((summaries, 1), 0), offset, ends)
        root = jnp.sqrt((last - first + 1).astype(F32))
        roots.append(root)
        for base in range(0, stack_ref.shape[0], 32):
            named = slots_ref[mi : mi + 1, 16 * base : 16 * base + 512]
            pick = jnp.where(iota((summaries, 1), 0) == named, 1.0, 0.0).astype(BF16)
            piece = jnp.concatenate(
                [
                    stack_ref[base : base + 32, 16 * lane : 16 * lane + 16, :].reshape(512, LANES)
                    for lane in range(D // LANES)
                ],
                axis=1,
            )
            found = dot(pick, piece)
            sums_ref[mi] = found if base == 0 else sums_ref[mi] + found
        summed = sums_ref[mi] * gain[...] + root * shift[...]
        high = summed.astype(BF16)
        rows_ref[mi, rows : rows + summaries, :] = high
        rows_ref[mi, rows + summaries : rows + 2 * summaries, :] = (summed - high.astype(F32)).astype(BF16)
    pltpu.make_async_copy(w_ref, w_ref, sem.at[0]).wait()
    none = jnp.zeros((1, LANES), F32)
    for m in range(4):
        lanes = slice(m * LANES, (m + 1) * LANES)
        cols = slice(m * 384, (m + 1) * 384)
        bias = jnp.concatenate((qbias[:, lanes], none, vbias[:, lanes]), axis=1)
        for mi in range(2):
            projected = dot(rows_ref[mi], w_ref[:, cols])
            qkv_ref[mi, :, cols] = (projected[:rows] + bias).astype(BF16)
            pooled = projected[rows : rows + summaries] + projected[rows + summaries :]
            skv_ref[mi, :, cols] = (pooled + roots[mi] * bias).astype(BF16)


def pair_of(ref, here, pair):
    def part(i):
        return ref[0, here, pl.ds(pl.multiple_of(pair * 384 + i * LANES, LANES), LANES)]

    return part(0), part(1), part(2)


def attend_kernel(mi, place, offsets, lengths, qkv_ref, skv_ref, *refs):
    att_ref, lse_ref, bias_ref = refs[-3:]
    rows = qkv_ref.shape[1]
    tiles = rows // SPAN
    summaries = skv_ref.shape[1]
    fill_masks(place, offsets, lengths, mi, bias_ref, tiles, summaries, summaries * SPAN)

    def heads(pair, carry):
        lanes = pl.ds(pl.multiple_of(pair * LANES, LANES), LANES)
        _, skeys, svalues = pair_of(skv_ref, slice(None), pair)
        svalues = svalues.T
        spans = [pair_of(qkv_ref, slice(t * SPAN, (t + 1) * SPAN), pair) for t in range(tiles)]
        scores = []
        for t, (queries, keys, _) in enumerate(spans):
            bias = bias_ref[t]
            keys = jnp.concatenate((keys, skeys), axis=0)
            scores.append(dot_cols(keys, split_heads(queries * SCALE)) + jnp.concatenate((bias, bias), axis=1))
        probs = []
        for t in range(tiles):
            top = jnp.max(scores[t], axis=0, keepdims=True)
            grown = jnp.exp(scores[t] - top)
            total = jnp.sum(grown, axis=0, keepdims=True)
            probs.append((grown * (1.0 / total)).astype(BF16))
            lse_ref[0, pair, t] = top + jnp.log(total)
        for t, (_, _, values) in enumerate(spans):
            values = jnp.concatenate((values.T, svalues), axis=1)
            att_ref[0, t * SPAN : (t + 1) * SPAN, lanes] = join_heads(dot(values, probs[t])).astype(BF16)
        return carry

    lax.fori_loop(0, 4, heads, 0)


def gelu_pair(u):
    c0 = math.sqrt(2.0 / math.pi)
    square = u * u
    t = jnp.tanh(c0 * u * (1.0 + 0.044715 * square))
    half = 0.5 * (1.0 + t)
    slope = half + (0.5 * c0) * u * (1.0 - t * t) * (1.0 + (3 * 0.044715) * square)
    return u * half, slope


def mlp_kernel(
    place_ref, offsets, block_of, row_of, xs_ref, att_ref, left_ref, obias, gain, shift, ubias, dbias, cot_ref,
    near_ref, far_ref,
    result_ref, gmid_ref, edge_ref, gatt_ref, small_ref, gub_ref, keep_ref, send_ref,
    wo_ref, wu_ref, wd_ref, resid_ref, acc_ref, gn_ref, n_ref, c_ref, nt_ref, ct_ref, gu_ref, gd_ref, go_ref,
    wide_ref, low_ref, sem, out_sem,
):
    rows = xs_ref.shape[1]
    tiles = rows // SPAN
    half, shard, _ = near_ref.shape
    own = pl.ds(pl.multiple_of(place_ref[1] * rows, SPAN), rows)
    own_copy = pltpu.make_async_copy(cot_ref.at[:, own, :], low_ref, sem.at[3])
    own_copy.start()

    def columns(block, width):
        return pl.ds(pl.multiple_of(block * width, 128), width)

    def place(first):
        def body(d, carry):
            for source, slot in ((near_ref, d), (far_ref, half + d)):
                here = pl.ds(pl.multiple_of(row_of[slot] * shard, 16), shard)
                block = block_of[slot]
                if first:
                    pltpu.make_async_copy(
                        source.at[d, :, 0:128], wo_ref.at[here, columns(block, 128)], sem.at[0]
                    ).start()
                else:
                    wide = columns(block, 512)
                    pltpu.make_async_copy(source.at[d, :, 128:640], wu_ref.at[here, wide], sem.at[1]).start()
                    pltpu.make_async_copy(source.at[d, :, 640:1152], wd_ref.at[here, wide], sem.at[2]).start()
            return carry

        lax.fori_loop(0, half, body, 0)

    place(True)
    place(False)
    small_ref[...] = jnp.zeros_like(small_ref)
    gub_ref[...] = jnp.zeros_like(gub_ref)
    own_copy.wait()
    pltpu.make_async_copy(wo_ref, wo_ref, sem.at[0]).wait()
    for mi in range(2):
        all_rows = slice(mi * rows, (mi + 1) * rows)
        wide_ref[0:SPAN, :] = left_ref[mi].astype(F32)
        wide_ref[SPAN : SPAN + rows, :] = low_ref[mi].astype(F32)
        for t in range(tiles):
            rolled = roll_rows(wide_ref, t * SPAN + offsets[mi])
            small_ref[3:4, :] += jnp.sum(rolled, axis=0, keepdims=True)
            c_ref[mi * rows + t * SPAN : mi * rows + (t + 1) * SPAN, :] = rolled.astype(BF16)
        resid = xs_ref[mi].astype(F32) + dot_cols(att_ref[mi], wo_ref[...]) + obias[...]
        resid_ref[all_rows, :] = resid
        hat, _ = unit(resid)
        normed = (hat * gain[...] + shift[...]).astype(BF16)
        n_ref[all_rows, :] = normed
        nt_ref[:, all_rows] = normed.T
        ct_ref[:, all_rows] = c_ref[all_rows, :].T
        acc_ref[all_rows, :] = resid + dbias[...]
        gn_ref[all_rows, :] = jnp.zeros((rows, D), F32)
    pltpu.make_async_copy(wu_ref, wu_ref, sem.at[1]).wait()
    pltpu.make_async_copy(wd_ref, wd_ref, sem.at[2]).wait()

    def emit(pick, copies):
        def body(d, carry):
            for target, slot in ((keep_ref, d), (send_ref, half + d)):

                @pl.when(pick(block_of[slot]))
                def _():
                    here = pl.ds(pl.multiple_of(row_of[slot] * shard, 16), shard)
                    for source, width, cols, i in copies:
                        pltpu.make_async_copy(
                            source.at[here, columns(block_of[slot], width)], target.at[d, :, cols], out_sem.at[i]
                        ).start()

            return carry

        lax.fori_loop(0, half, body, 0)

    def chunk(ch, carry):
        cols = columns(ch, 1024)
        halves = [slice(mi * rows, (mi + 1) * rows) for mi in range(2)]
        w_up, w_down = wu_ref[:, cols], wd_ref[:, cols]
        ups = [dot(n_ref[here, :], w_up) + ubias[:, cols] for here in halves]
        backs = [dot(c_ref[here, :], w_down) for here in halves]
        acts, grads = [], []
        for here, up, back in zip(halves, ups, backs):
            act, slope = gelu_pair(up)
            grad = back * slope
            gub_ref[:, cols] += jnp.sum(grad, axis=0, keepdims=True)
            acts.append(act.astype(BF16))
            grads.append(grad.astype(BF16))
            acc_ref[here, :] += dot_cols(acts[-1], w_down)
            gn_ref[here, :] += dot_cols(grads[-1], w_up)
        gu_ref[:, cols] = dot(nt_ref[...], jnp.concatenate(grads, axis=0)).astype(BF16)
        gd_ref[:, cols] = dot(ct_ref[...], jnp.concatenate(acts, axis=0)).astype(BF16)
        emit(lambda b: b // 2 == ch, ((gu_ref, 512, slice(128, 640), 1), (gd_ref, 512, slice(640, 1152), 2)))
        return carry

    lax.fori_loop(0, 2, chunk, 0)
    branches = []
    for mi in range(2):
        here = slice(mi * rows, (mi + 1) * rows)
        result_ref[mi] = acc_ref[here, :].astype(BF16)
        hat, inverse = unit(resid_ref[here, :])
        grad = gn_ref[here, :]
        small_ref[0:1, :] += jnp.sum(grad * hat, axis=0, keepdims=True)
        small_ref[1:2, :] += jnp.sum(grad, axis=0, keepdims=True)
        branch = (c_ref[here, :].astype(F32) + unit_back(grad * gain[...], hat, inverse)).astype(BF16)
        gmid_ref[mi] = branch
        edge_ref[mi] = result_ref[mi, 0:SPAN, :]
        small_ref[2:3, :] += jnp.sum(branch.astype(F32), axis=0, keepdims=True)
        gatt_ref[mi] = dot(branch, wo_ref[...]).astype(BF16)
        branches.append(branch.T)
    go_ref[...] = dot(jnp.concatenate(branches, axis=1), jnp.concatenate((att_ref[0], att_ref[1]), axis=0)).astype(BF16)
    emit(lambda b: b >= 0, ((go_ref, 128, slice(0, 128), 0),))
    pltpu.make_async_copy(gu_ref, gu_ref, out_sem.at[1]).wait()
    pltpu.make_async_copy(gd_ref, gd_ref, out_sem.at[2]).wait()
    pltpu.make_async_copy(go_ref, go_ref, out_sem.at[0]).wait()


def attend_back_kernel(mi, place, offsets, lengths, qkv_ref, skv_ref, lse_ref, gatt_ref, *refs):
    grad_ref, pooled_ref, bias_ref = refs[-3:]
    rows = qkv_ref.shape[1]
    tiles = rows // SPAN
    summaries = skv_ref.shape[1]
    fill_masks(place, offsets, lengths, mi, bias_ref, tiles, summaries, summaries * SPAN)

    def heads(pair, carry):
        lanes = pl.ds(pl.multiple_of(pair * LANES, LANES), LANES)

        def columns(i):
            return pl.ds(pl.multiple_of(pair * 384 + i * LANES, LANES), LANES)

        _, skeys, svalues = pair_of(skv_ref, slice(None), pair)
        skeys_t = skeys.T
        sum_k = jnp.zeros((summaries, LANES), F32)
        sum_v = jnp.zeros((summaries, LANES), F32)
        held = []
        for t in range(tiles):
            here = slice(t * SPAN, (t + 1) * SPAN)
            queries, keys, values = pair_of(qkv_ref, here, pair)
            queries = split_heads(queries * SCALE)
            grads = split_heads(gatt_ref[0, here, lanes])
            bias = bias_ref[t]
            scores = dot_cols(jnp.concatenate((keys, skeys), axis=0), queries)
            gprobs = dot_cols(jnp.concatenate((values, svalues), axis=0), grads)
            held.append((queries, keys, grads, scores + jnp.concatenate((bias, bias), axis=1), gprobs))
        for t, (queries, keys, grads, scores, gprobs) in enumerate(held):
            here = slice(t * SPAN, (t + 1) * SPAN)
            probs = jnp.exp(scores - lse_ref[0, pair, t])
            delta = jnp.sum(probs * gprobs, axis=0, keepdims=True)
            gscores = (probs * (gprobs - delta)).astype(BF16)
            keys_t = jnp.concatenate((keys.T, skeys_t), axis=1)
            grad_q = join_heads(dot(keys_t, gscores)) * SCALE
            grad_k = dot(gscores, queries)
            grad_v = dot(probs.astype(BF16), grads)
            grad_ref[0, here, columns(0)] = grad_q.astype(BF16)
            grad_ref[0, here, columns(1)] = grad_k[:SPAN].astype(BF16)
            grad_ref[0, here, columns(2)] = grad_v[:SPAN].astype(BF16)
            sum_k += grad_k[SPAN:]
            sum_v += grad_v[SPAN:]
        pooled_ref[0, :, columns(0)] = jnp.zeros((summaries, LANES), BF16)
        pooled_ref[0, :, columns(1)] = sum_k.astype(BF16)
        pooled_ref[0, :, columns(2)] = sum_v.astype(BF16)
        return carry

    lax.fori_loop(0, 4, heads, 0)


def weights_back_kernel(
    apart, place, offsets, lengths, block_of, row_of, slots_ref, xs_ref, grad_ref, pooled_ref, sums_ref, w_ref,
    gain, shift, small_ref, gub_ref, line_ref, keep_ref, send_ref, *refs
):
    if apart:
        all_ref, *refs = refs
    gwb_ref, back_ref, stack_ref, pad_ref, sem = refs
    rows = xs_ref.shape[1]
    summaries = pooled_ref.shape[1]
    half = block_of.shape[0] // 2
    shard = keep_ref.shape[0] // half
    turned = []
    column = jnp.zeros((1, 3 * D), F32)
    for mi in range(2):
        _, offset, ends = row_info(place, offsets, lengths, mi)
        first, last = summary_range(iota((summaries, 1), 0), offset, ends)
        root = jnp.sqrt((last - first + 1).astype(F32))
        hat, _ = unit(xs_ref[mi].astype(F32))
        turned += [hat.astype(BF16).T, sums_ref[mi].astype(BF16).T]
        column += jnp.sum(grad_ref[mi].astype(F32), axis=0, keepdims=True)
        column += jnp.sum(root * pooled_ref[mi].astype(F32), axis=0, keepdims=True)
        back_ref[mi] = dot_cols(pooled_ref[mi], w_ref[...]).astype(BF16)
    turned = jnp.concatenate(turned, axis=1)
    gain_col, shift_col = gain[...].T, shift[...].T
    grad_gain = jnp.zeros((D, 1), F32)
    grad_shift = jnp.zeros((D, 1), F32)
    for m in range(4):
        cols = slice(m * 384, (m + 1) * 384)
        lanes = slice(m * LANES, (m + 1) * LANES)
        grads = jnp.concatenate([ref[mi, :, cols] for mi in range(2) for ref in (grad_ref, pooled_ref)], axis=0)
        hats, w, sums = dot(turned, grads), w_ref[:, cols].astype(F32), column[:, cols]
        grad_gain += jnp.sum(hats * w, axis=1, keepdims=True)
        grad_shift += jnp.sum(sums * w, axis=1, keepdims=True)
        gwb_ref[:, cols] = (hats * gain_col + shift_col * sums).astype(BF16)
        line_ref[10:11, lanes] = sums[:, :128]
        line_ref[11:12, lanes] = sums[:, 256:]
    line_ref[8:9, :] = grad_gain.T
    line_ref[9:10, :] = grad_shift.T
    line_ref[0:4, :] = small_ref[0:4, :]
    for i in range(4):
        line_ref[4 + i : 5 + i, :] = gub_ref[:, i * D : (i + 1) * D]
    line_ref[12:16, :] = jnp.zeros((4, D), F32)
    for base in range(0, stack_ref.shape[0], 32):
        names = [slots_ref[mi : mi + 1, 16 * base : 16 * base + 512] for mi in range(2)]
        spread = [
            jnp.where(iota((summaries, 1), 0) == named, 1.0, 0.0).astype(BF16).T for named in names
        ]
        piece = (dot(spread[0], back_ref[0]) + dot(spread[1], back_ref[1])).astype(BF16)
        for lane in range(D // LANES):
            part = piece[:, lane * LANES : (lane + 1) * LANES]
            stack_ref[base : base + 32, 16 * lane : 16 * lane + 16, :] = part.reshape(32, 16, LANES)

    def emit(d, carry):
        for target, slot in ((keep_ref, d), (send_ref, half + d)):
            first_row = pl.multiple_of(row_of[slot] * shard, 16)
            cols = pl.ds(pl.multiple_of(block_of[slot] * 384, 128), 384)
            here = target.at[pl.ds(pl.multiple_of(d * shard, 16), shard), :]
            pltpu.make_async_copy(
                gwb_ref.at[pl.ds(first_row, shard), cols], here.at[:, 0:384], sem.at[0]
            ).start()
            if not apart:
                pltpu.make_async_copy(stack_ref.at[slot], here.at[:, 384:512], sem.at[1]).start()
        return carry

    lax.fori_loop(0, half, emit, 0)
    if apart:
        pltpu.make_async_copy(stack_ref, all_ref, sem.at[1]).start()
    else:
        high = line_ref[...].astype(BF16)
        pad_ref[0:16, :] = high
        pad_ref[16:32, :] = (line_ref[...] - high.astype(F32)).astype(BF16)
        size = half * shard
        copy = pltpu.make_async_copy(pad_ref, send_ref.at[size : size + 32, :], sem.at[2])
        copy.start()
        copy.wait()
    pltpu.make_async_copy(gwb_ref, gwb_ref, sem.at[0]).wait()
    pltpu.make_async_copy(stack_ref, stack_ref, sem.at[1]).wait()


def rows_back_kernel(grad_ref, w_ref, xs_ref, gmid_ref, gain, part_ref, edge_ref):
    grad = dot_cols(grad_ref[0], w_ref[...]) * gain[...]
    hat, inverse = unit(xs_ref[0].astype(F32))
    part = gmid_ref[0].astype(F32) + unit_back(grad, hat, inverse)
    part_ref[0] = part
    edge_ref[0] = part[0:SPAN].astype(BF16)


def fold_kernel(keep_ref, mine_ref, got_ref, next_ref, *send_refs):
    size = keep_ref.shape[0]
    part = size // (1 + len(send_refs))
    mine = mine_ref[0:16, :].astype(F32) + mine_ref[16:32, :].astype(F32)
    lines = mine + (got_ref[size : size + 16, :].astype(F32) + got_ref[size + 16 : size + 32, :].astype(F32))
    high = lines.astype(BF16)
    rest = (lines - high.astype(F32)).astype(BF16)
    next_ref[...] = keep_ref[0:part, :].astype(F32) + got_ref[0:part, :].astype(F32)
    for i, send_ref in enumerate(send_refs):
        here = slice((i + 1) * part, (i + 2) * part)
        send_ref[0:part, :] = (keep_ref[here, :].astype(F32) + got_ref[here, :].astype(F32)).astype(BF16)
        send_ref[part : part + 16, :] = high
        if len(send_refs) == 1:
            send_ref[part + 16 : part + 32, :] = rest


def lines_of(ref):
    return ref[ref.shape[0] - 16 :, :].astype(F32)


def two_tiles(ref, right, mi, t):
    if (t + 2) * SPAN <= ref.shape[1]:
        return ref[mi, t * SPAN : (t + 2) * SPAN, :]
    return jnp.concatenate((ref[mi, t * SPAN :, :], right[mi].astype(ref.dtype)), axis=0)


def unroll_kernel(offsets, result_ref, right_ref, x_ref, out_ref, hat_ref, inverse_ref, wide_ref):
    mi = pl.program_id(0)
    for t in range(result_ref.shape[1] // SPAN):
        here = slice(t * SPAN, (t + 1) * SPAN)
        wide_ref[...] = two_tiles(result_ref, right_ref, 0, t).astype(F32)
        out_ref[0, here, :] = roll_rows(wide_ref, SPAN - offsets[mi]).astype(BF16)
        hat, inverse = unit(x_ref[0, here, :].astype(F32))
        hat_ref[0, here, :] = hat.astype(BF16)
        inverse_ref[0, here, :] = jnp.broadcast_to(inverse, (SPAN, LANES))


def finish_rest_kernel(keep_ref, got_ref, wo_ref, wu_ref, wd_ref):
    total = keep_ref[0] + got_ref[0].astype(F32)
    wo_ref[...] = total[:, :128]
    wu_ref[...] = total[:, 128:640]
    wd_ref[...] = total[:, 640:]


def finish_kernel(
    direct, place, offsets, lengths, hat_ref, inverse_ref, part_ref, right_ref, gain, *refs
):
    if direct:
        keep_ref, mine_ref, a_ref, b_ref, c_ref, out_ref, wq_ref, wk_ref, wv_ref, *line_refs, wide_ref = refs
        size = keep_ref.shape[0]
        total = (keep_ref[...] + a_ref[0:size, :].astype(F32)) + (
            b_ref[0:size, :].astype(F32) + c_ref[0:size, :].astype(F32)
        )
        wq_ref[...], wk_ref[...], wv_ref[...] = total[:, :128], total[:, 128:256], total[:, 256:384]
        pooled = total[:, 384:]
        lines = (lines_of(mine_ref) + lines_of(a_ref)) + (lines_of(b_ref) + lines_of(c_ref))
        ub_ref, *line_refs = line_refs
        for i in range(4):
            ub_ref[:, i * D : (i + 1) * D] = lines[4 + i : 5 + i, :]
        for ref, i in zip(line_refs, (0, 1, 2, 3, 8, 9, 10, 11)):
            ref[...] = lines[i : i + 1, :]
    else:
        pooled_ref, out_ref, wide_ref = refs
        pooled = pooled_ref[...]
    rows = hat_ref.shape[1]
    for mi in range(2):
        dev, offset, ends = row_info(place, offsets, lengths, mi)
        first, last = summary_range(dev * (rows // SPAN) + iota((8, 1), 0), offset, ends)
        lows = jnp.concatenate(
            [pooled[16 * i + 8 * mi : 16 * i + 8 * mi + 8, :] for i in range(D // LANES)], axis=1
        )
        lows = lows * gain[...] * lax.rsqrt((last - first + 1).astype(F32))
        level = (lows - jnp.mean(lows, axis=-1, keepdims=True)).astype(BF16)
        lows = lows.astype(BF16)
        first, last = summary_range(dev * (rows // SPAN) + iota((1, 8), 1), offset, ends)
        for t in range(rows // SPAN):
            here = slice(t * SPAN, (t + 1) * SPAN)
            pos = dev * rows + t * SPAN + iota((SPAN, 1), 0)
            member = jnp.where((pos >= first) & (pos <= last), 1.0, 0.0)
            hat = hat_ref[mi, here, :]
            slope = jnp.sum(member * dot_cols(hat, lows), axis=1, keepdims=True) * (1.0 / D)
            inverse = inverse_ref[mi, here, 0:1]
            wide_ref[...] = two_tiles(part_ref, right_ref, mi, t)
            own = roll_rows(wide_ref, SPAN - offset)
            out_ref[mi, here, :] = own + (dot(member.astype(BF16), level) - hat.astype(F32) * slope) * inverse


def call(kernel, outs, in_specs, out_specs=None, scratch=(), limit=8, **more):
    return pl.pallas_call(
        kernel,
        out_shape=outs,
        in_specs=in_specs,
        out_specs=out_specs if out_specs is not None else [VMEM] * len(outs),
        scratch_shapes=list(scratch),
        compiler_params=pltpu.CompilerParams(vmem_limit_bytes=limit * MIB),
        cost_estimate=pl.CostEstimate(flops=1, bytes_accessed=1, transcendentals=0),
        **more,
    )


def call_row(kernel, mi, facts, arrays, outs, before, scratch, **more):
    def block(dims):
        return pl.BlockSpec((1,) + dims[1:], lambda i: (mi,) + (0,) * (len(dims) - 1))

    aliases = {3 + len(arrays) + i: i for i in range(len(before))}
    return call(
        partial(kernel, mi), outs, [SMEM] * 3 + [block(a.shape) for a in arrays] + [ANY] * len(before),
        [block(o.shape) for o in outs], scratch, grid=(1,), input_output_aliases=aliases, **more,
    )(*facts, *arrays, *before)


def tie(value, *others):
    return lax.optimization_barrier((value,) + others)[0]


def per_device(
    block_input, cotangent, span_offset, doc_lengths, ln1_gain, ln1_bias, w_query, w_key, w_value,
    query_bias, value_bias, w_out, out_bias, ln2_gain, ln2_bias, w_up, up_bias, w_down, down_bias,
):
    groups, ranks = lax.axis_size("seq"), lax.axis_size("mp")
    count = groups * ranks
    mp_index = lax.axis_index("mp")
    dev = lax.axis_index("seq") * ranks + mp_index
    rows = block_input.shape[1]
    tiles = rows // SPAN
    summaries = tiles * count
    shard = w_query.shape[0]
    bits = count.bit_length() - 1
    stages = [(b, b) for b in range(bits - 1, 2, -1)] + [(1, 2), (2, 1)]
    direct = shard == 64

    def swap(value, stage):
        pairs = [(i, i ^ (1 << stage[i & 1])) for i in range(count)]
        return lax.ppermute(value, AXES, pairs)

    def turn(value, by):
        return lax.ppermute(value, AXES, [(i, (i + by) % count) for i in range(count)])

    core = dev & 1
    slot = jnp.arange(count, dtype=jnp.int32)
    far = slot // (count // 2)
    mask = far
    for i, (even, odd) in enumerate(stages):
        where = jnp.where((core ^ far) == 0, even, odd)
        mask = mask | (((slot >> i) & 1) << where)
    owner = dev ^ mask
    if not direct:
        owner = slot
    member_slot = jnp.arange(16, dtype=jnp.int32)
    slots = owner[:, None] * tiles + (member_slot % 8)[None, :]
    valid = (member_slot % 8 <= tiles)[None, :]
    slots = jnp.stack(
        [
            jnp.where(valid & (member_slot // 8 == mi)[None, :], slots, -1).reshape(-1)
            for mi in range(2)
        ]
    )
    block_of, row_of = owner % ranks, owner // ranks
    facts = (jnp.stack((dev, mp_index)), span_offset, doc_lengths)

    def reach(value, flip):
        return lax.ppermute(value, AXES, [(i, i ^ flip) for i in range(count)])

    def spread(values):
        return [reach(value, flip) for value, flip in zip(values, (16, 8, 24))]

    def join(near, far):
        return jnp.concatenate((near, far), axis=0)

    def fold(keep, got):
        total = keep + got.astype(F32)
        half = total.shape[0] // 2
        return total[:half], total[half:].astype(BF16)

    def whole_blocks(arrays):
        return [pl.BlockSpec(a.shape, lambda i, n=len(a.shape): (0,) * n) for a in arrays]

    def fold_lines(keep, sent, got, sends=1):
        size = keep.shape[0]
        part = size // (1 + sends)
        outs = [shape((part, D), F32)] + [shape((part + (32 if sends == 1 else 16), D), BF16)] * sends
        mine = pl.BlockSpec((32, D), lambda i: (size // 32, 0))
        both = whole_blocks((keep, got))
        return call(fold_kernel, outs, [both[0], mine, both[1]], whole_blocks(outs), grid=(1,))(keep, sent, got)

    def gather_whole(value):
        both = lax.all_gather(value, "seq", axis=0, tiled=True)
        both = lax.all_gather(both, "mp", axis=0)
        return both[: ranks // 2], both[ranks // 2 :]

    def scatter_whole(keep, send):
        both = jnp.concatenate((keep, send), axis=0).astype(F32)
        total = lax.psum_scatter(both, "mp", scatter_dimension=0, tiled=True)[0]
        return lax.psum_scatter(total, "seq", scatter_dimension=0, tiled=True)

    def row(vector):
        return vector[None, :]

    def shape(dims, kind):
        return jax.ShapeDtypeStruct(dims, kind)

    half, tall = (count // 2, shard) if direct else (ranks // 2, shard * groups)
    width = 4 * LANES if direct else 3 * LANES
    apart = not direct
    wide, three = (2, rows, D), (2, rows, 3 * D)
    flat, pooled_dims = (2 * rows, D), (2, summaries, D)
    room = 12 if direct else 56
    masks = [pltpu.VMEM((tiles, SPAN + summaries, SPAN), F32)]
    w_rest = jnp.concatenate((w_out.T, w_up, w_down.T), axis=1)

    def prepare():
        return call(
            prepare_kernel, [shape((1, max(shard, 64), D), BF16), shape((2, SPAN, D), BF16)],
            [SMEM] * 3 + [HBM] * 5, [VMEM] * 2,
            scratch=[pltpu.VMEM(wide, BF16), pltpu.SemaphoreType.DMA((6,))],
            limit=56,
        )(*facts, block_input, cotangent, w_query, w_key, w_value)

    x_left = turn(block_input[:, rows - SPAN :], 1)
    part_a, cot_edge = prepare()
    if direct:
        got_a = spread([tie(part_a, x_left)] * 3)
        part_b = tie(w_rest[None], got_a[0])
        got_b = swap(part_b, stages[0])
        part_a = jnp.concatenate([part_a] + got_a, axis=0)
        part_a = tie(join(part_a, swap(part_a, stages[2])), got_b)
        part_b = join(part_b, got_b)
        got_b = swap(part_b, stages[1])
        got_a = swap(part_a, stages[3])
        near_a = join(part_a, tie(got_a, got_b))
        far_a = swap(near_a, (0, 0))
        part_b = join(part_b, tie(got_b, near_a))
        got_b = swap(part_b, stages[2])
        more = ()
    else:
        cot_left = turn(cot_edge, 1)
        near_a, far_a = gather_whole(part_a[0, :shard, :384])
        near_b, far_b = gather_whole(w_rest)
        more = (lax.all_gather(part_a[0, :64, 384:], AXES, axis=0),)
        block_of, row_of = jnp.arange(ranks, dtype=jnp.int32), jnp.zeros((ranks,), jnp.int32)

    xs, qkv, skv, sums, w_full = call(
        partial(project_kernel, apart),
        [shape(wide, BF16), shape(three, BF16), shape((2, summaries, 3 * D), BF16), shape(pooled_dims, F32)]
        + [shape((D, 3 * D), BF16)],
        [SMEM] * 5 + [VMEM] * 7 + [ANY] * (2 + len(more)),
        scratch=[
            pltpu.VMEM((count, 64, LANES), BF16),
            pltpu.VMEM((rows + SPAN, D), F32),
            pltpu.VMEM((2, rows + 2 * summaries, D), BF16),
            pltpu.SemaphoreType.DMA((2,)),
        ],
        limit=24 if direct else 56,
    )(
        *facts, block_of, row_of, slots, block_input, x_left, row(ln1_gain), row(ln1_bias),
        row(query_bias), row(value_bias), near_a, far_a, *more,
    )
    outs = [shape(wide, BF16), shape((2, 4, tiles, 1, 2 * SPAN), F32)]
    if direct:
        part_b = join(part_b, tie(got_b, skv))
        got_b = swap(part_b, stages[3])
        qkv = tie(qkv, part_b)
    seen = call_row(attend_kernel, 0, facts, (qkv, skv), outs, (), masks, limit=room)
    att, lse = call_row(attend_kernel, 1, facts, (qkv, skv), outs, tuple(seen), masks, limit=room)
    if direct:
        near_b = join(part_b, tie(got_b, att))
        far_b = swap(near_b, (0, 0))
        cot_left = turn(tie(cot_edge, near_b), 1)
    result, gmid, edge, gatt, small_b, grad_ub, keep_b, send_b = call(
        mlp_kernel,
        [shape(wide, BF16)] * 2 + [shape((2, SPAN, D), BF16), shape(wide, BF16)] + [shape((8, D), F32), shape((1, FF), F32)]
        + [shape((half, tall, 1152), BF16)] * 2,
        [SMEM] * 4 + [VMEM] * 8 + [HBM] + [ANY] * 2,
        [VMEM] * 6 + [ANY] * 2,
        scratch=[
            pltpu.VMEM((D, D), BF16), pltpu.VMEM((D, FF), BF16), pltpu.VMEM((D, FF), BF16),
            pltpu.VMEM(flat, F32), pltpu.VMEM(flat, F32), pltpu.VMEM(flat, F32),
            pltpu.VMEM(flat, BF16), pltpu.VMEM(flat, BF16),
            pltpu.VMEM((D, 2 * rows), BF16), pltpu.VMEM((D, 2 * rows), BF16),
            pltpu.VMEM((D, FF), BF16), pltpu.VMEM((D, FF), BF16), pltpu.VMEM((D, D), BF16),
            pltpu.VMEM((rows + SPAN, D), F32), pltpu.VMEM(wide, BF16),
            pltpu.SemaphoreType.DMA((4,)), pltpu.SemaphoreType.DMA((3,)),
        ],
        limit=40,
    )(
        facts[0], span_offset, block_of, row_of, xs, att, cot_left, row(out_bias), row(ln2_gain), row(ln2_bias),
        row(up_bias), row(down_bias), cotangent, near_b, far_b,
    )
    arrays = (qkv, skv, lse, gatt)
    outs = [shape(three, BF16), shape((2, summaries, 3 * D), BF16)]
    if direct:
        got_b = swap(send_b, (0, 0))
        back = turn(tie(edge, send_b), -1)
    grads = call_row(attend_back_kernel, 0, facts, arrays, outs, (), masks, limit=room)
    if direct:
        keep_b, send_b = fold(keep_b.astype(F32), tie(got_b, grads[0]))
        got_b = swap(send_b, stages[3])
        grads = [tie(grads[0], send_b)] + list(grads[1:])
    grads = call_row(attend_back_kernel, 1, facts, arrays, outs, tuple(grads), masks, limit=room)
    if direct:
        grads = [tie(grads[0], back), grads[1]]
    lines, keep_a, send_a, *more = call(
        partial(weights_back_kernel, apart),
        [shape((16, D), F32)]
        + [shape((half * tall, width), BF16), shape((half * tall + (32 if direct else 0), width), BF16)]
        + [shape((count, 64, LANES), BF16)] * apart,
        [SMEM] * 5 + [VMEM] * 10,
        [VMEM] + [ANY] * (2 + apart),
        scratch=[
            pltpu.VMEM((D, 3 * D), BF16), pltpu.VMEM(pooled_dims, BF16), pltpu.VMEM((count, 64, LANES), BF16),
            pltpu.VMEM((32, D), BF16), pltpu.SemaphoreType.DMA((3,)),
        ],
        limit=24 if direct else 56,
    )(
        *facts, block_of, row_of, slots, xs, *grads, sums, w_full, row(ln1_gain), row(ln1_bias), small_b, grad_ub,
    )

    def by_row(dims):
        return pl.BlockSpec((1,) + dims[1:], lambda i: (i,) + (0,) * (len(dims) - 1))

    once = pl.BlockSpec((1, D), lambda i: (0, 0))
    edge_dims = (2, SPAN, D)

    def rows_back(*after):
        return call(
            rows_back_kernel, [shape(wide, F32), shape(edge_dims, BF16)],
            [by_row(three), pl.BlockSpec((D, 3 * D), lambda i: (0, 0)), by_row(wide), by_row(wide), once],
            [by_row(wide), by_row(edge_dims)], grid=(2,), limit=16,
        )(grads[0], tie(w_full, *after), xs, gmid, row(ln1_gain))

    def unroll(back):
        return call(
            unroll_kernel, [shape(wide, BF16)] * 2 + [shape((2, rows, LANES), F32)],
            [SMEM, by_row(wide), by_row(edge_dims), by_row(wide)], [by_row(wide)] * 2 + [by_row((2, rows, LANES))],
            [pltpu.VMEM((2 * SPAN, D), F32)], grid=(2,),
        )(span_offset, result, back, block_input)

    final = [SMEM] * 3 + [VMEM] * 5
    rolled = [pltpu.VMEM((2 * SPAN, D), F32)]
    if direct:
        got_a = swap(send_a, (0, 0))
        keep_b, send_b = fold(keep_b, tie(got_b, send_a))
        got_b = swap(send_b, stages[2])
        part, edge = rows_back(send_b)
        keep_a, send_a = fold_lines(keep_a, send_a, tie(got_a, part))
        got_a = swap(send_a, stages[3])
        part_back = turn(tie(edge, send_a), -1)
        keep_b, send_b = fold(keep_b, tie(got_b, send_a))
        got_b = swap(send_b, stages[1])
        result_own, *hats = unroll(tie(back, send_a))
        keep_a, send_a = fold_lines(keep_a, send_a, tie(got_a, result_own))
        got_a = swap(send_a, stages[2])
        keep_b, send_b = fold(keep_b, tie(got_b, send_a))
        got_b = swap(send_b, stages[0])
        keep_a, *send_a = fold_lines(keep_a, send_a, tie(got_a, send_b), 3)
        got_a = spread(send_a)
        grad_wo, grad_wu, grad_wd = call(
            finish_rest_kernel, [shape((shard, LANES), F32), shape((shard, 512), F32), shape((shard, 512), F32)],
            [VMEM] * 2,
        )(keep_b, tie(got_b, send_a[0]))
        input_grad, grad_wq, grad_wk, grad_wv, grad_ub, *small = call(
            partial(finish_kernel, True),
            [shape(wide, F32)] + [shape((shard, LANES), F32)] * 3 + [shape((1, FF), F32)] + [shape((1, D), F32)] * 8,
            final + [VMEM] * 5, scratch=rolled, limit=16,
        )(*facts, *hats, part, part_back, row(ln1_gain), keep_a, send_a[0], *(tie(got, grad_wo) for got in got_a))
        grad_wo, grad_wd = grad_wo.T, grad_wd.T
        small = [a.reshape(D) for a in small]
        grad_ub = grad_ub.reshape(FF)
    else:
        keep_a, send_a = (a.reshape(half, tall, width) for a in (keep_a, send_a))
        result_own, *hats = unroll(turn(edge, -1))
        part, edge = rows_back()
        part_back = turn(edge, -1)
        sum_a, sum_b = scatter_whole(keep_a, send_a), scatter_whole(keep_b, send_b)
        grad_wq, grad_wk, grad_wv = (sum_a[:, i : i + LANES] for i in (0, 128, 256))
        grad_wo, grad_wu, grad_wd = sum_b[:, :128].T, sum_b[:, 128:640], sum_b[:, 640:].T
        pooled = lax.psum_scatter(more[0].astype(F32), AXES, scatter_dimension=0, tiled=True)[0]
        lines = lax.psum(lines, AXES)
        grad_ub = lines[4:8].reshape(FF)
        small = [lines[i] for i in (0, 1, 2, 3, 8, 9, 10, 11)]
        input_grad = call(partial(finish_kernel, False), [shape(wide, F32)], final + [VMEM], scratch=rolled, limit=16)(
            *facts, *hats, part, part_back, row(ln1_gain), pooled
        )[0]
    grad_gain_two, grad_shift_two, grad_obias, grad_dbias, grad_gain_one, grad_shift_one, grad_qb, grad_vb = small
    return (
        result_own,
        input_grad,
        grad_gain_one,
        grad_shift_one,
        grad_wq,
        grad_wk,
        grad_wv,
        grad_qb,
        grad_vb,
        grad_wo,
        grad_obias,
        grad_gain_two,
        grad_shift_two,
        grad_wu,
        grad_ub,
        grad_wd,
        grad_dbias,
    )


def solution(mesh):
    vector, matrix, turned = P(), P("seq", "mp"), P("mp", "seq")
    own, group = P(None, ("seq", "mp"), None), P(None, "seq", None)
    return jax.shard_map(
        per_device,
        mesh=mesh,
        in_specs=(own, group, vector, vector, vector, vector, matrix, matrix, matrix, vector, vector)
        + (turned, vector, vector, vector, matrix, vector, turned, vector),
        out_specs=(own, own, vector, vector, matrix, matrix, matrix, vector, vector, turned, vector)
        + (vector, vector, matrix, vector, turned, vector),
        check_vma=False,
    )
```

```python
from functools import partial
import math

import jax
import jax.numpy as jnp
from jax import lax
from jax.experimental import pallas as pl
from jax.experimental.pallas import tpu as pltpu
from jax.sharding import PartitionSpec as P

D = 512
FF = 2048
HEAD_DIM = 64
SPAN = 128
LANES = 128
EPSILON = 1e-05
NEGATIVE = -1e30
SCALE = 1.0 / math.sqrt(HEAD_DIM)
F32 = jnp.float32
BF16 = jnp.bfloat16
AXES = ("seq", "mp")
MIB = 1 << 20
VMEM = pl.BlockSpec(memory_space=pltpu.VMEM)
SMEM = pl.BlockSpec(memory_space=pltpu.SMEM)
ANY = pl.BlockSpec(memory_space=pl.ANY)
HBM = pl.BlockSpec(memory_space=pltpu.HBM)


def dot(left, right):
    return lax.dot_general(left, right, (((1,), (0,)), ((), ())), preferred_element_type=F32)


def dot_cols(left, right):
    return lax.dot_general(left, right, (((1,), (1,)), ((), ())), preferred_element_type=F32)


def unit(rows):
    centred = rows - jnp.mean(rows, axis=-1, keepdims=True)
    inverse = lax.rsqrt(jnp.mean(centred * centred, axis=-1, keepdims=True) + EPSILON)
    return centred * inverse, inverse


def unit_back(grad, hat, inverse):
    shift = jnp.mean(grad, axis=-1, keepdims=True)
    slope = jnp.mean(grad * hat, axis=-1, keepdims=True)
    return (grad - shift - hat * slope) * inverse


def row_info(place, offsets, lengths, mi):
    ends = []
    for c in range(lengths.shape[1]):
        ends.append(lengths[mi, c] + (ends[-1] if ends else 0))
    return place[0], offsets[mi], ends


def doc_start(positions, ends):
    start = jnp.zeros_like(positions)
    for end in ends:
        start = jnp.where(positions >= end, end, start)
    return start


def summary_range(summary_ids, offset, ends):
    last = offset - 1 + SPAN * summary_ids
    first = jnp.maximum(doc_start(last, ends), last - (SPAN - 1))
    return first, last


def iota(shape, dim):
    return lax.broadcasted_iota(jnp.int32, shape, dim)


def roll_rows(ref, by):
    whole = pl.multiple_of((by // 8) * 8, 8)
    return pltpu.roll(ref[pl.ds(whole, SPAN + 8), :], SPAN + 8 - (by - whole), axis=0)[:SPAN]


def prepare_kernel(
    place, offsets, lengths, x_ref, cot_ref, wq_ref, wk_ref, wv_ref, wo_ref, wu_ref, wd_ref,
    out_ref, rest_ref, edge_ref, rows_ref, sem
):
    rows = x_ref.shape[1]
    last_rows = pl.multiple_of(place[1] * rows + (rows - SPAN), SPAN)
    shard = wq_ref.shape[0]
    copies = [pltpu.make_async_copy(x_ref.at[mi], rows_ref.at[mi], sem.at[mi]) for mi in range(2)]
    copies += [
        pltpu.make_async_copy(ref, out_ref.at[0, 0:shard, i * LANES : (i + 1) * LANES], sem.at[2 + i])
        for i, ref in enumerate((wq_ref, wk_ref, wv_ref))
    ]
    copies.append(pltpu.make_async_copy(cot_ref.at[:, pl.ds(last_rows, SPAN), :], edge_ref, sem.at[5]))
    copies.append(pltpu.make_async_copy(wo_ref, rest_ref.at[0, :, 0:128], sem.at[6]))
    for i, (ref, first) in enumerate(((wu_ref, 0), (wd_ref, 0), (wu_ref, 256), (wd_ref, 256))):
        target = rest_ref.at[0, :, 128 + 256 * i : 384 + 256 * i]
        copies.append(pltpu.make_async_copy(ref.at[:, first : first + 256], target, sem.at[7 + i]))
    for copy in copies:
        copy.start()
    sums = []
    for mi in range(2):
        dev, offset, ends = row_info(place, offsets, lengths, mi)
        first, last = summary_range(dev * (rows // SPAN) + iota((8, 1), 0), offset, ends)
        pos = dev * rows + iota((1, rows), 1)
        member = jnp.where((pos >= first) & (pos <= last), 1.0, 0.0).astype(BF16)
        copies[mi].wait()
        hat, _ = unit(rows_ref[mi].astype(F32))
        high = hat.astype(BF16)
        rest = (hat - high.astype(F32)).astype(BF16)
        total = dot(member, high) + dot(member, rest)
        sums.append(total * lax.rsqrt((last - first + 1).astype(F32)))
    both = jnp.concatenate(sums, axis=0).astype(BF16)
    for copy in copies[2:]:
        copy.wait()
    for lane in range(D // LANES):
        out_ref[0, 16 * lane : 16 * lane + 16, 384:512] = both[:, lane * LANES : (lane + 1) * LANES]


def fill_masks(place, offsets, lengths, mi, bias_ref, tiles, summaries, length):
    dev, offset, ends = row_info(place, offsets, lengths, mi)
    ends_col = offset - 1 + SPAN * iota((summaries, 1), 0)
    for t in range(tiles):
        base = SPAN * (dev * tiles + t) + offset - SPAN
        qpos = base + iota((1, SPAN), 1)
        qpos = jnp.where(qpos < 0, qpos + length, qpos)
        kpos = base + iota((SPAN, 1), 0)
        kpos = jnp.where(kpos < 0, kpos + length, kpos)
        span_first = jnp.where(qpos >= base + SPAN, base + length, base)
        doc_first = doc_start(qpos, ends)
        local_ok = (kpos >= jnp.maximum(doc_first, span_first)) & (kpos <= qpos)
        summary_ok = (ends_col >= doc_first) & (ends_col < span_first)
        bias_ref[t, 0:SPAN, :] = jnp.where(local_ok, 0.0, NEGATIVE)
        bias_ref[t, SPAN : SPAN + summaries, :] = jnp.where(summary_ok, 0.0, NEGATIVE)


def split_heads(pair):
    low = iota(pair.shape, 1) < HEAD_DIM
    zero = jnp.zeros_like(pair)
    return jnp.concatenate((jnp.where(low, pair, zero), jnp.where(low, zero, pair)), axis=0)


def join_heads(turned):
    half = turned.shape[1] // 2
    return jnp.concatenate((turned[:HEAD_DIM, :half], turned[HEAD_DIM:, half:]), axis=0).T


def project_kernel(
    apart, place_ref, offsets, lengths, block_of, row_of, slots_ref, x_ref, left_ref, gain, shift, qbias, vbias,
    near_ref, far_ref, *refs
):
    if apart:
        all_ref, *refs = refs
    xs_ref, qkv_ref, skv_ref, sums_ref, w_ref, stack_ref, wide_ref, rows_ref, sem = refs
    rows = x_ref.shape[1]
    tiles = rows // SPAN
    summaries = skv_ref.shape[1]
    half, shard, _ = near_ref.shape

    def place(d, carry):
        for source, slot in ((near_ref, d), (far_ref, half + d)):
            here = pl.ds(pl.multiple_of(row_of[slot] * shard, 16), shard)
            cols = pl.ds(pl.multiple_of(block_of[slot] * 384, 128), 384)
            pltpu.make_async_copy(source.at[d, :, 0:384], w_ref.at[here, cols], sem.at[0]).start()
            if not apart:
                pltpu.make_async_copy(
                    source.at[d, 0:64, 384:512], stack_ref.at[slot], sem.at[1]
                ).start()
        return carry

    lax.fori_loop(0, half, place, 0)
    if apart:
        pltpu.make_async_copy(all_ref, stack_ref, sem.at[1]).start()
    for mi in range(2):
        wide_ref[0:SPAN, :] = left_ref[mi].astype(F32)
        wide_ref[SPAN : SPAN + rows, :] = x_ref[mi].astype(F32)
        for t in range(tiles):
            here = slice(t * SPAN, (t + 1) * SPAN)
            rolled = roll_rows(wide_ref, t * SPAN + offsets[mi])
            xs_ref[mi, here, :] = rolled.astype(BF16)
            hat, _ = unit(rolled)
            rows_ref[mi, here, :] = (hat * gain[...] + shift[...]).astype(BF16)
    pltpu.make_async_copy(stack_ref, stack_ref, sem.at[1]).wait()
    roots = []
    for mi in range(2):
        _, offset, ends = row_info(place_ref, offsets, lengths, mi)
        first, last = summary_range(iota((summaries, 1), 0), offset, ends)
        root = jnp.sqrt((last - first + 1).astype(F32))
        roots.append(root)
        for base in range(0, stack_ref.shape[0], 32):
            named = slots_ref[mi : mi + 1, 16 * base : 16 * base + 512]
            pick = jnp.where(iota((summaries, 1), 0) == named, 1.0, 0.0).astype(BF16)
            piece = jnp.concatenate(
                [
                    stack_ref[base : base + 32, 16 * lane : 16 * lane + 16, :].reshape(512, LANES)
                    for lane in range(D // LANES)
                ],
                axis=1,
            )
            found = dot(pick, piece)
            sums_ref[mi] = found if base == 0 else sums_ref[mi] + found
        summed = sums_ref[mi] * gain[...] + root * shift[...]
        high = summed.astype(BF16)
        rows_ref[mi, rows : rows + summaries, :] = high
        rows_ref[mi, rows + summaries : rows + 2 * summaries, :] = (summed - high.astype(F32)).astype(BF16)
    pltpu.make_async_copy(w_ref, w_ref, sem.at[0]).wait()
    none = jnp.zeros((1, LANES), F32)
    for m in range(4):
        lanes = slice(m * LANES, (m + 1) * LANES)
        cols = slice(m * 384, (m + 1) * 384)
        bias = jnp.concatenate((qbias[:, lanes], none, vbias[:, lanes]), axis=1)
        for mi in range(2):
            projected = dot(rows_ref[mi], w_ref[:, cols])
            qkv_ref[mi, :, cols] = (projected[:rows] + bias).astype(BF16)
            pooled = projected[rows : rows + summaries] + projected[rows + summaries :]
            skv_ref[mi, :, cols] = (pooled + roots[mi] * bias).astype(BF16)


def pair_of(ref, here, pair):
    def part(i):
        return ref[0, here, pl.ds(pl.multiple_of(pair * 384 + i * LANES, LANES), LANES)]

    return part(0), part(1), part(2)


def attend_kernel(mi, place, offsets, lengths, qkv_ref, skv_ref, *refs):
    att_ref, lse_ref, bias_ref = refs[-3:]
    rows = qkv_ref.shape[1]
    tiles = rows // SPAN
    summaries = skv_ref.shape[1]
    fill_masks(place, offsets, lengths, mi, bias_ref, tiles, summaries, summaries * SPAN)

    def heads(pair, carry):
        lanes = pl.ds(pl.multiple_of(pair * LANES, LANES), LANES)
        _, skeys, svalues = pair_of(skv_ref, slice(None), pair)
        svalues = svalues.T
        spans = [pair_of(qkv_ref, slice(t * SPAN, (t + 1) * SPAN), pair) for t in range(tiles)]
        scores = []
        for t, (queries, keys, _) in enumerate(spans):
            bias = bias_ref[t]
            keys = jnp.concatenate((keys, skeys), axis=0)
            scores.append(dot_cols(keys, split_heads(queries * SCALE)) + jnp.concatenate((bias, bias), axis=1))
        probs = []
        for t in range(tiles):
            top = jnp.max(scores[t], axis=0, keepdims=True)
            grown = jnp.exp(scores[t] - top)
            total = jnp.sum(grown, axis=0, keepdims=True)
            probs.append((grown * (1.0 / total)).astype(BF16))
            lse_ref[0, pair, t] = top + jnp.log(total)
        for t, (_, _, values) in enumerate(spans):
            values = jnp.concatenate((values.T, svalues), axis=1)
            att_ref[0, t * SPAN : (t + 1) * SPAN, lanes] = join_heads(dot(values, probs[t])).astype(BF16)
        return carry

    lax.fori_loop(0, 4, heads, 0)


def gelu_pair(u):
    c0 = math.sqrt(2.0 / math.pi)
    square = u * u
    t = jnp.tanh(c0 * u * (1.0 + 0.044715 * square))
    half = 0.5 * (1.0 + t)
    slope = half + (0.5 * c0) * u * (1.0 - t * t) * (1.0 + (3 * 0.044715) * square)
    return u * half, slope


def columns(block, width):
    return pl.ds(pl.multiple_of(block * width, 128), width)


def mlp_half(half_id, ubias, n_ref, c_ref, nt_ref, ct_ref, wu_ref, wd_ref, gu_ref, gd_ref, gub_ref):
    total = n_ref.shape[0]
    bias = jnp.concatenate([ubias[:, m * 512 + half_id * 256 : m * 512 + half_id * 256 + 256] for m in range(4)], axis=1)
    w_up, w_down = wu_ref[...], wd_ref[...]
    halves = [slice(i * total // 2, (i + 1) * total // 2) for i in range(2)]
    ups = [dot(n_ref[here, :], w_up) + bias for here in halves]
    backs = [dot(c_ref[here, :], w_down) for here in halves]
    acts, grads, sums = [], [], []
    gub = jnp.zeros_like(gub_ref)
    for up, back in zip(ups, backs):
        act, slope = gelu_pair(up)
        grad = back * slope
        gub += jnp.sum(grad, axis=0, keepdims=True)
        acts.append(act.astype(BF16))
        grads.append(grad.astype(BF16))
        sums.append((dot_cols(acts[-1], w_down), dot_cols(grads[-1], w_up)))
    gub_ref[...] = gub
    gu_ref[...] = dot(nt_ref[...], jnp.concatenate(grads, axis=0)).astype(BF16)
    gd_ref[...] = dot(ct_ref[...], jnp.concatenate(acts, axis=0)).astype(BF16)
    return halves, sums


def pull(block_of, row_of, near_ref, far_ref, parts):
    half, shard, _ = near_ref.shape

    def body(d, carry):
        for source, slot in ((near_ref, d), (far_ref, half + d)):
            here = pl.ds(pl.multiple_of(row_of[slot] * shard, 16), shard)
            for target, first, width, sem in parts:
                pltpu.make_async_copy(
                    source.at[d, :, first : first + width], target.at[here, columns(block_of[slot], width)], sem
                ).start()
        return carry

    lax.fori_loop(0, half, body, 0)


def push(block_of, row_of, keep_ref, send_ref, parts):
    half, shard, _ = keep_ref.shape

    def body(d, carry):
        for target, slot in ((keep_ref, d), (send_ref, half + d)):
            here = pl.ds(pl.multiple_of(row_of[slot] * shard, 16), shard)
            for source, first, width, sem in parts:
                pltpu.make_async_copy(
                    source.at[here, columns(block_of[slot], width)], target.at[d, :, first : first + width], sem
                ).start()
        return carry

    lax.fori_loop(0, half, body, 0)


def mlp_first_kernel(
    place_ref, offsets, block_of, row_of, xs_ref, att_ref, left_ref, obias, gain, shift, ubias, dbias, cot_ref,
    near_ref, far_ref,
    resid_ref, acc_ref, gn_ref, n_ref, c_ref, wo_ref, gub_ref, down_ref, keep_ref, send_ref,
    nt_ref, ct_ref, wu_ref, wd_ref, gu_ref, gd_ref, wide_ref, low_ref, sem, out_sem,
):
    rows = xs_ref.shape[1]
    own = pl.ds(pl.multiple_of(place_ref[1] * rows, SPAN), rows)
    own_copy = pltpu.make_async_copy(cot_ref.at[:, own, :], low_ref, sem.at[3])
    own_copy.start()
    pull(block_of, row_of, near_ref, far_ref, ((wo_ref, 0, 128, sem.at[0]),))
    pull(block_of, row_of, near_ref, far_ref, ((wu_ref, 128, 256, sem.at[1]), (wd_ref, 384, 256, sem.at[2])))
    down_ref[...] = jnp.zeros_like(down_ref)
    own_copy.wait()
    pltpu.make_async_copy(wo_ref, wo_ref, sem.at[0]).wait()
    for mi in range(2):
        all_rows = slice(mi * rows, (mi + 1) * rows)
        wide_ref[0:SPAN, :] = left_ref[mi].astype(F32)
        wide_ref[SPAN : SPAN + rows, :] = low_ref[mi].astype(F32)
        for t in range(rows // SPAN):
            rolled = roll_rows(wide_ref, t * SPAN + offsets[mi])
            down_ref[...] += jnp.sum(rolled, axis=0, keepdims=True)
            c_ref[mi * rows + t * SPAN : mi * rows + (t + 1) * SPAN, :] = rolled.astype(BF16)
        resid = xs_ref[mi].astype(F32) + dot_cols(att_ref[mi], wo_ref[...]) + obias[...]
        resid_ref[all_rows, :] = resid
        hat, _ = unit(resid)
        normed = (hat * gain[...] + shift[...]).astype(BF16)
        n_ref[all_rows, :] = normed
        nt_ref[:, all_rows] = normed.T
        ct_ref[:, all_rows] = c_ref[all_rows, :].T
    pltpu.make_async_copy(wu_ref, wu_ref, sem.at[1]).wait()
    pltpu.make_async_copy(wd_ref, wd_ref, sem.at[2]).wait()
    halves, sums = mlp_half(0, ubias, n_ref, c_ref, nt_ref, ct_ref, wu_ref, wd_ref, gu_ref, gd_ref, gub_ref)
    push(block_of, row_of, keep_ref, send_ref, ((gu_ref, 0, 256, out_sem.at[0]), (gd_ref, 256, 256, out_sem.at[1])))
    for here, (down, back) in zip(halves, sums):
        acc_ref[here, :] = (down + dbias[...]).astype(BF16)
        gn_ref[here, :] = back.astype(BF16)
    pltpu.make_async_copy(gu_ref, gu_ref, out_sem.at[0]).wait()
    pltpu.make_async_copy(gd_ref, gd_ref, out_sem.at[1]).wait()


def mlp_second_kernel(
    block_of, row_of, att_ref, gain, ubias, resid_ref, acc_ref, gn_ref, n_ref, c_ref, wo_ref,
    near_ref, far_ref,
    result_ref, gmid_ref, gatt_ref, small_ref, gub_ref, keep_ref, send_ref,
    nt_ref, ct_ref, wu_ref, wd_ref, gu_ref, gd_ref, go_ref, sem, out_sem,
):
    rows = att_ref.shape[1]
    pull(block_of, row_of, near_ref, far_ref, ((wu_ref, 0, 256, sem.at[0]), (wd_ref, 256, 256, sem.at[1])))
    small_ref[...] = jnp.zeros_like(small_ref)
    for mi in range(2):
        here = slice(mi * rows, (mi + 1) * rows)
        nt_ref[:, here] = n_ref[here, :].T
        ct_ref[:, here] = c_ref[here, :].T
    pltpu.make_async_copy(wu_ref, wu_ref, sem.at[0]).wait()
    pltpu.make_async_copy(wd_ref, wd_ref, sem.at[1]).wait()
    halves, sums = mlp_half(1, ubias, n_ref, c_ref, nt_ref, ct_ref, wu_ref, wd_ref, gu_ref, gd_ref, gub_ref)
    push(block_of, row_of, keep_ref, send_ref, ((gu_ref, 0, 256, out_sem.at[0]), (gd_ref, 256, 256, out_sem.at[1])))
    branches = []
    for mi, (here, (down, back)) in enumerate(zip(halves, sums)):
        result_ref[mi] = (resid_ref[here, :] + (acc_ref[here, :].astype(F32) + down)).astype(BF16)
        hat, inverse = unit(resid_ref[here, :])
        grad = gn_ref[here, :].astype(F32) + back
        small_ref[0:1, :] += jnp.sum(grad * hat, axis=0, keepdims=True)
        small_ref[1:2, :] += jnp.sum(grad, axis=0, keepdims=True)
        branch = (c_ref[here, :].astype(F32) + unit_back(grad * gain[...], hat, inverse)).astype(BF16)
        gmid_ref[mi] = branch
        small_ref[2:3, :] += jnp.sum(branch.astype(F32), axis=0, keepdims=True)
        gatt_ref[mi] = dot(branch, wo_ref[...]).astype(BF16)
        branches.append(branch.T)
    both = jnp.concatenate((att_ref[0], att_ref[1]), axis=0)
    go_ref[...] = dot(jnp.concatenate(branches, axis=1), both).astype(BF16)
    push(block_of, row_of, keep_ref, send_ref, ((go_ref, 512, 128, out_sem.at[2]),))
    pltpu.make_async_copy(gu_ref, gu_ref, out_sem.at[0]).wait()
    pltpu.make_async_copy(gd_ref, gd_ref, out_sem.at[1]).wait()
    pltpu.make_async_copy(go_ref, go_ref, out_sem.at[2]).wait()


def attend_back_kernel(mi, place, offsets, lengths, qkv_ref, skv_ref, lse_ref, gatt_ref, *refs):
    grad_ref, pooled_ref, bias_ref = refs[-3:]
    rows = qkv_ref.shape[1]
    tiles = rows // SPAN
    summaries = skv_ref.shape[1]
    fill_masks(place, offsets, lengths, mi, bias_ref, tiles, summaries, summaries * SPAN)

    def heads(pair, carry):
        lanes = pl.ds(pl.multiple_of(pair * LANES, LANES), LANES)

        def columns(i):
            return pl.ds(pl.multiple_of(pair * 384 + i * LANES, LANES), LANES)

        _, skeys, svalues = pair_of(skv_ref, slice(None), pair)
        skeys_t = skeys.T
        sum_k = jnp.zeros((summaries, LANES), F32)
        sum_v = jnp.zeros((summaries, LANES), F32)
        held = []
        for t in range(tiles):
            here = slice(t * SPAN, (t + 1) * SPAN)
            queries, keys, values = pair_of(qkv_ref, here, pair)
            queries = split_heads(queries * SCALE)
            grads = split_heads(gatt_ref[0, here, lanes])
            bias = bias_ref[t]
            scores = dot_cols(jnp.concatenate((keys, skeys), axis=0), queries)
            gprobs = dot_cols(jnp.concatenate((values, svalues), axis=0), grads)
            held.append((queries, keys, grads, scores + jnp.concatenate((bias, bias), axis=1), gprobs))
        for t, (queries, keys, grads, scores, gprobs) in enumerate(held):
            here = slice(t * SPAN, (t + 1) * SPAN)
            probs = jnp.exp(scores - lse_ref[0, pair, t])
            delta = jnp.sum(probs * gprobs, axis=0, keepdims=True)
            gscores = (probs * (gprobs - delta)).astype(BF16)
            keys_t = jnp.concatenate((keys.T, skeys_t), axis=1)
            grad_q = join_heads(dot(keys_t, gscores)) * SCALE
            grad_k = dot(gscores, queries)
            grad_v = dot(probs.astype(BF16), grads)
            grad_ref[0, here, columns(0)] = grad_q.astype(BF16)
            grad_ref[0, here, columns(1)] = grad_k[:SPAN].astype(BF16)
            grad_ref[0, here, columns(2)] = grad_v[:SPAN].astype(BF16)
            sum_k += grad_k[SPAN:]
            sum_v += grad_v[SPAN:]
        pooled_ref[0, :, columns(0)] = jnp.zeros((summaries, LANES), BF16)
        pooled_ref[0, :, columns(1)] = sum_k.astype(BF16)
        pooled_ref[0, :, columns(2)] = sum_v.astype(BF16)
        return carry

    lax.fori_loop(0, 4, heads, 0)


def weights_back_kernel(
    apart, place, offsets, lengths, block_of, row_of, slots_ref, xs_ref, grad_ref, pooled_ref, sums_ref, w_ref,
    gain, shift, small_ref, down_ref, gub1_ref, gub2_ref, line_ref, keep_ref, send_ref, *refs
):
    if apart:
        all_ref, *refs = refs
    gwb_ref, back_ref, stack_ref, pad_ref, sem = refs
    rows = xs_ref.shape[1]
    summaries = pooled_ref.shape[1]
    half = block_of.shape[0] // 2
    shard = keep_ref.shape[0] // half
    turned = []
    column = jnp.zeros((1, 3 * D), F32)
    for mi in range(2):
        _, offset, ends = row_info(place, offsets, lengths, mi)
        first, last = summary_range(iota((summaries, 1), 0), offset, ends)
        root = jnp.sqrt((last - first + 1).astype(F32))
        hat, _ = unit(xs_ref[mi].astype(F32))
        turned += [hat.astype(BF16).T, sums_ref[mi].astype(BF16).T]
        column += jnp.sum(grad_ref[mi].astype(F32), axis=0, keepdims=True)
        column += jnp.sum(root * pooled_ref[mi].astype(F32), axis=0, keepdims=True)
        back_ref[mi] = dot_cols(pooled_ref[mi], w_ref[...]).astype(BF16)
    turned = jnp.concatenate(turned, axis=1)
    gain_col, shift_col = gain[...].T, shift[...].T
    grad_gain = jnp.zeros((D, 1), F32)
    grad_shift = jnp.zeros((D, 1), F32)
    for m in range(4):
        cols = slice(m * 384, (m + 1) * 384)
        lanes = slice(m * LANES, (m + 1) * LANES)
        grads = jnp.concatenate([ref[mi, :, cols] for mi in range(2) for ref in (grad_ref, pooled_ref)], axis=0)
        hats, w, sums = dot(turned, grads), w_ref[:, cols].astype(F32), column[:, cols]
        grad_gain += jnp.sum(hats * w, axis=1, keepdims=True)
        grad_shift += jnp.sum(sums * w, axis=1, keepdims=True)
        gwb_ref[:, cols] = (hats * gain_col + shift_col * sums).astype(BF16)
        line_ref[10:11, lanes] = sums[:, :128]
        line_ref[11:12, lanes] = sums[:, 256:]
    line_ref[8:9, :] = grad_gain.T
    line_ref[9:10, :] = grad_shift.T
    line_ref[0:3, :] = small_ref[0:3, :]
    line_ref[3:4, :] = down_ref[...]
    for i in range(4):
        for j, ref in enumerate((gub1_ref, gub2_ref)):
            line_ref[4 + i : 5 + i, j * 256 : (j + 1) * 256] = ref[:, i * 256 : (i + 1) * 256]
    line_ref[12:16, :] = jnp.zeros((4, D), F32)
    for base in range(0, stack_ref.shape[0], 32):
        names = [slots_ref[mi : mi + 1, 16 * base : 16 * base + 512] for mi in range(2)]
        spread = [
            jnp.where(iota((summaries, 1), 0) == named, 1.0, 0.0).astype(BF16).T for named in names
        ]
        piece = (dot(spread[0], back_ref[0]) + dot(spread[1], back_ref[1])).astype(BF16)
        for lane in range(D // LANES):
            part = piece[:, lane * LANES : (lane + 1) * LANES]
            stack_ref[base : base + 32, 16 * lane : 16 * lane + 16, :] = part.reshape(32, 16, LANES)

    def emit(d, carry):
        for target, slot in ((keep_ref, d), (send_ref, half + d)):
            first_row = pl.multiple_of(row_of[slot] * shard, 16)
            cols = pl.ds(pl.multiple_of(block_of[slot] * 384, 128), 384)
            here = target.at[pl.ds(pl.multiple_of(d * shard, 16), shard), :]
            pltpu.make_async_copy(
                gwb_ref.at[pl.ds(first_row, shard), cols], here.at[:, 0:384], sem.at[0]
            ).start()
            if not apart:
                pltpu.make_async_copy(stack_ref.at[slot], here.at[:, 384:512], sem.at[1]).start()
        return carry

    lax.fori_loop(0, half, emit, 0)
    if apart:
        pltpu.make_async_copy(stack_ref, all_ref, sem.at[1]).start()
    else:
        high = line_ref[...].astype(BF16)
        pad_ref[0:16, :] = high
        pad_ref[16:32, :] = (line_ref[...] - high.astype(F32)).astype(BF16)
        size = half * shard
        copy = pltpu.make_async_copy(pad_ref, send_ref.at[size : size + 32, :], sem.at[2])
        copy.start()
        copy.wait()
    pltpu.make_async_copy(gwb_ref, gwb_ref, sem.at[0]).wait()
    pltpu.make_async_copy(stack_ref, stack_ref, sem.at[1]).wait()


def rows_back_kernel(grad_ref, w_ref, xs_ref, gmid_ref, result_ref, gain, part_ref, edge_ref):
    grad = dot_cols(grad_ref[0], w_ref[...]) * gain[...]
    hat, inverse = unit(xs_ref[0].astype(F32))
    part = gmid_ref[0].astype(F32) + unit_back(grad, hat, inverse)
    part_ref[0] = part
    edge_ref[0, 0] = part[0:SPAN].astype(BF16)
    edge_ref[1, 0] = result_ref[0]


def fold_kernel(keep_ref, mine_ref, got_ref, next_ref, *send_refs):
    size = keep_ref.shape[0]
    part = size // (1 + len(send_refs))
    mine = mine_ref[0:16, :].astype(F32) + mine_ref[16:32, :].astype(F32)
    lines = mine + (got_ref[size : size + 16, :].astype(F32) + got_ref[size + 16 : size + 32, :].astype(F32))
    high = lines.astype(BF16)
    rest = (lines - high.astype(F32)).astype(BF16)
    next_ref[...] = keep_ref[0:part, :].astype(F32) + got_ref[0:part, :].astype(F32)
    for i, send_ref in enumerate(send_refs):
        here = slice((i + 1) * part, (i + 2) * part)
        send_ref[0:part, :] = (keep_ref[here, :].astype(F32) + got_ref[here, :].astype(F32)).astype(BF16)
        send_ref[part : part + 16, :] = high
        if len(send_refs) == 1:
            send_ref[part + 16 : part + 32, :] = rest


def lines_of(ref):
    return ref[ref.shape[0] - 16 :, :].astype(F32)


def two_tiles(ref, right, mi, t):
    if (t + 2) * SPAN <= ref.shape[1]:
        return ref[mi, t * SPAN : (t + 2) * SPAN, :]
    return jnp.concatenate((ref[mi, t * SPAN :, :], right[mi].astype(ref.dtype)), axis=0)


def unroll_kernel(offsets, result_ref, right_ref, x_ref, out_ref, hat_ref, inverse_ref, wide_ref):
    mi = pl.program_id(0)
    for t in range(result_ref.shape[1] // SPAN):
        here = slice(t * SPAN, (t + 1) * SPAN)
        wide_ref[...] = two_tiles(result_ref, right_ref.at[0], 0, t).astype(F32)
        out_ref[0, here, :] = roll_rows(wide_ref, SPAN - offsets[mi]).astype(BF16)
        hat, inverse = unit(x_ref[0, here, :].astype(F32))
        hat_ref[0, here, :] = hat.astype(BF16)
        inverse_ref[0, here, :] = jnp.broadcast_to(inverse, (SPAN, LANES))


def finish_rest_kernel(keep_ref, got_ref, wo_ref, wu_ref, wd_ref):
    total = keep_ref[0] + got_ref[0].astype(F32)
    for i in range(2):
        wu_ref[:, i * 256 : (i + 1) * 256] = total[:, i * 512 : i * 512 + 256]
        wd_ref[:, i * 256 : (i + 1) * 256] = total[:, i * 512 + 256 : i * 512 + 512]
    wo_ref[...] = total[:, 1024:]


def finish_kernel(
    direct, place, offsets, lengths, hat_ref, inverse_ref, part_ref, right_ref, gain, *refs
):
    if direct:
        keep_ref, mine_ref, a_ref, b_ref, c_ref, out_ref, wq_ref, wk_ref, wv_ref, *line_refs, wide_ref = refs
        size = keep_ref.shape[0]
        total = (keep_ref[...] + a_ref[0:size, :].astype(F32)) + (
            b_ref[0:size, :].astype(F32) + c_ref[0:size, :].astype(F32)
        )
        wq_ref[...], wk_ref[...], wv_ref[...] = total[:, :128], total[:, 128:256], total[:, 256:384]
        pooled = total[:, 384:]
        lines = (lines_of(mine_ref) + lines_of(a_ref)) + (lines_of(b_ref) + lines_of(c_ref))
        ub_ref, *line_refs = line_refs
        for i in range(4):
            ub_ref[:, i * D : (i + 1) * D] = lines[4 + i : 5 + i, :]
        for ref, i in zip(line_refs, (0, 1, 2, 3, 8, 9, 10, 11)):
            ref[...] = lines[i : i + 1, :]
    else:
        pooled_ref, out_ref, wide_ref = refs
        pooled = pooled_ref[...]
    rows = hat_ref.shape[1]
    for mi in range(2):
        dev, offset, ends = row_info(place, offsets, lengths, mi)
        first, last = summary_range(dev * (rows // SPAN) + iota((8, 1), 0), offset, ends)
        lows = jnp.concatenate(
            [pooled[16 * i + 8 * mi : 16 * i + 8 * mi + 8, :] for i in range(D // LANES)], axis=1
        )
        lows = lows * gain[...] * lax.rsqrt((last - first + 1).astype(F32))
        level = (lows - jnp.mean(lows, axis=-1, keepdims=True)).astype(BF16)
        lows = lows.astype(BF16)
        first, last = summary_range(dev * (rows // SPAN) + iota((1, 8), 1), offset, ends)
        for t in range(rows // SPAN):
            here = slice(t * SPAN, (t + 1) * SPAN)
            pos = dev * rows + t * SPAN + iota((SPAN, 1), 0)
            member = jnp.where((pos >= first) & (pos <= last), 1.0, 0.0)
            hat = hat_ref[mi, here, :]
            slope = jnp.sum(member * dot_cols(hat, lows), axis=1, keepdims=True) * (1.0 / D)
            inverse = inverse_ref[mi, here, 0:1]
            wide_ref[...] = two_tiles(part_ref, right_ref.at[0], mi, t)
            own = roll_rows(wide_ref, SPAN - offset)
            out_ref[mi, here, :] = own + (dot(member.astype(BF16), level) - hat.astype(F32) * slope) * inverse


def call(kernel, outs, in_specs, out_specs=None, scratch=(), limit=8, **more):
    return pl.pallas_call(
        kernel,
        out_shape=outs,
        in_specs=in_specs,
        out_specs=out_specs if out_specs is not None else [VMEM] * len(outs),
        scratch_shapes=list(scratch),
        compiler_params=pltpu.CompilerParams(vmem_limit_bytes=limit * MIB),
        cost_estimate=pl.CostEstimate(flops=1, bytes_accessed=1, transcendentals=0),
        **more,
    )


def call_row(kernel, mi, facts, arrays, outs, before, scratch, **more):
    def block(dims):
        return pl.BlockSpec((1,) + dims[1:], lambda i: (mi,) + (0,) * (len(dims) - 1))

    aliases = {3 + len(arrays) + i: i for i in range(len(before))}
    return call(
        partial(kernel, mi), outs, [SMEM] * 3 + [block(a.shape) for a in arrays] + [ANY] * len(before),
        [block(o.shape) for o in outs], scratch, grid=(1,), input_output_aliases=aliases, **more,
    )(*facts, *arrays, *before)


def tie(value, *others):
    return lax.optimization_barrier((value,) + others)[0]


def per_device(
    block_input, cotangent, span_offset, doc_lengths, ln1_gain, ln1_bias, w_query, w_key, w_value,
    query_bias, value_bias, w_out, out_bias, ln2_gain, ln2_bias, w_up, up_bias, w_down, down_bias,
):
    groups, ranks = lax.axis_size("seq"), lax.axis_size("mp")
    count = groups * ranks
    mp_index = lax.axis_index("mp")
    dev = lax.axis_index("seq") * ranks + mp_index
    rows = block_input.shape[1]
    tiles = rows // SPAN
    summaries = tiles * count
    shard = w_query.shape[0]
    bits = count.bit_length() - 1
    stages = [(b, b) for b in range(bits - 1, 2, -1)] + [(1, 2), (2, 1)]
    direct = shard == 64

    def swap(value, stage):
        pairs = [(i, i ^ (1 << stage[i & 1])) for i in range(count)]
        return lax.ppermute(value, AXES, pairs)

    def turn(value, by):
        return lax.ppermute(value, AXES, [(i, (i + by) % count) for i in range(count)])

    core = dev & 1
    slot = jnp.arange(count, dtype=jnp.int32)
    far = slot // (count // 2)
    mask = far
    for i, (even, odd) in enumerate(stages):
        where = jnp.where((core ^ far) == 0, even, odd)
        mask = mask | (((slot >> i) & 1) << where)
    owner = dev ^ mask
    if not direct:
        owner = slot
    member_slot = jnp.arange(16, dtype=jnp.int32)
    slots = owner[:, None] * tiles + (member_slot % 8)[None, :]
    valid = (member_slot % 8 <= tiles)[None, :]
    slots = jnp.stack(
        [
            jnp.where(valid & (member_slot // 8 == mi)[None, :], slots, -1).reshape(-1)
            for mi in range(2)
        ]
    )
    block_of, row_of = owner % ranks, owner // ranks
    facts = (jnp.stack((dev, mp_index)), span_offset, doc_lengths)

    def reach(value, flip):
        return lax.ppermute(value, AXES, [(i, i ^ flip) for i in range(count)])

    def spread(values):
        return [reach(value, flip) for value, flip in zip(values, (16, 8, 24))]

    def join(near, far):
        return jnp.concatenate((near, far), axis=0)

    def fold(keep, got):
        total = keep + got.astype(F32)
        half = total.shape[0] // 2
        return total[:half], total[half:].astype(BF16)

    def whole_blocks(arrays):
        return [pl.BlockSpec(a.shape, lambda i, n=len(a.shape): (0,) * n) for a in arrays]

    def fold_lines(keep, sent, got, sends=1):
        size = keep.shape[0]
        part = size // (1 + sends)
        outs = [shape((part, D), F32)] + [shape((part + (32 if sends == 1 else 16), D), BF16)] * sends
        mine = pl.BlockSpec((32, D), lambda i: (size // 32, 0))
        both = whole_blocks((keep, got))
        return call(fold_kernel, outs, [both[0], mine, both[1]], whole_blocks(outs), grid=(1,))(keep, sent, got)

    def gather_whole(value):
        both = lax.all_gather(value, "seq", axis=0, tiled=True)
        both = lax.all_gather(both, "mp", axis=0)
        return both[: ranks // 2], both[ranks // 2 :]

    def scatter_whole(keep, send):
        both = jnp.concatenate((keep, send), axis=0).astype(F32)
        total = lax.psum_scatter(both, "mp", scatter_dimension=0, tiled=True)[0]
        return lax.psum_scatter(total, "seq", scatter_dimension=0, tiled=True)

    def row(vector):
        return vector[None, :]

    def shape(dims, kind):
        return jax.ShapeDtypeStruct(dims, kind)

    half, tall = (count // 2, shard) if direct else (ranks // 2, shard * groups)
    width = 4 * LANES if direct else 3 * LANES
    apart = not direct
    wide, three = (2, rows, D), (2, rows, 3 * D)
    flat, pooled_dims = (2 * rows, D), (2, summaries, D)
    room = 12 if direct else 56
    masks = [pltpu.VMEM((tiles, SPAN + summaries, SPAN), F32)]

    def prepare():
        return call(
            prepare_kernel, [shape((1, max(shard, 64), D), BF16), shape((1, shard, 1152), BF16), shape((2, SPAN, D), BF16)],
            [SMEM] * 3 + [HBM] * 8, [VMEM] * 3,
            scratch=[pltpu.VMEM(wide, BF16), pltpu.SemaphoreType.DMA((11,))],
            limit=56,
        )(*facts, block_input, cotangent, w_query, w_key, w_value, w_out.T, w_up, w_down.T)

    x_left = turn(block_input[:, rows - SPAN :], 1)
    part_a, w_rest, cot_edge = prepare()
    if direct:
        got_a = spread([part_a] * 3)
        part_b = tie(w_rest, got_a[0])
        got_b = swap(part_b, stages[0])
        part_a = jnp.concatenate([part_a] + got_a, axis=0)
        part_a = tie(join(part_a, swap(part_a, stages[2])), got_b)
        part_b = join(part_b, tie(got_b, x_left))
        got_b = swap(part_b, stages[1])
        got_a = swap(part_a, stages[3])
        near_a = join(part_a, tie(got_a, got_b))
        far_a = swap(near_a, (0, 0))
        part_b = join(part_b, tie(got_b, near_a))
        got_b = swap(part_b, stages[2])
        more = ()
    else:
        cot_left = turn(cot_edge, 1)
        near_a, far_a = gather_whole(part_a[0, :shard, :384])
        near_b, far_b = gather_whole(w_rest[0])
        near_1, near_2, far_1, far_2 = (a[:, :, i : i + w] for a in (near_b, far_b) for i, w in ((0, 640), (640, 512)))
        more = (lax.all_gather(part_a[0, :64, 384:], AXES, axis=0),)
        block_of, row_of = jnp.arange(ranks, dtype=jnp.int32), jnp.zeros((ranks,), jnp.int32)

    xs, qkv, skv, sums, w_full = call(
        partial(project_kernel, apart),
        [shape(wide, BF16), shape(three, BF16), shape((2, summaries, 3 * D), BF16), shape(pooled_dims, F32)]
        + [shape((D, 3 * D), BF16)],
        [SMEM] * 5 + [VMEM] * 7 + [ANY] * (2 + len(more)),
        scratch=[
            pltpu.VMEM((count, 64, LANES), BF16),
            pltpu.VMEM((rows + SPAN, D), F32),
            pltpu.VMEM((2, rows + 2 * summaries, D), BF16),
            pltpu.SemaphoreType.DMA((2,)),
        ],
        limit=24 if direct else 56,
    )(
        *facts, block_of, row_of, slots, block_input, x_left, row(ln1_gain), row(ln1_bias),
        row(query_bias), row(value_bias), near_a, far_a, *more,
    )
    outs = [shape(wide, BF16), shape((2, 4, tiles, 1, 2 * SPAN), F32)]
    if direct:
        part_b = join(part_b, tie(got_b, skv))
        part_1, part_2 = part_b[:, :, :640], part_b[:, :, 640:]
        got_1 = swap(part_1, stages[3])
        qkv = tie(qkv, part_1)
    seen = call_row(attend_kernel, 0, facts, (qkv, skv), outs, (), masks, limit=room)
    if direct:
        cot_left = turn(tie(cot_edge, part_1), 1)
    att, lse = call_row(attend_kernel, 1, facts, (qkv, skv), outs, tuple(seen), masks, limit=room)
    if direct:
        near_1 = join(part_1, tie(got_1, att, cot_left))
        far_1 = swap(near_1, (0, 0))
        got_2 = swap(tie(part_2, near_1), stages[3])
    tall_low, tall_float = shape(flat, BF16), shape(flat, F32)
    weights = [pltpu.VMEM((D, 2 * rows), BF16)] * 2 + [pltpu.VMEM((D, FF // 2), BF16)] * 4
    *kept, gub_1, down_b, keep_1, send_1 = call(
        mlp_first_kernel,
        [tall_float] + [tall_low] * 4 + [shape((D, D), BF16)]
        + [shape((1, FF // 2), F32), shape((1, D), F32)] + [shape((half, tall, 512), BF16)] * 2,
        [SMEM] * 4 + [VMEM] * 8 + [HBM] + [ANY] * 2,
        [VMEM] * 8 + [ANY] * 2,
        scratch=weights
        + [pltpu.VMEM((rows + SPAN, D), F32), pltpu.VMEM(wide, BF16)]
        + [pltpu.SemaphoreType.DMA((4,)), pltpu.SemaphoreType.DMA((2,))],
        limit=28,
    )(
        facts[0], span_offset, block_of, row_of, xs, att, cot_left, row(out_bias), row(ln2_gain), row(ln2_bias),
        row(up_bias), row(down_bias), cotangent, near_1, far_1,
    )
    if direct:
        near_2 = join(part_2, tie(got_2, kept[0]))
        far_2 = swap(near_2, (0, 0))
        got_1 = swap(tie(send_1, near_2), (0, 0))
        keep_1, send_1 = fold(keep_1.astype(F32), got_1)
        got_1 = swap(send_1, stages[3])
        near_2 = tie(near_2, send_1)
    result, gmid, gatt, small_b, gub_2, keep_2, send_2 = call(
        mlp_second_kernel,
        [shape(wide, BF16)] * 3 + [shape((8, D), F32)]
        + [shape((1, FF // 2), F32)] + [shape((half, tall, 640), BF16)] * 2,
        [SMEM] * 2 + [VMEM] * 9 + [ANY] * 2,
        [VMEM] * 5 + [ANY] * 2,
        scratch=weights
        + [pltpu.VMEM((D, D), BF16), pltpu.SemaphoreType.DMA((2,)), pltpu.SemaphoreType.DMA((3,))],
        limit=28,
    )(block_of, row_of, att, row(ln2_gain), row(up_bias), *kept, near_2, far_2)
    gubs = (gub_1, gub_2)
    arrays = (qkv, skv, lse, gatt)
    outs = [shape(three, BF16), shape((2, summaries, 3 * D), BF16)]
    if direct:
        keep_1, send_1 = fold(keep_1, tie(got_1, send_2))
        got_2 = swap(tie(send_2, send_1), (0, 0))
    grads = call_row(attend_back_kernel, 0, facts, arrays, outs, (), masks, limit=room)
    if direct:
        keep_2, send_2 = fold(keep_2.astype(F32), tie(got_2, grads[0]))
        got_2 = swap(send_2, stages[3])
        grads = [tie(grads[0], send_2)] + list(grads[1:])
    grads = call_row(attend_back_kernel, 1, facts, arrays, outs, tuple(grads), masks, limit=room)
    lines, keep_a, send_a, *more = call(
        partial(weights_back_kernel, apart),
        [shape((16, D), F32)]
        + [shape((half * tall, width), BF16), shape((half * tall + (32 if direct else 0), width), BF16)]
        + [shape((count, 64, LANES), BF16)] * apart,
        [SMEM] * 5 + [VMEM] * 12,
        [VMEM] + [ANY] * (2 + apart),
        scratch=[
            pltpu.VMEM((D, 3 * D), BF16), pltpu.VMEM(pooled_dims, BF16), pltpu.VMEM((count, 64, LANES), BF16),
            pltpu.VMEM((32, D), BF16), pltpu.SemaphoreType.DMA((3,)),
        ],
        limit=24 if direct else 56,
    )(
        *facts, block_of, row_of, slots, xs, *grads, sums, w_full, row(ln1_gain), row(ln1_bias), small_b, down_b, *gubs,
    )

    def by_row(dims):
        return pl.BlockSpec((1,) + dims[1:], lambda i: (i,) + (0,) * (len(dims) - 1))

    once = pl.BlockSpec((1, D), lambda i: (0, 0))
    edge_dims = (2, SPAN, D)

    def rows_back(*after):
        return call(
            rows_back_kernel, [shape(wide, F32), shape((2,) + edge_dims, BF16)],
            [by_row(three), pl.BlockSpec((D, 3 * D), lambda i: (0, 0)), by_row(wide), by_row(wide)]
            + [by_row(edge_dims), once],
            [by_row(wide), pl.BlockSpec((2, 1, SPAN, D), lambda i: (0, i, 0, 0))], grid=(2,), limit=16,
        )(grads[0], tie(w_full, *after), xs, gmid, result, row(ln1_gain))

    def unroll(back):
        return call(
            unroll_kernel, [shape(wide, BF16)] * 2 + [shape((2, rows, LANES), F32)],
            [SMEM, by_row(wide), pl.BlockSpec((1, 1, SPAN, D), lambda i: (1, i, 0, 0)), by_row(wide)], [by_row(wide)] * 2 + [by_row((2, rows, LANES))],
            [pltpu.VMEM((2 * SPAN, D), F32)], grid=(2,),
        )(span_offset, result, back, block_input)

    final = [SMEM] * 3 + [VMEM] * 5
    rolled = [pltpu.VMEM((2 * SPAN, D), F32)]
    if direct:
        got_a = swap(send_a, (0, 0))
        keep_2, send_2 = fold(keep_2, tie(got_2, send_a))
        keep_b, send_b = (jnp.concatenate(a, axis=2) for a in ((keep_1, keep_2), (send_1, send_2)))
        got_b = swap(send_b, stages[2])
        keep_a, send_a = fold_lines(keep_a, send_a, tie(got_a, send_b))
        got_a = swap(send_a, stages[3])
        part, edge = rows_back(send_a)
        keep_b, send_b = fold(keep_b, tie(got_b, part))
        got_b = swap(send_b, stages[1])
        back = turn(tie(edge, send_b), -1)
        keep_a, send_a = fold_lines(keep_a, send_a, tie(got_a, send_b))
        got_a = swap(send_a, stages[2])
        keep_b, send_b = fold(keep_b, tie(got_b, send_a))
        got_b = swap(send_b, stages[0])
        keep_a, *send_a = fold_lines(keep_a, send_a, tie(got_a, send_b), 3)
        got_a = spread(send_a)
        result_own, *hats = unroll(tie(back, send_a[0]))
        grad_wo, grad_wu, grad_wd = call(
            finish_rest_kernel, [shape((shard, LANES), F32), shape((shard, 512), F32), shape((shard, 512), F32)],
            [VMEM] * 2,
        )(keep_b, tie(got_b, send_a[0]))
        input_grad, grad_wq, grad_wk, grad_wv, grad_ub, *small = call(
            partial(finish_kernel, True),
            [shape(wide, F32)] + [shape((shard, LANES), F32)] * 3 + [shape((1, FF), F32)] + [shape((1, D), F32)] * 8,
            final + [VMEM] * 5, scratch=rolled, limit=16,
        )(*facts, *hats, part, back, row(ln1_gain), keep_a, send_a[0], *(tie(got, grad_wo) for got in got_a))
        grad_wo, grad_wd = grad_wo.T, grad_wd.T
        small = [a.reshape(D) for a in small]
        grad_ub = grad_ub.reshape(FF)
    else:
        keep_a, send_a = (a.reshape(half, tall, width) for a in (keep_a, send_a))
        part, edge = rows_back()
        back = turn(edge, -1)
        result_own, *hats = unroll(back)
        sum_a, sum_1, sum_2 = (scatter_whole(*a) for a in ((keep_a, send_a), (keep_1, send_1), (keep_2, send_2)))
        grad_wq, grad_wk, grad_wv = (sum_a[:, i : i + LANES] for i in (0, 128, 256))
        grad_wo = sum_2[:, 512:].T
        grad_wu, grad_wd = (
            jnp.concatenate((sum_1[:, i : i + 256], sum_2[:, i : i + 256]), axis=1) for i in (0, 256)
        )
        grad_wd = grad_wd.T
        pooled = lax.psum_scatter(more[0].astype(F32), AXES, scatter_dimension=0, tiled=True)[0]
        lines = lax.psum(lines, AXES)
        grad_ub = lines[4:8].reshape(FF)
        small = [lines[i] for i in (0, 1, 2, 3, 8, 9, 10, 11)]
        input_grad = call(partial(finish_kernel, False), [shape(wide, F32)], final + [VMEM], scratch=rolled, limit=16)(
            *facts, *hats, part, back, row(ln1_gain), pooled
        )[0]
    grad_gain_two, grad_shift_two, grad_obias, grad_dbias, grad_gain_one, grad_shift_one, grad_qb, grad_vb = small
    return (
        result_own,
        input_grad,
        grad_gain_one,
        grad_shift_one,
        grad_wq,
        grad_wk,
        grad_wv,
        grad_qb,
        grad_vb,
        grad_wo,
        grad_obias,
        grad_gain_two,
        grad_shift_two,
        grad_wu,
        grad_ub,
        grad_wd,
        grad_dbias,
    )


def solution(mesh):
    vector, matrix, turned = P(), P("seq", "mp"), P("mp", "seq")
    own, group = P(None, ("seq", "mp"), None), P(None, "seq", None)
    return jax.shard_map(
        per_device,
        mesh=mesh,
        in_specs=(own, group, vector, vector, vector, vector, matrix, matrix, matrix, vector, vector)
        + (turned, vector, vector, vector, matrix, vector, turned, vector),
        out_specs=(own, own, vector, vector, matrix, matrix, matrix, vector, vector, turned, vector)
        + (vector, vector, matrix, vector, turned, vector),
        check_vma=False,
    )
```

```python
from functools import partial
import math

import jax
import jax.numpy as jnp
from jax import lax
from jax.experimental import pallas as pl
from jax.experimental.pallas import tpu as pltpu
from jax.sharding import PartitionSpec as P

D = 512
FF = 2048
HEAD_DIM = 64
SPAN = 128
LANES = 128
EPSILON = 1e-05
NEGATIVE = -1e30
SCALE = 1.0 / math.sqrt(HEAD_DIM)
F32 = jnp.float32
BF16 = jnp.bfloat16
AXES = ("seq", "mp")
MIB = 1 << 20
VMEM = pl.BlockSpec(memory_space=pltpu.VMEM)
SMEM = pl.BlockSpec(memory_space=pltpu.SMEM)
ANY = pl.BlockSpec(memory_space=pl.ANY)
HBM = pl.BlockSpec(memory_space=pltpu.HBM)


def dot(left, right):
    return lax.dot_general(left, right, (((1,), (0,)), ((), ())), preferred_element_type=F32)


def dot_cols(left, right):
    return lax.dot_general(left, right, (((1,), (1,)), ((), ())), preferred_element_type=F32)


def unit(rows):
    centred = rows - jnp.mean(rows, axis=-1, keepdims=True)
    inverse = lax.rsqrt(jnp.mean(centred * centred, axis=-1, keepdims=True) + EPSILON)
    return centred * inverse, inverse


def unit_back(grad, hat, inverse):
    shift = jnp.mean(grad, axis=-1, keepdims=True)
    slope = jnp.mean(grad * hat, axis=-1, keepdims=True)
    return (grad - shift - hat * slope) * inverse


def row_info(place, offsets, lengths, mi):
    ends = []
    for c in range(lengths.shape[1]):
        ends.append(lengths[mi, c] + (ends[-1] if ends else 0))
    return place[0], offsets[mi], ends


def doc_start(positions, ends):
    start = jnp.zeros_like(positions)
    for end in ends:
        start = jnp.where(positions >= end, end, start)
    return start


def summary_range(summary_ids, offset, ends):
    last = offset - 1 + SPAN * summary_ids
    first = jnp.maximum(doc_start(last, ends), last - (SPAN - 1))
    return first, last


def iota(shape, dim):
    return lax.broadcasted_iota(jnp.int32, shape, dim)


def roll_rows(ref, by):
    whole = pl.multiple_of((by // 8) * 8, 8)
    return pltpu.roll(ref[pl.ds(whole, SPAN + 8), :], SPAN + 8 - (by - whole), axis=0)[:SPAN]


def prepare_kernel(
    place, offsets, lengths, x_ref, cot_ref, wq_ref, wk_ref, wv_ref, wo_ref, wu_ref, wd_ref,
    out_ref, rest_ref, edge_ref, rows_ref, sem
):
    rows = x_ref.shape[1]
    last_rows = pl.multiple_of(place[1] * rows + (rows - SPAN), SPAN)
    shard = wq_ref.shape[0]
    copies = [pltpu.make_async_copy(x_ref.at[mi], rows_ref.at[mi], sem.at[mi]) for mi in range(2)]
    copies += [
        pltpu.make_async_copy(ref, out_ref.at[0, 0:shard, i * LANES : (i + 1) * LANES], sem.at[2 + i])
        for i, ref in enumerate((wq_ref, wk_ref, wv_ref))
    ]
    copies.append(pltpu.make_async_copy(cot_ref.at[:, pl.ds(last_rows, SPAN), :], edge_ref, sem.at[5]))
    copies.append(pltpu.make_async_copy(wo_ref, rest_ref.at[0, :, 0:128], sem.at[6]))
    for i, (ref, first) in enumerate(((wu_ref, 0), (wd_ref, 0), (wu_ref, 256), (wd_ref, 256))):
        target = rest_ref.at[0, :, 128 + 256 * i : 384 + 256 * i]
        copies.append(pltpu.make_async_copy(ref.at[:, first : first + 256], target, sem.at[7 + i]))
    for copy in copies:
        copy.start()
    sums = []
    for mi in range(2):
        dev, offset, ends = row_info(place, offsets, lengths, mi)
        first, last = summary_range(dev * (rows // SPAN) + iota((8, 1), 0), offset, ends)
        pos = dev * rows + iota((1, rows), 1)
        member = jnp.where((pos >= first) & (pos <= last), 1.0, 0.0).astype(BF16)
        copies[mi].wait()
        hat, _ = unit(rows_ref[mi].astype(F32))
        high = hat.astype(BF16)
        rest = (hat - high.astype(F32)).astype(BF16)
        total = dot(member, high) + dot(member, rest)
        sums.append(total * lax.rsqrt((last - first + 1).astype(F32)))
    both = jnp.concatenate(sums, axis=0).astype(BF16)
    for copy in copies[2:]:
        copy.wait()
    for lane in range(D // LANES):
        out_ref[0, 16 * lane : 16 * lane + 16, 384:512] = both[:, lane * LANES : (lane + 1) * LANES]


def fill_masks(place, offsets, lengths, mi, bias_ref, tiles, summaries, length):
    dev, offset, ends = row_info(place, offsets, lengths, mi)
    ends_col = offset - 1 + SPAN * iota((summaries, 1), 0)
    for t in range(tiles):
        base = SPAN * (dev * tiles + t) + offset - SPAN
        qpos = base + iota((1, SPAN), 1)
        qpos = jnp.where(qpos < 0, qpos + length, qpos)
        kpos = base + iota((SPAN, 1), 0)
        kpos = jnp.where(kpos < 0, kpos + length, kpos)
        span_first = jnp.where(qpos >= base + SPAN, base + length, base)
        doc_first = doc_start(qpos, ends)
        local_ok = (kpos >= jnp.maximum(doc_first, span_first)) & (kpos <= qpos)
        summary_ok = (ends_col >= doc_first) & (ends_col < span_first)
        bias_ref[t, 0:SPAN, :] = jnp.where(local_ok, 0.0, NEGATIVE)
        bias_ref[t, SPAN : SPAN + summaries, :] = jnp.where(summary_ok, 0.0, NEGATIVE)


def split_heads(pair):
    low = iota(pair.shape, 1) < HEAD_DIM
    zero = jnp.zeros_like(pair)
    return jnp.concatenate((jnp.where(low, pair, zero), jnp.where(low, zero, pair)), axis=0)


def join_heads(turned):
    half = turned.shape[1] // 2
    return jnp.concatenate((turned[:HEAD_DIM, :half], turned[HEAD_DIM:, half:]), axis=0).T


def project_kernel(
    apart, place_ref, offsets, lengths, block_of, row_of, slots_ref, x_ref, left_ref, gain, shift, qbias, vbias,
    near_ref, far_ref, *refs
):
    if apart:
        all_ref, *refs = refs
    xs_ref, qkv_ref, skv_ref, sums_ref, w_ref, stack_ref, wide_ref, rows_ref, sem = refs
    rows = x_ref.shape[1]
    tiles = rows // SPAN
    summaries = skv_ref.shape[1]
    half, shard, _ = near_ref.shape

    def place(d, carry):
        for source, slot in ((near_ref, d), (far_ref, half + d)):
            here = pl.ds(pl.multiple_of(row_of[slot] * shard, 16), shard)
            cols = pl.ds(pl.multiple_of(block_of[slot] * 384, 128), 384)
            pltpu.make_async_copy(source.at[d, :, 0:384], w_ref.at[here, cols], sem.at[0]).start()
            if not apart:
                pltpu.make_async_copy(
                    source.at[d, 0:64, 384:512], stack_ref.at[slot], sem.at[1]
                ).start()
        return carry

    lax.fori_loop(0, half, place, 0)
    if apart:
        pltpu.make_async_copy(all_ref, stack_ref, sem.at[1]).start()
    for mi in range(2):
        wide_ref[0:SPAN, :] = left_ref[mi].astype(F32)
        wide_ref[SPAN : SPAN + rows, :] = x_ref[mi].astype(F32)
        for t in range(tiles):
            here = slice(t * SPAN, (t + 1) * SPAN)
            rolled = roll_rows(wide_ref, t * SPAN + offsets[mi])
            xs_ref[mi, here, :] = rolled.astype(BF16)
            hat, _ = unit(rolled)
            rows_ref[mi, here, :] = (hat * gain[...] + shift[...]).astype(BF16)
    pltpu.make_async_copy(stack_ref, stack_ref, sem.at[1]).wait()
    roots = []
    for mi in range(2):
        _, offset, ends = row_info(place_ref, offsets, lengths, mi)
        first, last = summary_range(iota((summaries, 1), 0), offset, ends)
        root = jnp.sqrt((last - first + 1).astype(F32))
        roots.append(root)
        for base in range(0, stack_ref.shape[0], 32):
            named = slots_ref[mi : mi + 1, 16 * base : 16 * base + 512]
            pick = jnp.where(iota((summaries, 1), 0) == named, 1.0, 0.0).astype(BF16)
            piece = jnp.concatenate(
                [
                    stack_ref[base : base + 32, 16 * lane : 16 * lane + 16, :].reshape(512, LANES)
                    for lane in range(D // LANES)
                ],
                axis=1,
            )
            found = dot(pick, piece)
            sums_ref[mi] = found if base == 0 else sums_ref[mi] + found
        summed = sums_ref[mi] * gain[...] + root * shift[...]
        high = summed.astype(BF16)
        rows_ref[mi, rows : rows + summaries, :] = high
        rows_ref[mi, rows + summaries : rows + 2 * summaries, :] = (summed - high.astype(F32)).astype(BF16)
    pltpu.make_async_copy(w_ref, w_ref, sem.at[0]).wait()
    none = jnp.zeros((1, LANES), F32)
    for m in range(4):
        lanes = slice(m * LANES, (m + 1) * LANES)
        cols = slice(m * 384, (m + 1) * 384)
        bias = jnp.concatenate((qbias[:, lanes], none, vbias[:, lanes]), axis=1)
        for mi in range(2):
            projected = dot(rows_ref[mi], w_ref[:, cols])
            qkv_ref[mi, :, cols] = (projected[:rows] + bias).astype(BF16)
            pooled = projected[rows : rows + summaries] + projected[rows + summaries :]
            skv_ref[mi, :, cols] = (pooled + roots[mi] * bias).astype(BF16)


def pair_of(ref, here, pair):
    def part(i):
        return ref[0, here, pl.ds(pl.multiple_of(pair * 384 + i * LANES, LANES), LANES)]

    return part(0), part(1), part(2)


def attend_kernel(mi, place, offsets, lengths, qkv_ref, skv_ref, *refs):
    att_ref, lse_ref, bias_ref = refs[-3:]
    rows = qkv_ref.shape[1]
    tiles = rows // SPAN
    summaries = skv_ref.shape[1]
    fill_masks(place, offsets, lengths, mi, bias_ref, tiles, summaries, summaries * SPAN)

    def heads(pair, carry):
        lanes = pl.ds(pl.multiple_of(pair * LANES, LANES), LANES)
        _, skeys, svalues = pair_of(skv_ref, slice(None), pair)
        svalues = svalues.T
        spans = [pair_of(qkv_ref, slice(t * SPAN, (t + 1) * SPAN), pair) for t in range(tiles)]
        scores = []
        for t, (queries, keys, _) in enumerate(spans):
            bias = bias_ref[t]
            keys = jnp.concatenate((keys, skeys), axis=0)
            scores.append(dot_cols(keys, split_heads(queries * SCALE)) + jnp.concatenate((bias, bias), axis=1))
        probs = []
        for t in range(tiles):
            top = jnp.max(scores[t], axis=0, keepdims=True)
            grown = jnp.exp(scores[t] - top)
            total = jnp.sum(grown, axis=0, keepdims=True)
            probs.append((grown * (1.0 / total)).astype(BF16))
            lse_ref[0, pair, t] = top + jnp.log(total)
        for t, (_, _, values) in enumerate(spans):
            values = jnp.concatenate((values.T, svalues), axis=1)
            att_ref[0, t * SPAN : (t + 1) * SPAN, lanes] = join_heads(dot(values, probs[t])).astype(BF16)
        return carry

    lax.fori_loop(0, 4, heads, 0)


def gelu_pair(u):
    c0 = math.sqrt(2.0 / math.pi)
    square = u * u
    t = jnp.tanh(c0 * u * (1.0 + 0.044715 * square))
    half = 0.5 * (1.0 + t)
    slope = half + (0.5 * c0) * u * (1.0 - t * t) * (1.0 + (3 * 0.044715) * square)
    return u * half, slope


def columns(block, width):
    return pl.ds(pl.multiple_of(block * width, 128), width)


def mlp_half(half_id, ubias, n_ref, c_ref, nt_ref, ct_ref, wu_ref, wd_ref, gu_ref, gd_ref, gub_ref):
    total = n_ref.shape[0]
    bias = jnp.concatenate([ubias[:, m * 512 + half_id * 256 : m * 512 + half_id * 256 + 256] for m in range(4)], axis=1)
    w_up, w_down = wu_ref[...], wd_ref[...]
    halves = [slice(i * total // 2, (i + 1) * total // 2) for i in range(2)]
    ups = [dot(n_ref[here, :], w_up) + bias for here in halves]
    backs = [dot(c_ref[here, :], w_down) for here in halves]
    acts, grads, sums = [], [], []
    gub = jnp.zeros_like(gub_ref)
    for up, back in zip(ups, backs):
        act, slope = gelu_pair(up)
        grad = back * slope
        gub += jnp.sum(grad, axis=0, keepdims=True)
        acts.append(act.astype(BF16))
        grads.append(grad.astype(BF16))
        sums.append((dot_cols(acts[-1], w_down), dot_cols(grads[-1], w_up)))
    gub_ref[...] = gub
    gu_ref[...] = dot(nt_ref[...], jnp.concatenate(grads, axis=0)).astype(BF16)
    gd_ref[...] = dot(ct_ref[...], jnp.concatenate(acts, axis=0)).astype(BF16)
    return halves, sums


def pull(block_of, row_of, near_ref, far_ref, parts):
    half, shard, _ = near_ref.shape

    def body(d, carry):
        for source, slot in ((near_ref, d), (far_ref, half + d)):
            here = pl.ds(pl.multiple_of(row_of[slot] * shard, 16), shard)
            for target, first, width, sem in parts:
                pltpu.make_async_copy(
                    source.at[d, :, first : first + width], target.at[here, columns(block_of[slot], width)], sem
                ).start()
        return carry

    lax.fori_loop(0, half, body, 0)


def push(block_of, row_of, keep_ref, send_ref, parts):
    half, shard, _ = keep_ref.shape

    def body(d, carry):
        for target, slot in ((keep_ref, d), (send_ref, half + d)):
            here = pl.ds(pl.multiple_of(row_of[slot] * shard, 16), shard)
            for source, first, width, sem in parts:
                pltpu.make_async_copy(
                    source.at[here, columns(block_of[slot], width)], target.at[d, :, first : first + width], sem
                ).start()
        return carry

    lax.fori_loop(0, half, body, 0)


def mlp_first_kernel(
    place_ref, offsets, block_of, row_of, xs_ref, att_ref, left_ref, obias, gain, shift, ubias, dbias, cot_ref,
    near_ref, far_ref,
    resid_ref, acc_ref, gn_ref, n_ref, c_ref, wo_ref, gub_ref, down_ref, keep_ref, send_ref,
    nt_ref, ct_ref, wu_ref, wd_ref, gu_ref, gd_ref, wide_ref, low_ref, sem, out_sem,
):
    rows = xs_ref.shape[1]
    own = pl.ds(pl.multiple_of(place_ref[1] * rows, SPAN), rows)
    own_copy = pltpu.make_async_copy(cot_ref.at[:, own, :], low_ref, sem.at[3])
    own_copy.start()
    pull(block_of, row_of, near_ref, far_ref, ((wo_ref, 0, 128, sem.at[0]),))
    pull(block_of, row_of, near_ref, far_ref, ((wu_ref, 128, 256, sem.at[1]), (wd_ref, 384, 256, sem.at[2])))
    down_ref[...] = jnp.zeros_like(down_ref)
    own_copy.wait()
    pltpu.make_async_copy(wo_ref, wo_ref, sem.at[0]).wait()
    for mi in range(2):
        all_rows = slice(mi * rows, (mi + 1) * rows)
        wide_ref[0:SPAN, :] = left_ref[mi].astype(F32)
        wide_ref[SPAN : SPAN + rows, :] = low_ref[mi].astype(F32)
        for t in range(rows // SPAN):
            rolled = roll_rows(wide_ref, t * SPAN + offsets[mi])
            down_ref[...] += jnp.sum(rolled, axis=0, keepdims=True)
            c_ref[mi * rows + t * SPAN : mi * rows + (t + 1) * SPAN, :] = rolled.astype(BF16)
        resid = xs_ref[mi].astype(F32) + dot_cols(att_ref[mi], wo_ref[...]) + obias[...]
        resid_ref[all_rows, :] = resid
        hat, _ = unit(resid)
        normed = (hat * gain[...] + shift[...]).astype(BF16)
        n_ref[all_rows, :] = normed
        nt_ref[:, all_rows] = normed.T
        ct_ref[:, all_rows] = c_ref[all_rows, :].T
    pltpu.make_async_copy(wu_ref, wu_ref, sem.at[1]).wait()
    pltpu.make_async_copy(wd_ref, wd_ref, sem.at[2]).wait()
    halves, sums = mlp_half(0, ubias, n_ref, c_ref, nt_ref, ct_ref, wu_ref, wd_ref, gu_ref, gd_ref, gub_ref)
    push(block_of, row_of, keep_ref, send_ref, ((gu_ref, 0, 256, out_sem.at[0]), (gd_ref, 256, 256, out_sem.at[1])))
    for here, (down, back) in zip(halves, sums):
        acc_ref[here, :] = (down + dbias[...]).astype(BF16)
        gn_ref[here, :] = back.astype(BF16)
    pltpu.make_async_copy(gu_ref, gu_ref, out_sem.at[0]).wait()
    pltpu.make_async_copy(gd_ref, gd_ref, out_sem.at[1]).wait()


def mlp_second_kernel(
    block_of, row_of, att_ref, gain, ubias, resid_ref, acc_ref, gn_ref, n_ref, c_ref, wo_ref,
    near_ref, far_ref,
    result_ref, gmid_ref, gatt_ref, small_ref, gub_ref, keep_ref, send_ref,
    nt_ref, ct_ref, wu_ref, wd_ref, gu_ref, gd_ref, go_ref, sem, out_sem,
):
    rows = att_ref.shape[1]
    pull(block_of, row_of, near_ref, far_ref, ((wu_ref, 0, 256, sem.at[0]), (wd_ref, 256, 256, sem.at[1])))
    small_ref[...] = jnp.zeros_like(small_ref)
    for mi in range(2):
        here = slice(mi * rows, (mi + 1) * rows)
        nt_ref[:, here] = n_ref[here, :].T
        ct_ref[:, here] = c_ref[here, :].T
    pltpu.make_async_copy(wu_ref, wu_ref, sem.at[0]).wait()
    pltpu.make_async_copy(wd_ref, wd_ref, sem.at[1]).wait()
    halves, sums = mlp_half(1, ubias, n_ref, c_ref, nt_ref, ct_ref, wu_ref, wd_ref, gu_ref, gd_ref, gub_ref)
    push(block_of, row_of, keep_ref, send_ref, ((gu_ref, 0, 256, out_sem.at[0]), (gd_ref, 256, 256, out_sem.at[1])))
    branches = []
    for mi, (here, (down, back)) in enumerate(zip(halves, sums)):
        result_ref[mi] = (resid_ref[here, :] + (acc_ref[here, :].astype(F32) + down)).astype(BF16)
        hat, inverse = unit(resid_ref[here, :])
        grad = gn_ref[here, :].astype(F32) + back
        small_ref[0:1, :] += jnp.sum(grad * hat, axis=0, keepdims=True)
        small_ref[1:2, :] += jnp.sum(grad, axis=0, keepdims=True)
        branch = (c_ref[here, :].astype(F32) + unit_back(grad * gain[...], hat, inverse)).astype(BF16)
        gmid_ref[mi] = branch
        small_ref[2:3, :] += jnp.sum(branch.astype(F32), axis=0, keepdims=True)
        gatt_ref[mi] = dot(branch, wo_ref[...]).astype(BF16)
        branches.append(branch.T)
    both = jnp.concatenate((att_ref[0], att_ref[1]), axis=0)
    go_ref[...] = dot(jnp.concatenate(branches, axis=1), both).astype(BF16)
    push(block_of, row_of, keep_ref, send_ref, ((go_ref, 512, 128, out_sem.at[2]),))
    pltpu.make_async_copy(gu_ref, gu_ref, out_sem.at[0]).wait()
    pltpu.make_async_copy(gd_ref, gd_ref, out_sem.at[1]).wait()
    pltpu.make_async_copy(go_ref, go_ref, out_sem.at[2]).wait()


def attend_back_kernel(mi, place, offsets, lengths, qkv_ref, skv_ref, lse_ref, gatt_ref, *refs):
    grad_ref, pooled_ref, bias_ref = refs[-3:]
    rows = qkv_ref.shape[1]
    tiles = rows // SPAN
    summaries = skv_ref.shape[1]
    fill_masks(place, offsets, lengths, mi, bias_ref, tiles, summaries, summaries * SPAN)

    def heads(pair, carry):
        lanes = pl.ds(pl.multiple_of(pair * LANES, LANES), LANES)

        def columns(i):
            return pl.ds(pl.multiple_of(pair * 384 + i * LANES, LANES), LANES)

        _, skeys, svalues = pair_of(skv_ref, slice(None), pair)
        skeys_t = skeys.T
        sum_k = jnp.zeros((summaries, LANES), F32)
        sum_v = jnp.zeros((summaries, LANES), F32)
        held = []
        for t in range(tiles):
            here = slice(t * SPAN, (t + 1) * SPAN)
            queries, keys, values = pair_of(qkv_ref, here, pair)
            queries = split_heads(queries * SCALE)
            grads = split_heads(gatt_ref[0, here, lanes])
            bias = bias_ref[t]
            scores = dot_cols(jnp.concatenate((keys, skeys), axis=0), queries)
            gprobs = dot_cols(jnp.concatenate((values, svalues), axis=0), grads)
            held.append((queries, keys, grads, scores + jnp.concatenate((bias, bias), axis=1), gprobs))
        for t, (queries, keys, grads, scores, gprobs) in enumerate(held):
            here = slice(t * SPAN, (t + 1) * SPAN)
            probs = jnp.exp(scores - lse_ref[0, pair, t])
            delta = jnp.sum(probs * gprobs, axis=0, keepdims=True)
            gscores = (probs * (gprobs - delta)).astype(BF16)
            keys_t = jnp.concatenate((keys.T, skeys_t), axis=1)
            grad_q = join_heads(dot(keys_t, gscores)) * SCALE
            grad_k = dot(gscores, queries)
            grad_v = dot(probs.astype(BF16), grads)
            grad_ref[0, here, columns(0)] = grad_q.astype(BF16)
            grad_ref[0, here, columns(1)] = grad_k[:SPAN].astype(BF16)
            grad_ref[0, here, columns(2)] = grad_v[:SPAN].astype(BF16)
            sum_k += grad_k[SPAN:]
            sum_v += grad_v[SPAN:]
        pooled_ref[0, :, columns(0)] = jnp.zeros((summaries, LANES), BF16)
        pooled_ref[0, :, columns(1)] = sum_k.astype(BF16)
        pooled_ref[0, :, columns(2)] = sum_v.astype(BF16)
        return carry

    lax.fori_loop(0, 4, heads, 0)


def weights_back_kernel(
    apart, place, offsets, lengths, block_of, row_of, slots_ref, xs_ref, grad_ref, pooled_ref, sums_ref, w_ref,
    gain, shift, small_ref, down_ref, gub1_ref, gub2_ref, line_ref, keep_ref, send_ref, *refs
):
    if apart:
        all_ref, *refs = refs
    gwb_ref, back_ref, stack_ref, pad_ref, sem = refs
    rows = xs_ref.shape[1]
    summaries = pooled_ref.shape[1]
    half = block_of.shape[0] // 2
    shard = keep_ref.shape[0] // half
    turned = []
    column = jnp.zeros((1, 3 * D), F32)
    for mi in range(2):
        _, offset, ends = row_info(place, offsets, lengths, mi)
        first, last = summary_range(iota((summaries, 1), 0), offset, ends)
        root = jnp.sqrt((last - first + 1).astype(F32))
        hat, _ = unit(xs_ref[mi].astype(F32))
        turned += [hat.astype(BF16).T, sums_ref[mi].astype(BF16).T]
        column += jnp.sum(grad_ref[mi].astype(F32), axis=0, keepdims=True)
        column += jnp.sum(root * pooled_ref[mi].astype(F32), axis=0, keepdims=True)
        back_ref[mi] = dot_cols(pooled_ref[mi], w_ref[...]).astype(BF16)
    turned = jnp.concatenate(turned, axis=1)
    gain_col, shift_col = gain[...].T, shift[...].T
    grad_gain = jnp.zeros((D, 1), F32)
    grad_shift = jnp.zeros((D, 1), F32)
    for m in range(4):
        cols = slice(m * 384, (m + 1) * 384)
        lanes = slice(m * LANES, (m + 1) * LANES)
        grads = jnp.concatenate([ref[mi, :, cols] for mi in range(2) for ref in (grad_ref, pooled_ref)], axis=0)
        hats, w, sums = dot(turned, grads), w_ref[:, cols].astype(F32), column[:, cols]
        grad_gain += jnp.sum(hats * w, axis=1, keepdims=True)
        grad_shift += jnp.sum(sums * w, axis=1, keepdims=True)
        gwb_ref[:, cols] = (hats * gain_col + shift_col * sums).astype(BF16)
        line_ref[10:11, lanes] = sums[:, :128]
        line_ref[11:12, lanes] = sums[:, 256:]
    line_ref[8:9, :] = grad_gain.T
    line_ref[9:10, :] = grad_shift.T
    line_ref[0:3, :] = small_ref[0:3, :]
    line_ref[3:4, :] = down_ref[...]
    for i in range(4):
        for j, ref in enumerate((gub1_ref, gub2_ref)):
            line_ref[4 + i : 5 + i, j * 256 : (j + 1) * 256] = ref[:, i * 256 : (i + 1) * 256]
    line_ref[12:16, :] = jnp.zeros((4, D), F32)
    for base in range(0, stack_ref.shape[0], 32):
        names = [slots_ref[mi : mi + 1, 16 * base : 16 * base + 512] for mi in range(2)]
        spread = [
            jnp.where(iota((summaries, 1), 0) == named, 1.0, 0.0).astype(BF16).T for named in names
        ]
        piece = (dot(spread[0], back_ref[0]) + dot(spread[1], back_ref[1])).astype(BF16)
        for lane in range(D // LANES):
            part = piece[:, lane * LANES : (lane + 1) * LANES]
            stack_ref[base : base + 32, 16 * lane : 16 * lane + 16, :] = part.reshape(32, 16, LANES)

    def emit(d, carry):
        for target, slot in ((keep_ref, d), (send_ref, half + d)):
            first_row = pl.multiple_of(row_of[slot] * shard, 16)
            cols = pl.ds(pl.multiple_of(block_of[slot] * 384, 128), 384)
            here = target.at[pl.ds(pl.multiple_of(d * shard, 16), shard), :]
            pltpu.make_async_copy(
                gwb_ref.at[pl.ds(first_row, shard), cols], here.at[:, 0:384], sem.at[0]
            ).start()
            if not apart:
                pltpu.make_async_copy(stack_ref.at[slot], here.at[:, 384:512], sem.at[1]).start()
        return carry

    lax.fori_loop(0, half, emit, 0)
    if apart:
        pltpu.make_async_copy(stack_ref, all_ref, sem.at[1]).start()
    else:
        high = line_ref[...].astype(BF16)
        pad_ref[0:16, :] = high
        pad_ref[16:32, :] = (line_ref[...] - high.astype(F32)).astype(BF16)
        size = half * shard
        copy = pltpu.make_async_copy(pad_ref, send_ref.at[size : size + 32, :], sem.at[2])
        copy.start()
        copy.wait()
    pltpu.make_async_copy(gwb_ref, gwb_ref, sem.at[0]).wait()
    pltpu.make_async_copy(stack_ref, stack_ref, sem.at[1]).wait()


def rows_back_kernel(grad_ref, w_ref, xs_ref, gmid_ref, result_ref, gain, part_ref, edge_ref):
    grad = dot_cols(grad_ref[0], w_ref[...]) * gain[...]
    hat, inverse = unit(xs_ref[0].astype(F32))
    part = gmid_ref[0].astype(F32) + unit_back(grad, hat, inverse)
    part_ref[0] = part
    edge_ref[0, 0] = part[0:SPAN].astype(BF16)
    edge_ref[1, 0] = result_ref[0]


def fold_kernel(keep_ref, mine_ref, got_ref, next_ref, *send_refs):
    size = keep_ref.shape[0]
    part = size // (1 + len(send_refs))
    mine = mine_ref[0:16, :].astype(F32) + mine_ref[16:32, :].astype(F32)
    lines = mine + (got_ref[size : size + 16, :].astype(F32) + got_ref[size + 16 : size + 32, :].astype(F32))
    high = lines.astype(BF16)
    rest = (lines - high.astype(F32)).astype(BF16)
    next_ref[...] = keep_ref[0:part, :].astype(F32) + got_ref[0:part, :].astype(F32)
    for i, send_ref in enumerate(send_refs):
        here = slice((i + 1) * part, (i + 2) * part)
        send_ref[0:part, :] = (keep_ref[here, :].astype(F32) + got_ref[here, :].astype(F32)).astype(BF16)
        send_ref[part : part + 16, :] = high
        if len(send_refs) == 1:
            send_ref[part + 16 : part + 32, :] = rest


def lines_of(ref):
    return ref[ref.shape[0] - 16 :, :].astype(F32)


def two_tiles(ref, right, mi, t):
    if (t + 2) * SPAN <= ref.shape[1]:
        return ref[mi, t * SPAN : (t + 2) * SPAN, :]
    return jnp.concatenate((ref[mi, t * SPAN :, :], right[mi].astype(ref.dtype)), axis=0)


def unroll_kernel(offsets, result_ref, right_ref, x_ref, out_ref, hat_ref, inverse_ref, wide_ref):
    mi = pl.program_id(0)
    for t in range(result_ref.shape[1] // SPAN):
        here = slice(t * SPAN, (t + 1) * SPAN)
        wide_ref[...] = two_tiles(result_ref, right_ref.at[0], 0, t).astype(F32)
        out_ref[0, here, :] = roll_rows(wide_ref, SPAN - offsets[mi]).astype(BF16)
        hat, inverse = unit(x_ref[0, here, :].astype(F32))
        hat_ref[0, here, :] = hat.astype(BF16)
        inverse_ref[0, here, :] = jnp.broadcast_to(inverse, (SPAN, LANES))


def finish_rest_kernel(keep_ref, got_ref, wo_ref, wu_ref, wd_ref):
    total = keep_ref[0] + got_ref[0].astype(F32)
    for i in range(2):
        wu_ref[:, i * 256 : (i + 1) * 256] = total[:, i * 512 : i * 512 + 256]
        wd_ref[:, i * 256 : (i + 1) * 256] = total[:, i * 512 + 256 : i * 512 + 512]
    wo_ref[...] = total[:, 1024:]


def finish_kernel(
    direct, place, offsets, lengths, hat_ref, inverse_ref, part_ref, right_ref, gain, *refs
):
    if direct:
        keep_ref, mine_ref, a_ref, b_ref, c_ref, out_ref, wq_ref, wk_ref, wv_ref, *line_refs, wide_ref = refs
        size = keep_ref.shape[0]
        total = (keep_ref[...] + a_ref[0:size, :].astype(F32)) + (
            b_ref[0:size, :].astype(F32) + c_ref[0:size, :].astype(F32)
        )
        wq_ref[...], wk_ref[...], wv_ref[...] = total[:, :128], total[:, 128:256], total[:, 256:384]
        pooled = total[:, 384:]
        lines = (lines_of(mine_ref) + lines_of(a_ref)) + (lines_of(b_ref) + lines_of(c_ref))
        ub_ref, *line_refs = line_refs
        for i in range(4):
            ub_ref[:, i * D : (i + 1) * D] = lines[4 + i : 5 + i, :]
        for ref, i in zip(line_refs, (0, 1, 2, 3, 8, 9, 10, 11)):
            ref[...] = lines[i : i + 1, :]
    else:
        pooled_ref, out_ref, wide_ref = refs
        pooled = pooled_ref[...]
    rows = hat_ref.shape[1]
    for mi in range(2):
        dev, offset, ends = row_info(place, offsets, lengths, mi)
        first, last = summary_range(dev * (rows // SPAN) + iota((8, 1), 0), offset, ends)
        lows = jnp.concatenate(
            [pooled[16 * i + 8 * mi : 16 * i + 8 * mi + 8, :] for i in range(D // LANES)], axis=1
        )
        lows = lows * gain[...] * lax.rsqrt((last - first + 1).astype(F32))
        level = (lows - jnp.mean(lows, axis=-1, keepdims=True)).astype(BF16)
        lows = lows.astype(BF16)
        first, last = summary_range(dev * (rows // SPAN) + iota((1, 8), 1), offset, ends)
        for t in range(rows // SPAN):
            here = slice(t * SPAN, (t + 1) * SPAN)
            pos = dev * rows + t * SPAN + iota((SPAN, 1), 0)
            member = jnp.where((pos >= first) & (pos <= last), 1.0, 0.0)
            hat = hat_ref[mi, here, :]
            slope = jnp.sum(member * dot_cols(hat, lows), axis=1, keepdims=True) * (1.0 / D)
            inverse = inverse_ref[mi, here, 0:1]
            wide_ref[...] = two_tiles(part_ref, right_ref.at[0], mi, t)
            own = roll_rows(wide_ref, SPAN - offset)
            out_ref[mi, here, :] = own + (dot(member.astype(BF16), level) - hat.astype(F32) * slope) * inverse


def call(kernel, outs, in_specs, out_specs=None, scratch=(), limit=8, **more):
    return pl.pallas_call(
        kernel,
        out_shape=outs,
        in_specs=in_specs,
        out_specs=out_specs if out_specs is not None else [VMEM] * len(outs),
        scratch_shapes=list(scratch),
        compiler_params=pltpu.CompilerParams(vmem_limit_bytes=limit * MIB),
        cost_estimate=pl.CostEstimate(flops=1, bytes_accessed=1, transcendentals=0),
        **more,
    )


def call_row(kernel, mi, facts, arrays, outs, before, scratch, **more):
    def block(dims):
        return pl.BlockSpec((1,) + dims[1:], lambda i: (mi,) + (0,) * (len(dims) - 1))

    aliases = {3 + len(arrays) + i: i for i in range(len(before))}
    return call(
        partial(kernel, mi), outs, [SMEM] * 3 + [block(a.shape) for a in arrays] + [ANY] * len(before),
        [block(o.shape) for o in outs], scratch, grid=(1,), input_output_aliases=aliases, **more,
    )(*facts, *arrays, *before)


def tie(value, *others):
    return lax.optimization_barrier((value,) + others)[0]


def per_device(
    block_input, cotangent, span_offset, doc_lengths, ln1_gain, ln1_bias, w_query, w_key, w_value,
    query_bias, value_bias, w_out, out_bias, ln2_gain, ln2_bias, w_up, up_bias, w_down, down_bias,
):
    groups, ranks = lax.axis_size("seq"), lax.axis_size("mp")
    count = groups * ranks
    mp_index = lax.axis_index("mp")
    dev = lax.axis_index("seq") * ranks + mp_index
    rows = block_input.shape[1]
    tiles = rows // SPAN
    summaries = tiles * count
    shard = w_query.shape[0]
    bits = count.bit_length() - 1
    stages = [(b, b) for b in range(bits - 1, 2, -1)] + [(1, 2), (2, 1)]
    direct = shard == 64

    def swap(value, stage):
        pairs = [(i, i ^ (1 << stage[i & 1])) for i in range(count)]
        return lax.ppermute(value, AXES, pairs)

    def turn(value, by):
        return lax.ppermute(value, AXES, [(i, (i + by) % count) for i in range(count)])

    core = dev & 1
    slot = jnp.arange(count, dtype=jnp.int32)
    far = slot // (count // 2)
    mask = far
    for i, (even, odd) in enumerate(stages):
        where = jnp.where((core ^ far) == 0, even, odd)
        mask = mask | (((slot >> i) & 1) << where)
    owner = dev ^ mask
    if not direct:
        owner = slot
    member_slot = jnp.arange(16, dtype=jnp.int32)
    slots = owner[:, None] * tiles + (member_slot % 8)[None, :]
    valid = (member_slot % 8 <= tiles)[None, :]
    slots = jnp.stack(
        [
            jnp.where(valid & (member_slot // 8 == mi)[None, :], slots, -1).reshape(-1)
            for mi in range(2)
        ]
    )
    block_of, row_of = owner % ranks, owner // ranks
    facts = (jnp.stack((dev, mp_index)), span_offset, doc_lengths)

    def reach(value, flip):
        return lax.ppermute(value, AXES, [(i, i ^ flip) for i in range(count)])

    def spread(values):
        return [reach(value, flip) for value, flip in zip(values, (16, 8, 24))]

    def join(near, far):
        return jnp.concatenate((near, far), axis=0)

    def fold(keep, got):
        total = keep + got.astype(F32)
        half = total.shape[0] // 2
        return total[:half], total[half:].astype(BF16)

    def whole_blocks(arrays):
        return [pl.BlockSpec(a.shape, lambda i, n=len(a.shape): (0,) * n) for a in arrays]

    def fold_lines(keep, sent, got, sends=1):
        size = keep.shape[0]
        part = size // (1 + sends)
        outs = [shape((part, D), F32)] + [shape((part + (32 if sends == 1 else 16), D), BF16)] * sends
        mine = pl.BlockSpec((32, D), lambda i: (size // 32, 0))
        both = whole_blocks((keep, got))
        return call(fold_kernel, outs, [both[0], mine, both[1]], whole_blocks(outs), grid=(1,))(keep, sent, got)

    def gather_whole(value):
        both = lax.all_gather(value, "seq", axis=0, tiled=True)
        both = lax.all_gather(both, "mp", axis=0)
        return both[: ranks // 2], both[ranks // 2 :]

    def scatter_whole(keep, send):
        both = jnp.concatenate((keep, send), axis=0).astype(F32)
        total = lax.psum_scatter(both, "mp", scatter_dimension=0, tiled=True)[0]
        return lax.psum_scatter(total, "seq", scatter_dimension=0, tiled=True)

    def row(vector):
        return vector[None, :]

    def shape(dims, kind):
        return jax.ShapeDtypeStruct(dims, kind)

    half, tall = (count // 2, shard) if direct else (ranks // 2, shard * groups)
    width = 4 * LANES if direct else 3 * LANES
    apart = not direct
    wide, three = (2, rows, D), (2, rows, 3 * D)
    flat, pooled_dims = (2 * rows, D), (2, summaries, D)
    room = 12 if direct else 56
    masks = [pltpu.VMEM((tiles, SPAN + summaries, SPAN), F32)]

    def prepare():
        return call(
            prepare_kernel, [shape((1, max(shard, 64), D), BF16), shape((1, shard, 1152), BF16), shape((2, SPAN, D), BF16)],
            [SMEM] * 3 + [HBM] * 8, [VMEM] * 3,
            scratch=[pltpu.VMEM(wide, BF16), pltpu.SemaphoreType.DMA((11,))],
            limit=56,
        )(*facts, block_input, cotangent, w_query, w_key, w_value, w_out.T, w_up, w_down.T)

    part_a, w_rest, cot_edge = prepare()
    x_edge = block_input[:, rows - SPAN :]
    if direct:
        got_a = spread([part_a] * 3)
        part_b = tie(w_rest, got_a[0])
        got_b = swap(part_b, stages[0])
        part_a = jnp.concatenate([part_a] + got_a, axis=0)
        x_left = turn(tie(x_edge, part_a), 1)
        got_a = swap(part_a, stages[2])
        part_a = join(part_a, got_a)
        part_b = join(part_b, tie(got_b, part_a))
        got_a, got_b = swap(part_a, stages[3]), swap(part_b, stages[1])
        near_a = join(part_a, tie(got_a, x_left))
        far_a = swap(near_a, (0, 0))
        part_b = join(part_b, tie(got_b, near_a))
        got_b = swap(part_b, stages[2])
        more = ()
    else:
        x_left, cot_left = turn(x_edge, 1), turn(cot_edge, 1)
        near_a, far_a = gather_whole(part_a[0, :shard, :384])
        near_b, far_b = gather_whole(w_rest[0])
        near_1, near_2, far_1, far_2 = (a[:, :, i : i + w] for a in (near_b, far_b) for i, w in ((0, 640), (640, 512)))
        more = (lax.all_gather(part_a[0, :64, 384:], AXES, axis=0),)
        block_of, row_of = jnp.arange(ranks, dtype=jnp.int32), jnp.zeros((ranks,), jnp.int32)

    xs, qkv, skv, sums, w_full = call(
        partial(project_kernel, apart),
        [shape(wide, BF16), shape(three, BF16), shape((2, summaries, 3 * D), BF16), shape(pooled_dims, F32)]
        + [shape((D, 3 * D), BF16)],
        [SMEM] * 5 + [VMEM] * 7 + [ANY] * (2 + len(more)),
        scratch=[
            pltpu.VMEM((count, 64, LANES), BF16),
            pltpu.VMEM((rows + SPAN, D), F32),
            pltpu.VMEM((2, rows + 2 * summaries, D), BF16),
            pltpu.SemaphoreType.DMA((2,)),
        ],
        limit=24 if direct else 56,
    )(
        *facts, block_of, row_of, slots, block_input, x_left, row(ln1_gain), row(ln1_bias),
        row(query_bias), row(value_bias), near_a, far_a, *more,
    )
    outs = [shape(wide, BF16), shape((2, 4, tiles, 1, 2 * SPAN), F32)]
    if direct:
        cot_left = turn(tie(cot_edge, near_a), 1)
        part_b = join(part_b, tie(got_b, skv, cot_left))
        part_1, part_2 = part_b[:, :, :640], part_b[:, :, 640:]
        got_1 = swap(part_1, stages[3])
        qkv = tie(qkv, part_1)
    seen = call_row(attend_kernel, 0, facts, (qkv, skv), outs, (), masks, limit=room)
    att, lse = call_row(attend_kernel, 1, facts, (qkv, skv), outs, tuple(seen), masks, limit=room)
    if direct:
        near_1 = join(part_1, tie(got_1, att))
        far_1 = swap(near_1, (0, 0))
        got_2 = swap(tie(part_2, near_1), stages[3])
    tall_low, tall_float = shape(flat, BF16), shape(flat, F32)
    weights = [pltpu.VMEM((D, 2 * rows), BF16)] * 2 + [pltpu.VMEM((D, FF // 2), BF16)] * 4
    *kept, gub_1, down_b, keep_1, send_1 = call(
        mlp_first_kernel,
        [tall_float] + [tall_low] * 4 + [shape((D, D), BF16)]
        + [shape((1, FF // 2), F32), shape((1, D), F32)] + [shape((half, tall, 512), BF16)] * 2,
        [SMEM] * 4 + [VMEM] * 8 + [HBM] + [ANY] * 2,
        [VMEM] * 8 + [ANY] * 2,
        scratch=weights
        + [pltpu.VMEM((rows + SPAN, D), F32), pltpu.VMEM(wide, BF16)]
        + [pltpu.SemaphoreType.DMA((4,)), pltpu.SemaphoreType.DMA((2,))],
        limit=28,
    )(
        facts[0], span_offset, block_of, row_of, xs, att, cot_left, row(out_bias), row(ln2_gain), row(ln2_bias),
        row(up_bias), row(down_bias), cotangent, near_1, far_1,
    )
    if direct:
        near_2 = join(part_2, tie(got_2, kept[0]))
        far_2 = swap(near_2, (0, 0))
        got_1 = swap(tie(send_1, near_2), (0, 0))
        keep_1, send_1 = fold(keep_1.astype(F32), got_1)
        got_1 = swap(send_1, stages[3])
        near_2 = tie(near_2, send_1)
    result, gmid, gatt, small_b, gub_2, keep_2, send_2 = call(
        mlp_second_kernel,
        [shape(wide, BF16)] * 3 + [shape((8, D), F32)]
        + [shape((1, FF // 2), F32)] + [shape((half, tall, 640), BF16)] * 2,
        [SMEM] * 2 + [VMEM] * 9 + [ANY] * 2,
        [VMEM] * 5 + [ANY] * 2,
        scratch=weights
        + [pltpu.VMEM((D, D), BF16), pltpu.SemaphoreType.DMA((2,)), pltpu.SemaphoreType.DMA((3,))],
        limit=28,
    )(block_of, row_of, att, row(ln2_gain), row(up_bias), *kept, near_2, far_2)
    gubs = (gub_1, gub_2)
    arrays = (qkv, skv, lse, gatt)
    outs = [shape(three, BF16), shape((2, summaries, 3 * D), BF16)]
    if direct:
        keep_1, send_1 = fold(keep_1, tie(got_1, send_2))
        got_2 = swap(tie(send_2, send_1), (0, 0))
        got_1 = swap(send_1, stages[2])
    grads = call_row(attend_back_kernel, 0, facts, arrays, outs, (), masks, limit=room)
    if direct:
        keep_2, send_2 = fold(keep_2.astype(F32), tie(got_2, grads[0]))
        got_2 = swap(send_2, stages[3])
        grads = [tie(grads[0], send_2)] + list(grads[1:])
    grads = call_row(attend_back_kernel, 1, facts, arrays, outs, tuple(grads), masks, limit=room)
    if direct:
        keep_1, send_1 = fold(keep_1, tie(got_1, grads[0]))
        grads = [tie(grads[0], send_1), grads[1]]
    lines, keep_a, send_a, *more = call(
        partial(weights_back_kernel, apart),
        [shape((16, D), F32)]
        + [shape((half * tall, width), BF16), shape((half * tall + (32 if direct else 0), width), BF16)]
        + [shape((count, 64, LANES), BF16)] * apart,
        [SMEM] * 5 + [VMEM] * 12,
        [VMEM] + [ANY] * (2 + apart),
        scratch=[
            pltpu.VMEM((D, 3 * D), BF16), pltpu.VMEM(pooled_dims, BF16), pltpu.VMEM((count, 64, LANES), BF16),
            pltpu.VMEM((32, D), BF16), pltpu.SemaphoreType.DMA((3,)),
        ],
        limit=24 if direct else 56,
    )(
        *facts, block_of, row_of, slots, xs, *grads, sums, w_full, row(ln1_gain), row(ln1_bias), small_b, down_b, *gubs,
    )

    def by_row(dims):
        return pl.BlockSpec((1,) + dims[1:], lambda i: (i,) + (0,) * (len(dims) - 1))

    once = pl.BlockSpec((1, D), lambda i: (0, 0))
    edge_dims = (2, SPAN, D)

    def rows_back(*after):
        return call(
            rows_back_kernel, [shape(wide, F32), shape((2,) + edge_dims, BF16)],
            [by_row(three), pl.BlockSpec((D, 3 * D), lambda i: (0, 0)), by_row(wide), by_row(wide)]
            + [by_row(edge_dims), once],
            [by_row(wide), pl.BlockSpec((2, 1, SPAN, D), lambda i: (0, i, 0, 0))], grid=(2,), limit=16,
        )(grads[0], tie(w_full, *after), xs, gmid, result, row(ln1_gain))

    def unroll(back):
        return call(
            unroll_kernel, [shape(wide, BF16)] * 2 + [shape((2, rows, LANES), F32)],
            [SMEM, by_row(wide), pl.BlockSpec((1, 1, SPAN, D), lambda i: (1, i, 0, 0)), by_row(wide)], [by_row(wide)] * 2 + [by_row((2, rows, LANES))],
            [pltpu.VMEM((2 * SPAN, D), F32)], grid=(2,),
        )(span_offset, result, back, block_input)

    final = [SMEM] * 3 + [VMEM] * 5
    rolled = [pltpu.VMEM((2 * SPAN, D), F32)]
    if direct:
        got_a = swap(send_a, (0, 0))
        keep_2, send_2 = fold(keep_2, tie(got_2, send_a))
        got_2 = swap(send_2, stages[2])
        keep_a, send_a = fold_lines(keep_a, send_a, tie(got_a, send_2))
        got_a = swap(send_a, stages[3])
        part, edge = rows_back(send_a)
        keep_2, send_2 = fold(keep_2, tie(got_2, part))
        keep_b, send_b = (jnp.concatenate(a, axis=2) for a in ((keep_1, keep_2), (send_1, send_2)))
        got_b = swap(send_b, stages[1])
        back = turn(tie(edge, send_b), -1)
        keep_a, send_a = fold_lines(keep_a, send_a, tie(got_a, send_b))
        got_a = swap(send_a, stages[2])
        keep_b, send_b = fold(keep_b, tie(got_b, send_a))
        got_b = swap(send_b, stages[0])
        keep_a, *send_a = fold_lines(keep_a, send_a, tie(got_a, send_b), 3)
        got_a = spread(send_a)
        result_own, *hats = unroll(tie(back, send_a[0]))
        grad_wo, grad_wu, grad_wd = call(
            finish_rest_kernel, [shape((shard, LANES), F32), shape((shard, 512), F32), shape((shard, 512), F32)],
            [VMEM] * 2,
        )(keep_b, tie(got_b, send_a[0]))
        input_grad, grad_wq, grad_wk, grad_wv, grad_ub, *small = call(
            partial(finish_kernel, True),
            [shape(wide, F32)] + [shape((shard, LANES), F32)] * 3 + [shape((1, FF), F32)] + [shape((1, D), F32)] * 8,
            final + [VMEM] * 5, scratch=rolled, limit=16,
        )(*facts, *hats, part, back, row(ln1_gain), keep_a, send_a[0], *(tie(got, grad_wo) for got in got_a))
        grad_wo, grad_wd = grad_wo.T, grad_wd.T
        small = [a.reshape(D) for a in small]
        grad_ub = grad_ub.reshape(FF)
    else:
        keep_a, send_a = (a.reshape(half, tall, width) for a in (keep_a, send_a))
        part, edge = rows_back()
        back = turn(edge, -1)
        result_own, *hats = unroll(back)
        sum_a, sum_1, sum_2 = (scatter_whole(*a) for a in ((keep_a, send_a), (keep_1, send_1), (keep_2, send_2)))
        grad_wq, grad_wk, grad_wv = (sum_a[:, i : i + LANES] for i in (0, 128, 256))
        grad_wo = sum_2[:, 512:].T
        grad_wu, grad_wd = (
            jnp.concatenate((sum_1[:, i : i + 256], sum_2[:, i : i + 256]), axis=1) for i in (0, 256)
        )
        grad_wd = grad_wd.T
        pooled = lax.psum_scatter(more[0].astype(F32), AXES, scatter_dimension=0, tiled=True)[0]
        lines = lax.psum(lines, AXES)
        grad_ub = lines[4:8].reshape(FF)
        small = [lines[i] for i in (0, 1, 2, 3, 8, 9, 10, 11)]
        input_grad = call(partial(finish_kernel, False), [shape(wide, F32)], final + [VMEM], scratch=rolled, limit=16)(
            *facts, *hats, part, back, row(ln1_gain), pooled
        )[0]
    grad_gain_two, grad_shift_two, grad_obias, grad_dbias, grad_gain_one, grad_shift_one, grad_qb, grad_vb = small
    return (
        result_own,
        input_grad,
        grad_gain_one,
        grad_shift_one,
        grad_wq,
        grad_wk,
        grad_wv,
        grad_qb,
        grad_vb,
        grad_wo,
        grad_obias,
        grad_gain_two,
        grad_shift_two,
        grad_wu,
        grad_ub,
        grad_wd,
        grad_dbias,
    )


def solution(mesh):
    vector, matrix, turned = P(), P("seq", "mp"), P("mp", "seq")
    own, group = P(None, ("seq", "mp"), None), P(None, "seq", None)
    return jax.shard_map(
        per_device,
        mesh=mesh,
        in_specs=(own, group, vector, vector, vector, vector, matrix, matrix, matrix, vector, vector)
        + (turned, vector, vector, vector, matrix, vector, turned, vector),
        out_specs=(own, own, vector, vector, matrix, matrix, matrix, vector, vector, turned, vector)
        + (vector, vector, matrix, vector, turned, vector),
        check_vma=False,
    )
```

```python
from functools import partial
import math

import jax
import jax.numpy as jnp
from jax import lax
from jax.experimental import pallas as pl
from jax.experimental.pallas import tpu as pltpu
from jax.sharding import PartitionSpec as P

D = 512
FF = 2048
HEAD_DIM = 64
SPAN = 128
LANES = 128
STEP = 256
EPSILON = 1e-05
NEGATIVE = -1e30
SCALE = 1.0 / math.sqrt(HEAD_DIM)
F32 = jnp.float32
BF16 = jnp.bfloat16
AXES = ("seq", "mp")
MIB = 1 << 20
VMEM = pl.BlockSpec(memory_space=pltpu.VMEM)
SMEM = pl.BlockSpec(memory_space=pltpu.SMEM)
ANY = pl.BlockSpec(memory_space=pl.ANY)
HBM = pl.BlockSpec(memory_space=pltpu.HBM)


def dot(left, right):
    return lax.dot_general(left, right, (((1,), (0,)), ((), ())), preferred_element_type=F32)


def dot_cols(left, right):
    return lax.dot_general(left, right, (((1,), (1,)), ((), ())), preferred_element_type=F32)


def unit(rows):
    centred = rows - jnp.mean(rows, axis=-1, keepdims=True)
    inverse = lax.rsqrt(jnp.mean(centred * centred, axis=-1, keepdims=True) + EPSILON)
    return centred * inverse, inverse


def unit_back(grad, hat, inverse):
    shift = jnp.mean(grad, axis=-1, keepdims=True)
    slope = jnp.mean(grad * hat, axis=-1, keepdims=True)
    return (grad - shift - hat * slope) * inverse


def row_info(place, offsets, lengths, mi):
    ends = []
    for c in range(lengths.shape[1]):
        ends.append(lengths[mi, c] + (ends[-1] if ends else 0))
    return place[0], offsets[mi], ends


def doc_start(positions, ends):
    start = jnp.zeros_like(positions)
    for end in ends:
        start = jnp.where(positions >= end, end, start)
    return start


def summary_range(summary_ids, offset, ends):
    last = offset - 1 + SPAN * summary_ids
    first = jnp.maximum(doc_start(last, ends), last - (SPAN - 1))
    return first, last


def iota(shape, dim):
    return lax.broadcasted_iota(jnp.int32, shape, dim)


def roll_rows(ref, by):
    whole = pl.multiple_of((by // 8) * 8, 8)
    return pltpu.roll(ref[pl.ds(whole, SPAN + 8), :], SPAN + 8 - (by - whole), axis=0)[:SPAN]


def prepare_kernel(
    place, offsets, lengths, x_ref, cot_ref, wq_ref, wk_ref, wv_ref, wo_ref, wu_ref, wd_ref,
    out_ref, rest_ref, edge_ref, rows_ref, sem
):
    rows = x_ref.shape[1]
    last_rows = pl.multiple_of(place[1] * rows + (rows - SPAN), SPAN)
    shard = wq_ref.shape[0]
    copies = [pltpu.make_async_copy(x_ref.at[mi], rows_ref.at[mi], sem.at[mi]) for mi in range(2)]
    copies += [
        pltpu.make_async_copy(ref, out_ref.at[0, 0:shard, i * LANES : (i + 1) * LANES], sem.at[2 + i])
        for i, ref in enumerate((wq_ref, wk_ref, wv_ref))
    ]
    copies.append(pltpu.make_async_copy(cot_ref.at[:, pl.ds(last_rows, SPAN), :], edge_ref, sem.at[5]))
    copies.append(pltpu.make_async_copy(wo_ref, rest_ref.at[0, :, 0:128], sem.at[6]))
    for i, (ref, first) in enumerate(((wu_ref, 0), (wd_ref, 0), (wu_ref, 256), (wd_ref, 256))):
        target = rest_ref.at[0, :, 128 + 256 * i : 384 + 256 * i]
        copies.append(pltpu.make_async_copy(ref.at[:, first : first + 256], target, sem.at[7 + i]))
    for copy in copies:
        copy.start()
    sums = []
    for mi in range(2):
        dev, offset, ends = row_info(place, offsets, lengths, mi)
        first, last = summary_range(dev * (rows // SPAN) + iota((8, 1), 0), offset, ends)
        pos = dev * rows + iota((1, rows), 1)
        member = jnp.where((pos >= first) & (pos <= last), 1.0, 0.0).astype(BF16)
        copies[mi].wait()
        hat, _ = unit(rows_ref[mi].astype(F32))
        high = hat.astype(BF16)
        rest = (hat - high.astype(F32)).astype(BF16)
        total = dot(member, high) + dot(member, rest)
        sums.append(total * lax.rsqrt((last - first + 1).astype(F32)))
    both = jnp.concatenate(sums, axis=0).astype(BF16)
    for copy in copies[2:]:
        copy.wait()
    for lane in range(D // LANES):
        out_ref[0, 16 * lane : 16 * lane + 16, 384:512] = both[:, lane * LANES : (lane + 1) * LANES]


def fill_masks(place, offsets, lengths, mi, bias_ref, tiles, summaries, length):
    dev, offset, ends = row_info(place, offsets, lengths, mi)
    ends_col = offset - 1 + SPAN * iota((summaries, 1), 0)
    for t in range(tiles):
        base = SPAN * (dev * tiles + t) + offset - SPAN
        qpos = base + iota((1, SPAN), 1)
        qpos = jnp.where(qpos < 0, qpos + length, qpos)
        kpos = base + iota((SPAN, 1), 0)
        kpos = jnp.where(kpos < 0, kpos + length, kpos)
        span_first = jnp.where(qpos >= base + SPAN, base + length, base)
        doc_first = doc_start(qpos, ends)
        local_ok = (kpos >= jnp.maximum(doc_first, span_first)) & (kpos <= qpos)
        summary_ok = (ends_col >= doc_first) & (ends_col < span_first)
        bias_ref[t, 0:SPAN, :] = jnp.where(local_ok, 0.0, NEGATIVE)
        bias_ref[t, SPAN : SPAN + summaries, :] = jnp.where(summary_ok, 0.0, NEGATIVE)


def split_heads(pair):
    low = iota(pair.shape, 1) < HEAD_DIM
    zero = jnp.zeros_like(pair)
    return jnp.concatenate((jnp.where(low, pair, zero), jnp.where(low, zero, pair)), axis=0)


def join_heads(turned):
    half = turned.shape[1] // 2
    return jnp.concatenate((turned[:HEAD_DIM, :half], turned[HEAD_DIM:, half:]), axis=0).T


def project_kernel(
    apart, place_ref, offsets, lengths, block_of, row_of, slots_ref, x_ref, left_ref, gain, shift, qbias, vbias,
    near_ref, far_ref, *refs
):
    if apart:
        all_ref, *refs = refs
    xs_ref, qkv_ref, skv_ref, sums_ref, w_ref, stack_ref, wide_ref, rows_ref, sem = refs
    rows = x_ref.shape[1]
    tiles = rows // SPAN
    summaries = skv_ref.shape[1]
    half, shard, _ = near_ref.shape

    def place(d, carry):
        for source, slot in ((near_ref, d), (far_ref, half + d)):
            here = pl.ds(pl.multiple_of(row_of[slot] * shard, 16), shard)
            cols = pl.ds(pl.multiple_of(block_of[slot] * 384, 128), 384)
            pltpu.make_async_copy(source.at[d, :, 0:384], w_ref.at[here, cols], sem.at[0]).start()
            if not apart:
                pltpu.make_async_copy(
                    source.at[d, 0:64, 384:512], stack_ref.at[slot], sem.at[1]
                ).start()
        return carry

    lax.fori_loop(0, half, place, 0)
    if apart:
        pltpu.make_async_copy(all_ref, stack_ref, sem.at[1]).start()
    for mi in range(2):
        wide_ref[0:SPAN, :] = left_ref[mi].astype(F32)
        wide_ref[SPAN : SPAN + rows, :] = x_ref[mi].astype(F32)
        for t in range(tiles):
            here = slice(t * SPAN, (t + 1) * SPAN)
            rolled = roll_rows(wide_ref, t * SPAN + offsets[mi])
            xs_ref[mi, here, :] = rolled.astype(BF16)
            hat, _ = unit(rolled)
            rows_ref[mi, here, :] = (hat * gain[...] + shift[...]).astype(BF16)
    pltpu.make_async_copy(stack_ref, stack_ref, sem.at[1]).wait()
    roots = []
    for mi in range(2):
        _, offset, ends = row_info(place_ref, offsets, lengths, mi)
        first, last = summary_range(iota((summaries, 1), 0), offset, ends)
        root = jnp.sqrt((last - first + 1).astype(F32))
        roots.append(root)
        for base in range(0, stack_ref.shape[0], 32):
            named = slots_ref[mi : mi + 1, 16 * base : 16 * base + 512]
            pick = jnp.where(iota((summaries, 1), 0) == named, 1.0, 0.0).astype(BF16)
            piece = jnp.concatenate(
                [
                    stack_ref[base : base + 32, 16 * lane : 16 * lane + 16, :].reshape(512, LANES)
                    for lane in range(D // LANES)
                ],
                axis=1,
            )
            found = dot(pick, piece)
            sums_ref[mi] = found if base == 0 else sums_ref[mi] + found
        summed = sums_ref[mi] * gain[...] + root * shift[...]
        high = summed.astype(BF16)
        rows_ref[mi, rows : rows + summaries, :] = high
        rows_ref[mi, rows + summaries : rows + 2 * summaries, :] = (summed - high.astype(F32)).astype(BF16)
    pltpu.make_async_copy(w_ref, w_ref, sem.at[0]).wait()
    none = jnp.zeros((1, LANES), F32)
    for m in range(4):
        lanes = slice(m * LANES, (m + 1) * LANES)
        cols = slice(m * 384, (m + 1) * 384)
        bias = jnp.concatenate((qbias[:, lanes], none, vbias[:, lanes]), axis=1)
        for mi in range(2):
            projected = dot(rows_ref[mi], w_ref[:, cols])
            qkv_ref[mi, :, cols] = (projected[:rows] + bias).astype(BF16)
            pooled = projected[rows : rows + summaries] + projected[rows + summaries :]
            skv_ref[mi, :, cols] = (pooled + roots[mi] * bias).astype(BF16)


def pair_of(ref, here, pair):
    def part(i):
        return ref[0, here, pl.ds(pl.multiple_of(pair * 384 + i * LANES, LANES), LANES)]

    return part(0), part(1), part(2)


def attend_kernel(mi, place, offsets, lengths, qkv_ref, skv_ref, *refs):
    att_ref, lse_ref, bias_ref = refs[-3:]
    rows = qkv_ref.shape[1]
    tiles = rows // SPAN
    summaries = skv_ref.shape[1]
    fill_masks(place, offsets, lengths, mi, bias_ref, tiles, summaries, summaries * SPAN)

    def heads(pair, carry):
        lanes = pl.ds(pl.multiple_of(pair * LANES, LANES), LANES)
        _, skeys, svalues = pair_of(skv_ref, slice(None), pair)
        svalues = svalues.T
        spans = [pair_of(qkv_ref, slice(t * SPAN, (t + 1) * SPAN), pair) for t in range(tiles)]
        scores = []
        for t, (queries, keys, _) in enumerate(spans):
            bias = bias_ref[t]
            keys = jnp.concatenate((keys, skeys), axis=0)
            scores.append(dot_cols(keys, split_heads(queries * SCALE)) + jnp.concatenate((bias, bias), axis=1))
        probs = []
        for t in range(tiles):
            top = jnp.max(scores[t], axis=0, keepdims=True)
            grown = jnp.exp(scores[t] - top)
            total = jnp.sum(grown, axis=0, keepdims=True)
            probs.append((grown * (1.0 / total)).astype(BF16))
            lse_ref[0, pair, t] = top + jnp.log(total)
        for t, (_, _, values) in enumerate(spans):
            values = jnp.concatenate((values.T, svalues), axis=1)
            att_ref[0, t * SPAN : (t + 1) * SPAN, lanes] = join_heads(dot(values, probs[t])).astype(BF16)
        return carry

    lax.fori_loop(0, 4, heads, 0)


def gelu_pair(u):
    c0 = math.sqrt(2.0 / math.pi)
    square = u * u
    t = jnp.tanh(c0 * u * (1.0 + 0.044715 * square))
    half = 0.5 * (1.0 + t)
    slope = half + (0.5 * c0) * u * (1.0 - t * t) * (1.0 + (3 * 0.044715) * square)
    return u * half, slope


def columns(block, width):
    return pl.ds(pl.multiple_of(block * width, 128), width)


def mlp_half(half_id, ubias, n_ref, c_ref, nt_ref, ct_ref, wu_ref, wd_ref, gu_ref, gd_ref, gub_ref, act_ref, grad_ref, add):
    bias = jnp.concatenate([ubias[:, m * 512 + half_id * 256 : m * 512 + half_id * 256 + 256] for m in range(4)], axis=1)
    step = STEP
    gub_ref[...] = jnp.zeros_like(gub_ref)

    def block(r, carry):
        here = pl.ds(pl.multiple_of(r * step, step), step)
        w_up, w_down = wu_ref[...], wd_ref[...]
        act, slope = gelu_pair(dot(n_ref[here, :], w_up) + bias)
        act = act.astype(BF16)
        grad = dot(c_ref[here, :], w_down) * slope
        gub_ref[...] += jnp.sum(grad, axis=0, keepdims=True)
        grad = grad.astype(BF16)
        act_ref[here, :] = act
        grad_ref[here, :] = grad
        add(r, here, dot_cols(act, w_down), dot_cols(grad, w_up))
        return carry

    lax.fori_loop(0, n_ref.shape[0] // step, block, 0)
    gu_ref[...] = dot(nt_ref[...], grad_ref[...]).astype(BF16)
    gd_ref[...] = dot(ct_ref[...], act_ref[...]).astype(BF16)


def pull(block_of, row_of, near_ref, far_ref, parts):
    half, shard, _ = near_ref.shape

    def body(d, carry):
        for source, slot in ((near_ref, d), (far_ref, half + d)):
            here = pl.ds(pl.multiple_of(row_of[slot] * shard, 16), shard)
            for target, first, width, sem in parts:
                pltpu.make_async_copy(
                    source.at[d, :, first : first + width], target.at[here, columns(block_of[slot], width)], sem
                ).start()
        return carry

    lax.fori_loop(0, half, body, 0)


def push(block_of, row_of, keep_ref, send_ref, parts):
    half, shard, _ = keep_ref.shape

    def body(d, carry):
        for target, slot in ((keep_ref, d), (send_ref, half + d)):
            here = pl.ds(pl.multiple_of(row_of[slot] * shard, 16), shard)
            for source, first, width, sem in parts:
                pltpu.make_async_copy(
                    source.at[here, columns(block_of[slot], width)], target.at[d, :, first : first + width], sem
                ).start()
        return carry

    lax.fori_loop(0, half, body, 0)


def mlp_first_kernel(
    place_ref, offsets, block_of, row_of, xs_ref, att_ref, left_ref, obias, gain, shift, ubias, dbias, cot_ref,
    near_ref, far_ref,
    resid_ref, acc_ref, gn_ref, n_ref, c_ref, wo_ref, gub_ref, down_ref, keep_ref, send_ref,
    nt_ref, ct_ref, wu_ref, wd_ref, gu_ref, gd_ref, act_ref, grad_ref, wide_ref, low_ref, sem, out_sem,
):
    rows = xs_ref.shape[1]
    own = pl.ds(pl.multiple_of(place_ref[1] * rows, SPAN), rows)
    own_copy = pltpu.make_async_copy(cot_ref.at[:, own, :], low_ref, sem.at[3])
    own_copy.start()
    pull(block_of, row_of, near_ref, far_ref, ((wo_ref, 0, 128, sem.at[0]),))
    pull(block_of, row_of, near_ref, far_ref, ((wu_ref, 128, 256, sem.at[1]), (wd_ref, 384, 256, sem.at[2])))
    down_ref[...] = jnp.zeros_like(down_ref)
    own_copy.wait()
    pltpu.make_async_copy(wo_ref, wo_ref, sem.at[0]).wait()
    for mi in range(2):
        all_rows = slice(mi * rows, (mi + 1) * rows)
        wide_ref[0:SPAN, :] = left_ref[mi].astype(F32)
        wide_ref[SPAN : SPAN + rows, :] = low_ref[mi].astype(F32)
        for t in range(rows // SPAN):
            rolled = roll_rows(wide_ref, t * SPAN + offsets[mi])
            down_ref[...] += jnp.sum(rolled, axis=0, keepdims=True)
            c_ref[mi * rows + t * SPAN : mi * rows + (t + 1) * SPAN, :] = rolled.astype(BF16)
        resid = xs_ref[mi].astype(F32) + dot_cols(att_ref[mi], wo_ref[...]) + obias[...]
        resid_ref[all_rows, :] = resid
        hat, _ = unit(resid)
        normed = (hat * gain[...] + shift[...]).astype(BF16)
        n_ref[all_rows, :] = normed
        nt_ref[:, all_rows] = normed.T
        ct_ref[:, all_rows] = c_ref[all_rows, :].T
    pltpu.make_async_copy(wu_ref, wu_ref, sem.at[1]).wait()
    pltpu.make_async_copy(wd_ref, wd_ref, sem.at[2]).wait()

    def add(r, here, down, back):
        acc_ref[here, :] = (down + dbias[...]).astype(BF16)
        gn_ref[here, :] = back.astype(BF16)

    mlp_half(
        0, ubias, n_ref, c_ref, nt_ref, ct_ref, wu_ref, wd_ref, gu_ref, gd_ref, gub_ref, act_ref, grad_ref, add
    )
    push(block_of, row_of, keep_ref, send_ref, ((gu_ref, 0, 256, out_sem.at[0]), (gd_ref, 256, 256, out_sem.at[1])))
    pltpu.make_async_copy(gu_ref, gu_ref, out_sem.at[0]).wait()
    pltpu.make_async_copy(gd_ref, gd_ref, out_sem.at[1]).wait()


def mlp_second_kernel(
    block_of, row_of, att_ref, gain, ubias, resid_ref, acc_ref, gn_ref, n_ref, c_ref, wo_ref,
    near_ref, far_ref,
    result_ref, gmid_ref, gatt_ref, small_ref, gub_ref, keep_ref, send_ref,
    nt_ref, ct_ref, wu_ref, wd_ref, gu_ref, gd_ref, act_ref, grad_ref, go_ref, turned_ref, sem, out_sem,
):
    rows = att_ref.shape[1]
    pull(block_of, row_of, near_ref, far_ref, ((wu_ref, 0, 256, sem.at[0]), (wd_ref, 256, 256, sem.at[1])))
    small_ref[...] = jnp.zeros_like(small_ref)
    for mi in range(2):
        here = slice(mi * rows, (mi + 1) * rows)
        nt_ref[:, here] = n_ref[here, :].T
        ct_ref[:, here] = c_ref[here, :].T
    pltpu.make_async_copy(wu_ref, wu_ref, sem.at[0]).wait()
    pltpu.make_async_copy(wd_ref, wd_ref, sem.at[1]).wait()

    def add(r, here, down, back):
        mi = r // (rows // STEP)
        own = pl.ds(pl.multiple_of((r % (rows // STEP)) * STEP, STEP), STEP)
        result_ref[mi, own, :] = (resid_ref[here, :] + (acc_ref[here, :].astype(F32) + down)).astype(BF16)
        hat, inverse = unit(resid_ref[here, :])
        grad = gn_ref[here, :].astype(F32) + back
        small_ref[0:1, :] += jnp.sum(grad * hat, axis=0, keepdims=True)
        small_ref[1:2, :] += jnp.sum(grad, axis=0, keepdims=True)
        branch = (c_ref[here, :].astype(F32) + unit_back(grad * gain[...], hat, inverse)).astype(BF16)
        gmid_ref[mi, own, :] = branch
        small_ref[2:3, :] += jnp.sum(branch.astype(F32), axis=0, keepdims=True)
        gatt_ref[mi, own, :] = dot(branch, wo_ref[...]).astype(BF16)
        turned_ref[:, here] = branch.T

    mlp_half(
        1, ubias, n_ref, c_ref, nt_ref, ct_ref, wu_ref, wd_ref, gu_ref, gd_ref, gub_ref, act_ref, grad_ref, add
    )
    push(block_of, row_of, keep_ref, send_ref, ((gu_ref, 0, 256, out_sem.at[0]), (gd_ref, 256, 256, out_sem.at[1])))
    both = jnp.concatenate((att_ref[0], att_ref[1]), axis=0)
    go_ref[...] = dot(turned_ref[...], both).astype(BF16)
    push(block_of, row_of, keep_ref, send_ref, ((go_ref, 512, 128, out_sem.at[2]),))
    pltpu.make_async_copy(gu_ref, gu_ref, out_sem.at[0]).wait()
    pltpu.make_async_copy(gd_ref, gd_ref, out_sem.at[1]).wait()
    pltpu.make_async_copy(go_ref, go_ref, out_sem.at[2]).wait()


def attend_back_kernel(mi, place, offsets, lengths, qkv_ref, skv_ref, lse_ref, gatt_ref, *refs):
    grad_ref, pooled_ref, bias_ref = refs[-3:]
    rows = qkv_ref.shape[1]
    tiles = rows // SPAN
    summaries = skv_ref.shape[1]
    fill_masks(place, offsets, lengths, mi, bias_ref, tiles, summaries, summaries * SPAN)

    def heads(pair, carry):
        lanes = pl.ds(pl.multiple_of(pair * LANES, LANES), LANES)

        def columns(i):
            return pl.ds(pl.multiple_of(pair * 384 + i * LANES, LANES), LANES)

        _, skeys, svalues = pair_of(skv_ref, slice(None), pair)
        skeys_t = skeys.T
        sum_k = jnp.zeros((summaries, LANES), F32)
        sum_v = jnp.zeros((summaries, LANES), F32)
        held = []
        for t in range(tiles):
            here = slice(t * SPAN, (t + 1) * SPAN)
            queries, keys, values = pair_of(qkv_ref, here, pair)
            queries = split_heads(queries * SCALE)
            grads = split_heads(gatt_ref[0, here, lanes])
            bias = bias_ref[t]
            scores = dot_cols(jnp.concatenate((keys, skeys), axis=0), queries)
            gprobs = dot_cols(jnp.concatenate((values, svalues), axis=0), grads)
            held.append((queries, keys, grads, scores + jnp.concatenate((bias, bias), axis=1), gprobs))
        for t, (queries, keys, grads, scores, gprobs) in enumerate(held):
            here = slice(t * SPAN, (t + 1) * SPAN)
            probs = jnp.exp(scores - lse_ref[0, pair, t])
            delta = jnp.sum(probs * gprobs, axis=0, keepdims=True)
            gscores = (probs * (gprobs - delta)).astype(BF16)
            keys_t = jnp.concatenate((keys.T, skeys_t), axis=1)
            grad_q = join_heads(dot(keys_t, gscores)) * SCALE
            grad_k = dot(gscores, queries)
            grad_v = dot(probs.astype(BF16), grads)
            grad_ref[0, here, columns(0)] = grad_q.astype(BF16)
            grad_ref[0, here, columns(1)] = grad_k[:SPAN].astype(BF16)
            grad_ref[0, here, columns(2)] = grad_v[:SPAN].astype(BF16)
            sum_k += grad_k[SPAN:]
            sum_v += grad_v[SPAN:]
        pooled_ref[0, :, columns(0)] = jnp.zeros((summaries, LANES), BF16)
        pooled_ref[0, :, columns(1)] = sum_k.astype(BF16)
        pooled_ref[0, :, columns(2)] = sum_v.astype(BF16)
        return carry

    lax.fori_loop(0, 4, heads, 0)


def weights_back_kernel(
    apart, place, offsets, lengths, block_of, row_of, slots_ref, xs_ref, grad_ref, pooled_ref, sums_ref, w_ref,
    gain, shift, small_ref, down_ref, gub1_ref, gub2_ref, line_ref, keep_ref, send_ref, *refs
):
    if apart:
        all_ref, *refs = refs
    gwb_ref, back_ref, stack_ref, pad_ref, sem = refs
    rows = xs_ref.shape[1]
    summaries = pooled_ref.shape[1]
    half = block_of.shape[0] // 2
    shard = keep_ref.shape[0] // half
    turned = []
    column = jnp.zeros((1, 3 * D), F32)
    for mi in range(2):
        _, offset, ends = row_info(place, offsets, lengths, mi)
        first, last = summary_range(iota((summaries, 1), 0), offset, ends)
        root = jnp.sqrt((last - first + 1).astype(F32))
        hat, _ = unit(xs_ref[mi].astype(F32))
        turned += [hat.astype(BF16).T, sums_ref[mi].astype(BF16).T]
        column += jnp.sum(grad_ref[mi].astype(F32), axis=0, keepdims=True)
        column += jnp.sum(root * pooled_ref[mi].astype(F32), axis=0, keepdims=True)
        back_ref[mi] = dot_cols(pooled_ref[mi], w_ref[...]).astype(BF16)
    turned = jnp.concatenate(turned, axis=1)
    gain_col, shift_col = gain[...].T, shift[...].T
    grad_gain = jnp.zeros((D, 1), F32)
    grad_shift = jnp.zeros((D, 1), F32)
    for m in range(4):
        cols = slice(m * 384, (m + 1) * 384)
        lanes = slice(m * LANES, (m + 1) * LANES)
        grads = jnp.concatenate([ref[mi, :, cols] for mi in range(2) for ref in (grad_ref, pooled_ref)], axis=0)
        hats, w, sums = dot(turned, grads), w_ref[:, cols].astype(F32), column[:, cols]
        grad_gain += jnp.sum(hats * w, axis=1, keepdims=True)
        grad_shift += jnp.sum(sums * w, axis=1, keepdims=True)
        gwb_ref[:, cols] = (hats * gain_col + shift_col * sums).astype(BF16)
        line_ref[10:11, lanes] = sums[:, :128]
        line_ref[11:12, lanes] = sums[:, 256:]
    line_ref[8:9, :] = grad_gain.T
    line_ref[9:10, :] = grad_shift.T
    line_ref[0:3, :] = small_ref[0:3, :]
    line_ref[3:4, :] = down_ref[...]
    for i in range(4):
        for j, ref in enumerate((gub1_ref, gub2_ref)):
            line_ref[4 + i : 5 + i, j * 256 : (j + 1) * 256] = ref[:, i * 256 : (i + 1) * 256]
    line_ref[12:16, :] = jnp.zeros((4, D), F32)
    for base in range(0, stack_ref.shape[0], 32):
        names = [slots_ref[mi : mi + 1, 16 * base : 16 * base + 512] for mi in range(2)]
        spread = [
            jnp.where(iota((summaries, 1), 0) == named, 1.0, 0.0).astype(BF16).T for named in names
        ]
        piece = (dot(spread[0], back_ref[0]) + dot(spread[1], back_ref[1])).astype(BF16)
        for lane in range(D // LANES):
            part = piece[:, lane * LANES : (lane + 1) * LANES]
            stack_ref[base : base + 32, 16 * lane : 16 * lane + 16, :] = part.reshape(32, 16, LANES)

    def emit(d, carry):
        for target, slot in ((keep_ref, d), (send_ref, half + d)):
            first_row = pl.multiple_of(row_of[slot] * shard, 16)
            cols = pl.ds(pl.multiple_of(block_of[slot] * 384, 128), 384)
            here = target.at[pl.ds(pl.multiple_of(d * shard, 16), shard), :]
            pltpu.make_async_copy(
                gwb_ref.at[pl.ds(first_row, shard), cols], here.at[:, 0:384], sem.at[0]
            ).start()
            if not apart:
                pltpu.make_async_copy(stack_ref.at[slot], here.at[:, 384:512], sem.at[1]).start()
        return carry

    lax.fori_loop(0, half, emit, 0)
    if apart:
        pltpu.make_async_copy(stack_ref, all_ref, sem.at[1]).start()
    else:
        high = line_ref[...].astype(BF16)
        pad_ref[0:16, :] = high
        pad_ref[16:32, :] = (line_ref[...] - high.astype(F32)).astype(BF16)
        size = half * shard
        copy = pltpu.make_async_copy(pad_ref, send_ref.at[size : size + 32, :], sem.at[2])
        copy.start()
        copy.wait()
    pltpu.make_async_copy(gwb_ref, gwb_ref, sem.at[0]).wait()
    pltpu.make_async_copy(stack_ref, stack_ref, sem.at[1]).wait()


def rows_back_kernel(grad_ref, w_ref, xs_ref, gmid_ref, result_ref, gain, part_ref, edge_ref):
    grad = dot_cols(grad_ref[0], w_ref[...]) * gain[...]
    hat, inverse = unit(xs_ref[0].astype(F32))
    part = gmid_ref[0].astype(F32) + unit_back(grad, hat, inverse)
    part_ref[0] = part
    edge_ref[0, 0] = part[0:SPAN].astype(BF16)
    edge_ref[1, 0] = result_ref[0]


def fold_kernel(keep_ref, mine_ref, got_ref, next_ref, *send_refs):
    size = keep_ref.shape[0]
    part = size // (1 + len(send_refs))
    mine = mine_ref[0:16, :].astype(F32) + mine_ref[16:32, :].astype(F32)
    lines = mine + (got_ref[size : size + 16, :].astype(F32) + got_ref[size + 16 : size + 32, :].astype(F32))
    high = lines.astype(BF16)
    rest = (lines - high.astype(F32)).astype(BF16)
    next_ref[...] = keep_ref[0:part, :].astype(F32) + got_ref[0:part, :].astype(F32)
    for i, send_ref in enumerate(send_refs):
        here = slice((i + 1) * part, (i + 2) * part)
        send_ref[0:part, :] = (keep_ref[here, :].astype(F32) + got_ref[here, :].astype(F32)).astype(BF16)
        send_ref[part : part + 16, :] = high
        if len(send_refs) == 1:
            send_ref[part + 16 : part + 32, :] = rest


def lines_of(ref):
    return ref[ref.shape[0] - 16 :, :].astype(F32)


def two_tiles(ref, right, mi, t):
    if (t + 2) * SPAN <= ref.shape[1]:
        return ref[mi, t * SPAN : (t + 2) * SPAN, :]
    return jnp.concatenate((ref[mi, t * SPAN :, :], right[mi].astype(ref.dtype)), axis=0)


def unroll_kernel(offsets, result_ref, right_ref, x_ref, out_ref, hat_ref, inverse_ref, wide_ref):
    mi = pl.program_id(0)
    for t in range(result_ref.shape[1] // SPAN):
        here = slice(t * SPAN, (t + 1) * SPAN)
        wide_ref[...] = two_tiles(result_ref, right_ref.at[0], 0, t).astype(F32)
        out_ref[0, here, :] = roll_rows(wide_ref, SPAN - offsets[mi]).astype(BF16)
        hat, inverse = unit(x_ref[0, here, :].astype(F32))
        hat_ref[0, here, :] = hat.astype(BF16)
        inverse_ref[0, here, :] = jnp.broadcast_to(inverse, (SPAN, LANES))


def finish_rest_kernel(keep_ref, got_ref, wo_ref, wu_ref, wd_ref):
    total = keep_ref[0] + got_ref[0].astype(F32)
    for i in range(2):
        wu_ref[:, i * 256 : (i + 1) * 256] = total[:, i * 512 : i * 512 + 256]
        wd_ref[:, i * 256 : (i + 1) * 256] = total[:, i * 512 + 256 : i * 512 + 512]
    wo_ref[...] = total[:, 1024:]


def finish_kernel(
    direct, place, offsets, lengths, hat_ref, inverse_ref, part_ref, right_ref, gain, *refs
):
    if direct:
        keep_ref, mine_ref, a_ref, b_ref, c_ref, out_ref, wq_ref, wk_ref, wv_ref, *line_refs, wide_ref = refs
        size = keep_ref.shape[0]
        total = (keep_ref[...] + a_ref[0:size, :].astype(F32)) + (
            b_ref[0:size, :].astype(F32) + c_ref[0:size, :].astype(F32)
        )
        wq_ref[...], wk_ref[...], wv_ref[...] = total[:, :128], total[:, 128:256], total[:, 256:384]
        pooled = total[:, 384:]
        lines = (lines_of(mine_ref) + lines_of(a_ref)) + (lines_of(b_ref) + lines_of(c_ref))
        ub_ref, *line_refs = line_refs
        for i in range(4):
            ub_ref[:, i * D : (i + 1) * D] = lines[4 + i : 5 + i, :]
        for ref, i in zip(line_refs, (0, 1, 2, 3, 8, 9, 10, 11)):
            ref[...] = lines[i : i + 1, :]
    else:
        pooled_ref, out_ref, wide_ref = refs
        pooled = pooled_ref[...]
    rows = hat_ref.shape[1]
    for mi in range(2):
        dev, offset, ends = row_info(place, offsets, lengths, mi)
        first, last = summary_range(dev * (rows // SPAN) + iota((8, 1), 0), offset, ends)
        lows = jnp.concatenate(
            [pooled[16 * i + 8 * mi : 16 * i + 8 * mi + 8, :] for i in range(D // LANES)], axis=1
        )
        lows = lows * gain[...] * lax.rsqrt((last - first + 1).astype(F32))
        level = (lows - jnp.mean(lows, axis=-1, keepdims=True)).astype(BF16)
        lows = lows.astype(BF16)
        first, last = summary_range(dev * (rows // SPAN) + iota((1, 8), 1), offset, ends)
        for t in range(rows // SPAN):
            here = slice(t * SPAN, (t + 1) * SPAN)
            pos = dev * rows + t * SPAN + iota((SPAN, 1), 0)
            member = jnp.where((pos >= first) & (pos <= last), 1.0, 0.0)
            hat = hat_ref[mi, here, :]
            slope = jnp.sum(member * dot_cols(hat, lows), axis=1, keepdims=True) * (1.0 / D)
            inverse = inverse_ref[mi, here, 0:1]
            wide_ref[...] = two_tiles(part_ref, right_ref.at[0], mi, t)
            own = roll_rows(wide_ref, SPAN - offset)
            out_ref[mi, here, :] = own + (dot(member.astype(BF16), level) - hat.astype(F32) * slope) * inverse


def call(kernel, outs, in_specs, out_specs=None, scratch=(), limit=8, **more):
    return pl.pallas_call(
        kernel,
        out_shape=outs,
        in_specs=in_specs,
        out_specs=out_specs if out_specs is not None else [VMEM] * len(outs),
        scratch_shapes=list(scratch),
        compiler_params=pltpu.CompilerParams(vmem_limit_bytes=limit * MIB),
        cost_estimate=pl.CostEstimate(flops=1, bytes_accessed=1, transcendentals=0),
        **more,
    )


def call_row(kernel, mi, facts, arrays, outs, before, scratch, **more):
    def block(dims):
        return pl.BlockSpec((1,) + dims[1:], lambda i: (mi,) + (0,) * (len(dims) - 1))

    aliases = {3 + len(arrays) + i: i for i in range(len(before))}
    return call(
        partial(kernel, mi), outs, [SMEM] * 3 + [block(a.shape) for a in arrays] + [ANY] * len(before),
        [block(o.shape) for o in outs], scratch, grid=(1,), input_output_aliases=aliases, **more,
    )(*facts, *arrays, *before)


def tie(value, *others):
    return lax.optimization_barrier((value,) + others)[0]


def per_device(
    block_input, cotangent, span_offset, doc_lengths, ln1_gain, ln1_bias, w_query, w_key, w_value,
    query_bias, value_bias, w_out, out_bias, ln2_gain, ln2_bias, w_up, up_bias, w_down, down_bias,
):
    groups, ranks = lax.axis_size("seq"), lax.axis_size("mp")
    count = groups * ranks
    mp_index = lax.axis_index("mp")
    dev = lax.axis_index("seq") * ranks + mp_index
    rows = block_input.shape[1]
    tiles = rows // SPAN
    summaries = tiles * count
    shard = w_query.shape[0]
    bits = count.bit_length() - 1
    stages = [(b, b) for b in range(bits - 1, 2, -1)] + [(1, 2), (2, 1)]
    direct = shard == 64

    def swap(value, stage):
        pairs = [(i, i ^ (1 << stage[i & 1])) for i in range(count)]
        return lax.ppermute(value, AXES, pairs)

    def turn(value, by):
        return lax.ppermute(value, AXES, [(i, (i + by) % count) for i in range(count)])

    core = dev & 1
    slot = jnp.arange(count, dtype=jnp.int32)
    far = slot // (count // 2)
    mask = far
    for i, (even, odd) in enumerate(stages):
        where = jnp.where((core ^ far) == 0, even, odd)
        mask = mask | (((slot >> i) & 1) << where)
    owner = dev ^ mask
    if not direct:
        owner = slot
    member_slot = jnp.arange(16, dtype=jnp.int32)
    slots = owner[:, None] * tiles + (member_slot % 8)[None, :]
    valid = (member_slot % 8 <= tiles)[None, :]
    slots = jnp.stack(
        [
            jnp.where(valid & (member_slot // 8 == mi)[None, :], slots, -1).reshape(-1)
            for mi in range(2)
        ]
    )
    block_of, row_of = owner % ranks, owner // ranks
    facts = (jnp.stack((dev, mp_index)), span_offset, doc_lengths)

    def reach(value, flip):
        return lax.ppermute(value, AXES, [(i, i ^ flip) for i in range(count)])

    def spread(values):
        return [reach(value, flip) for value, flip in zip(values, (16, 8, 24))]

    def join(near, far):
        return jnp.concatenate((near, far), axis=0)

    def fold(keep, got):
        total = keep + got.astype(F32)
        half = total.shape[0] // 2
        return total[:half], total[half:].astype(BF16)

    def whole_blocks(arrays):
        return [pl.BlockSpec(a.shape, lambda i, n=len(a.shape): (0,) * n) for a in arrays]

    def fold_lines(keep, sent, got, sends=1):
        size = keep.shape[0]
        part = size // (1 + sends)
        outs = [shape((part, D), F32)] + [shape((part + (32 if sends == 1 else 16), D), BF16)] * sends
        mine = pl.BlockSpec((32, D), lambda i: (size // 32, 0))
        both = whole_blocks((keep, got))
        return call(fold_kernel, outs, [both[0], mine, both[1]], whole_blocks(outs), grid=(1,))(keep, sent, got)

    def gather_whole(value):
        both = lax.all_gather(value, "seq", axis=0, tiled=True)
        both = lax.all_gather(both, "mp", axis=0)
        return both[: ranks // 2], both[ranks // 2 :]

    def scatter_whole(keep, send):
        both = jnp.concatenate((keep, send), axis=0).astype(F32)
        total = lax.psum_scatter(both, "mp", scatter_dimension=0, tiled=True)[0]
        return lax.psum_scatter(total, "seq", scatter_dimension=0, tiled=True)

    def row(vector):
        return vector[None, :]

    def shape(dims, kind):
        return jax.ShapeDtypeStruct(dims, kind)

    half, tall = (count // 2, shard) if direct else (ranks // 2, shard * groups)
    width = 4 * LANES if direct else 3 * LANES
    apart = not direct
    wide, three = (2, rows, D), (2, rows, 3 * D)
    flat, pooled_dims = (2 * rows, D), (2, summaries, D)
    room = 12 if direct else 56
    masks = [pltpu.VMEM((tiles, SPAN + summaries, SPAN), F32)]

    def prepare():
        return call(
            prepare_kernel, [shape((1, max(shard, 64), D), BF16), shape((1, shard, 1152), BF16), shape((2, SPAN, D), BF16)],
            [SMEM] * 3 + [HBM] * 8, [VMEM] * 3,
            scratch=[pltpu.VMEM(wide, BF16), pltpu.SemaphoreType.DMA((11,))],
            limit=56,
        )(*facts, block_input, cotangent, w_query, w_key, w_value, w_out.T, w_up, w_down.T)

    part_a, w_rest, cot_edge = prepare()
    x_edge = block_input[:, rows - SPAN :]
    if direct:
        got_a = spread([part_a] * 3)
        part_b = tie(w_rest, got_a[0])
        got_b = swap(part_b, stages[0])
        part_a = jnp.concatenate([part_a] + got_a, axis=0)
        x_left = turn(tie(x_edge, part_a), 1)
        got_a = swap(part_a, stages[2])
        part_a = join(part_a, got_a)
        part_b = join(part_b, tie(got_b, part_a))
        got_a, got_b = swap(part_a, stages[3]), swap(part_b, stages[1])
        near_a = join(part_a, tie(got_a, x_left))
        far_a = swap(near_a, (0, 0))
        part_b = join(part_b, tie(got_b, near_a))
        got_b = swap(part_b, stages[2])
        more = ()
    else:
        x_left, cot_left = turn(x_edge, 1), turn(cot_edge, 1)
        near_a, far_a = gather_whole(part_a[0, :shard, :384])
        near_b, far_b = gather_whole(w_rest[0])
        near_1, near_2, far_1, far_2 = (a[:, :, i : i + w] for a in (near_b, far_b) for i, w in ((0, 640), (640, 512)))
        more = (lax.all_gather(part_a[0, :64, 384:], AXES, axis=0),)
        block_of, row_of = jnp.arange(ranks, dtype=jnp.int32), jnp.zeros((ranks,), jnp.int32)

    xs, qkv, skv, sums, w_full = call(
        partial(project_kernel, apart),
        [shape(wide, BF16), shape(three, BF16), shape((2, summaries, 3 * D), BF16), shape(pooled_dims, F32)]
        + [shape((D, 3 * D), BF16)],
        [SMEM] * 5 + [VMEM] * 7 + [ANY] * (2 + len(more)),
        scratch=[
            pltpu.VMEM((count, 64, LANES), BF16),
            pltpu.VMEM((rows + SPAN, D), F32),
            pltpu.VMEM((2, rows + 2 * summaries, D), BF16),
            pltpu.SemaphoreType.DMA((2,)),
        ],
        limit=24 if direct else 56,
    )(
        *facts, block_of, row_of, slots, block_input, x_left, row(ln1_gain), row(ln1_bias),
        row(query_bias), row(value_bias), near_a, far_a, *more,
    )
    outs = [shape(wide, BF16), shape((2, 4, tiles, 1, 2 * SPAN), F32)]
    if direct:
        cot_left = turn(tie(cot_edge, near_a), 1)
        part_b = join(part_b, tie(got_b, skv, cot_left))
        part_1, part_2 = part_b[:, :, :640], part_b[:, :, 640:]
        got_1 = swap(part_1, stages[3])
        qkv = tie(qkv, part_1)
    seen = call_row(attend_kernel, 0, facts, (qkv, skv), outs, (), masks, limit=room)
    att, lse = call_row(attend_kernel, 1, facts, (qkv, skv), outs, tuple(seen), masks, limit=room)
    if direct:
        near_1 = join(part_1, tie(got_1, att))
        far_1 = swap(near_1, (0, 0))
        got_2 = swap(tie(part_2, near_1), stages[3])
    tall_low, tall_float = shape(flat, BF16), shape(flat, F32)
    weights = [pltpu.VMEM((D, 2 * rows), BF16)] * 2 + [pltpu.VMEM((D, FF // 2), BF16)] * 4
    weights += [pltpu.VMEM((2 * rows, FF // 2), BF16)] * 2
    *kept, gub_1, down_b, keep_1, send_1 = call(
        mlp_first_kernel,
        [tall_float] + [tall_low] * 4 + [shape((D, D), BF16)]
        + [shape((1, FF // 2), F32), shape((1, D), F32)] + [shape((half, tall, 512), BF16)] * 2,
        [SMEM] * 4 + [VMEM] * 8 + [HBM] + [ANY] * 2,
        [VMEM] * 8 + [ANY] * 2,
        scratch=weights
        + [pltpu.VMEM((rows + SPAN, D), F32), pltpu.VMEM(wide, BF16)]
        + [pltpu.SemaphoreType.DMA((4,)), pltpu.SemaphoreType.DMA((2,))],
        limit=28,
    )(
        facts[0], span_offset, block_of, row_of, xs, att, cot_left, row(out_bias), row(ln2_gain), row(ln2_bias),
        row(up_bias), row(down_bias), cotangent, near_1, far_1,
    )
    if direct:
        near_2 = join(part_2, tie(got_2, kept[0]))
        far_2 = swap(near_2, (0, 0))
        got_1 = swap(tie(send_1, near_2), (0, 0))
        keep_1, send_1 = fold(keep_1.astype(F32), got_1)
        got_1 = swap(send_1, stages[3])
        near_2 = tie(near_2, send_1)
    result, gmid, gatt, small_b, gub_2, keep_2, send_2 = call(
        mlp_second_kernel,
        [shape(wide, BF16)] * 3 + [shape((8, D), F32)]
        + [shape((1, FF // 2), F32)] + [shape((half, tall, 640), BF16)] * 2,
        [SMEM] * 2 + [VMEM] * 9 + [ANY] * 2,
        [VMEM] * 5 + [ANY] * 2,
        scratch=weights
        + [pltpu.VMEM((D, D), BF16), pltpu.VMEM((D, 2 * rows), BF16)]
        + [pltpu.SemaphoreType.DMA((2,)), pltpu.SemaphoreType.DMA((3,))],
        limit=28,
    )(block_of, row_of, att, row(ln2_gain), row(up_bias), *kept, near_2, far_2)
    gubs = (gub_1, gub_2)
    arrays = (qkv, skv, lse, gatt)
    outs = [shape(three, BF16), shape((2, summaries, 3 * D), BF16)]
    if direct:
        keep_1, send_1 = fold(keep_1, tie(got_1, send_2))
        got_2 = swap(tie(send_2, send_1), (0, 0))
        got_1 = swap(send_1, stages[2])
    grads = call_row(attend_back_kernel, 0, facts, arrays, outs, (), masks, limit=room)
    if direct:
        keep_2, send_2 = fold(keep_2.astype(F32), tie(got_2, grads[0]))
        got_2 = swap(send_2, stages[3])
        grads = [tie(grads[0], send_2)] + list(grads[1:])
    grads = call_row(attend_back_kernel, 1, facts, arrays, outs, tuple(grads), masks, limit=room)
    if direct:
        keep_1, send_1 = fold(keep_1, tie(got_1, grads[0]))
        grads = [tie(grads[0], send_1), grads[1]]
    lines, keep_a, send_a, *more = call(
        partial(weights_back_kernel, apart),
        [shape((16, D), F32)]
        + [shape((half * tall, width), BF16), shape((half * tall + (32 if direct else 0), width), BF16)]
        + [shape((count, 64, LANES), BF16)] * apart,
        [SMEM] * 5 + [VMEM] * 12,
        [VMEM] + [ANY] * (2 + apart),
        scratch=[
            pltpu.VMEM((D, 3 * D), BF16), pltpu.VMEM(pooled_dims, BF16), pltpu.VMEM((count, 64, LANES), BF16),
            pltpu.VMEM((32, D), BF16), pltpu.SemaphoreType.DMA((3,)),
        ],
        limit=24 if direct else 56,
    )(
        *facts, block_of, row_of, slots, xs, *grads, sums, w_full, row(ln1_gain), row(ln1_bias), small_b, down_b, *gubs,
    )

    def by_row(dims):
        return pl.BlockSpec((1,) + dims[1:], lambda i: (i,) + (0,) * (len(dims) - 1))

    once = pl.BlockSpec((1, D), lambda i: (0, 0))
    edge_dims = (2, SPAN, D)

    def rows_back(*after):
        return call(
            rows_back_kernel, [shape(wide, F32), shape((2,) + edge_dims, BF16)],
            [by_row(three), pl.BlockSpec((D, 3 * D), lambda i: (0, 0)), by_row(wide), by_row(wide)]
            + [by_row(edge_dims), once],
            [by_row(wide), pl.BlockSpec((2, 1, SPAN, D), lambda i: (0, i, 0, 0))], grid=(2,), limit=16,
        )(grads[0], tie(w_full, *after), xs, gmid, result, row(ln1_gain))

    def unroll(back):
        return call(
            unroll_kernel, [shape(wide, BF16)] * 2 + [shape((2, rows, LANES), F32)],
            [SMEM, by_row(wide), pl.BlockSpec((1, 1, SPAN, D), lambda i: (1, i, 0, 0)), by_row(wide)], [by_row(wide)] * 2 + [by_row((2, rows, LANES))],
            [pltpu.VMEM((2 * SPAN, D), F32)], grid=(2,),
        )(span_offset, result, back, block_input)

    final = [SMEM] * 3 + [VMEM] * 5
    rolled = [pltpu.VMEM((2 * SPAN, D), F32)]
    if direct:
        got_a = swap(send_a, (0, 0))
        keep_2, send_2 = fold(keep_2, tie(got_2, send_a))
        got_2 = swap(send_2, stages[2])
        keep_a, send_a = fold_lines(keep_a, send_a, tie(got_a, send_2))
        got_a = swap(send_a, stages[3])
        part, edge = rows_back(send_a)
        keep_2, send_2 = fold(keep_2, tie(got_2, part))
        keep_b, send_b = (jnp.concatenate(a, axis=2) for a in ((keep_1, keep_2), (send_1, send_2)))
        got_b = swap(send_b, stages[1])
        back = turn(tie(edge, send_b), -1)
        keep_a, send_a = fold_lines(keep_a, send_a, tie(got_a, send_b))
        got_a = swap(send_a, stages[2])
        keep_b, send_b = fold(keep_b, tie(got_b, send_a))
        got_b = swap(send_b, stages[0])
        keep_a, *send_a = fold_lines(keep_a, send_a, tie(got_a, send_b), 3)
        got_a = spread(send_a)
        result_own, *hats = unroll(tie(back, send_a[0]))
        grad_wo, grad_wu, grad_wd = call(
            finish_rest_kernel, [shape((shard, LANES), F32), shape((shard, 512), F32), shape((shard, 512), F32)],
            [VMEM] * 2,
        )(keep_b, tie(got_b, send_a[0]))
        input_grad, grad_wq, grad_wk, grad_wv, grad_ub, *small = call(
            partial(finish_kernel, True),
            [shape(wide, F32)] + [shape((shard, LANES), F32)] * 3 + [shape((1, FF), F32)] + [shape((1, D), F32)] * 8,
            final + [VMEM] * 5, scratch=rolled, limit=16,
        )(*facts, *hats, part, back, row(ln1_gain), keep_a, send_a[0], *(tie(got, grad_wo) for got in got_a))
        grad_wo, grad_wd = grad_wo.T, grad_wd.T
        small = [a.reshape(D) for a in small]
        grad_ub = grad_ub.reshape(FF)
    else:
        keep_a, send_a = (a.reshape(half, tall, width) for a in (keep_a, send_a))
        part, edge = rows_back()
        back = turn(edge, -1)
        result_own, *hats = unroll(back)
        sum_a, sum_1, sum_2 = (scatter_whole(*a) for a in ((keep_a, send_a), (keep_1, send_1), (keep_2, send_2)))
        grad_wq, grad_wk, grad_wv = (sum_a[:, i : i + LANES] for i in (0, 128, 256))
        grad_wo = sum_2[:, 512:].T
        grad_wu, grad_wd = (
            jnp.concatenate((sum_1[:, i : i + 256], sum_2[:, i : i + 256]), axis=1) for i in (0, 256)
        )
        grad_wd = grad_wd.T
        pooled = lax.psum_scatter(more[0].astype(F32), AXES, scatter_dimension=0, tiled=True)[0]
        lines = lax.psum(lines, AXES)
        grad_ub = lines[4:8].reshape(FF)
        small = [lines[i] for i in (0, 1, 2, 3, 8, 9, 10, 11)]
        input_grad = call(partial(finish_kernel, False), [shape(wide, F32)], final + [VMEM], scratch=rolled, limit=16)(
            *facts, *hats, part, back, row(ln1_gain), pooled
        )[0]
    grad_gain_two, grad_shift_two, grad_obias, grad_dbias, grad_gain_one, grad_shift_one, grad_qb, grad_vb = small
    return (
        result_own,
        input_grad,
        grad_gain_one,
        grad_shift_one,
        grad_wq,
        grad_wk,
        grad_wv,
        grad_qb,
        grad_vb,
        grad_wo,
        grad_obias,
        grad_gain_two,
        grad_shift_two,
        grad_wu,
        grad_ub,
        grad_wd,
        grad_dbias,
    )


def solution(mesh):
    vector, matrix, turned = P(), P("seq", "mp"), P("mp", "seq")
    own, group = P(None, ("seq", "mp"), None), P(None, "seq", None)
    return jax.shard_map(
        per_device,
        mesh=mesh,
        in_specs=(own, group, vector, vector, vector, vector, matrix, matrix, matrix, vector, vector)
        + (turned, vector, vector, vector, matrix, vector, turned, vector),
        out_specs=(own, own, vector, vector, matrix, matrix, matrix, vector, vector, turned, vector)
        + (vector, vector, matrix, vector, turned, vector),
        check_vma=False,
    )
```

```python
from functools import partial
import math

import jax
import jax.numpy as jnp
from jax import lax
from jax.experimental import pallas as pl
from jax.experimental.pallas import tpu as pltpu
from jax.sharding import PartitionSpec as P

D = 512
FF = 2048
HEAD_DIM = 64
SPAN = 128
LANES = 128
STEP = 512
EPSILON = 1e-05
NEGATIVE = -1e30
SCALE = 1.0 / math.sqrt(HEAD_DIM)
F32 = jnp.float32
BF16 = jnp.bfloat16
AXES = ("seq", "mp")
MIB = 1 << 20
VMEM = pl.BlockSpec(memory_space=pltpu.VMEM)
SMEM = pl.BlockSpec(memory_space=pltpu.SMEM)
ANY = pl.BlockSpec(memory_space=pl.ANY)
HBM = pl.BlockSpec(memory_space=pltpu.HBM)


def dot(left, right):
    return lax.dot_general(left, right, (((1,), (0,)), ((), ())), preferred_element_type=F32)


def dot_cols(left, right):
    return lax.dot_general(left, right, (((1,), (1,)), ((), ())), preferred_element_type=F32)


def unit(rows):
    centred = rows - jnp.mean(rows, axis=-1, keepdims=True)
    inverse = lax.rsqrt(jnp.mean(centred * centred, axis=-1, keepdims=True) + EPSILON)
    return centred * inverse, inverse


def unit_back(grad, hat, inverse):
    shift = jnp.mean(grad, axis=-1, keepdims=True)
    slope = jnp.mean(grad * hat, axis=-1, keepdims=True)
    return (grad - shift - hat * slope) * inverse


def row_info(place, offsets, lengths, mi):
    ends = []
    for c in range(lengths.shape[1]):
        ends.append(lengths[mi, c] + (ends[-1] if ends else 0))
    return place[0], offsets[mi], ends


def doc_start(positions, ends):
    start = jnp.zeros_like(positions)
    for end in ends:
        start = jnp.where(positions >= end, end, start)
    return start


def summary_range(summary_ids, offset, ends):
    last = offset - 1 + SPAN * summary_ids
    first = jnp.maximum(doc_start(last, ends), last - (SPAN - 1))
    return first, last


def iota(shape, dim):
    return lax.broadcasted_iota(jnp.int32, shape, dim)


def roll_rows(ref, by):
    whole = pl.multiple_of((by // 8) * 8, 8)
    return pltpu.roll(ref[pl.ds(whole, SPAN + 8), :], SPAN + 8 - (by - whole), axis=0)[:SPAN]


def prepare_kernel(
    place, offsets, lengths, x_ref, cot_ref, wq_ref, wk_ref, wv_ref, wo_ref, wu_ref, wd_ref,
    out_ref, rest_ref, edge_ref, rows_ref, sem
):
    rows = x_ref.shape[1]
    last_rows = pl.multiple_of(place[1] * rows + (rows - SPAN), SPAN)
    shard = wq_ref.shape[0]
    copies = [pltpu.make_async_copy(x_ref.at[mi], rows_ref.at[mi], sem.at[mi]) for mi in range(2)]
    copies += [
        pltpu.make_async_copy(ref, out_ref.at[0, 0:shard, i * LANES : (i + 1) * LANES], sem.at[2 + i])
        for i, ref in enumerate((wq_ref, wk_ref, wv_ref))
    ]
    copies.append(pltpu.make_async_copy(cot_ref.at[:, pl.ds(last_rows, SPAN), :], edge_ref, sem.at[5]))
    copies.append(pltpu.make_async_copy(wo_ref, rest_ref.at[0, :, 0:128], sem.at[6]))
    for i, (ref, first) in enumerate(((wu_ref, 0), (wd_ref, 0), (wu_ref, 256), (wd_ref, 256))):
        target = rest_ref.at[0, :, 128 + 256 * i : 384 + 256 * i]
        copies.append(pltpu.make_async_copy(ref.at[:, first : first + 256], target, sem.at[7 + i]))
    for copy in copies:
        copy.start()
    sums = []
    for mi in range(2):
        dev, offset, ends = row_info(place, offsets, lengths, mi)
        first, last = summary_range(dev * (rows // SPAN) + iota((8, 1), 0), offset, ends)
        pos = dev * rows + iota((1, rows), 1)
        member = jnp.where((pos >= first) & (pos <= last), 1.0, 0.0).astype(BF16)
        copies[mi].wait()
        hat, _ = unit(rows_ref[mi].astype(F32))
        high = hat.astype(BF16)
        rest = (hat - high.astype(F32)).astype(BF16)
        total = dot(member, high) + dot(member, rest)
        sums.append(total * lax.rsqrt((last - first + 1).astype(F32)))
    both = jnp.concatenate(sums, axis=0).astype(BF16)
    for copy in copies[2:]:
        copy.wait()
    for lane in range(D // LANES):
        out_ref[0, 16 * lane : 16 * lane + 16, 384:512] = both[:, lane * LANES : (lane + 1) * LANES]


def fill_masks(place, offsets, lengths, mi, bias_ref, tiles, summaries, length):
    dev, offset, ends = row_info(place, offsets, lengths, mi)
    ends_col = offset - 1 + SPAN * iota((summaries, 1), 0)
    for t in range(tiles):
        base = SPAN * (dev * tiles + t) + offset - SPAN
        qpos = base + iota((1, SPAN), 1)
        qpos = jnp.where(qpos < 0, qpos + length, qpos)
        kpos = base + iota((SPAN, 1), 0)
        kpos = jnp.where(kpos < 0, kpos + length, kpos)
        span_first = jnp.where(qpos >= base + SPAN, base + length, base)
        doc_first = doc_start(qpos, ends)
        local_ok = (kpos >= jnp.maximum(doc_first, span_first)) & (kpos <= qpos)
        summary_ok = (ends_col >= doc_first) & (ends_col < span_first)
        bias_ref[t, 0:SPAN, :] = jnp.where(local_ok, 0.0, NEGATIVE)
        bias_ref[t, SPAN : SPAN + summaries, :] = jnp.where(summary_ok, 0.0, NEGATIVE)


def split_heads(pair):
    low = iota(pair.shape, 1) < HEAD_DIM
    zero = jnp.zeros_like(pair)
    return jnp.concatenate((jnp.where(low, pair, zero), jnp.where(low, zero, pair)), axis=0)


def join_heads(turned):
    half = turned.shape[1] // 2
    return jnp.concatenate((turned[:HEAD_DIM, :half], turned[HEAD_DIM:, half:]), axis=0).T


def project_kernel(
    apart, place_ref, offsets, lengths, block_of, row_of, slots_ref, x_ref, left_ref, gain, shift, qbias, vbias,
    near_ref, far_ref, *refs
):
    if apart:
        all_ref, *refs = refs
    xs_ref, qkv_ref, skv_ref, sums_ref, w_ref, stack_ref, wide_ref, rows_ref, sem = refs
    rows = x_ref.shape[1]
    tiles = rows // SPAN
    summaries = skv_ref.shape[1]
    half, shard, _ = near_ref.shape

    def place(d, carry):
        for source, slot in ((near_ref, d), (far_ref, half + d)):
            here = pl.ds(pl.multiple_of(row_of[slot] * shard, 16), shard)
            cols = pl.ds(pl.multiple_of(block_of[slot] * 384, 128), 384)
            pltpu.make_async_copy(source.at[d, :, 0:384], w_ref.at[here, cols], sem.at[0]).start()
            if not apart:
                pltpu.make_async_copy(
                    source.at[d, 0:64, 384:512], stack_ref.at[slot], sem.at[1]
                ).start()
        return carry

    lax.fori_loop(0, half, place, 0)
    if apart:
        pltpu.make_async_copy(all_ref, stack_ref, sem.at[1]).start()
    for mi in range(2):
        wide_ref[0:SPAN, :] = left_ref[mi].astype(F32)
        wide_ref[SPAN : SPAN + rows, :] = x_ref[mi].astype(F32)
        for t in range(tiles):
            here = slice(t * SPAN, (t + 1) * SPAN)
            rolled = roll_rows(wide_ref, t * SPAN + offsets[mi])
            xs_ref[mi, here, :] = rolled.astype(BF16)
            hat, _ = unit(rolled)
            rows_ref[mi, here, :] = (hat * gain[...] + shift[...]).astype(BF16)
    pltpu.make_async_copy(stack_ref, stack_ref, sem.at[1]).wait()
    roots = []
    for mi in range(2):
        _, offset, ends = row_info(place_ref, offsets, lengths, mi)
        first, last = summary_range(iota((summaries, 1), 0), offset, ends)
        root = jnp.sqrt((last - first + 1).astype(F32))
        roots.append(root)
        for base in range(0, stack_ref.shape[0], 32):
            named = slots_ref[mi : mi + 1, 16 * base : 16 * base + 512]
            pick = jnp.where(iota((summaries, 1), 0) == named, 1.0, 0.0).astype(BF16)
            piece = jnp.concatenate(
                [
                    stack_ref[base : base + 32, 16 * lane : 16 * lane + 16, :].reshape(512, LANES)
                    for lane in range(D // LANES)
                ],
                axis=1,
            )
            found = dot(pick, piece)
            sums_ref[mi] = found if base == 0 else sums_ref[mi] + found
        summed = sums_ref[mi] * gain[...] + root * shift[...]
        high = summed.astype(BF16)
        rows_ref[mi, rows : rows + summaries, :] = high
        rows_ref[mi, rows + summaries : rows + 2 * summaries, :] = (summed - high.astype(F32)).astype(BF16)
    pltpu.make_async_copy(w_ref, w_ref, sem.at[0]).wait()
    none = jnp.zeros((1, LANES), F32)

    def block(m, carry):
        lanes, cols = columns(m, LANES), columns(m, 384)
        bias = jnp.concatenate((qbias[:, lanes], none, vbias[:, lanes]), axis=1)
        for mi in range(2):
            projected = dot(rows_ref[mi], w_ref[:, cols])
            qkv_ref[mi, :, cols] = (projected[:rows] + bias).astype(BF16)
            pooled = projected[rows : rows + summaries] + projected[rows + summaries :]
            skv_ref[mi, :, cols] = (pooled + roots[mi] * bias).astype(BF16)
        return carry

    lax.fori_loop(0, 4, block, 0)


def pair_of(ref, here, pair):
    def part(i):
        return ref[0, here, pl.ds(pl.multiple_of(pair * 384 + i * LANES, LANES), LANES)]

    return part(0), part(1), part(2)


def attend_kernel(mi, place, offsets, lengths, qkv_ref, skv_ref, *refs):
    att_ref, lse_ref, bias_ref = refs[-3:]
    rows = qkv_ref.shape[1]
    tiles = rows // SPAN
    summaries = skv_ref.shape[1]
    fill_masks(place, offsets, lengths, mi, bias_ref, tiles, summaries, summaries * SPAN)

    def heads(pair, carry):
        lanes = pl.ds(pl.multiple_of(pair * LANES, LANES), LANES)
        _, skeys, svalues = pair_of(skv_ref, slice(None), pair)
        svalues = svalues.T
        spans = [pair_of(qkv_ref, slice(t * SPAN, (t + 1) * SPAN), pair) for t in range(tiles)]
        scores = []
        for t, (queries, keys, _) in enumerate(spans):
            bias = bias_ref[t]
            keys = jnp.concatenate((keys, skeys), axis=0)
            scores.append(dot_cols(keys, split_heads(queries * SCALE)) + jnp.concatenate((bias, bias), axis=1))
        probs = []
        for t in range(tiles):
            top = jnp.max(scores[t], axis=0, keepdims=True)
            grown = jnp.exp(scores[t] - top)
            total = jnp.sum(grown, axis=0, keepdims=True)
            probs.append((grown * (1.0 / total)).astype(BF16))
            lse_ref[0, pair, t] = top + jnp.log(total)
        for t, (_, _, values) in enumerate(spans):
            values = jnp.concatenate((values.T, svalues), axis=1)
            att_ref[0, t * SPAN : (t + 1) * SPAN, lanes] = join_heads(dot(values, probs[t])).astype(BF16)
        return carry

    lax.fori_loop(0, 4, heads, 0)


def gelu_pair(u):
    c0 = math.sqrt(2.0 / math.pi)
    square = u * u
    t = jnp.tanh(c0 * u * (1.0 + 0.044715 * square))
    half = 0.5 * (1.0 + t)
    slope = half + (0.5 * c0) * u * (1.0 - t * t) * (1.0 + (3 * 0.044715) * square)
    return u * half, slope


def columns(block, width):
    return pl.ds(pl.multiple_of(block * width, 128), width)


def mlp_half(half_id, ubias, n_ref, c_ref, nt_ref, ct_ref, wu_ref, wd_ref, gu_ref, gd_ref, gub_ref, act_ref, grad_ref, add):
    bias = jnp.concatenate([ubias[:, m * 512 + half_id * 256 : m * 512 + half_id * 256 + 256] for m in range(4)], axis=1)
    step = STEP
    gub_ref[...] = jnp.zeros_like(gub_ref)

    def block(r, carry):
        here = pl.ds(pl.multiple_of(r * step, step), step)
        w_up, w_down = wu_ref[...], wd_ref[...]
        act, slope = gelu_pair(dot(n_ref[here, :], w_up) + bias)
        act = act.astype(BF16)
        grad = dot(c_ref[here, :], w_down) * slope
        gub_ref[...] += jnp.sum(grad, axis=0, keepdims=True)
        grad = grad.astype(BF16)
        act_ref[here, :] = act
        grad_ref[here, :] = grad
        add(r, here, dot_cols(act, w_down), dot_cols(grad, w_up))
        return carry

    lax.fori_loop(0, n_ref.shape[0] // step, block, 0)
    gu_ref[...] = dot(nt_ref[...], grad_ref[...]).astype(BF16)
    gd_ref[...] = dot(ct_ref[...], act_ref[...]).astype(BF16)


def pull(block_of, row_of, near_ref, far_ref, parts):
    half, shard, _ = near_ref.shape

    def body(d, carry):
        for source, slot in ((near_ref, d), (far_ref, half + d)):
            here = pl.ds(pl.multiple_of(row_of[slot] * shard, 16), shard)
            for target, first, width, sem in parts:
                pltpu.make_async_copy(
                    source.at[d, :, first : first + width], target.at[here, columns(block_of[slot], width)], sem
                ).start()
        return carry

    lax.fori_loop(0, half, body, 0)


def push(block_of, row_of, keep_ref, send_ref, parts):
    half, shard, _ = keep_ref.shape

    def body(d, carry):
        for target, slot in ((keep_ref, d), (send_ref, half + d)):
            here = pl.ds(pl.multiple_of(row_of[slot] * shard, 16), shard)
            for source, first, width, sem in parts:
                pltpu.make_async_copy(
                    source.at[here, columns(block_of[slot], width)], target.at[d, :, first : first + width], sem
                ).start()
        return carry

    lax.fori_loop(0, half, body, 0)


def mlp_first_kernel(
    place_ref, offsets, block_of, row_of, xs_ref, att_ref, left_ref, obias, gain, shift, ubias, dbias, cot_ref,
    near_ref, far_ref,
    resid_ref, acc_ref, gn_ref, n_ref, c_ref, wo_ref, gub_ref, down_ref, keep_ref, send_ref,
    nt_ref, ct_ref, wu_ref, wd_ref, gu_ref, gd_ref, act_ref, grad_ref, wide_ref, low_ref, sem, out_sem,
):
    rows = xs_ref.shape[1]
    own = pl.ds(pl.multiple_of(place_ref[1] * rows, SPAN), rows)
    own_copy = pltpu.make_async_copy(cot_ref.at[:, own, :], low_ref, sem.at[3])
    own_copy.start()
    pull(block_of, row_of, near_ref, far_ref, ((wo_ref, 0, 128, sem.at[0]),))
    pull(block_of, row_of, near_ref, far_ref, ((wu_ref, 128, 256, sem.at[1]), (wd_ref, 384, 256, sem.at[2])))
    down_ref[...] = jnp.zeros_like(down_ref)
    own_copy.wait()
    pltpu.make_async_copy(wo_ref, wo_ref, sem.at[0]).wait()
    for mi in range(2):
        all_rows = slice(mi * rows, (mi + 1) * rows)
        wide_ref[0:SPAN, :] = left_ref[mi].astype(F32)
        wide_ref[SPAN : SPAN + rows, :] = low_ref[mi].astype(F32)
        for t in range(rows // SPAN):
            rolled = roll_rows(wide_ref, t * SPAN + offsets[mi])
            down_ref[...] += jnp.sum(rolled, axis=0, keepdims=True)
            c_ref[mi * rows + t * SPAN : mi * rows + (t + 1) * SPAN, :] = rolled.astype(BF16)
        resid = xs_ref[mi].astype(F32) + dot_cols(att_ref[mi], wo_ref[...]) + obias[...]
        resid_ref[all_rows, :] = resid
        hat, _ = unit(resid)
        normed = (hat * gain[...] + shift[...]).astype(BF16)
        n_ref[all_rows, :] = normed
        nt_ref[:, all_rows] = normed.T
        ct_ref[:, all_rows] = c_ref[all_rows, :].T
    pltpu.make_async_copy(wu_ref, wu_ref, sem.at[1]).wait()
    pltpu.make_async_copy(wd_ref, wd_ref, sem.at[2]).wait()

    def add(r, here, down, back):
        acc_ref[here, :] = (down + dbias[...]).astype(BF16)
        gn_ref[here, :] = back.astype(BF16)

    mlp_half(
        0, ubias, n_ref, c_ref, nt_ref, ct_ref, wu_ref, wd_ref, gu_ref, gd_ref, gub_ref, act_ref, grad_ref, add
    )
    push(block_of, row_of, keep_ref, send_ref, ((gu_ref, 0, 256, out_sem.at[0]), (gd_ref, 256, 256, out_sem.at[1])))
    pltpu.make_async_copy(gu_ref, gu_ref, out_sem.at[0]).wait()
    pltpu.make_async_copy(gd_ref, gd_ref, out_sem.at[1]).wait()


def mlp_second_kernel(
    block_of, row_of, att_ref, gain, ubias, resid_ref, acc_ref, gn_ref, n_ref, c_ref, wo_ref,
    near_ref, far_ref,
    result_ref, gmid_ref, gatt_ref, small_ref, gub_ref, keep_ref, send_ref,
    nt_ref, ct_ref, wu_ref, wd_ref, gu_ref, gd_ref, act_ref, grad_ref, go_ref, turned_ref, sem, out_sem,
):
    rows = att_ref.shape[1]
    pull(block_of, row_of, near_ref, far_ref, ((wu_ref, 0, 256, sem.at[0]), (wd_ref, 256, 256, sem.at[1])))
    small_ref[...] = jnp.zeros_like(small_ref)
    for mi in range(2):
        here = slice(mi * rows, (mi + 1) * rows)
        nt_ref[:, here] = n_ref[here, :].T
        ct_ref[:, here] = c_ref[here, :].T
    pltpu.make_async_copy(wu_ref, wu_ref, sem.at[0]).wait()
    pltpu.make_async_copy(wd_ref, wd_ref, sem.at[1]).wait()

    def add(r, here, down, back):
        mi = r // (rows // STEP)
        own = pl.ds(pl.multiple_of((r % (rows // STEP)) * STEP, STEP), STEP)
        result_ref[mi, own, :] = (resid_ref[here, :] + (acc_ref[here, :].astype(F32) + down)).astype(BF16)
        hat, inverse = unit(resid_ref[here, :])
        grad = gn_ref[here, :].astype(F32) + back
        small_ref[0:1, :] += jnp.sum(grad * hat, axis=0, keepdims=True)
        small_ref[1:2, :] += jnp.sum(grad, axis=0, keepdims=True)
        branch = (c_ref[here, :].astype(F32) + unit_back(grad * gain[...], hat, inverse)).astype(BF16)
        gmid_ref[mi, own, :] = branch
        small_ref[2:3, :] += jnp.sum(branch.astype(F32), axis=0, keepdims=True)
        gatt_ref[mi, own, :] = dot(branch, wo_ref[...]).astype(BF16)
        turned_ref[:, here] = branch.T

    mlp_half(
        1, ubias, n_ref, c_ref, nt_ref, ct_ref, wu_ref, wd_ref, gu_ref, gd_ref, gub_ref, act_ref, grad_ref, add
    )
    push(block_of, row_of, keep_ref, send_ref, ((gu_ref, 0, 256, out_sem.at[0]), (gd_ref, 256, 256, out_sem.at[1])))
    both = jnp.concatenate((att_ref[0], att_ref[1]), axis=0)
    go_ref[...] = dot(turned_ref[...], both).astype(BF16)
    push(block_of, row_of, keep_ref, send_ref, ((go_ref, 512, 128, out_sem.at[2]),))
    pltpu.make_async_copy(gu_ref, gu_ref, out_sem.at[0]).wait()
    pltpu.make_async_copy(gd_ref, gd_ref, out_sem.at[1]).wait()
    pltpu.make_async_copy(go_ref, go_ref, out_sem.at[2]).wait()


def attend_back_kernel(mi, place, offsets, lengths, qkv_ref, skv_ref, lse_ref, gatt_ref, *refs):
    grad_ref, pooled_ref, bias_ref = refs[-3:]
    rows = qkv_ref.shape[1]
    tiles = rows // SPAN
    summaries = skv_ref.shape[1]
    fill_masks(place, offsets, lengths, mi, bias_ref, tiles, summaries, summaries * SPAN)

    def heads(pair, carry):
        lanes = pl.ds(pl.multiple_of(pair * LANES, LANES), LANES)

        def columns(i):
            return pl.ds(pl.multiple_of(pair * 384 + i * LANES, LANES), LANES)

        _, skeys, svalues = pair_of(skv_ref, slice(None), pair)
        skeys_t = skeys.T
        sum_k = jnp.zeros((summaries, LANES), F32)
        sum_v = jnp.zeros((summaries, LANES), F32)
        held = []
        for t in range(tiles):
            here = slice(t * SPAN, (t + 1) * SPAN)
            queries, keys, values = pair_of(qkv_ref, here, pair)
            queries = split_heads(queries * SCALE)
            grads = split_heads(gatt_ref[0, here, lanes])
            bias = bias_ref[t]
            scores = dot_cols(jnp.concatenate((keys, skeys), axis=0), queries)
            gprobs = dot_cols(jnp.concatenate((values, svalues), axis=0), grads)
            held.append((queries, keys, grads, scores + jnp.concatenate((bias, bias), axis=1), gprobs))
        for t, (queries, keys, grads, scores, gprobs) in enumerate(held):
            here = slice(t * SPAN, (t + 1) * SPAN)
            probs = jnp.exp(scores - lse_ref[0, pair, t])
            delta = jnp.sum(probs * gprobs, axis=0, keepdims=True)
            gscores = (probs * (gprobs - delta)).astype(BF16)
            keys_t = jnp.concatenate((keys.T, skeys_t), axis=1)
            grad_q = join_heads(dot(keys_t, gscores)) * SCALE
            grad_k = dot(gscores, queries)
            grad_v = dot(probs.astype(BF16), grads)
            grad_ref[0, here, columns(0)] = grad_q.astype(BF16)
            grad_ref[0, here, columns(1)] = grad_k[:SPAN].astype(BF16)
            grad_ref[0, here, columns(2)] = grad_v[:SPAN].astype(BF16)
            sum_k += grad_k[SPAN:]
            sum_v += grad_v[SPAN:]
        pooled_ref[0, :, columns(0)] = jnp.zeros((summaries, LANES), BF16)
        pooled_ref[0, :, columns(1)] = sum_k.astype(BF16)
        pooled_ref[0, :, columns(2)] = sum_v.astype(BF16)
        return carry

    lax.fori_loop(0, 4, heads, 0)


def weights_back_kernel(
    apart, place, offsets, lengths, block_of, row_of, slots_ref, xs_ref, grad_ref, pooled_ref, sums_ref, w_ref,
    gain, shift, small_ref, down_ref, gub1_ref, gub2_ref, line_ref, keep_ref, send_ref, *refs
):
    if apart:
        all_ref, *refs = refs
    gwb_ref, back_ref, stack_ref, pad_ref, sem = refs
    rows = xs_ref.shape[1]
    summaries = pooled_ref.shape[1]
    half = block_of.shape[0] // 2
    shard = keep_ref.shape[0] // half
    turned = []
    column = jnp.zeros((1, 3 * D), F32)
    for mi in range(2):
        _, offset, ends = row_info(place, offsets, lengths, mi)
        first, last = summary_range(iota((summaries, 1), 0), offset, ends)
        root = jnp.sqrt((last - first + 1).astype(F32))
        hat, _ = unit(xs_ref[mi].astype(F32))
        turned += [hat.astype(BF16).T, sums_ref[mi].astype(BF16).T]
        column += jnp.sum(grad_ref[mi].astype(F32), axis=0, keepdims=True)
        column += jnp.sum(root * pooled_ref[mi].astype(F32), axis=0, keepdims=True)
        back_ref[mi] = dot_cols(pooled_ref[mi], w_ref[...]).astype(BF16)
    turned = jnp.concatenate(turned, axis=1)
    gain_col, shift_col = gain[...].T, shift[...].T
    grad_gain = jnp.zeros((D, 1), F32)
    grad_shift = jnp.zeros((D, 1), F32)
    for m in range(4):
        cols = slice(m * 384, (m + 1) * 384)
        lanes = slice(m * LANES, (m + 1) * LANES)
        grads = jnp.concatenate([ref[mi, :, cols] for mi in range(2) for ref in (grad_ref, pooled_ref)], axis=0)
        hats, w, sums = dot(turned, grads), w_ref[:, cols].astype(F32), column[:, cols]
        grad_gain += jnp.sum(hats * w, axis=1, keepdims=True)
        grad_shift += jnp.sum(sums * w, axis=1, keepdims=True)
        gwb_ref[:, cols] = (hats * gain_col + shift_col * sums).astype(BF16)
        line_ref[10:11, lanes] = sums[:, :128]
        line_ref[11:12, lanes] = sums[:, 256:]
    line_ref[8:9, :] = grad_gain.T
    line_ref[9:10, :] = grad_shift.T
    line_ref[0:3, :] = small_ref[0:3, :]
    line_ref[3:4, :] = down_ref[...]
    for i in range(4):
        for j, ref in enumerate((gub1_ref, gub2_ref)):
            line_ref[4 + i : 5 + i, j * 256 : (j + 1) * 256] = ref[:, i * 256 : (i + 1) * 256]
    line_ref[12:16, :] = jnp.zeros((4, D), F32)
    for base in range(0, stack_ref.shape[0], 32):
        names = [slots_ref[mi : mi + 1, 16 * base : 16 * base + 512] for mi in range(2)]
        spread = [
            jnp.where(iota((summaries, 1), 0) == named, 1.0, 0.0).astype(BF16).T for named in names
        ]
        piece = (dot(spread[0], back_ref[0]) + dot(spread[1], back_ref[1])).astype(BF16)
        for lane in range(D // LANES):
            part = piece[:, lane * LANES : (lane + 1) * LANES]
            stack_ref[base : base + 32, 16 * lane : 16 * lane + 16, :] = part.reshape(32, 16, LANES)

    def emit(d, carry):
        for target, slot in ((keep_ref, d), (send_ref, half + d)):
            first_row = pl.multiple_of(row_of[slot] * shard, 16)
            cols = pl.ds(pl.multiple_of(block_of[slot] * 384, 128), 384)
            here = target.at[pl.ds(pl.multiple_of(d * shard, 16), shard), :]
            pltpu.make_async_copy(
                gwb_ref.at[pl.ds(first_row, shard), cols], here.at[:, 0:384], sem.at[0]
            ).start()
            if not apart:
                pltpu.make_async_copy(stack_ref.at[slot], here.at[:, 384:512], sem.at[1]).start()
        return carry

    lax.fori_loop(0, half, emit, 0)
    if apart:
        pltpu.make_async_copy(stack_ref, all_ref, sem.at[1]).start()
    else:
        high = line_ref[...].astype(BF16)
        pad_ref[0:16, :] = high
        pad_ref[16:32, :] = (line_ref[...] - high.astype(F32)).astype(BF16)
        size = half * shard
        copy = pltpu.make_async_copy(pad_ref, send_ref.at[size : size + 32, :], sem.at[2])
        copy.start()
        copy.wait()
    pltpu.make_async_copy(gwb_ref, gwb_ref, sem.at[0]).wait()
    pltpu.make_async_copy(stack_ref, stack_ref, sem.at[1]).wait()


def rows_back_kernel(grad_ref, w_ref, xs_ref, gmid_ref, result_ref, gain, part_ref, edge_ref):
    grad = dot_cols(grad_ref[0], w_ref[...]) * gain[...]
    hat, inverse = unit(xs_ref[0].astype(F32))
    part = gmid_ref[0].astype(F32) + unit_back(grad, hat, inverse)
    part_ref[0] = part
    edge_ref[0, 0] = part[0:SPAN].astype(BF16)
    edge_ref[1, 0] = result_ref[0]


def fold_kernel(keep_ref, mine_ref, got_ref, next_ref, *send_refs):
    size = keep_ref.shape[0]
    part = size // (1 + len(send_refs))
    mine = mine_ref[0:16, :].astype(F32) + mine_ref[16:32, :].astype(F32)
    lines = mine + (got_ref[size : size + 16, :].astype(F32) + got_ref[size + 16 : size + 32, :].astype(F32))
    high = lines.astype(BF16)
    rest = (lines - high.astype(F32)).astype(BF16)
    next_ref[...] = keep_ref[0:part, :].astype(F32) + got_ref[0:part, :].astype(F32)
    for i, send_ref in enumerate(send_refs):
        here = slice((i + 1) * part, (i + 2) * part)
        send_ref[0:part, :] = (keep_ref[here, :].astype(F32) + got_ref[here, :].astype(F32)).astype(BF16)
        send_ref[part : part + 16, :] = high
        if len(send_refs) == 1:
            send_ref[part + 16 : part + 32, :] = rest


def lines_of(ref):
    return ref[ref.shape[0] - 16 :, :].astype(F32)


def two_tiles(ref, right, mi, t):
    if (t + 2) * SPAN <= ref.shape[1]:
        return ref[mi, t * SPAN : (t + 2) * SPAN, :]
    return jnp.concatenate((ref[mi, t * SPAN :, :], right[mi].astype(ref.dtype)), axis=0)


def unroll_kernel(offsets, result_ref, right_ref, x_ref, out_ref, hat_ref, inverse_ref, wide_ref):
    mi = pl.program_id(0)
    for t in range(result_ref.shape[1] // SPAN):
        here = slice(t * SPAN, (t + 1) * SPAN)
        wide_ref[...] = two_tiles(result_ref, right_ref.at[0], 0, t).astype(F32)
        out_ref[0, here, :] = roll_rows(wide_ref, SPAN - offsets[mi]).astype(BF16)
        hat, inverse = unit(x_ref[0, here, :].astype(F32))
        hat_ref[0, here, :] = hat.astype(BF16)
        inverse_ref[0, here, :] = jnp.broadcast_to(inverse, (SPAN, LANES))


def finish_rest_kernel(keep_ref, got_ref, wo_ref, wu_ref, wd_ref):
    total = keep_ref[0] + got_ref[0].astype(F32)
    for i in range(2):
        wu_ref[:, i * 256 : (i + 1) * 256] = total[:, i * 512 : i * 512 + 256]
        wd_ref[:, i * 256 : (i + 1) * 256] = total[:, i * 512 + 256 : i * 512 + 512]
    wo_ref[...] = total[:, 1024:]


def finish_kernel(
    direct, place, offsets, lengths, hat_ref, inverse_ref, part_ref, right_ref, gain, *refs
):
    if direct:
        keep_ref, mine_ref, a_ref, b_ref, c_ref, out_ref, wq_ref, wk_ref, wv_ref, *line_refs, wide_ref = refs
        size = keep_ref.shape[0]
        total = (keep_ref[...] + a_ref[0:size, :].astype(F32)) + (
            b_ref[0:size, :].astype(F32) + c_ref[0:size, :].astype(F32)
        )
        wq_ref[...], wk_ref[...], wv_ref[...] = total[:, :128], total[:, 128:256], total[:, 256:384]
        pooled = total[:, 384:]
        lines = (lines_of(mine_ref) + lines_of(a_ref)) + (lines_of(b_ref) + lines_of(c_ref))
        ub_ref, *line_refs = line_refs
        for i in range(4):
            ub_ref[:, i * D : (i + 1) * D] = lines[4 + i : 5 + i, :]
        for ref, i in zip(line_refs, (0, 1, 2, 3, 8, 9, 10, 11)):
            ref[...] = lines[i : i + 1, :]
    else:
        pooled_ref, out_ref, wide_ref = refs
        pooled = pooled_ref[...]
    rows = hat_ref.shape[1]
    for mi in range(2):
        dev, offset, ends = row_info(place, offsets, lengths, mi)
        first, last = summary_range(dev * (rows // SPAN) + iota((8, 1), 0), offset, ends)
        lows = jnp.concatenate(
            [pooled[16 * i + 8 * mi : 16 * i + 8 * mi + 8, :] for i in range(D // LANES)], axis=1
        )
        lows = lows * gain[...] * lax.rsqrt((last - first + 1).astype(F32))
        level = (lows - jnp.mean(lows, axis=-1, keepdims=True)).astype(BF16)
        lows = lows.astype(BF16)
        first, last = summary_range(dev * (rows // SPAN) + iota((1, 8), 1), offset, ends)
        for t in range(rows // SPAN):
            here = slice(t * SPAN, (t + 1) * SPAN)
            pos = dev * rows + t * SPAN + iota((SPAN, 1), 0)
            member = jnp.where((pos >= first) & (pos <= last), 1.0, 0.0)
            hat = hat_ref[mi, here, :]
            slope = jnp.sum(member * dot_cols(hat, lows), axis=1, keepdims=True) * (1.0 / D)
            inverse = inverse_ref[mi, here, 0:1]
            wide_ref[...] = two_tiles(part_ref, right_ref.at[0], mi, t)
            own = roll_rows(wide_ref, SPAN - offset)
            out_ref[mi, here, :] = own + (dot(member.astype(BF16), level) - hat.astype(F32) * slope) * inverse


def call(kernel, outs, in_specs, out_specs=None, scratch=(), limit=8, **more):
    return pl.pallas_call(
        kernel,
        out_shape=outs,
        in_specs=in_specs,
        out_specs=out_specs if out_specs is not None else [VMEM] * len(outs),
        scratch_shapes=list(scratch),
        compiler_params=pltpu.CompilerParams(vmem_limit_bytes=limit * MIB),
        cost_estimate=pl.CostEstimate(flops=1, bytes_accessed=1, transcendentals=0),
        **more,
    )


def call_row(kernel, mi, facts, arrays, outs, before, scratch, **more):
    def block(dims):
        return pl.BlockSpec((1,) + dims[1:], lambda i: (mi,) + (0,) * (len(dims) - 1))

    aliases = {3 + len(arrays) + i: i for i in range(len(before))}
    return call(
        partial(kernel, mi), outs, [SMEM] * 3 + [block(a.shape) for a in arrays] + [ANY] * len(before),
        [block(o.shape) for o in outs], scratch, grid=(1,), input_output_aliases=aliases, **more,
    )(*facts, *arrays, *before)


def tie(value, *others):
    return lax.optimization_barrier((value,) + others)[0]


def per_device(
    block_input, cotangent, span_offset, doc_lengths, ln1_gain, ln1_bias, w_query, w_key, w_value,
    query_bias, value_bias, w_out, out_bias, ln2_gain, ln2_bias, w_up, up_bias, w_down, down_bias,
):
    groups, ranks = lax.axis_size("seq"), lax.axis_size("mp")
    count = groups * ranks
    mp_index = lax.axis_index("mp")
    dev = lax.axis_index("seq") * ranks + mp_index
    rows = block_input.shape[1]
    tiles = rows // SPAN
    summaries = tiles * count
    shard = w_query.shape[0]
    bits = count.bit_length() - 1
    stages = [(b, b) for b in range(bits - 1, 2, -1)] + [(1, 2), (2, 1)]
    direct = shard == 64

    def swap(value, stage):
        pairs = [(i, i ^ (1 << stage[i & 1])) for i in range(count)]
        return lax.ppermute(value, AXES, pairs)

    def turn(value, by):
        return lax.ppermute(value, AXES, [(i, (i + by) % count) for i in range(count)])

    core = dev & 1
    slot = jnp.arange(count, dtype=jnp.int32)
    far = slot // (count // 2)
    mask = far
    for i, (even, odd) in enumerate(stages):
        where = jnp.where((core ^ far) == 0, even, odd)
        mask = mask | (((slot >> i) & 1) << where)
    owner = dev ^ mask
    if not direct:
        owner = slot
    member_slot = jnp.arange(16, dtype=jnp.int32)
    slots = owner[:, None] * tiles + (member_slot % 8)[None, :]
    valid = (member_slot % 8 <= tiles)[None, :]
    slots = jnp.stack(
        [
            jnp.where(valid & (member_slot // 8 == mi)[None, :], slots, -1).reshape(-1)
            for mi in range(2)
        ]
    )
    block_of, row_of = owner % ranks, owner // ranks
    facts = (jnp.stack((dev, mp_index)), span_offset, doc_lengths)

    def reach(value, flip):
        return lax.ppermute(value, AXES, [(i, i ^ flip) for i in range(count)])

    def spread(values):
        return [reach(value, flip) for value, flip in zip(values, (16, 8, 24))]

    def join(near, far):
        return jnp.concatenate((near, far), axis=0)

    def fold(keep, got):
        total = keep + got.astype(F32)
        half = total.shape[0] // 2
        return total[:half], total[half:].astype(BF16)

    def whole_blocks(arrays):
        return [pl.BlockSpec(a.shape, lambda i, n=len(a.shape): (0,) * n) for a in arrays]

    def fold_lines(keep, sent, got, sends=1):
        size = keep.shape[0]
        part = size // (1 + sends)
        outs = [shape((part, D), F32)] + [shape((part + (32 if sends == 1 else 16), D), BF16)] * sends
        mine = pl.BlockSpec((32, D), lambda i: (size // 32, 0))
        both = whole_blocks((keep, got))
        return call(fold_kernel, outs, [both[0], mine, both[1]], whole_blocks(outs), grid=(1,))(keep, sent, got)

    def gather_whole(value):
        both = lax.all_gather(value, "seq", axis=0, tiled=True)
        both = lax.all_gather(both, "mp", axis=0)
        return both[: ranks // 2], both[ranks // 2 :]

    def scatter_whole(keep, send):
        both = jnp.concatenate((keep, send), axis=0).astype(F32)
        total = lax.psum_scatter(both, "mp", scatter_dimension=0, tiled=True)[0]
        return lax.psum_scatter(total, "seq", scatter_dimension=0, tiled=True)

    def row(vector):
        return vector[None, :]

    def shape(dims, kind):
        return jax.ShapeDtypeStruct(dims, kind)

    half, tall = (count // 2, shard) if direct else (ranks // 2, shard * groups)
    width = 4 * LANES if direct else 3 * LANES
    apart = not direct
    wide, three = (2, rows, D), (2, rows, 3 * D)
    flat, pooled_dims = (2 * rows, D), (2, summaries, D)
    room = 12 if direct else 56
    masks = [pltpu.VMEM((tiles, SPAN + summaries, SPAN), F32)]

    def prepare():
        return call(
            prepare_kernel, [shape((1, max(shard, 64), D), BF16), shape((1, shard, 1152), BF16), shape((2, SPAN, D), BF16)],
            [SMEM] * 3 + [HBM] * 8, [VMEM] * 3,
            scratch=[pltpu.VMEM(wide, BF16), pltpu.SemaphoreType.DMA((11,))],
            limit=56,
        )(*facts, block_input, cotangent, w_query, w_key, w_value, w_out.T, w_up, w_down.T)

    part_a, w_rest, cot_edge = prepare()
    x_edge = block_input[:, rows - SPAN :]
    if direct:
        got_a = spread([part_a] * 3)
        part_b = tie(w_rest, got_a[0])
        got_b = swap(part_b, stages[0])
        part_a = jnp.concatenate([part_a] + got_a, axis=0)
        x_left = turn(tie(x_edge, part_a), 1)
        got_a = swap(part_a, stages[2])
        part_a = join(part_a, got_a)
        part_b = join(part_b, tie(got_b, part_a))
        got_a, got_b = swap(part_a, stages[3]), swap(part_b, stages[1])
        near_a = join(part_a, tie(got_a, x_left))
        far_a = swap(near_a, (0, 0))
        part_b = join(part_b, tie(got_b, near_a))
        got_b = swap(part_b, stages[2])
        more = ()
    else:
        x_left, cot_left = turn(x_edge, 1), turn(cot_edge, 1)
        near_a, far_a = gather_whole(part_a[0, :shard, :384])
        near_b, far_b = gather_whole(w_rest[0])
        near_1, near_2, far_1, far_2 = (a[:, :, i : i + w] for a in (near_b, far_b) for i, w in ((0, 640), (640, 512)))
        more = (lax.all_gather(part_a[0, :64, 384:], AXES, axis=0),)
        block_of, row_of = jnp.arange(ranks, dtype=jnp.int32), jnp.zeros((ranks,), jnp.int32)

    xs, qkv, skv, sums, w_full = call(
        partial(project_kernel, apart),
        [shape(wide, BF16), shape(three, BF16), shape((2, summaries, 3 * D), BF16), shape(pooled_dims, F32)]
        + [shape((D, 3 * D), BF16)],
        [SMEM] * 5 + [VMEM] * 7 + [ANY] * (2 + len(more)),
        scratch=[
            pltpu.VMEM((count, 64, LANES), BF16),
            pltpu.VMEM((rows + SPAN, D), F32),
            pltpu.VMEM((2, rows + 2 * summaries, D), BF16),
            pltpu.SemaphoreType.DMA((2,)),
        ],
        limit=24 if direct else 56,
    )(
        *facts, block_of, row_of, slots, block_input, x_left, row(ln1_gain), row(ln1_bias),
        row(query_bias), row(value_bias), near_a, far_a, *more,
    )
    outs = [shape(wide, BF16), shape((2, 4, tiles, 1, 2 * SPAN), F32)]
    if direct:
        cot_left = turn(tie(cot_edge, near_a), 1)
        part_b = join(part_b, tie(got_b, skv, cot_left))
        part_1, part_2 = part_b[:, :, :640], part_b[:, :, 640:]
        got_1 = swap(part_1, stages[3])
        qkv = tie(qkv, part_1)
    seen = call_row(attend_kernel, 0, facts, (qkv, skv), outs, (), masks, limit=room)
    att, lse = call_row(attend_kernel, 1, facts, (qkv, skv), outs, tuple(seen), masks, limit=room)
    if direct:
        near_1 = join(part_1, tie(got_1, att))
        far_1 = swap(near_1, (0, 0))
        got_2 = swap(tie(part_2, near_1), stages[3])
    tall_low, tall_float = shape(flat, BF16), shape(flat, F32)
    weights = [pltpu.VMEM((D, 2 * rows), BF16)] * 2 + [pltpu.VMEM((D, FF // 2), BF16)] * 4
    weights += [pltpu.VMEM((2 * rows, FF // 2), BF16)] * 2
    *kept, gub_1, down_b, keep_1, send_1 = call(
        mlp_first_kernel,
        [tall_float] + [tall_low] * 4 + [shape((D, D), BF16)]
        + [shape((1, FF // 2), F32), shape((1, D), F32)] + [shape((half, tall, 512), BF16)] * 2,
        [SMEM] * 4 + [VMEM] * 8 + [HBM] + [ANY] * 2,
        [VMEM] * 8 + [ANY] * 2,
        scratch=weights
        + [pltpu.VMEM((rows + SPAN, D), F32), pltpu.VMEM(wide, BF16)]
        + [pltpu.SemaphoreType.DMA((4,)), pltpu.SemaphoreType.DMA((2,))],
        limit=28,
    )(
        facts[0], span_offset, block_of, row_of, xs, att, cot_left, row(out_bias), row(ln2_gain), row(ln2_bias),
        row(up_bias), row(down_bias), cotangent, near_1, far_1,
    )
    if direct:
        near_2 = join(part_2, tie(got_2, kept[0]))
        far_2 = swap(near_2, (0, 0))
        got_1 = swap(tie(send_1, near_2), (0, 0))
        keep_1, send_1 = fold(keep_1.astype(F32), got_1)
        got_1 = swap(send_1, stages[3])
        near_2 = tie(near_2, send_1)
    result, gmid, gatt, small_b, gub_2, keep_2, send_2 = call(
        mlp_second_kernel,
        [shape(wide, BF16)] * 3 + [shape((8, D), F32)]
        + [shape((1, FF // 2), F32)] + [shape((half, tall, 640), BF16)] * 2,
        [SMEM] * 2 + [VMEM] * 9 + [ANY] * 2,
        [VMEM] * 5 + [ANY] * 2,
        scratch=weights
        + [pltpu.VMEM((D, D), BF16), pltpu.VMEM((D, 2 * rows), BF16)]
        + [pltpu.SemaphoreType.DMA((2,)), pltpu.SemaphoreType.DMA((3,))],
        limit=28,
    )(block_of, row_of, att, row(ln2_gain), row(up_bias), *kept, near_2, far_2)
    gubs = (gub_1, gub_2)
    arrays = (qkv, skv, lse, gatt)
    outs = [shape(three, BF16), shape((2, summaries, 3 * D), BF16)]
    if direct:
        keep_1, send_1 = fold(keep_1, tie(got_1, send_2))
        got_2 = swap(tie(send_2, send_1), (0, 0))
        got_1 = swap(send_1, stages[2])
    grads = call_row(attend_back_kernel, 0, facts, arrays, outs, (), masks, limit=room)
    if direct:
        keep_2, send_2 = fold(keep_2.astype(F32), tie(got_2, grads[0]))
        got_2 = swap(send_2, stages[3])
        grads = [tie(grads[0], send_2)] + list(grads[1:])
    grads = call_row(attend_back_kernel, 1, facts, arrays, outs, tuple(grads), masks, limit=room)
    if direct:
        keep_1, send_1 = fold(keep_1, tie(got_1, grads[0]))
        grads = [tie(grads[0], send_1), grads[1]]
    lines, keep_a, send_a, *more = call(
        partial(weights_back_kernel, apart),
        [shape((16, D), F32)]
        + [shape((half * tall, width), BF16), shape((half * tall + (32 if direct else 0), width), BF16)]
        + [shape((count, 64, LANES), BF16)] * apart,
        [SMEM] * 5 + [VMEM] * 12,
        [VMEM] + [ANY] * (2 + apart),
        scratch=[
            pltpu.VMEM((D, 3 * D), BF16), pltpu.VMEM(pooled_dims, BF16), pltpu.VMEM((count, 64, LANES), BF16),
            pltpu.VMEM((32, D), BF16), pltpu.SemaphoreType.DMA((3,)),
        ],
        limit=24 if direct else 56,
    )(
        *facts, block_of, row_of, slots, xs, *grads, sums, w_full, row(ln1_gain), row(ln1_bias), small_b, down_b, *gubs,
    )

    def by_row(dims):
        return pl.BlockSpec((1,) + dims[1:], lambda i: (i,) + (0,) * (len(dims) - 1))

    once = pl.BlockSpec((1, D), lambda i: (0, 0))
    edge_dims = (2, SPAN, D)

    def rows_back(*after):
        return call(
            rows_back_kernel, [shape(wide, F32), shape((2,) + edge_dims, BF16)],
            [by_row(three), pl.BlockSpec((D, 3 * D), lambda i: (0, 0)), by_row(wide), by_row(wide)]
            + [by_row(edge_dims), once],
            [by_row(wide), pl.BlockSpec((2, 1, SPAN, D), lambda i: (0, i, 0, 0))], grid=(2,), limit=16,
        )(grads[0], tie(w_full, *after), xs, gmid, result, row(ln1_gain))

    def unroll(back):
        return call(
            unroll_kernel, [shape(wide, BF16)] * 2 + [shape((2, rows, LANES), F32)],
            [SMEM, by_row(wide), pl.BlockSpec((1, 1, SPAN, D), lambda i: (1, i, 0, 0)), by_row(wide)], [by_row(wide)] * 2 + [by_row((2, rows, LANES))],
            [pltpu.VMEM((2 * SPAN, D), F32)], grid=(2,),
        )(span_offset, result, back, block_input)

    final = [SMEM] * 3 + [VMEM] * 5
    rolled = [pltpu.VMEM((2 * SPAN, D), F32)]
    if direct:
        got_a = swap(send_a, (0, 0))
        keep_2, send_2 = fold(keep_2, tie(got_2, send_a))
        got_2 = swap(send_2, stages[2])
        keep_a, send_a = fold_lines(keep_a, send_a, tie(got_a, send_2))
        got_a = swap(send_a, stages[3])
        part, edge = rows_back(send_a)
        keep_2, send_2 = fold(keep_2, tie(got_2, part))
        keep_b, send_b = (jnp.concatenate(a, axis=2) for a in ((keep_1, keep_2), (send_1, send_2)))
        got_b = swap(send_b, stages[1])
        back = turn(tie(edge, send_b), -1)
        keep_a, send_a = fold_lines(keep_a, send_a, tie(got_a, send_b))
        got_a = swap(send_a, stages[2])
        keep_b, send_b = fold(keep_b, tie(got_b, send_a))
        got_b = swap(send_b, stages[0])
        keep_a, *send_a = fold_lines(keep_a, send_a, tie(got_a, send_b), 3)
        got_a = spread(send_a)
        result_own, *hats = unroll(tie(back, send_a[0]))
        grad_wo, grad_wu, grad_wd = call(
            finish_rest_kernel, [shape((shard, LANES), F32), shape((shard, 512), F32), shape((shard, 512), F32)],
            [VMEM] * 2,
        )(keep_b, tie(got_b, send_a[0]))
        input_grad, grad_wq, grad_wk, grad_wv, grad_ub, *small = call(
            partial(finish_kernel, True),
            [shape(wide, F32)] + [shape((shard, LANES), F32)] * 3 + [shape((1, FF), F32)] + [shape((1, D), F32)] * 8,
            final + [VMEM] * 5, scratch=rolled, limit=16,
        )(*facts, *hats, part, back, row(ln1_gain), keep_a, send_a[0], *(tie(got, grad_wo) for got in got_a))
        grad_wo, grad_wd = grad_wo.T, grad_wd.T
        small = [a.reshape(D) for a in small]
        grad_ub = grad_ub.reshape(FF)
    else:
        keep_a, send_a = (a.reshape(half, tall, width) for a in (keep_a, send_a))
        part, edge = rows_back()
        back = turn(edge, -1)
        result_own, *hats = unroll(back)
        sum_a, sum_1, sum_2 = (scatter_whole(*a) for a in ((keep_a, send_a), (keep_1, send_1), (keep_2, send_2)))
        grad_wq, grad_wk, grad_wv = (sum_a[:, i : i + LANES] for i in (0, 128, 256))
        grad_wo = sum_2[:, 512:].T
        grad_wu, grad_wd = (
            jnp.concatenate((sum_1[:, i : i + 256], sum_2[:, i : i + 256]), axis=1) for i in (0, 256)
        )
        grad_wd = grad_wd.T
        pooled = lax.psum_scatter(more[0].astype(F32), AXES, scatter_dimension=0, tiled=True)[0]
        lines = lax.psum(lines, AXES)
        grad_ub = lines[4:8].reshape(FF)
        small = [lines[i] for i in (0, 1, 2, 3, 8, 9, 10, 11)]
        input_grad = call(partial(finish_kernel, False), [shape(wide, F32)], final + [VMEM], scratch=rolled, limit=16)(
            *facts, *hats, part, back, row(ln1_gain), pooled
        )[0]
    grad_gain_two, grad_shift_two, grad_obias, grad_dbias, grad_gain_one, grad_shift_one, grad_qb, grad_vb = small
    return (
        result_own,
        input_grad,
        grad_gain_one,
        grad_shift_one,
        grad_wq,
        grad_wk,
        grad_wv,
        grad_qb,
        grad_vb,
        grad_wo,
        grad_obias,
        grad_gain_two,
        grad_shift_two,
        grad_wu,
        grad_ub,
        grad_wd,
        grad_dbias,
    )


def solution(mesh):
    vector, matrix, turned = P(), P("seq", "mp"), P("mp", "seq")
    own, group = P(None, ("seq", "mp"), None), P(None, "seq", None)
    return jax.shard_map(
        per_device,
        mesh=mesh,
        in_specs=(own, group, vector, vector, vector, vector, matrix, matrix, matrix, vector, vector)
        + (turned, vector, vector, vector, matrix, vector, turned, vector),
        out_specs=(own, own, vector, vector, matrix, matrix, matrix, vector, vector, turned, vector)
        + (vector, vector, matrix, vector, turned, vector),
        check_vma=False,
    )
```

```python
from functools import partial
import math

import jax
import jax.numpy as jnp
from jax import lax
from jax.experimental import pallas as pl
from jax.experimental.pallas import tpu as pltpu
from jax.sharding import PartitionSpec as P

D = 512
FF = 2048
HEAD_DIM = 64
SPAN = 128
LANES = 128
STEP = 512
EPSILON = 1e-05
NEGATIVE = -1e30
SCALE = 1.0 / math.sqrt(HEAD_DIM)
F32 = jnp.float32
BF16 = jnp.bfloat16
AXES = ("seq", "mp")
MIB = 1 << 20
VMEM = pl.BlockSpec(memory_space=pltpu.VMEM)
SMEM = pl.BlockSpec(memory_space=pltpu.SMEM)
ANY = pl.BlockSpec(memory_space=pl.ANY)
HBM = pl.BlockSpec(memory_space=pltpu.HBM)


def dot(left, right):
    return lax.dot_general(left, right, (((1,), (0,)), ((), ())), preferred_element_type=F32)


def dot_cols(left, right):
    return lax.dot_general(left, right, (((1,), (1,)), ((), ())), preferred_element_type=F32)


def unit(rows):
    centred = rows - jnp.mean(rows, axis=-1, keepdims=True)
    inverse = lax.rsqrt(jnp.mean(centred * centred, axis=-1, keepdims=True) + EPSILON)
    return centred * inverse, inverse


def unit_back(grad, hat, inverse):
    shift = jnp.mean(grad, axis=-1, keepdims=True)
    slope = jnp.mean(grad * hat, axis=-1, keepdims=True)
    return (grad - shift - hat * slope) * inverse


def row_info(place, offsets, lengths, mi):
    ends = []
    for c in range(lengths.shape[1]):
        ends.append(lengths[mi, c] + (ends[-1] if ends else 0))
    return place[0], offsets[mi], ends


def doc_start(positions, ends):
    start = jnp.zeros_like(positions)
    for end in ends:
        start = jnp.where(positions >= end, end, start)
    return start


def summary_range(summary_ids, offset, ends):
    last = offset - 1 + SPAN * summary_ids
    first = jnp.maximum(doc_start(last, ends), last - (SPAN - 1))
    return first, last


def iota(shape, dim):
    return lax.broadcasted_iota(jnp.int32, shape, dim)


def roll_rows(ref, by):
    whole = pl.multiple_of((by // 8) * 8, 8)
    return pltpu.roll(ref[pl.ds(whole, SPAN + 8), :], SPAN + 8 - (by - whole), axis=0)[:SPAN]


def prepare_kernel(
    place, offsets, lengths, x_ref, cot_ref, wq_ref, wk_ref, wv_ref, wo_ref, wu_ref, wd_ref,
    out_ref, rest_ref, edge_ref, rows_ref, sem
):
    rows = x_ref.shape[1]
    last_rows = pl.multiple_of(place[1] * rows + (rows - SPAN), SPAN)
    shard = wq_ref.shape[0]
    copies = [pltpu.make_async_copy(x_ref.at[mi], rows_ref.at[mi], sem.at[mi]) for mi in range(2)]
    copies += [
        pltpu.make_async_copy(ref, out_ref.at[0, 0:shard, i * LANES : (i + 1) * LANES], sem.at[2 + i])
        for i, ref in enumerate((wq_ref, wk_ref, wv_ref))
    ]
    copies.append(pltpu.make_async_copy(cot_ref.at[:, pl.ds(last_rows, SPAN), :], edge_ref, sem.at[5]))
    copies.append(pltpu.make_async_copy(wo_ref, rest_ref.at[0, :, 0:128], sem.at[6]))
    for i, (ref, first) in enumerate(((wu_ref, 0), (wd_ref, 0), (wu_ref, 256), (wd_ref, 256))):
        target = rest_ref.at[0, :, 128 + 256 * i : 384 + 256 * i]
        copies.append(pltpu.make_async_copy(ref.at[:, first : first + 256], target, sem.at[7 + i]))
    for copy in copies:
        copy.start()
    sums = []
    for mi in range(2):
        dev, offset, ends = row_info(place, offsets, lengths, mi)
        first, last = summary_range(dev * (rows // SPAN) + iota((8, 1), 0), offset, ends)
        pos = dev * rows + iota((1, rows), 1)
        member = jnp.where((pos >= first) & (pos <= last), 1.0, 0.0).astype(BF16)
        copies[mi].wait()
        hat, _ = unit(rows_ref[mi].astype(F32))
        high = hat.astype(BF16)
        rest = (hat - high.astype(F32)).astype(BF16)
        total = dot(member, high) + dot(member, rest)
        sums.append(total * lax.rsqrt((last - first + 1).astype(F32)))
    both = jnp.concatenate(sums, axis=0).astype(BF16)
    for copy in copies[2:]:
        copy.wait()
    for lane in range(D // LANES):
        out_ref[0, 16 * lane : 16 * lane + 16, 384:512] = both[:, lane * LANES : (lane + 1) * LANES]


def fill_masks(place, offsets, lengths, mi, bias_ref, tiles, summaries, length):
    dev, offset, ends = row_info(place, offsets, lengths, mi)
    ends_col = offset - 1 + SPAN * iota((summaries, 1), 0)
    for t in range(tiles):
        base = SPAN * (dev * tiles + t) + offset - SPAN
        qpos = base + iota((1, SPAN), 1)
        qpos = jnp.where(qpos < 0, qpos + length, qpos)
        kpos = base + iota((SPAN, 1), 0)
        kpos = jnp.where(kpos < 0, kpos + length, kpos)
        span_first = jnp.where(qpos >= base + SPAN, base + length, base)
        doc_first = doc_start(qpos, ends)
        local_ok = (kpos >= jnp.maximum(doc_first, span_first)) & (kpos <= qpos)
        summary_ok = (ends_col >= doc_first) & (ends_col < span_first)
        bias_ref[t, 0:SPAN, :] = jnp.where(local_ok, 0.0, NEGATIVE)
        bias_ref[t, SPAN : SPAN + summaries, :] = jnp.where(summary_ok, 0.0, NEGATIVE)


def split_heads(pair):
    low = iota(pair.shape, 1) < HEAD_DIM
    zero = jnp.zeros_like(pair)
    return jnp.concatenate((jnp.where(low, pair, zero), jnp.where(low, zero, pair)), axis=0)


def join_heads(turned):
    half = turned.shape[1] // 2
    return jnp.concatenate((turned[:HEAD_DIM, :half], turned[HEAD_DIM:, half:]), axis=0).T


def project_kernel(
    apart, place_ref, offsets, lengths, block_of, row_of, slots_ref, x_ref, left_ref, gain, shift, qbias, vbias,
    near_ref, far_ref, *refs
):
    if apart:
        all_ref, *refs = refs
    xs_ref, qkv_ref, skv_ref, sums_ref, w_ref, stack_ref, wide_ref, rows_ref, sem = refs
    rows = x_ref.shape[1]
    tiles = rows // SPAN
    summaries = skv_ref.shape[1]
    half, shard, _ = near_ref.shape

    def place(d, carry):
        for source, slot in ((near_ref, d), (far_ref, half + d)):
            here = pl.ds(pl.multiple_of(row_of[slot] * shard, 16), shard)
            cols = pl.ds(pl.multiple_of(block_of[slot] * 384, 128), 384)
            pltpu.make_async_copy(source.at[d, :, 0:384], w_ref.at[here, cols], sem.at[0]).start()
            if not apart:
                pltpu.make_async_copy(
                    source.at[d, 0:64, 384:512], stack_ref.at[slot], sem.at[1]
                ).start()
        return carry

    lax.fori_loop(0, half, place, 0)
    if apart:
        pltpu.make_async_copy(all_ref, stack_ref, sem.at[1]).start()
    for mi in range(2):
        wide_ref[0:SPAN, :] = left_ref[mi].astype(F32)
        wide_ref[SPAN : SPAN + rows, :] = x_ref[mi].astype(F32)
        for t in range(tiles):
            here = slice(t * SPAN, (t + 1) * SPAN)
            rolled = roll_rows(wide_ref, t * SPAN + offsets[mi])
            xs_ref[mi, here, :] = rolled.astype(BF16)
            hat, _ = unit(rolled)
            rows_ref[mi, here, :] = (hat * gain[...] + shift[...]).astype(BF16)
    pltpu.make_async_copy(stack_ref, stack_ref, sem.at[1]).wait()
    roots = []
    for mi in range(2):
        _, offset, ends = row_info(place_ref, offsets, lengths, mi)
        first, last = summary_range(iota((summaries, 1), 0), offset, ends)
        root = jnp.sqrt((last - first + 1).astype(F32))
        roots.append(root)
        for base in range(0, stack_ref.shape[0], 32):
            named = slots_ref[mi : mi + 1, 16 * base : 16 * base + 512]
            pick = jnp.where(iota((summaries, 1), 0) == named, 1.0, 0.0).astype(BF16)
            piece = jnp.concatenate(
                [
                    stack_ref[base : base + 32, 16 * lane : 16 * lane + 16, :].reshape(512, LANES)
                    for lane in range(D // LANES)
                ],
                axis=1,
            )
            found = dot(pick, piece)
            sums_ref[mi] = found if base == 0 else sums_ref[mi] + found
        summed = sums_ref[mi] * gain[...] + root * shift[...]
        high = summed.astype(BF16)
        rows_ref[mi, rows : rows + summaries, :] = high
        rows_ref[mi, rows + summaries : rows + 2 * summaries, :] = (summed - high.astype(F32)).astype(BF16)
    pltpu.make_async_copy(w_ref, w_ref, sem.at[0]).wait()
    none = jnp.zeros((1, LANES), F32)

    def block(m, carry):
        lanes, cols = columns(m, LANES), columns(m, 384)
        bias = jnp.concatenate((qbias[:, lanes], none, vbias[:, lanes]), axis=1)
        for mi in range(2):
            projected = dot(rows_ref[mi], w_ref[:, cols])
            qkv_ref[mi, :, cols] = (projected[:rows] + bias).astype(BF16)
            pooled = projected[rows : rows + summaries] + projected[rows + summaries :]
            skv_ref[mi, :, cols] = (pooled + roots[mi] * bias).astype(BF16)
        return carry

    lax.fori_loop(0, 4, block, 0)


def pair_of(ref, here, pair):
    def part(i):
        return ref[0, here, pl.ds(pl.multiple_of(pair * 384 + i * LANES, LANES), LANES)]

    return part(0), part(1), part(2)


def attend_kernel(mi, place, offsets, lengths, qkv_ref, skv_ref, *refs):
    att_ref, lse_ref, bias_ref = refs[-3:]
    rows = qkv_ref.shape[1]
    tiles = rows // SPAN
    summaries = skv_ref.shape[1]
    fill_masks(place, offsets, lengths, mi, bias_ref, tiles, summaries, summaries * SPAN)

    def heads(pair, carry):
        lanes = pl.ds(pl.multiple_of(pair * LANES, LANES), LANES)
        _, skeys, svalues = pair_of(skv_ref, slice(None), pair)
        svalues = svalues.T
        spans = [pair_of(qkv_ref, slice(t * SPAN, (t + 1) * SPAN), pair) for t in range(tiles)]
        scores = []
        for t, (queries, keys, _) in enumerate(spans):
            bias = bias_ref[t]
            keys = jnp.concatenate((keys, skeys), axis=0)
            scores.append(dot_cols(keys, split_heads(queries * SCALE)) + jnp.concatenate((bias, bias), axis=1))
        probs = []
        for t in range(tiles):
            top = jnp.max(scores[t], axis=0, keepdims=True)
            grown = jnp.exp(scores[t] - top)
            total = jnp.sum(grown, axis=0, keepdims=True)
            probs.append((grown * (1.0 / total)).astype(BF16))
            lse_ref[0, pair, t] = top + jnp.log(total)
        for t, (_, _, values) in enumerate(spans):
            values = jnp.concatenate((values.T, svalues), axis=1)
            att_ref[0, t * SPAN : (t + 1) * SPAN, lanes] = join_heads(dot(values, probs[t])).astype(BF16)
        return carry

    lax.fori_loop(0, 4, heads, 0)


def gelu_pair(u):
    c0 = math.sqrt(2.0 / math.pi)
    square = u * u
    t = jnp.tanh(c0 * u * (1.0 + 0.044715 * square))
    half = 0.5 * (1.0 + t)
    slope = half + (0.5 * c0) * u * (1.0 - t * t) * (1.0 + (3 * 0.044715) * square)
    return u * half, slope


def columns(block, width):
    return pl.ds(pl.multiple_of(block * width, 128), width)


def mlp_half(half_id, ubias, n_ref, c_ref, nt_ref, ct_ref, wu_ref, wd_ref, gu_ref, gd_ref, gub_ref, act_ref, grad_ref, add):
    bias = jnp.concatenate([ubias[:, m * 512 + half_id * 256 : m * 512 + half_id * 256 + 256] for m in range(4)], axis=1)
    step = STEP
    gub_ref[...] = jnp.zeros_like(gub_ref)

    def block(r, carry):
        here = pl.ds(pl.multiple_of(r * step, step), step)
        w_up, w_down = wu_ref[...], wd_ref[...]
        act, slope = gelu_pair(dot(n_ref[here, :], w_up) + bias)
        act = act.astype(BF16)
        grad = dot(c_ref[here, :], w_down) * slope
        gub_ref[...] += jnp.sum(grad, axis=0, keepdims=True)
        grad = grad.astype(BF16)
        act_ref[here, :] = act
        grad_ref[here, :] = grad
        add(r, here, dot_cols(act, w_down), dot_cols(grad, w_up))
        return carry

    lax.fori_loop(0, n_ref.shape[0] // step, block, 0)
    gu_ref[...] = dot(nt_ref[...], grad_ref[...]).astype(BF16)
    gd_ref[...] = dot(ct_ref[...], act_ref[...]).astype(BF16)


def pull(block_of, row_of, near_ref, far_ref, parts):
    half, shard, _ = near_ref.shape

    def body(d, carry):
        for source, slot in ((near_ref, d), (far_ref, half + d)):
            here = pl.ds(pl.multiple_of(row_of[slot] * shard, 16), shard)
            for target, first, width, sem in parts:
                pltpu.make_async_copy(
                    source.at[d, :, first : first + width], target.at[here, columns(block_of[slot], width)], sem
                ).start()
        return carry

    lax.fori_loop(0, half, body, 0)


def push(block_of, row_of, keep_ref, send_ref, parts):
    half, shard, _ = keep_ref.shape

    def body(d, carry):
        for target, slot in ((keep_ref, d), (send_ref, half + d)):
            here = pl.ds(pl.multiple_of(row_of[slot] * shard, 16), shard)
            for source, first, width, sem in parts:
                pltpu.make_async_copy(
                    source.at[here, columns(block_of[slot], width)], target.at[d, :, first : first + width], sem
                ).start()
        return carry

    lax.fori_loop(0, half, body, 0)


def mlp_first_kernel(
    place_ref, offsets, block_of, row_of, xs_ref, att_ref, left_ref, obias, gain, shift, ubias, dbias, cot_ref,
    near_ref, far_ref,
    resid_ref, acc_ref, gn_ref, n_ref, c_ref, wo_ref, gub_ref, down_ref, keep_ref, send_ref,
    nt_ref, ct_ref, wu_ref, wd_ref, gu_ref, gd_ref, act_ref, grad_ref, wide_ref, low_ref, sem, out_sem,
):
    rows = xs_ref.shape[1]
    own = pl.ds(pl.multiple_of(place_ref[1] * rows, SPAN), rows)
    own_copy = pltpu.make_async_copy(cot_ref.at[:, own, :], low_ref, sem.at[3])
    own_copy.start()
    pull(block_of, row_of, near_ref, far_ref, ((wo_ref, 0, 128, sem.at[0]),))
    pull(block_of, row_of, near_ref, far_ref, ((wu_ref, 128, 256, sem.at[1]), (wd_ref, 384, 256, sem.at[2])))
    down_ref[...] = jnp.zeros_like(down_ref)
    own_copy.wait()
    pltpu.make_async_copy(wo_ref, wo_ref, sem.at[0]).wait()
    for mi in range(2):
        all_rows = slice(mi * rows, (mi + 1) * rows)
        wide_ref[0:SPAN, :] = left_ref[mi].astype(F32)
        wide_ref[SPAN : SPAN + rows, :] = low_ref[mi].astype(F32)
        for t in range(rows // SPAN):
            rolled = roll_rows(wide_ref, t * SPAN + offsets[mi])
            down_ref[...] += jnp.sum(rolled, axis=0, keepdims=True)
            c_ref[mi * rows + t * SPAN : mi * rows + (t + 1) * SPAN, :] = rolled.astype(BF16)
        resid = xs_ref[mi].astype(F32) + dot_cols(att_ref[mi], wo_ref[...]) + obias[...]
        resid_ref[all_rows, :] = resid
        hat, _ = unit(resid)
        normed = (hat * gain[...] + shift[...]).astype(BF16)
        n_ref[all_rows, :] = normed
        nt_ref[:, all_rows] = normed.T
        ct_ref[:, all_rows] = c_ref[all_rows, :].T
    pltpu.make_async_copy(wu_ref, wu_ref, sem.at[1]).wait()
    pltpu.make_async_copy(wd_ref, wd_ref, sem.at[2]).wait()

    def add(r, here, down, back):
        acc_ref[here, :] = (down + dbias[...]).astype(BF16)
        gn_ref[here, :] = back.astype(BF16)

    mlp_half(
        0, ubias, n_ref, c_ref, nt_ref, ct_ref, wu_ref, wd_ref, gu_ref, gd_ref, gub_ref, act_ref, grad_ref, add
    )
    push(block_of, row_of, keep_ref, send_ref, ((gu_ref, 0, 256, out_sem.at[0]), (gd_ref, 256, 256, out_sem.at[1])))
    pltpu.make_async_copy(gu_ref, gu_ref, out_sem.at[0]).wait()
    pltpu.make_async_copy(gd_ref, gd_ref, out_sem.at[1]).wait()


def mlp_second_kernel(
    block_of, row_of, att_ref, gain, ubias, resid_ref, acc_ref, gn_ref, n_ref, c_ref, wo_ref,
    near_ref, far_ref,
    result_ref, gmid_ref, gatt_ref, small_ref, gub_ref, keep_ref, send_ref,
    nt_ref, ct_ref, wu_ref, wd_ref, gu_ref, gd_ref, act_ref, grad_ref, go_ref, turned_ref, sem, out_sem,
):
    rows = att_ref.shape[1]
    pull(block_of, row_of, near_ref, far_ref, ((wu_ref, 0, 256, sem.at[0]), (wd_ref, 256, 256, sem.at[1])))
    small_ref[...] = jnp.zeros_like(small_ref)
    for mi in range(2):
        here = slice(mi * rows, (mi + 1) * rows)
        nt_ref[:, here] = n_ref[here, :].T
        ct_ref[:, here] = c_ref[here, :].T
    pltpu.make_async_copy(wu_ref, wu_ref, sem.at[0]).wait()
    pltpu.make_async_copy(wd_ref, wd_ref, sem.at[1]).wait()

    def add(r, here, down, back):
        mi = r // (rows // STEP)
        own = pl.ds(pl.multiple_of((r % (rows // STEP)) * STEP, STEP), STEP)
        result_ref[mi, own, :] = (resid_ref[here, :] + (acc_ref[here, :].astype(F32) + down)).astype(BF16)
        hat, inverse = unit(resid_ref[here, :])
        grad = gn_ref[here, :].astype(F32) + back
        small_ref[0:1, :] += jnp.sum(grad * hat, axis=0, keepdims=True)
        small_ref[1:2, :] += jnp.sum(grad, axis=0, keepdims=True)
        branch = (c_ref[here, :].astype(F32) + unit_back(grad * gain[...], hat, inverse)).astype(BF16)
        gmid_ref[mi, own, :] = branch
        small_ref[2:3, :] += jnp.sum(branch.astype(F32), axis=0, keepdims=True)
        gatt_ref[mi, own, :] = dot(branch, wo_ref[...]).astype(BF16)
        turned_ref[:, here] = branch.T

    mlp_half(
        1, ubias, n_ref, c_ref, nt_ref, ct_ref, wu_ref, wd_ref, gu_ref, gd_ref, gub_ref, act_ref, grad_ref, add
    )
    push(block_of, row_of, keep_ref, send_ref, ((gu_ref, 0, 256, out_sem.at[0]), (gd_ref, 256, 256, out_sem.at[1])))
    both = jnp.concatenate((att_ref[0], att_ref[1]), axis=0)
    go_ref[...] = dot(turned_ref[...], both).astype(BF16)
    push(block_of, row_of, keep_ref, send_ref, ((go_ref, 512, 128, out_sem.at[2]),))
    pltpu.make_async_copy(gu_ref, gu_ref, out_sem.at[0]).wait()
    pltpu.make_async_copy(gd_ref, gd_ref, out_sem.at[1]).wait()
    pltpu.make_async_copy(go_ref, go_ref, out_sem.at[2]).wait()


def attend_back_kernel(mi, place, offsets, lengths, qkv_ref, skv_ref, lse_ref, gatt_ref, *refs):
    grad_ref, pooled_ref, bias_ref = refs[-3:]
    rows = qkv_ref.shape[1]
    tiles = rows // SPAN
    summaries = skv_ref.shape[1]
    fill_masks(place, offsets, lengths, mi, bias_ref, tiles, summaries, summaries * SPAN)

    def heads(pair, carry):
        lanes = pl.ds(pl.multiple_of(pair * LANES, LANES), LANES)

        def columns(i):
            return pl.ds(pl.multiple_of(pair * 384 + i * LANES, LANES), LANES)

        _, skeys, svalues = pair_of(skv_ref, slice(None), pair)
        skeys_t = skeys.T
        sum_k = jnp.zeros((summaries, LANES), F32)
        sum_v = jnp.zeros((summaries, LANES), F32)
        held = []
        for t in range(tiles):
            here = slice(t * SPAN, (t + 1) * SPAN)
            queries, keys, values = pair_of(qkv_ref, here, pair)
            queries = split_heads(queries * SCALE)
            grads = split_heads(gatt_ref[0, here, lanes])
            bias = bias_ref[t]
            scores = dot_cols(jnp.concatenate((keys, skeys), axis=0), queries)
            gprobs = dot_cols(jnp.concatenate((values, svalues), axis=0), grads)
            held.append((queries, keys, grads, scores + jnp.concatenate((bias, bias), axis=1), gprobs))
        for t, (queries, keys, grads, scores, gprobs) in enumerate(held):
            here = slice(t * SPAN, (t + 1) * SPAN)
            probs = jnp.exp(scores - lse_ref[0, pair, t])
            delta = jnp.sum(probs * gprobs, axis=0, keepdims=True)
            gscores = (probs * (gprobs - delta)).astype(BF16)
            keys_t = jnp.concatenate((keys.T, skeys_t), axis=1)
            grad_q = join_heads(dot(keys_t, gscores)) * SCALE
            grad_k = dot(gscores, queries)
            grad_v = dot(probs.astype(BF16), grads)
            grad_ref[0, here, columns(0)] = grad_q.astype(BF16)
            grad_ref[0, here, columns(1)] = grad_k[:SPAN].astype(BF16)
            grad_ref[0, here, columns(2)] = grad_v[:SPAN].astype(BF16)
            sum_k += grad_k[SPAN:]
            sum_v += grad_v[SPAN:]
        pooled_ref[0, :, columns(0)] = jnp.zeros((summaries, LANES), BF16)
        pooled_ref[0, :, columns(1)] = sum_k.astype(BF16)
        pooled_ref[0, :, columns(2)] = sum_v.astype(BF16)
        return carry

    lax.fori_loop(0, 4, heads, 0)


def weights_back_kernel(
    apart, place_ref, offsets, lengths, block_of, row_of, slots_ref, xs_ref, grad_ref, pooled_ref, sums_ref, w_ref,
    gain, shift, small_ref, down_ref, gub1_ref, gub2_ref, line_ref, keep_ref, send_ref, *refs
):
    if apart:
        all_ref, *refs = refs
    gwb_ref, back_ref, stack_ref, pad_ref, sem = refs
    rows = xs_ref.shape[1]
    summaries = pooled_ref.shape[1]
    half = block_of.shape[0] // 2
    shard = keep_ref.shape[0] // half
    turned = []
    column = jnp.zeros((1, 3 * D), F32)
    for mi in range(2):
        _, offset, ends = row_info(place_ref, offsets, lengths, mi)
        first, last = summary_range(iota((summaries, 1), 0), offset, ends)
        root = jnp.sqrt((last - first + 1).astype(F32))
        hat, _ = unit(xs_ref[mi].astype(F32))
        turned += [hat.astype(BF16).T, sums_ref[mi].astype(BF16).T]
        column += jnp.sum(grad_ref[mi].astype(F32), axis=0, keepdims=True)
        column += jnp.sum(root * pooled_ref[mi].astype(F32), axis=0, keepdims=True)
        back_ref[mi] = dot_cols(pooled_ref[mi], w_ref[...]).astype(BF16)
    for base in range(0, stack_ref.shape[0], 32):
        names = [slots_ref[mi : mi + 1, 16 * base : 16 * base + 512] for mi in range(2)]
        spread = [
            jnp.where(iota((summaries, 1), 0) == named, 1.0, 0.0).astype(BF16).T for named in names
        ]
        piece = (dot(spread[0], back_ref[0]) + dot(spread[1], back_ref[1])).astype(BF16)
        for lane in range(D // LANES):
            part = piece[:, lane * LANES : (lane + 1) * LANES]
            stack_ref[base : base + 32, 16 * lane : 16 * lane + 16, :] = part.reshape(32, 16, LANES)

    def place(d):
        return pl.ds(pl.multiple_of(d * shard, 16), shard)

    def emit_sums(d, carry):
        for target, slot in ((keep_ref, d), (send_ref, half + d)):
            pltpu.make_async_copy(stack_ref.at[slot], target.at[place(d), 384:512], sem.at[1]).start()
        return carry

    def emit(m):
        def body(d, carry):
            for target, slot in ((keep_ref, d), (send_ref, half + d)):

                @pl.when(block_of[slot] == m)
                def _():
                    source = gwb_ref.at[pl.ds(pl.multiple_of(row_of[slot] * shard, 16), shard), m * 384 : (m + 1) * 384]
                    pltpu.make_async_copy(source, target.at[place(d), 0:384], sem.at[0]).start()

            return carry

        lax.fori_loop(0, half, body, 0)

    if not apart:
        lax.fori_loop(0, half, emit_sums, 0)
    turned = jnp.concatenate(turned, axis=1)
    gain_col, shift_col = gain[...].T, shift[...].T
    grad_gain = jnp.zeros((D, 1), F32)
    grad_shift = jnp.zeros((D, 1), F32)
    for m in range(4):
        cols = slice(m * 384, (m + 1) * 384)
        lanes = slice(m * LANES, (m + 1) * LANES)
        grads = jnp.concatenate([ref[mi, :, cols] for mi in range(2) for ref in (grad_ref, pooled_ref)], axis=0)
        hats, w, sums = dot(turned, grads), w_ref[:, cols].astype(F32), column[:, cols]
        grad_gain += jnp.sum(hats * w, axis=1, keepdims=True)
        grad_shift += jnp.sum(sums * w, axis=1, keepdims=True)
        gwb_ref[:, cols] = (hats * gain_col + shift_col * sums).astype(BF16)
        emit(m)
        line_ref[10:11, lanes] = sums[:, :128]
        line_ref[11:12, lanes] = sums[:, 256:]
    line_ref[8:9, :] = grad_gain.T
    line_ref[9:10, :] = grad_shift.T
    line_ref[0:3, :] = small_ref[0:3, :]
    line_ref[3:4, :] = down_ref[...]
    for i in range(4):
        for j, ref in enumerate((gub1_ref, gub2_ref)):
            line_ref[4 + i : 5 + i, j * 256 : (j + 1) * 256] = ref[:, i * 256 : (i + 1) * 256]
    line_ref[12:16, :] = jnp.zeros((4, D), F32)
    if apart:
        pltpu.make_async_copy(stack_ref, all_ref, sem.at[1]).start()
    else:
        high = line_ref[...].astype(BF16)
        pad_ref[0:16, :] = high
        pad_ref[16:32, :] = (line_ref[...] - high.astype(F32)).astype(BF16)
        size = half * shard
        copy = pltpu.make_async_copy(pad_ref, send_ref.at[size : size + 32, :], sem.at[2])
        copy.start()
        copy.wait()
    pltpu.make_async_copy(gwb_ref, gwb_ref, sem.at[0]).wait()
    pltpu.make_async_copy(stack_ref, stack_ref, sem.at[1]).wait()


def rows_back_kernel(grad_ref, w_ref, xs_ref, gmid_ref, result_ref, gain, part_ref, edge_ref):
    grad = dot_cols(grad_ref[0], w_ref[...]) * gain[...]
    hat, inverse = unit(xs_ref[0].astype(F32))
    part = gmid_ref[0].astype(F32) + unit_back(grad, hat, inverse)
    part_ref[0] = part
    edge_ref[0, 0] = part[0:SPAN].astype(BF16)
    edge_ref[1, 0] = result_ref[0]


def fold_kernel(keep_ref, mine_ref, got_ref, next_ref, *send_refs):
    size = keep_ref.shape[0]
    part = size // (1 + len(send_refs))
    mine = mine_ref[0:16, :].astype(F32) + mine_ref[16:32, :].astype(F32)
    lines = mine + (got_ref[size : size + 16, :].astype(F32) + got_ref[size + 16 : size + 32, :].astype(F32))
    high = lines.astype(BF16)
    rest = (lines - high.astype(F32)).astype(BF16)
    next_ref[...] = keep_ref[0:part, :].astype(F32) + got_ref[0:part, :].astype(F32)
    for i, send_ref in enumerate(send_refs):
        here = slice((i + 1) * part, (i + 2) * part)
        send_ref[0:part, :] = (keep_ref[here, :].astype(F32) + got_ref[here, :].astype(F32)).astype(BF16)
        send_ref[part : part + 16, :] = high
        if len(send_refs) == 1:
            send_ref[part + 16 : part + 32, :] = rest


def lines_of(ref):
    return ref[ref.shape[0] - 16 :, :].astype(F32)


def two_tiles(ref, right, mi, t):
    if (t + 2) * SPAN <= ref.shape[1]:
        return ref[mi, t * SPAN : (t + 2) * SPAN, :]
    return jnp.concatenate((ref[mi, t * SPAN :, :], right[mi].astype(ref.dtype)), axis=0)


def unroll_kernel(offsets, result_ref, right_ref, x_ref, out_ref, hat_ref, inverse_ref, wide_ref):
    mi = pl.program_id(0)
    for t in range(result_ref.shape[1] // SPAN):
        here = slice(t * SPAN, (t + 1) * SPAN)
        wide_ref[...] = two_tiles(result_ref, right_ref.at[0], 0, t).astype(F32)
        out_ref[0, here, :] = roll_rows(wide_ref, SPAN - offsets[mi]).astype(BF16)
        hat, inverse = unit(x_ref[0, here, :].astype(F32))
        hat_ref[0, here, :] = hat.astype(BF16)
        inverse_ref[0, here, :] = jnp.broadcast_to(inverse, (SPAN, LANES))


def finish_rest_kernel(keep_ref, got_ref, wo_ref, wu_ref, wd_ref):
    total = keep_ref[0] + got_ref[0].astype(F32)
    for i in range(2):
        wu_ref[:, i * 256 : (i + 1) * 256] = total[:, i * 512 : i * 512 + 256]
        wd_ref[:, i * 256 : (i + 1) * 256] = total[:, i * 512 + 256 : i * 512 + 512]
    wo_ref[...] = total[:, 1024:]


def finish_kernel(
    direct, place, offsets, lengths, hat_ref, inverse_ref, part_ref, right_ref, gain, *refs
):
    if direct:
        keep_ref, mine_ref, a_ref, b_ref, c_ref, out_ref, wq_ref, wk_ref, wv_ref, *line_refs, wide_ref = refs
        size = keep_ref.shape[0]
        total = (keep_ref[...] + a_ref[0:size, :].astype(F32)) + (
            b_ref[0:size, :].astype(F32) + c_ref[0:size, :].astype(F32)
        )
        wq_ref[...], wk_ref[...], wv_ref[...] = total[:, :128], total[:, 128:256], total[:, 256:384]
        pooled = total[:, 384:]
        lines = (lines_of(mine_ref) + lines_of(a_ref)) + (lines_of(b_ref) + lines_of(c_ref))
        ub_ref, *line_refs = line_refs
        for i in range(4):
            ub_ref[:, i * D : (i + 1) * D] = lines[4 + i : 5 + i, :]
        for ref, i in zip(line_refs, (0, 1, 2, 3, 8, 9, 10, 11)):
            ref[...] = lines[i : i + 1, :]
    else:
        pooled_ref, out_ref, wide_ref = refs
        pooled = pooled_ref[...]
    rows = hat_ref.shape[1]
    for mi in range(2):
        dev, offset, ends = row_info(place, offsets, lengths, mi)
        first, last = summary_range(dev * (rows // SPAN) + iota((8, 1), 0), offset, ends)
        lows = jnp.concatenate(
            [pooled[16 * i + 8 * mi : 16 * i + 8 * mi + 8, :] for i in range(D // LANES)], axis=1
        )
        lows = lows * gain[...] * lax.rsqrt((last - first + 1).astype(F32))
        level = (lows - jnp.mean(lows, axis=-1, keepdims=True)).astype(BF16)
        lows = lows.astype(BF16)
        first, last = summary_range(dev * (rows // SPAN) + iota((1, 8), 1), offset, ends)
        for t in range(rows // SPAN):
            here = slice(t * SPAN, (t + 1) * SPAN)
            pos = dev * rows + t * SPAN + iota((SPAN, 1), 0)
            member = jnp.where((pos >= first) & (pos <= last), 1.0, 0.0)
            hat = hat_ref[mi, here, :]
            slope = jnp.sum(member * dot_cols(hat, lows), axis=1, keepdims=True) * (1.0 / D)
            inverse = inverse_ref[mi, here, 0:1]
            wide_ref[...] = two_tiles(part_ref, right_ref.at[0], mi, t)
            own = roll_rows(wide_ref, SPAN - offset)
            out_ref[mi, here, :] = own + (dot(member.astype(BF16), level) - hat.astype(F32) * slope) * inverse


def call(kernel, outs, in_specs, out_specs=None, scratch=(), limit=8, **more):
    return pl.pallas_call(
        kernel,
        out_shape=outs,
        in_specs=in_specs,
        out_specs=out_specs if out_specs is not None else [VMEM] * len(outs),
        scratch_shapes=list(scratch),
        compiler_params=pltpu.CompilerParams(vmem_limit_bytes=limit * MIB),
        cost_estimate=pl.CostEstimate(flops=1, bytes_accessed=1, transcendentals=0),
        **more,
    )


def call_row(kernel, mi, facts, arrays, outs, before, scratch, **more):
    def block(dims):
        return pl.BlockSpec((1,) + dims[1:], lambda i: (mi,) + (0,) * (len(dims) - 1))

    aliases = {3 + len(arrays) + i: i for i in range(len(before))}
    return call(
        partial(kernel, mi), outs, [SMEM] * 3 + [block(a.shape) for a in arrays] + [ANY] * len(before),
        [block(o.shape) for o in outs], scratch, grid=(1,), input_output_aliases=aliases, **more,
    )(*facts, *arrays, *before)


def tie(value, *others):
    return lax.optimization_barrier((value,) + others)[0]


def per_device(
    block_input, cotangent, span_offset, doc_lengths, ln1_gain, ln1_bias, w_query, w_key, w_value,
    query_bias, value_bias, w_out, out_bias, ln2_gain, ln2_bias, w_up, up_bias, w_down, down_bias,
):
    groups, ranks = lax.axis_size("seq"), lax.axis_size("mp")
    count = groups * ranks
    mp_index = lax.axis_index("mp")
    dev = lax.axis_index("seq") * ranks + mp_index
    rows = block_input.shape[1]
    tiles = rows // SPAN
    summaries = tiles * count
    shard = w_query.shape[0]
    bits = count.bit_length() - 1
    stages = [(b, b) for b in range(bits - 1, 2, -1)] + [(1, 2), (2, 1)]
    direct = shard == 64

    def swap(value, stage):
        pairs = [(i, i ^ (1 << stage[i & 1])) for i in range(count)]
        return lax.ppermute(value, AXES, pairs)

    def turn(value, by):
        return lax.ppermute(value, AXES, [(i, (i + by) % count) for i in range(count)])

    core = dev & 1
    slot = jnp.arange(count, dtype=jnp.int32)
    far = slot // (count // 2)
    mask = far
    for i, (even, odd) in enumerate(stages):
        where = jnp.where((core ^ far) == 0, even, odd)
        mask = mask | (((slot >> i) & 1) << where)
    owner = dev ^ mask
    if not direct:
        owner = slot
    member_slot = jnp.arange(16, dtype=jnp.int32)
    slots = owner[:, None] * tiles + (member_slot % 8)[None, :]
    valid = (member_slot % 8 <= tiles)[None, :]
    slots = jnp.stack(
        [
            jnp.where(valid & (member_slot // 8 == mi)[None, :], slots, -1).reshape(-1)
            for mi in range(2)
        ]
    )
    block_of, row_of = owner % ranks, owner // ranks
    facts = (jnp.stack((dev, mp_index)), span_offset, doc_lengths)

    def reach(value, flip):
        return lax.ppermute(value, AXES, [(i, i ^ flip) for i in range(count)])

    def spread(values):
        return [reach(value, flip) for value, flip in zip(values, (16, 8, 24))]

    def join(near, far):
        return jnp.concatenate((near, far), axis=0)

    def fold(keep, got):
        total = keep + got.astype(F32)
        half = total.shape[0] // 2
        return total[:half], total[half:].astype(BF16)

    def whole_blocks(arrays):
        return [pl.BlockSpec(a.shape, lambda i, n=len(a.shape): (0,) * n) for a in arrays]

    def fold_lines(keep, sent, got, sends=1):
        size = keep.shape[0]
        part = size // (1 + sends)
        outs = [shape((part, D), F32)] + [shape((part + (32 if sends == 1 else 16), D), BF16)] * sends
        mine = pl.BlockSpec((32, D), lambda i: (size // 32, 0))
        both = whole_blocks((keep, got))
        return call(fold_kernel, outs, [both[0], mine, both[1]], whole_blocks(outs), grid=(1,))(keep, sent, got)

    def gather_whole(value):
        both = lax.all_gather(value, "seq", axis=0, tiled=True)
        both = lax.all_gather(both, "mp", axis=0)
        return both[: ranks // 2], both[ranks // 2 :]

    def scatter_whole(keep, send):
        both = jnp.concatenate((keep, send), axis=0).astype(F32)
        total = lax.psum_scatter(both, "mp", scatter_dimension=0, tiled=True)[0]
        return lax.psum_scatter(total, "seq", scatter_dimension=0, tiled=True)

    def row(vector):
        return vector[None, :]

    def shape(dims, kind):
        return jax.ShapeDtypeStruct(dims, kind)

    half, tall = (count // 2, shard) if direct else (ranks // 2, shard * groups)
    width = 4 * LANES if direct else 3 * LANES
    apart = not direct
    wide, three = (2, rows, D), (2, rows, 3 * D)
    flat, pooled_dims = (2 * rows, D), (2, summaries, D)
    room = 12 if direct else 56
    masks = [pltpu.VMEM((tiles, SPAN + summaries, SPAN), F32)]

    def prepare():
        return call(
            prepare_kernel, [shape((1, max(shard, 64), D), BF16), shape((1, shard, 1152), BF16), shape((2, SPAN, D), BF16)],
            [SMEM] * 3 + [HBM] * 8, [VMEM] * 3,
            scratch=[pltpu.VMEM(wide, BF16), pltpu.SemaphoreType.DMA((11,))],
            limit=56,
        )(*facts, block_input, cotangent, w_query, w_key, w_value, w_out.T, w_up, w_down.T)

    part_a, w_rest, cot_edge = prepare()
    x_edge = block_input[:, rows - SPAN :]
    if direct:
        got_a = spread([part_a] * 3)
        part_b = tie(w_rest, got_a[0])
        got_b = swap(part_b, stages[0])
        part_a = jnp.concatenate([part_a] + got_a, axis=0)
        x_left = turn(tie(x_edge, part_a), 1)
        got_a = swap(part_a, stages[2])
        part_a = join(part_a, got_a)
        part_b = join(part_b, tie(got_b, part_a))
        got_a, got_b = swap(part_a, stages[3]), swap(part_b, stages[1])
        near_a = join(part_a, tie(got_a, x_left))
        far_a = swap(near_a, (0, 0))
        part_b = join(part_b, tie(got_b, near_a))
        got_b = swap(part_b, stages[2])
        more = ()
    else:
        x_left, cot_left = turn(x_edge, 1), turn(cot_edge, 1)
        near_a, far_a = gather_whole(part_a[0, :shard, :384])
        near_b, far_b = gather_whole(w_rest[0])
        near_1, near_2, far_1, far_2 = (a[:, :, i : i + w] for a in (near_b, far_b) for i, w in ((0, 640), (640, 512)))
        more = (lax.all_gather(part_a[0, :64, 384:], AXES, axis=0),)
        block_of, row_of = jnp.arange(ranks, dtype=jnp.int32), jnp.zeros((ranks,), jnp.int32)

    xs, qkv, skv, sums, w_full = call(
        partial(project_kernel, apart),
        [shape(wide, BF16), shape(three, BF16), shape((2, summaries, 3 * D), BF16), shape(pooled_dims, F32)]
        + [shape((D, 3 * D), BF16)],
        [SMEM] * 5 + [VMEM] * 7 + [ANY] * (2 + len(more)),
        scratch=[
            pltpu.VMEM((count, 64, LANES), BF16),
            pltpu.VMEM((rows + SPAN, D), F32),
            pltpu.VMEM((2, rows + 2 * summaries, D), BF16),
            pltpu.SemaphoreType.DMA((2,)),
        ],
        limit=24 if direct else 56,
    )(
        *facts, block_of, row_of, slots, block_input, x_left, row(ln1_gain), row(ln1_bias),
        row(query_bias), row(value_bias), near_a, far_a, *more,
    )
    outs = [shape(wide, BF16), shape((2, 4, tiles, 1, 2 * SPAN), F32)]
    if direct:
        cot_left = turn(tie(cot_edge, near_a), 1)
        part_b = join(part_b, tie(got_b, skv, cot_left))
        part_1, part_2 = part_b[:, :, :640], part_b[:, :, 640:]
        got_1 = swap(part_1, stages[3])
        qkv = tie(qkv, part_1)
    seen = call_row(attend_kernel, 0, facts, (qkv, skv), outs, (), masks, limit=room)
    att, lse = call_row(attend_kernel, 1, facts, (qkv, skv), outs, tuple(seen), masks, limit=room)
    if direct:
        near_1 = join(part_1, tie(got_1, att))
        far_1 = swap(near_1, (0, 0))
        got_2 = swap(tie(part_2, near_1), stages[3])
    tall_low, tall_float = shape(flat, BF16), shape(flat, F32)
    weights = [pltpu.VMEM((D, 2 * rows), BF16)] * 2 + [pltpu.VMEM((D, FF // 2), BF16)] * 4
    weights += [pltpu.VMEM((2 * rows, FF // 2), BF16)] * 2
    *kept, gub_1, down_b, keep_1, send_1 = call(
        mlp_first_kernel,
        [tall_float] + [tall_low] * 4 + [shape((D, D), BF16)]
        + [shape((1, FF // 2), F32), shape((1, D), F32)] + [shape((half, tall, 512), BF16)] * 2,
        [SMEM] * 4 + [VMEM] * 8 + [HBM] + [ANY] * 2,
        [VMEM] * 8 + [ANY] * 2,
        scratch=weights
        + [pltpu.VMEM((rows + SPAN, D), F32), pltpu.VMEM(wide, BF16)]
        + [pltpu.SemaphoreType.DMA((4,)), pltpu.SemaphoreType.DMA((2,))],
        limit=28,
    )(
        facts[0], span_offset, block_of, row_of, xs, att, cot_left, row(out_bias), row(ln2_gain), row(ln2_bias),
        row(up_bias), row(down_bias), cotangent, near_1, far_1,
    )
    if direct:
        near_2 = join(part_2, tie(got_2, kept[0]))
        far_2 = swap(near_2, (0, 0))
        got_1 = swap(tie(send_1, near_2), (0, 0))
        keep_1, send_1 = fold(keep_1.astype(F32), got_1)
        got_1 = swap(send_1, stages[3])
        near_2 = tie(near_2, send_1)
    result, gmid, gatt, small_b, gub_2, keep_2, send_2 = call(
        mlp_second_kernel,
        [shape(wide, BF16)] * 3 + [shape((8, D), F32)]
        + [shape((1, FF // 2), F32)] + [shape((half, tall, 640), BF16)] * 2,
        [SMEM] * 2 + [VMEM] * 9 + [ANY] * 2,
        [VMEM] * 5 + [ANY] * 2,
        scratch=weights
        + [pltpu.VMEM((D, D), BF16), pltpu.VMEM((D, 2 * rows), BF16)]
        + [pltpu.SemaphoreType.DMA((2,)), pltpu.SemaphoreType.DMA((3,))],
        limit=28,
    )(block_of, row_of, att, row(ln2_gain), row(up_bias), *kept, near_2, far_2)
    gubs = (gub_1, gub_2)
    arrays = (qkv, skv, lse, gatt)
    outs = [shape(three, BF16), shape((2, summaries, 3 * D), BF16)]
    if direct:
        keep_1, send_1 = fold(keep_1, tie(got_1, send_2))
        got_2 = swap(tie(send_2, send_1), (0, 0))
        got_1 = swap(send_1, stages[2])
    grads = call_row(attend_back_kernel, 0, facts, arrays, outs, (), masks, limit=room)
    if direct:
        keep_2, send_2 = fold(keep_2.astype(F32), tie(got_2, grads[0]))
        got_2 = swap(send_2, stages[3])
        grads = [tie(grads[0], send_2)] + list(grads[1:])
    grads = call_row(attend_back_kernel, 1, facts, arrays, outs, tuple(grads), masks, limit=room)
    if direct:
        keep_1, send_1 = fold(keep_1, tie(got_1, grads[0]))
        grads = [tie(grads[0], send_1), grads[1]]
    lines, keep_a, send_a, *more = call(
        partial(weights_back_kernel, apart),
        [shape((16, D), F32)]
        + [shape((half * tall, width), BF16), shape((half * tall + (32 if direct else 0), width), BF16)]
        + [shape((count, 64, LANES), BF16)] * apart,
        [SMEM] * 5 + [VMEM] * 12,
        [VMEM] + [ANY] * (2 + apart),
        scratch=[
            pltpu.VMEM((D, 3 * D), BF16), pltpu.VMEM(pooled_dims, BF16), pltpu.VMEM((count, 64, LANES), BF16),
            pltpu.VMEM((32, D), BF16), pltpu.SemaphoreType.DMA((3,)),
        ],
        limit=24 if direct else 56,
    )(
        *facts, block_of, row_of, slots, xs, *grads, sums, w_full, row(ln1_gain), row(ln1_bias), small_b, down_b, *gubs,
    )

    def by_row(dims):
        return pl.BlockSpec((1,) + dims[1:], lambda i: (i,) + (0,) * (len(dims) - 1))

    once = pl.BlockSpec((1, D), lambda i: (0, 0))
    edge_dims = (2, SPAN, D)

    def rows_back(*after):
        return call(
            rows_back_kernel, [shape(wide, F32), shape((2,) + edge_dims, BF16)],
            [by_row(three), pl.BlockSpec((D, 3 * D), lambda i: (0, 0)), by_row(wide), by_row(wide)]
            + [by_row(edge_dims), once],
            [by_row(wide), pl.BlockSpec((2, 1, SPAN, D), lambda i: (0, i, 0, 0))], grid=(2,), limit=16,
        )(grads[0], tie(w_full, *after), xs, gmid, result, row(ln1_gain))

    def unroll(back):
        return call(
            unroll_kernel, [shape(wide, BF16)] * 2 + [shape((2, rows, LANES), F32)],
            [SMEM, by_row(wide), pl.BlockSpec((1, 1, SPAN, D), lambda i: (1, i, 0, 0)), by_row(wide)], [by_row(wide)] * 2 + [by_row((2, rows, LANES))],
            [pltpu.VMEM((2 * SPAN, D), F32)], grid=(2,),
        )(span_offset, result, back, block_input)

    final = [SMEM] * 3 + [VMEM] * 5
    rolled = [pltpu.VMEM((2 * SPAN, D), F32)]
    if direct:
        got_a = swap(send_a, (0, 0))
        keep_2, send_2 = fold(keep_2, tie(got_2, send_a))
        got_2 = swap(send_2, stages[2])
        keep_a, send_a = fold_lines(keep_a, send_a, tie(got_a, send_2))
        got_a = swap(send_a, stages[3])
        part, edge = rows_back(send_a)
        keep_2, send_2 = fold(keep_2, tie(got_2, part))
        keep_b, send_b = (jnp.concatenate(a, axis=2) for a in ((keep_1, keep_2), (send_1, send_2)))
        got_b = swap(send_b, stages[1])
        back = turn(tie(edge, send_b), -1)
        keep_a, send_a = fold_lines(keep_a, send_a, tie(got_a, send_b))
        got_a = swap(send_a, stages[2])
        keep_b, send_b = fold(keep_b, tie(got_b, send_a))
        got_b = swap(send_b, stages[0])
        keep_a, *send_a = fold_lines(keep_a, send_a, tie(got_a, send_b), 3)
        got_a = spread(send_a)
        result_own, *hats = unroll(tie(back, send_a[0]))
        grad_wo, grad_wu, grad_wd = call(
            finish_rest_kernel, [shape((shard, LANES), F32), shape((shard, 512), F32), shape((shard, 512), F32)],
            [VMEM] * 2,
        )(keep_b, tie(got_b, send_a[0]))
        input_grad, grad_wq, grad_wk, grad_wv, grad_ub, *small = call(
            partial(finish_kernel, True),
            [shape(wide, F32)] + [shape((shard, LANES), F32)] * 3 + [shape((1, FF), F32)] + [shape((1, D), F32)] * 8,
            final + [VMEM] * 5, scratch=rolled, limit=16,
        )(*facts, *hats, part, back, row(ln1_gain), keep_a, send_a[0], *(tie(got, grad_wo) for got in got_a))
        grad_wo, grad_wd = grad_wo.T, grad_wd.T
        small = [a.reshape(D) for a in small]
        grad_ub = grad_ub.reshape(FF)
    else:
        keep_a, send_a = (a.reshape(half, tall, width) for a in (keep_a, send_a))
        part, edge = rows_back()
        back = turn(edge, -1)
        result_own, *hats = unroll(back)
        sum_a, sum_1, sum_2 = (scatter_whole(*a) for a in ((keep_a, send_a), (keep_1, send_1), (keep_2, send_2)))
        grad_wq, grad_wk, grad_wv = (sum_a[:, i : i + LANES] for i in (0, 128, 256))
        grad_wo = sum_2[:, 512:].T
        grad_wu, grad_wd = (
            jnp.concatenate((sum_1[:, i : i + 256], sum_2[:, i : i + 256]), axis=1) for i in (0, 256)
        )
        grad_wd = grad_wd.T
        pooled = lax.psum_scatter(more[0].astype(F32), AXES, scatter_dimension=0, tiled=True)[0]
        lines = lax.psum(lines, AXES)
        grad_ub = lines[4:8].reshape(FF)
        small = [lines[i] for i in (0, 1, 2, 3, 8, 9, 10, 11)]
        input_grad = call(partial(finish_kernel, False), [shape(wide, F32)], final + [VMEM], scratch=rolled, limit=16)(
            *facts, *hats, part, back, row(ln1_gain), pooled
        )[0]
    grad_gain_two, grad_shift_two, grad_obias, grad_dbias, grad_gain_one, grad_shift_one, grad_qb, grad_vb = small
    return (
        result_own,
        input_grad,
        grad_gain_one,
        grad_shift_one,
        grad_wq,
        grad_wk,
        grad_wv,
        grad_qb,
        grad_vb,
        grad_wo,
        grad_obias,
        grad_gain_two,
        grad_shift_two,
        grad_wu,
        grad_ub,
        grad_wd,
        grad_dbias,
    )


def solution(mesh):
    vector, matrix, turned = P(), P("seq", "mp"), P("mp", "seq")
    own, group = P(None, ("seq", "mp"), None), P(None, "seq", None)
    return jax.shard_map(
        per_device,
        mesh=mesh,
        in_specs=(own, group, vector, vector, vector, vector, matrix, matrix, matrix, vector, vector)
        + (turned, vector, vector, vector, matrix, vector, turned, vector),
        out_specs=(own, own, vector, vector, matrix, matrix, matrix, vector, vector, turned, vector)
        + (vector, vector, matrix, vector, turned, vector),
        check_vma=False,
    )
```
